32 devices in a mesh: species: 2 (over x), cells: 16 (over z, y, core).
Axes of the slice: x: 2, y: 2, z: 4, core: 2. Of those that a mesh axis runs over, the one named last changes fastest.
Arguments:
- tokens: bfloat16 [2, 32, 256, 768], P('species', 'cells'), may hold values from -6 to 6
- lengths: int32 [2, 32], P('species', 'cells'), may hold values from 1 to 256, as said below
- cotangent: bfloat16 [2, 32, 256, 768], P('species', 'cells'), may hold values from -6 to 6
- first_gain: bfloat16 [768], P('cells'), may hold values from 0.099609375 to 1.8984375
- first_shift: bfloat16 [768], P('cells'), may hold values from -1.75 to 1.75
- qkv_weight: bfloat16 [768, 2304], P('cells'), may hold values from -0.21875 to 0.21875
- qv_bias: bfloat16 [1536], P('cells'), may hold values from -3 to 3
- out_weight: bfloat16 [768, 768], P('cells'), may hold values from -1.25 to 1.25
- out_bias: bfloat16 [768], P('cells'), may hold values from -1.75 to 1.75
- second_gain: bfloat16 [768], P('cells'), may hold values from 0.099609375 to 1.8984375
- second_shift: bfloat16 [768], P('cells'), may hold values from -1.75 to 1.75
- in_weight: bfloat16 [768, 3072], P('cells'), may hold values from -0.21875 to 0.21875
- in_bias: bfloat16 [3072], P('cells'), may hold values from -3 to 3
- down_weight: bfloat16 [3072, 768], P('cells'), may hold values from -0.109375 to 0.109375
- down_bias: bfloat16 [768], P('cells'), may hold values from -1.75 to 1.75
Outputs:
- out_tokens: bfloat16 [2, 32, 256, 768], P('species', 'cells')
- grad_tokens: bfloat16 [2, 32, 256, 768], P('species', 'cells')
- grad_first_gain: float32 [768], P('cells')
- grad_first_shift: float32 [768], P('cells')
- grad_qkv_weight: float32 [768, 2304], P('cells')
- grad_qv_bias: float32 [1536], P('cells')
- grad_out_weight: float32 [768, 768], P('cells')
- grad_out_bias: float32 [768], P('cells')
- grad_second_gain: float32 [768], P('cells')
- grad_second_shift: float32 [768], P('cells')
- grad_in_weight: float32 [768, 3072], P('cells')
- grad_in_bias: float32 [3072], P('cells')
- grad_down_weight: float32 [3072, 768], P('cells')
- grad_down_bias: float32 [768], P('cells')
The draws below stay inside these ranges and needn't reach their ends.
Inputs may be any that keep to these rules, and one draw needn't show every extreme that they name: `lengths`: some cell has exactly 256 true tokens.
All inputs are finite; a program needn't handle non-finite values.
Results may differ from the reference program's by a relative error of at most 0.013.
Values may be sent and summed in bfloat16 or wider, within the bound.
No kernel may reach another device: no remote copies, remote signals or barrier semaphores. Data moves between devices by JAX's collectives and lax.ppermute only.
A program may use at most 128 MiB of HBM per device.

```python
import jax
import jax.numpy as jnp
from jax import lax

D = 768
HEAD = 64
FF = 3072
LEN = 256
NSEQ = 32
N_SPECIES = 2


def draw_lengths(key, part):
    key = jax.random.fold_in(key, 11)
    first_key, second_key, third_key = jax.random.split(key, 3)
    position = jnp.arange(NSEQ, dtype=jnp.int32)
    ceiling = LEN // 3 + (LEN - LEN // 3) * position // max(NSEQ - 1, 1)
    ceiling = jnp.stack([ceiling, jnp.maximum(ceiling * 3 // 4, 1)])
    factor_one = jax.random.randint(first_key, (N_SPECIES, NSEQ), 0, 16)
    factor_two = jax.random.randint(second_key, (N_SPECIES, NSEQ), 0, 16)
    lengths_out = ceiling - ceiling * factor_one * factor_two // 512
    chosen = jax.random.randint(third_key, (), 0, NSEQ)
    longest = (position == chosen)[None, :] & (jnp.arange(N_SPECIES)[:, None] == 0)
    return jnp.where(longest, LEN, lengths_out).astype(jnp.int32)


def spiked(entries, key, source, target, parts, factor):
    owner, partner = [(jnp.arange(entries.shape[dim]) // (entries.shape[dim] // parts)).reshape([-1 if axis == dim else 1 for axis in range(entries.ndim)]) for dim in (source, target)]
    chosen = jax.random.permutation(key, parts)[partner]
    strong = (owner == chosen) | (owner == (partner + parts // 2) % parts)
    return jnp.where(strong, factor * entries, entries)


def steps_of(own_key, shape, pieces, least, high):
    loudness = 1.0
    for dim, parts in pieces:
        heights = jax.random.uniform(jax.random.fold_in(jax.random.fold_in(own_key, 6), dim), (parts,), jnp.float32, least / len(pieces), high / len(pieces))
        loudness = loudness * jnp.repeat(jnp.exp(heights), shape[dim] // parts).reshape((-1,) + (1,) * (len(shape) - 1 - dim))
    return loudness


def noise(rng, shape, scale, bound, pieces=(), kind=jnp.bfloat16):
    array = scale * jax.random.normal(rng, shape, jnp.float32)
    if pieces:
        array = array * steps_of(rng, shape, pieces, -0.22, 0.18)
    return jnp.clip(array, -bound, bound).astype(kind)


def bell_draw_with(key, shape, deviation, reach, pieces, heavy, held_as=jnp.bfloat16):
    array = deviation * jax.random.normal(key, shape, jnp.float32)
    if pieces:
        array = array * steps_of(key, shape, pieces, -0.22, 0.18)
    return jnp.clip(spiked(array, jax.random.fold_in(key, 3), *heavy), -reach, reach).astype(held_as)


def setup_inputs(seed: int = 0) -> dict:
    key_of = jax.random.split(jax.random.key(seed), 16)
    tokens = bell_draw_with(key_of[0], (N_SPECIES, NSEQ, LEN, D), 1.0, 6.0, ((0, 2), (1, 16)), (1, 3, 16, 2.0))
    lengths = draw_lengths(jax.random.fold_in(key_of[15], 71), 0)
    cotangent = noise(key_of[2], (N_SPECIES, NSEQ, LEN, D), 1.0, 6.0, ((0, 2), (1, 16)))
    first_gain = jnp.clip(1.0 + 0.18 * jax.random.normal(key_of[3], (D,), jnp.float32), 0.099609375, 1.8984375).astype(jnp.bfloat16)
    first_shift = noise(key_of[4], (D,), 0.3, 1.75, ((0, 16),))
    qkv_weight = noise(key_of[5], (D, 3 * D), D ** -0.5, 0.21875, ((0, 16),))
    qv_bias = noise(key_of[6], (2 * D,), 0.5, 3.0, ((0, 16),))
    out_weight = noise(key_of[7], (D, D), (D // 32) ** -0.5, 1.25, ((0, 16),))
    out_bias = noise(key_of[8], (D,), 0.3, 1.75, ((0, 16),))
    second_gain = jnp.clip(1.0 + 0.18 * jax.random.normal(key_of[9], (D,), jnp.float32), 0.099609375, 1.8984375).astype(jnp.bfloat16)
    second_shift = noise(key_of[10], (D,), 0.3, 1.75, ((0, 16),))
    in_weight = noise(key_of[11], (D, FF), D ** -0.5, 0.21875, ((0, 16),))
    in_bias = noise(key_of[12], (FF,), 0.5, 3.0, ((0, 16),))
    down_weight = noise(key_of[13], (FF, D), FF ** -0.5, 0.109375, ((0, 16),))
    down_bias = noise(key_of[14], (D,), 0.3, 1.75, ((0, 16),))
    return {"tokens": tokens, "lengths": lengths, "cotangent": cotangent, "first_gain": first_gain, "first_shift": first_shift, "qkv_weight": qkv_weight, "qv_bias": qv_bias, "out_weight": out_weight, "out_bias": out_bias, "second_gain": second_gain, "second_shift": second_shift, "in_weight": in_weight, "in_bias": in_bias, "down_weight": down_weight, "down_bias": down_bias}


@jax.custom_vjp
def low(v):
    return lax.optimization_barrier(v.astype(jnp.bfloat16)).astype(jnp.float32)

@jax.custom_vjp
def low_back(v):
    return v

def low_keep(v):
    return (low(v), None)

def low_pass(kept, grad):
    return (grad,)

def back_keep(v):
    return (v, None)

def back_low(kept, grad):
    return (low(grad),)
low.defvjp(low_keep, low_pass)
low_back.defvjp(back_keep, back_low)
HIGHEST_PRECISION = lax.Precision.HIGHEST
EPSILON = 1e-12
NEGATIVE = -1e+30

def normalize(values, gain_vec, shift_vec):
    center = values - lax.optimization_barrier(jnp.mean(values, axis=-1, keepdims=True))
    spread = lax.optimization_barrier(jnp.mean(center * center, axis=-1, keepdims=True))
    return center * lax.rsqrt(spread + EPSILON) * gain_vec + shift_vec

def sequence_layer(inputs, length, weights):
    first_gain, first_shift, qkv_weight, qv_bias, out_weight, out_bias, second_gain, second_shift, in_weight, in_bias, down_weight, down_bias = weights
    seq_rows = inputs.shape[0]
    model_width = inputs.shape[1]
    heads_count = model_width // HEAD
    first_low = low(normalize(inputs, first_gain, first_shift))
    full_bias = jnp.concatenate([qv_bias[:model_width], jnp.zeros((model_width,), inputs.dtype), qv_bias[model_width:]])
    projected = low_back(low(jnp.dot(first_low, qkv_weight, precision=HIGHEST_PRECISION) + full_bias))
    split_heads = projected.reshape(seq_rows, 3, heads_count, HEAD)
    queries = split_heads[:, 0]
    keys_part = split_heads[:, 1]
    values_part = split_heads[:, 2]
    raw_scores = jnp.einsum('qhd,khd->hqk', queries, keys_part, precision=HIGHEST_PRECISION)
    scaled = low_back(raw_scores * float(HEAD) ** (-0.5))
    visible = jnp.arange(seq_rows) < length
    masked = jnp.where(visible[None, None, :], scaled, NEGATIVE)
    attention = low(jax.nn.softmax(masked, axis=-1))
    mixed = jnp.einsum('hqk,khd->qhd', attention, values_part, precision=HIGHEST_PRECISION)
    mixed = low_back(low(mixed.reshape(seq_rows, model_width)))
    middle = inputs + low_back(jnp.dot(mixed, out_weight, precision=HIGHEST_PRECISION) + out_bias)
    second_low = low(normalize(middle, second_gain, second_shift))
    inner = low_back(jnp.dot(second_low, in_weight, precision=HIGHEST_PRECISION) + in_bias)
    active = low(jax.nn.gelu(inner, approximate=False))
    return middle + low_back(jnp.dot(active, down_weight, precision=HIGHEST_PRECISION) + down_bias)

def group_layer(weights, group_rows, group_lengths):

    def single(seq_input, seq_length):
        return sequence_layer(seq_input, seq_length, weights)
    return jax.vmap(single)(group_rows, group_lengths)

def forward_all(inputs_all, flat_lengths, weights):
    per_step = 4
    grouped = inputs_all.reshape(-1, per_step, inputs_all.shape[1], inputs_all.shape[2])
    grouped_lengths = flat_lengths.reshape(-1, per_step)
    checked = jax.checkpoint(group_layer)

    def scan_step(carry, item):
        return (carry, checked(weights, item[0], item[1]))
    _, results = lax.scan(scan_step, jnp.zeros((), jnp.float32), (grouped, grouped_lengths))
    return results.reshape(inputs_all.shape)

def reference(tokens, lengths, cotangent, first_gain, first_shift, qkv_weight, qv_bias, out_weight, out_bias, second_gain, second_shift, in_weight, in_bias, down_weight, down_bias):
    weights = jax.tree.map(lambda entry: entry.astype(jnp.float32), (first_gain, first_shift, qkv_weight, qv_bias, out_weight, out_bias, second_gain, second_shift, in_weight, in_bias, down_weight, down_bias))
    inputs_all = tokens.astype(jnp.float32).reshape(-1, LEN, D)
    flat_lengths = lengths.reshape(-1)
    count = jnp.sum(lengths).astype(jnp.float32)

    def whole_layer(layer_inputs, layer_weights):
        return forward_all(layer_inputs, flat_lengths, layer_weights)
    outputs, pullback = jax.vjp(whole_layer, inputs_all, weights)
    visible = (jnp.arange(LEN)[None, :] < flat_lengths[:, None]).astype(jnp.float32)
    factor = float(N_SPECIES * NSEQ * LEN) / count
    upstream = cotangent.astype(jnp.float32).reshape(inputs_all.shape) * visible[:, :, None] * factor
    grad_inputs, grad_weights = pullback(upstream)
    return (outputs.reshape(tokens.shape).astype(jnp.bfloat16), grad_inputs.reshape(tokens.shape).astype(jnp.bfloat16), grad_weights[0], grad_weights[1], grad_weights[2], grad_weights[3], grad_weights[4], grad_weights[5], grad_weights[6], grad_weights[7], grad_weights[8], grad_weights[9], grad_weights[10], grad_weights[11])
```

```python
import jax
import jax.numpy as jnp
from jax import lax
from jax.experimental import pallas as pl
from jax.experimental.pallas import tpu as pltpu
from jax.sharding import PartitionSpec as P

HEAD = 64


EPSILON = 1e-12
NEGATIVE = -1e30


def normalize(values, gain_vec, shift_vec):
    center = values - jnp.mean(values, axis=-1, keepdims=True)
    spread = jnp.mean(center * center, axis=-1, keepdims=True)
    return center * lax.rsqrt(spread + EPSILON) * gain_vec + shift_vec


def smooth_gate(values):
    return jax.nn.gelu(values, approximate=False)


def times_left(left_side, right_side):
    return lax.dot_general(
        left_side, right_side, (((0,), (0,)), ((), ())), preferred_element_type=jnp.float32
    )


def times_right(left_side, right_side):
    return lax.dot_general(
        left_side, right_side, (((1,), (1,)), ((), ())), preferred_element_type=jnp.float32
    )


def sequence_pass(weights, inputs, length, cot_rows, factor):
    (
        first_gain,
        first_shift,
        qkv_weight,
        qv_bias,
        out_weight,
        out_bias,
        second_gain,
        second_shift,
        in_weight,
        in_bias,
        down_weight,
        down_bias,
    ) = weights
    seq_rows = inputs.shape[0]
    model_width = inputs.shape[1]
    heads_count = model_width // HEAD
    scale_qk = float(HEAD) ** (-0.5)
    as_float = inputs.astype(jnp.float32)
    hidden_one, first_pull = jax.vjp(
        normalize, as_float, first_gain.astype(jnp.float32), first_shift.astype(jnp.float32)
    )
    first_low = hidden_one.astype(jnp.bfloat16)
    bias_float = qv_bias.astype(jnp.float32)
    full_bias = jnp.concatenate(
        [bias_float[:model_width], jnp.zeros((model_width,), jnp.float32), bias_float[model_width:]]
    )
    projected = (
        jnp.dot(first_low, qkv_weight, preferred_element_type=jnp.float32) + full_bias
    ).astype(jnp.bfloat16)
    split_heads = projected.reshape(seq_rows, 3, heads_count, HEAD)
    queries = split_heads[:, 0]
    keys_part = split_heads[:, 1]
    values_part = split_heads[:, 2]
    visible = jnp.arange(seq_rows) < length

    def scores_of():
        raw_scores = (
            jnp.einsum("qhd,khd->hqk", queries, keys_part, preferred_element_type=jnp.float32)
            * scale_qk
        )
        return jnp.where(visible[None, None, :], raw_scores, NEGATIVE)

    scores = scores_of()
    top_score = jnp.max(scores, axis=-1, keepdims=True)
    expo = jnp.exp(scores - top_score)
    total_exp = jnp.sum(expo, axis=-1, keepdims=True)
    log_total = top_score + jnp.log(total_exp)
    attention = (expo / total_exp).astype(jnp.bfloat16)
    mixed = jnp.einsum("hqk,khd->qhd", attention, values_part, preferred_element_type=jnp.float32)
    mixed = mixed.reshape(seq_rows, model_width).astype(jnp.bfloat16)
    middle = (
        as_float
        + jnp.dot(mixed, out_weight, preferred_element_type=jnp.float32)
        + out_bias.astype(jnp.float32)
    )
    hidden_two, second_pull = jax.vjp(
        normalize, middle, second_gain.astype(jnp.float32), second_shift.astype(jnp.float32)
    )
    second_low = hidden_two.astype(jnp.bfloat16)
    inner = jnp.dot(second_low, in_weight, preferred_element_type=jnp.float32) + in_bias.astype(
        jnp.float32
    )
    active, gate_pull = jax.vjp(smooth_gate, inner)
    active_low = active.astype(jnp.bfloat16)
    output = (
        middle
        + jnp.dot(active_low, down_weight, preferred_element_type=jnp.float32)
        + down_bias.astype(jnp.float32)
    )
    upstream = cot_rows.astype(jnp.float32) * visible[:, None].astype(jnp.float32) * factor
    up_low = upstream.astype(jnp.bfloat16)
    grad_down_bias = jnp.sum(up_low.astype(jnp.float32), axis=0)
    grad_down = times_left(active_low, up_low)
    grad_active = times_right(up_low, down_weight)
    (grad_inner,) = gate_pull(grad_active)
    inner_low = grad_inner.astype(jnp.bfloat16)
    grad_in_bias = jnp.sum(inner_low.astype(jnp.float32), axis=0)
    grad_in = times_left(second_low, inner_low)
    grad_second = times_right(inner_low, in_weight)
    grad_middle_norm, grad_second_gain, grad_second_shift = second_pull(grad_second)
    grad_middle = upstream + grad_middle_norm
    middle_low = grad_middle.astype(jnp.bfloat16)
    grad_out_bias = jnp.sum(middle_low.astype(jnp.float32), axis=0)
    grad_out = times_left(mixed, middle_low)
    grad_mixed = (
        times_right(middle_low, out_weight)
        .astype(jnp.bfloat16)
        .reshape(seq_rows, heads_count, HEAD)
    )
    probs_again = jnp.exp(scores_of() - log_total)
    grad_probs = jnp.einsum(
        "qhd,khd->hqk", grad_mixed, values_part, preferred_element_type=jnp.float32
    )
    grad_values = jnp.einsum(
        "hqk,qhd->khd", attention, grad_mixed, preferred_element_type=jnp.float32
    )
    delta = jnp.sum(probs_again * grad_probs, axis=-1, keepdims=True)
    grad_scores = (probs_again * (grad_probs - delta)).astype(jnp.bfloat16)
    grad_queries = (
        jnp.einsum("hqk,khd->qhd", grad_scores, keys_part, preferred_element_type=jnp.float32)
        * scale_qk
    )
    grad_keys = (
        jnp.einsum("hqk,qhd->khd", grad_scores, queries, preferred_element_type=jnp.float32)
        * scale_qk
    )
    grad_projected = jnp.stack([grad_queries, grad_keys, grad_values], axis=1)
    grad_projected = grad_projected.reshape(seq_rows, 3 * model_width).astype(jnp.bfloat16)
    column_sums = jnp.sum(grad_projected.astype(jnp.float32), axis=0)
    grad_qv = jnp.concatenate([column_sums[:model_width], column_sums[2 * model_width :]])
    grad_qkv = times_left(first_low, grad_projected)
    grad_first = times_right(grad_projected, qkv_weight)
    grad_input_norm, grad_first_gain, grad_first_shift = first_pull(grad_first)
    grad_inputs = grad_middle + grad_input_norm
    grads = (
        grad_first_gain,
        grad_first_shift,
        grad_qkv,
        grad_qv,
        grad_out,
        grad_out_bias,
        grad_second_gain,
        grad_second_shift,
        grad_in,
        grad_in_bias,
        grad_down,
        grad_down_bias,
    )
    return (output.astype(jnp.bfloat16), grad_inputs.astype(jnp.bfloat16), grads)


RING = (0, 2, 4, 6, 7, 5, 3, 1)
RING_SIZE = len(RING)


def ring_pairs():
    pairs = []
    for place in range(RING_SIZE):
        chip = RING[place]
        right = RING[(place + 1) % RING_SIZE]
        left = RING[(place - 1) % RING_SIZE]
        pairs.append((2 * chip, 2 * right))
        pairs.append((2 * chip + 1, 2 * left + 1))
    return pairs


def hop(block):
    return lax.ppermute(block, "cells", ring_pairs())


def to_partner(block):
    return lax.ppermute(block, "cells", [(i, i ^ 1) for i in range(2 * RING_SIZE)])


def across(block):
    return lax.ppermute(block, "species", [(0, 1), (1, 0)])


def here():
    index = lax.axis_index("cells")
    core = index % 2
    chip = index // 2
    place = jnp.int32(0)
    for i, ring_chip in enumerate(RING):
        place = jnp.where(chip == ring_chip, i, place)
    return core, place


def chip_at(place):
    place = place % RING_SIZE
    chip = jnp.zeros_like(place)
    for i, ring_chip in enumerate(RING):
        chip = jnp.where(place == i, ring_chip, chip)
    return chip


def gather_blocks(block):
    core, _ = here()
    other = to_partner(block)
    first = jnp.where(core == 0, block, other)
    second = jnp.where(core == 0, other, block)
    own = jnp.stack([first, second])
    got = [own]
    moving = own
    for step in range(1, 4):
        moving = hop(moving)
        got.append(moving)
        got.append(to_partner(moving))
    half = jnp.where(core == 0, moving[0], moving[1])[None]
    half = hop(half)
    got.append(half)
    got.append(to_partner(half))
    return got


def gather_order():
    core, place = here()
    sign = 1 - 2 * core
    order = []

    def pair(at):
        order.append(2 * chip_at(at))
        order.append(2 * chip_at(at) + 1)

    pair(place)
    for step in range(1, 4):
        pair(place - sign * step)
        pair(place + sign * step)
    order.append(2 * chip_at(place + 4) + core)
    order.append(2 * chip_at(place + 4) + 1 - core)
    return jnp.stack(order).astype(jnp.int32)


def assemble(got, order, rows, extra):
    width = got[0].shape[-1]
    sizes = [item.shape[0] for item in got]

    def body(order_ref, *refs):
        ins = refs[: len(sizes)]
        outs = refs[len(sizes) : -1]
        sem = refs[-1]
        copies = []
        index = 0
        for source, size in zip(ins, sizes):
            for part in range(size):
                at = order_ref[index]
                copies.append(
                    pltpu.make_async_copy(
                        source.at[part, pl.ds(0, rows)],
                        outs[0].at[pl.ds(pl.multiple_of(at * rows, 16), rows)],
                        sem.at[index],
                    )
                )
                if extra:
                    copies.append(
                        pltpu.make_async_copy(
                            source.at[part, pl.ds(rows, extra)], outs[1].at[at], sem.at[16 + index]
                        )
                    )
                index += 1
        for item in copies:
            item.start()
        for item in copies:
            item.wait()

    count = 2 * RING_SIZE
    shapes = [jax.ShapeDtypeStruct((count * rows, width), jnp.bfloat16)]
    if extra:
        shapes.append(jax.ShapeDtypeStruct((count, extra, width), jnp.bfloat16))
    any_spec = pl.BlockSpec(memory_space=pl.ANY)
    return pl.pallas_call(
        body,
        out_shape=shapes,
        in_specs=[pl.BlockSpec(memory_space=pltpu.SMEM)] + [any_spec] * len(got),
        out_specs=[any_spec] * len(shapes),
        scratch_shapes=[pltpu.SemaphoreType.DMA((2 * count,))],
        cost_estimate=pl.CostEstimate(
            flops=0, bytes_accessed=2 * count * rows * width * 2, transcendentals=0
        ),
    )(order, *got)


def scatter_order():
    core, place = here()

    def kept(core_now):
        sign = 1 - 2 * core_now
        order = [2 * chip_at(place + 4) + core_now]
        for step in (3, 2, 1):
            order.append(2 * chip_at(place + sign * step))
            order.append(2 * chip_at(place + sign * step) + 1)
        order.append(2 * chip_at(place) + core_now)
        return order

    return jnp.stack(kept(core) + kept(1 - core)).astype(jnp.int32)


def split_blocks(grad, order):
    count, rows, width = grad.shape
    half = count // 2

    def body(order_ref, source, keep, away, sem):
        copies = []
        for index in range(count):
            target = keep if index < half else away
            copies.append(
                pltpu.make_async_copy(
                    source.at[order_ref[index]], target.at[index % half], sem.at[index]
                )
            )
        for item in copies:
            item.start()
        for item in copies:
            item.wait()

    any_spec = pl.BlockSpec(memory_space=pl.ANY)
    shape = jax.ShapeDtypeStruct((half, rows, width), grad.dtype)
    return pl.pallas_call(
        body,
        out_shape=[shape, shape],
        in_specs=[pl.BlockSpec(memory_space=pltpu.SMEM), any_spec],
        out_specs=[any_spec, any_spec],
        scratch_shapes=[pltpu.SemaphoreType.DMA((count,))],
        cost_estimate=pl.CostEstimate(
            flops=0, bytes_accessed=2 * count * rows * width * 2, transcendentals=0
        ),
    )(order, grad)


def add_low(left, right):
    return (left.astype(jnp.float32) + right.astype(jnp.float32)).astype(jnp.bfloat16)


def reduce_blocks(grad, order):
    core, _ = here()
    keep, away = split_blocks(grad, order)
    keep = add_low(keep, to_partner(away))
    moving = hop(keep[0:1])
    wide = jnp.stack([jnp.where(core == 0, moving[0], 0), jnp.where(core == 0, 0, moving[0])])
    moving = hop(add_low(keep[1:3], wide))
    moving = hop(add_low(keep[3:5], moving))
    moving = hop(add_low(keep[5:7], moving))
    mine = jnp.where(core == 0, moving[0], moving[1])
    other = jnp.where(core == 0, moving[1], moving[0])
    got = to_partner(other)
    total = (
        keep[7].astype(jnp.float32) + mine.astype(jnp.float32) + got.astype(jnp.float32)
    ).astype(jnp.bfloat16)
    return total.astype(jnp.float32) + across(total).astype(jnp.float32)


SMALL_ROWS = 16


def pack_small(vectors, width):
    flat = jnp.concatenate(vectors)
    flat = jnp.pad(flat, (0, width - flat.shape[0]))[None]
    return jnp.pad(flat, ((0, SMALL_ROWS - 1), (0, 0)))


def on_device_ring(
    tokens,
    lengths,
    cotangent,
    first_gain,
    first_shift,
    qkv_weight,
    qv_bias,
    out_weight,
    out_bias,
    second_gain,
    second_shift,
    in_weight,
    in_bias,
    down_weight,
    down_bias,
):
    cells = 2 * RING_SIZE
    micro_count = tokens.shape[1]
    seq_rows = tokens.shape[2]
    model_width = tokens.shape[3]
    rows = qkv_weight.shape[0]
    down_rows = down_weight.shape[0]
    local_count = jnp.sum(lengths).astype(jnp.float32)
    small = [
        first_gain,
        first_shift,
        qv_bias,
        out_bias,
        second_gain,
        second_shift,
        in_bias,
        down_bias,
        lengths[0].astype(jnp.bfloat16),
    ]
    lane_sizes = [item.shape[0] for item in small]
    order = gather_order()
    qkv_block = jnp.concatenate([qkv_weight, pack_small(small, qkv_weight.shape[1])])
    in_block = jnp.concatenate([in_weight, out_weight], axis=1)
    qkv_got = gather_blocks(qkv_block)
    in_got = gather_blocks(in_block)
    down_got = gather_blocks(down_weight)
    qkv_full, small_full = assemble(qkv_got, order, rows, SMALL_ROWS)
    (in_full,) = assemble(in_got, order, rows, 0)
    (down_full,) = assemble(down_got, order, down_rows, 0)
    ff = in_weight.shape[1]
    out_full = in_full[:, ff:]
    in_full = in_full[:, :ff]
    vectors = []
    start = 0
    for size in lane_sizes:
        vectors.append(small_full[:, 0, start : start + size].reshape(cells * size))
        start += size
    stream_count = jnp.sum(vectors[-1].astype(jnp.float32))
    count_block = jnp.full((8, 128), stream_count, jnp.float32)
    count = (count_block + across(count_block))[0, 0]
    factor = float(lax.axis_size("species") * cells * micro_count * seq_rows) / count
    weights = (
        vectors[0],
        vectors[1],
        qkv_full,
        vectors[2],
        out_full,
        vectors[3],
        vectors[4],
        vectors[5],
        in_full,
        vectors[6],
        down_full,
        vectors[7],
    )
    output_rows = []
    gradient_rows = []
    summed = None
    for micro_step in range(micro_count):
        out_seq, grad_seq, grads = sequence_pass(
            weights,
            tokens[0, micro_step],
            lengths[0, micro_step],
            cotangent[0, micro_step],
            factor,
        )
        output_rows.append(out_seq)
        gradient_rows.append(grad_seq)
        summed = grads if summed is None else jax.tree.map(jnp.add, summed, grads)
    places = scatter_order()
    low = jnp.bfloat16
    down_sum = reduce_blocks(summed[10].astype(low).reshape(cells, down_rows, model_width), places)
    in_out = jnp.concatenate([summed[8].astype(low), summed[4].astype(low)], axis=1)
    in_sum = reduce_blocks(in_out.reshape(cells, rows, ff + model_width), places)
    small_grads = jnp.concatenate(
        [summed[i].astype(low).reshape(cells, -1) for i in (0, 1, 3, 5, 6, 7, 9, 11)], axis=1
    )
    qkv_width = qkv_weight.shape[1]
    small_grads = jnp.pad(
        small_grads[:, None], ((0, 0), (0, SMALL_ROWS - 1), (0, qkv_width - small_grads.shape[1]))
    )
    qkv_grad = jnp.concatenate(
        [summed[2].astype(low).reshape(cells, rows, qkv_width), small_grads], axis=1
    )
    qkv_sum = reduce_blocks(qkv_grad, places)
    pieces = []
    start = 0
    for size in lane_sizes[:-1]:
        pieces.append(qkv_sum[rows, start : start + size])
        start += size
    out_tokens = jnp.stack(output_rows)[None]
    grad_tokens = jnp.stack(gradient_rows)[None]
    return (
        out_tokens,
        grad_tokens,
        pieces[0],
        pieces[1],
        qkv_sum[:rows],
        pieces[2],
        in_sum[:, ff:],
        pieces[3],
        pieces[4],
        pieces[5],
        in_sum[:, :ff],
        pieces[6],
        down_sum,
        pieces[7],
    )


def on_device(
    tokens,
    lengths,
    cotangent,
    first_gain,
    first_shift,
    qkv_weight,
    qv_bias,
    out_weight,
    out_bias,
    second_gain,
    second_shift,
    in_weight,
    in_bias,
    down_weight,
    down_bias,
):
    local_count = jnp.sum(lengths).astype(jnp.float32)
    count = lax.psum(local_count, ("species", "cells"))
    micro_count = tokens.shape[1]
    seq_rows = tokens.shape[2]
    factor = (
        float(lax.axis_size("species") * lax.axis_size("cells") * micro_count * seq_rows) / count
    )
    output_rows = []
    gradient_rows = []
    summed = None
    for micro_step in range(micro_count):
        gathered = (
            lax.all_gather(first_gain, "cells", axis=0, tiled=True),
            lax.all_gather(first_shift, "cells", axis=0, tiled=True),
            lax.all_gather(qkv_weight, "cells", axis=0, tiled=True),
            lax.all_gather(qv_bias, "cells", axis=0, tiled=True),
            lax.all_gather(out_weight, "cells", axis=0, tiled=True),
            lax.all_gather(out_bias, "cells", axis=0, tiled=True),
            lax.all_gather(second_gain, "cells", axis=0, tiled=True),
            lax.all_gather(second_shift, "cells", axis=0, tiled=True),
            lax.all_gather(in_weight, "cells", axis=0, tiled=True),
            lax.all_gather(in_bias, "cells", axis=0, tiled=True),
            lax.all_gather(down_weight, "cells", axis=0, tiled=True),
            lax.all_gather(down_bias, "cells", axis=0, tiled=True),
        )
        out_seq, grad_seq, grads = sequence_pass(
            gathered,
            tokens[0, micro_step],
            lengths[0, micro_step],
            cotangent[0, micro_step],
            factor,
        )
        output_rows.append(out_seq)
        gradient_rows.append(grad_seq)
        shares = (
            lax.psum_scatter(grads[0], "cells", scatter_dimension=0, tiled=True),
            lax.psum_scatter(grads[1], "cells", scatter_dimension=0, tiled=True),
            lax.psum_scatter(grads[2], "cells", scatter_dimension=0, tiled=True),
            lax.psum_scatter(grads[3], "cells", scatter_dimension=0, tiled=True),
            lax.psum_scatter(grads[4], "cells", scatter_dimension=0, tiled=True),
            lax.psum_scatter(grads[5], "cells", scatter_dimension=0, tiled=True),
            lax.psum_scatter(grads[6], "cells", scatter_dimension=0, tiled=True),
            lax.psum_scatter(grads[7], "cells", scatter_dimension=0, tiled=True),
            lax.psum_scatter(grads[8], "cells", scatter_dimension=0, tiled=True),
            lax.psum_scatter(grads[9], "cells", scatter_dimension=0, tiled=True),
            lax.psum_scatter(grads[10], "cells", scatter_dimension=0, tiled=True),
            lax.psum_scatter(grads[11], "cells", scatter_dimension=0, tiled=True),
        )
        summed = shares if summed is None else jax.tree.map(jnp.add, summed, shares)
    final = (
        lax.psum(summed[0].astype(jnp.bfloat16), "species").astype(jnp.float32),
        lax.psum(summed[1].astype(jnp.bfloat16), "species").astype(jnp.float32),
        lax.psum(summed[2].astype(jnp.bfloat16), "species").astype(jnp.float32),
        lax.psum(summed[3].astype(jnp.bfloat16), "species").astype(jnp.float32),
        lax.psum(summed[4].astype(jnp.bfloat16), "species").astype(jnp.float32),
        lax.psum(summed[5].astype(jnp.bfloat16), "species").astype(jnp.float32),
        lax.psum(summed[6].astype(jnp.bfloat16), "species").astype(jnp.float32),
        lax.psum(summed[7].astype(jnp.bfloat16), "species").astype(jnp.float32),
        lax.psum(summed[8].astype(jnp.bfloat16), "species").astype(jnp.float32),
        lax.psum(summed[9].astype(jnp.bfloat16), "species").astype(jnp.float32),
        lax.psum(summed[10].astype(jnp.bfloat16), "species").astype(jnp.float32),
        lax.psum(summed[11].astype(jnp.bfloat16), "species").astype(jnp.float32),
    )
    out_tokens = jnp.stack(output_rows)[None]
    grad_tokens = jnp.stack(gradient_rows)[None]
    return (out_tokens, grad_tokens) + tuple(final)


def solution(mesh):
    in_specs = (
        P("species", "cells", None, None),
        P("species", "cells"),
        P("species", "cells", None, None),
        P("cells"),
        P("cells"),
        P("cells", None),
        P("cells"),
        P("cells", None),
        P("cells"),
        P("cells"),
        P("cells"),
        P("cells", None),
        P("cells"),
        P("cells", None),
        P("cells"),
    )
    out_specs = (
        P("species", "cells", None, None),
        P("species", "cells", None, None),
        P("cells"),
        P("cells"),
        P("cells", None),
        P("cells"),
        P("cells", None),
        P("cells"),
        P("cells"),
        P("cells"),
        P("cells", None),
        P("cells"),
        P("cells", None),
        P("cells"),
    )
    program = on_device_ring if mesh.shape["cells"] == 2 * RING_SIZE else on_device
    return jax.shard_map(
        program, mesh=mesh, in_specs=in_specs, out_specs=out_specs, check_vma=False
    )
```

```python
import jax
import jax.numpy as jnp
from jax import lax
from jax.experimental import pallas as pl
from jax.experimental.pallas import tpu as pltpu
from jax.sharding import PartitionSpec as P

HEAD = 64


EPSILON = 1e-12
NEGATIVE = -1e30


def normalize(values, gain_vec, shift_vec):
    center = values - jnp.mean(values, axis=-1, keepdims=True)
    spread = jnp.mean(center * center, axis=-1, keepdims=True)
    return center * lax.rsqrt(spread + EPSILON) * gain_vec + shift_vec


def smooth_gate(values):
    return jax.nn.gelu(values, approximate=False)


def times_left(left_side, right_side):
    return lax.dot_general(
        left_side, right_side, (((0,), (0,)), ((), ())), preferred_element_type=jnp.float32
    )


def times_right(left_side, right_side):
    return lax.dot_general(
        left_side, right_side, (((1,), (1,)), ((), ())), preferred_element_type=jnp.float32
    )


def sequence_pass(weights, inputs, length, cot_rows, factor):
    (
        first_gain,
        first_shift,
        qkv_weight,
        qv_bias,
        out_weight,
        out_bias,
        second_gain,
        second_shift,
        in_weight,
        in_bias,
        down_weight,
        down_bias,
    ) = weights
    seq_rows = inputs.shape[0]
    model_width = inputs.shape[1]
    heads_count = model_width // HEAD
    scale_qk = float(HEAD) ** (-0.5)
    as_float = inputs.astype(jnp.float32)
    hidden_one, first_pull = jax.vjp(
        normalize, as_float, first_gain.astype(jnp.float32), first_shift.astype(jnp.float32)
    )
    first_low = hidden_one.astype(jnp.bfloat16)
    bias_float = qv_bias.astype(jnp.float32)
    full_bias = jnp.concatenate(
        [bias_float[:model_width], jnp.zeros((model_width,), jnp.float32), bias_float[model_width:]]
    )
    projected = (
        jnp.dot(first_low, qkv_weight, preferred_element_type=jnp.float32) + full_bias
    ).astype(jnp.bfloat16)
    split_heads = projected.reshape(seq_rows, 3, heads_count, HEAD)
    queries = split_heads[:, 0]
    keys_part = split_heads[:, 1]
    values_part = split_heads[:, 2]
    visible = jnp.arange(seq_rows) < length

    def scores_of():
        raw_scores = (
            jnp.einsum("qhd,khd->hqk", queries, keys_part, preferred_element_type=jnp.float32)
            * scale_qk
        )
        return jnp.where(visible[None, None, :], raw_scores, NEGATIVE)

    scores = scores_of()
    top_score = jnp.max(scores, axis=-1, keepdims=True)
    expo = jnp.exp(scores - top_score)
    total_exp = jnp.sum(expo, axis=-1, keepdims=True)
    log_total = top_score + jnp.log(total_exp)
    attention = (expo / total_exp).astype(jnp.bfloat16)
    mixed = jnp.einsum("hqk,khd->qhd", attention, values_part, preferred_element_type=jnp.float32)
    mixed = mixed.reshape(seq_rows, model_width).astype(jnp.bfloat16)
    middle = (
        as_float
        + jnp.dot(mixed, out_weight, preferred_element_type=jnp.float32)
        + out_bias.astype(jnp.float32)
    )
    hidden_two, second_pull = jax.vjp(
        normalize, middle, second_gain.astype(jnp.float32), second_shift.astype(jnp.float32)
    )
    second_low = hidden_two.astype(jnp.bfloat16)
    inner = jnp.dot(second_low, in_weight, preferred_element_type=jnp.float32) + in_bias.astype(
        jnp.float32
    )
    active, gate_pull = jax.vjp(smooth_gate, inner)
    active_low = active.astype(jnp.bfloat16)
    output = (
        middle
        + jnp.dot(active_low, down_weight, preferred_element_type=jnp.float32)
        + down_bias.astype(jnp.float32)
    )
    upstream = cot_rows.astype(jnp.float32) * visible[:, None].astype(jnp.float32) * factor
    up_low = upstream.astype(jnp.bfloat16)
    grad_down_bias = jnp.sum(up_low.astype(jnp.float32), axis=0)
    grad_down = times_left(active_low, up_low)
    grad_active = times_right(up_low, down_weight)
    (grad_inner,) = gate_pull(grad_active)
    inner_low = grad_inner.astype(jnp.bfloat16)
    grad_in_bias = jnp.sum(inner_low.astype(jnp.float32), axis=0)
    grad_in = times_left(second_low, inner_low)
    grad_second = times_right(inner_low, in_weight)
    grad_middle_norm, grad_second_gain, grad_second_shift = second_pull(grad_second)
    grad_middle = upstream + grad_middle_norm
    middle_low = grad_middle.astype(jnp.bfloat16)
    grad_out_bias = jnp.sum(middle_low.astype(jnp.float32), axis=0)
    grad_out = times_left(mixed, middle_low)
    grad_mixed = (
        times_right(middle_low, out_weight)
        .astype(jnp.bfloat16)
        .reshape(seq_rows, heads_count, HEAD)
    )
    probs_again = jnp.exp(scores_of() - log_total)
    grad_probs = jnp.einsum(
        "qhd,khd->hqk", grad_mixed, values_part, preferred_element_type=jnp.float32
    )
    grad_values = jnp.einsum(
        "hqk,qhd->khd", attention, grad_mixed, preferred_element_type=jnp.float32
    )
    delta = jnp.sum(probs_again * grad_probs, axis=-1, keepdims=True)
    grad_scores = (probs_again * (grad_probs - delta)).astype(jnp.bfloat16)
    grad_queries = (
        jnp.einsum("hqk,khd->qhd", grad_scores, keys_part, preferred_element_type=jnp.float32)
        * scale_qk
    )
    grad_keys = (
        jnp.einsum("hqk,qhd->khd", grad_scores, queries, preferred_element_type=jnp.float32)
        * scale_qk
    )
    grad_projected = jnp.stack([grad_queries, grad_keys, grad_values], axis=1)
    grad_projected = grad_projected.reshape(seq_rows, 3 * model_width).astype(jnp.bfloat16)
    column_sums = jnp.sum(grad_projected.astype(jnp.float32), axis=0)
    grad_qv = jnp.concatenate([column_sums[:model_width], column_sums[2 * model_width :]])
    grad_qkv = times_left(first_low, grad_projected)
    grad_first = times_right(grad_projected, qkv_weight)
    grad_input_norm, grad_first_gain, grad_first_shift = first_pull(grad_first)
    grad_inputs = grad_middle + grad_input_norm
    grads = (
        grad_first_gain,
        grad_first_shift,
        grad_qkv,
        grad_qv,
        grad_out,
        grad_out_bias,
        grad_second_gain,
        grad_second_shift,
        grad_in,
        grad_in_bias,
        grad_down,
        grad_down_bias,
    )
    return (output.astype(jnp.bfloat16), grad_inputs.astype(jnp.bfloat16), grads)


RING = (0, 2, 4, 6, 7, 5, 3, 1)
RING_SIZE = len(RING)
CELLS = 2 * RING_SIZE
ANY = pl.BlockSpec(memory_space=pl.ANY)
VMEM = pl.BlockSpec(memory_space=pltpu.VMEM)
SMEM = pl.BlockSpec(memory_space=pltpu.SMEM)
LOW = jnp.bfloat16
FULL = jnp.float32
ROWS = {
    "first_gain": 0,
    "first_shift": 1,
    "qv_bias": 2,
    "out_bias": 4,
    "second_gain": 5,
    "second_shift": 6,
    "in_bias": 7,
    "down_bias": 11,
    "lengths": 12,
}
SMALL_ROWS = 16
SMALL_LANES = 256


def ring_pairs():
    pairs = []
    for place in range(RING_SIZE):
        chip = RING[place]
        right = RING[(place + 1) % RING_SIZE]
        left = RING[(place - 1) % RING_SIZE]
        pairs.append((2 * chip, 2 * right))
        pairs.append((2 * chip + 1, 2 * left + 1))
    return pairs


def hop(block):
    return lax.ppermute(block, "cells", ring_pairs())


def to_partner(block):
    return lax.ppermute(block, "cells", [(i, i ^ 1) for i in range(CELLS)])


def across(block):
    return lax.ppermute(block, "species", [(0, 1), (1, 0)])


def after(value, *others):
    return lax.optimization_barrier((value,) + others)[0]


def here():
    index = lax.axis_index("cells")
    core = index % 2
    chip = index // 2
    place = jnp.int32(0)
    for i, ring_chip in enumerate(RING):
        place = jnp.where(chip == ring_chip, i, place)
    return index, core, place


def chip_at(place):
    place = place % RING_SIZE
    chip = jnp.zeros_like(place)
    for i, ring_chip in enumerate(RING):
        chip = jnp.where(place == i, ring_chip, chip)
    return chip


def gather_order(core, place):
    sign = 1 - 2 * core
    order = []

    def pair(at):
        order.append(2 * chip_at(at))
        order.append(2 * chip_at(at) + 1)

    pair(place)
    for step in range(1, 4):
        pair(place - sign * step)
        pair(place + sign * step)
    order.append(2 * chip_at(place + 4) + core)
    order.append(2 * chip_at(place + 4) + 1 - core)
    return order


def scatter_slots(core, place):
    def kept(core_now):
        sign = 1 - 2 * core_now
        order = [2 * chip_at(place + 4) + core_now]
        for step in (3, 2, 1):
            order.append(2 * chip_at(place + sign * step))
            order.append(2 * chip_at(place + sign * step) + 1)
        order.append(2 * chip_at(place) + core_now)
        return order

    order = kept(core) + kept(1 - core)
    slots = []
    for device in range(CELLS):
        slot = jnp.int32(0)
        for i, who in enumerate(order):
            slot = jnp.where(who == device, i, slot)
        slots.append(slot)
    return slots


def both_blocks(block, core):
    other = to_partner(block)
    return jnp.stack([jnp.where(core == 0, block, other), jnp.where(core == 0, other, block)])


def half_of(pair, core):
    return jnp.where(core == 0, pair[0], pair[1])[None]


def add_low(*parts):
    total = parts[0].astype(FULL)
    for part in parts[1:]:
        total = total + part.astype(FULL)
    return total.astype(LOW)


def reduce_blocks(keep, away, core):
    got = to_partner(away)
    moving = hop(add_low(keep[0:1], got[0:1]))
    wide = jnp.stack([jnp.where(core == 0, moving[0], 0), jnp.where(core == 0, 0, moving[0])])
    moving = hop(add_low(keep[1:3], got[1:3], wide))
    moving = hop(add_low(keep[3:5], got[3:5], moving))
    moving = hop(add_low(keep[5:7], got[5:7], moving))
    mine = jnp.where(core == 0, moving[0], moving[1])
    other = jnp.where(core == 0, moving[1], moving[0])
    total = add_low(keep[7], got[7], mine, to_partner(other))
    return total, across(total)


def dot(left, right, dims=((1,), (0,))):
    return lax.dot_general(left, right, (dims, ((), ())), preferred_element_type=FULL)


def call(body, out_shape, ins, specs, out_specs=None, scratch=(), vmem=48, flops=0, moved=0):
    return pl.pallas_call(
        body,
        out_shape=out_shape,
        in_specs=specs,
        out_specs=[VMEM] * len(out_shape) if out_specs is None else out_specs,
        scratch_shapes=list(scratch),
        compiler_params=pltpu.CompilerParams(vmem_limit_bytes=vmem * 2**20),
        cost_estimate=pl.CostEstimate(flops=flops, bytes_accessed=moved, transcendentals=0),
    )(*ins)


def shape(dims, kind=LOW):
    return jax.ShapeDtypeStruct(dims, kind)


def block_sizes(blocks):
    return [item.shape[0] for item in blocks]


def fetch(order_ref, refs, sizes, rows, lanes, target, sem, extra=None, extra_sem=None):
    copies = []
    index = 0
    for source, size in zip(refs, sizes):
        for part in range(size):
            at = order_ref[index]
            copies.append(
                pltpu.make_async_copy(
                    source.at[part, :, pl.ds(0, lanes)],
                    target.at[pl.ds(pl.multiple_of(at * rows, 16), rows)],
                    sem.at[index],
                )
            )
            if extra is not None:
                copies.append(
                    pltpu.make_async_copy(
                        source.at[part, :, pl.ds(lanes, SMALL_LANES)],
                        extra.at[at],
                        extra_sem.at[index],
                    )
                )
            index += 1
    for item in copies:
        item.start()
    return copies


def one_hot(rows, lanes, offset):
    row = lax.broadcasted_iota(jnp.int32, (rows, lanes), 0)
    lane = lax.broadcasted_iota(jnp.int32, (rows, lanes), 1)
    return lane == row + offset


def pack_body(
    who_ref, gain_ref, shift_ref, qv_ref, out_b_ref, gain2_ref, shift2_ref, in_b_ref, down_b_ref,
    lengths_ref, weight_ref, block_ref,
):
    me = who_ref[0]
    width = weight_ref.shape[1]
    model = 16 * gain_ref.shape[1]
    row = lax.broadcasted_iota(jnp.int32, (SMALL_ROWS, model), 0)
    lane = lax.broadcasted_iota(jnp.int32, (SMALL_ROWS, model), 1)
    small = jnp.zeros((SMALL_ROWS, model), FULL)

    def put(ref, at):
        size = ref.shape[1]
        per_row = model // size
        placed = dot(ref[...], one_hot(size, model, size * (me % per_row)).astype(LOW))
        return jnp.where(row == at + me // per_row, placed, 0.0)

    for name, ref in (
        ("first_gain", gain_ref),
        ("first_shift", shift_ref),
        ("qv_bias", qv_ref),
        ("out_bias", out_b_ref),
        ("second_gain", gain2_ref),
        ("second_shift", shift2_ref),
        ("in_bias", in_b_ref),
        ("down_bias", down_b_ref),
    ):
        small = small + put(ref, ROWS[name])
    for i in range(2):
        at = (row == ROWS["lengths"]) & (lane == 2 * me + i)
        small = small + jnp.where(at, lengths_ref[i].astype(FULL), 0.0)
    small = small.astype(LOW)
    block_ref[:, 0:width] = weight_ref[...]
    for i in range(3):
        block_ref[16 * i : 16 * i + 16, width : width + SMALL_LANES] = small[
            :, SMALL_LANES * i : SMALL_LANES * (i + 1)
        ]


def norm_parts(values):
    center = values - jnp.mean(values, axis=-1, keepdims=True)
    spread = jnp.mean(center * center, axis=-1, keepdims=True)
    return center, lax.rsqrt(spread + EPSILON)


def norm_back(center, scale, gain, grad):
    weighted = grad * gain
    mean_one = jnp.mean(weighted, axis=-1, keepdims=True)
    mean_two = jnp.mean(weighted * center, axis=-1, keepdims=True)
    back = scale * (weighted - mean_one - center * (scale * scale * mean_two))
    return back, jnp.sum(grad * center * scale, axis=0, keepdims=True), jnp.sum(
        grad, axis=0, keepdims=True
    )


def small_row(small_ref, name, count=1):
    return small_ref[ROWS[name] : ROWS[name] + count, :]


def attend_body(sizes, seq, order_ref, lengths_ref, x_ref, *refs):
    blocks = refs[: len(sizes)]
    (
        low_ref, proj_ref, att_ref, mixed_ref, small_ref, count_ref, weight, extra, sem, extra_sem,
    ) = refs[len(sizes) :]
    model = x_ref.shape[1]
    copies = fetch(
        order_ref, blocks, sizes, model // CELLS, 3 * model, weight, sem, extra, extra_sem
    )
    for item in copies:
        item.wait()
    total = extra[0].astype(FULL)
    for i in range(1, CELLS):
        total = total + extra[i].astype(FULL)
    for i in range(3):
        small_ref[:, SMALL_LANES * i : SMALL_LANES * (i + 1)] = total[16 * i : 16 * i + 16]
    count_ref[...] = jnp.broadcast_to(
        jnp.sum(small_row(small_ref, "lengths"), axis=-1, keepdims=True), count_ref.shape
    )
    gain = small_row(small_ref, "first_gain")
    shift = small_row(small_ref, "first_shift")
    bias = small_row(small_ref, "qv_bias", 2)
    cells = x_ref.shape[0] // seq
    for s in range(cells):
        rows = slice(s * seq, (s + 1) * seq)
        center, scale = norm_parts(x_ref[rows, :].astype(FULL))
        low = (center * scale * gain + shift).astype(LOW)
        low_ref[rows, :] = low
        for j in range(3):
            part = dot(low, weight[:, j * model : (j + 1) * model])
            if j != 1:
                part = part + bias[j // 2 : j // 2 + 1]
            proj_ref[rows, j * model : (j + 1) * model] = part.astype(LOW)
    pairs = model // (2 * HEAD)
    lane = lax.broadcasted_iota(jnp.int32, (seq, 2 * HEAD), 1)
    key = lax.broadcasted_iota(jnp.int32, (seq, seq), 0)

    def step(index, carry):
        s = index // pairs
        p = index % pairs
        rows = pl.ds(pl.multiple_of(s * seq, seq), seq)
        at = pl.multiple_of(p * 2 * HEAD, 2 * HEAD)
        q = proj_ref[rows, pl.ds(at, 2 * HEAD)] * jnp.asarray(HEAD ** (-0.5), LOW)
        k = proj_ref[rows, pl.ds(at + model, 2 * HEAD)]
        v_turned = proj_ref[rows, pl.ds(at + 2 * model, 2 * HEAD)].T
        visible = key < lengths_ref[s]
        mixed = []
        for i in range(2):
            own = (lane >= i * HEAD) & (lane < (i + 1) * HEAD)
            scores = dot(jnp.where(own, k, jnp.zeros_like(k)), q, ((1,), (1,)))
            scores = jnp.where(visible, scores, NEGATIVE)
            expo = jnp.exp(scores - jnp.max(scores, axis=0, keepdims=True))
            probs = expo * (1.0 / jnp.sum(expo, axis=0, keepdims=True))
            probs = probs.astype(LOW)
            att_ref[2 * index + i] = probs
            mixed.append(dot(v_turned[i * HEAD : (i + 1) * HEAD], probs))
        mixed_ref[rows, pl.ds(at, 2 * HEAD)] = jnp.concatenate(mixed, axis=0).T.astype(LOW)
        return carry

    lax.fori_loop(0, cells * pairs, step, 0)


ERFC_STEP = 0.33
ERFC = (
    0.1863578228018033,
    0.18295566386742124,
    0.2012255082472392,
    0.04721561458875723,
    0.4085089979423051,
    -0.35115900736338407,
    0.4602422572120205,
    -0.13534686486277223,
)


def gelu_parts(inner):
    z = jnp.abs(inner) * (0.5**0.5)
    t = 1.0 / (1.0 + ERFC_STEP * z)
    tail = jnp.full_like(t, 0.5 * ERFC[-1])
    for factor in ERFC[-2::-1]:
        tail = tail * t + 0.5 * factor
    bell = jnp.exp(-(z * z))
    tail = tail * t * bell
    area = jnp.where(inner < 0.0, tail, 1.0 - tail)
    return inner * area, area + inner * bell * (0.5 / 3.141592653589793) ** 0.5


def row_mask(lengths_ref, rows, seq):
    at = lax.broadcasted_iota(jnp.int32, (rows, 1), 0)
    true = (at < lengths_ref[0]).astype(FULL)
    for s in range(1, rows // seq):
        true = jnp.where(at < s * seq, true, (at < lengths_ref[s] + s * seq).astype(FULL))
    return true


def loss_rows(lengths_ref, count_ref, other_ref, cot_ref, seq, whole):
    factor = whole / (count_ref[0:1, 0:1] + other_ref[0:1, 0:1])
    return cot_ref[...].astype(FULL) * (row_mask(lengths_ref, cot_ref.shape[0], seq) * factor)


def put_slots(keep_buf, slot_ref, values, first, lanes):
    rows = keep_buf.shape[1]
    for i in range(values.shape[0] // rows):
        keep_buf[slot_ref[first + i], :, lanes] = values[i * rows : (i + 1) * rows].astype(LOW)


def send_slots(buf, keep_ref, away_ref, sem):
    half = RING_SIZE
    copies = [
        pltpu.make_async_copy(buf.at[pl.ds(half, half)], away_ref, sem.at[0]),
        pltpu.make_async_copy(buf.at[pl.ds(0, half)], keep_ref, sem.at[1]),
    ]
    for item in copies:
        item.start()
    return copies


def inner_body(
    sizes, seq, whole, order_ref, slot_ref, lengths_ref, x_ref, mixed_ref, cot_ref, small_ref,
    count_ref, other_ref, *refs,
):
    blocks = refs[: len(sizes)]
    (
        middle_ref, low_ref, active_ref, slope_ref, up_ref, down_b_ref, keep_ref, away_ref,
        weight, slots, sem, out_sem,
    ) = refs[len(sizes) :]
    model = x_ref.shape[1]
    ff = active_ref.shape[1]
    copies = fetch(order_ref, blocks, sizes, model // CELLS, ff + model, weight, sem)
    up_low = loss_rows(lengths_ref, count_ref, other_ref, cot_ref, seq, whole).astype(LOW)
    up_ref[...] = up_low
    down_b_ref[...] = jnp.sum(up_low.astype(FULL), axis=0, keepdims=True)
    for item in copies:
        item.wait()
    middle = (
        x_ref[...].astype(FULL)
        + dot(mixed_ref[...], weight[:, ff:])
        + small_row(small_ref, "out_bias")
    )
    middle_ref[...] = middle
    center, scale = norm_parts(middle)
    low = center * scale * small_row(small_ref, "second_gain") + small_row(
        small_ref, "second_shift"
    )
    low_ref[...] = low.astype(LOW)
    step = 2 * (ff // RING_SIZE)
    bias = small_row(small_ref, "in_bias", 4)
    for j in range(ff // step):
        lanes = slice(j * step, (j + 1) * step)
        inner = dot(low_ref[...], weight[:, lanes]) + bias[j : j + 1]
        active, slope = gelu_parts(inner)
        active_ref[:, lanes] = active.astype(LOW)
        slope_ref[:, lanes] = slope.astype(LOW)
        grad = dot(active_ref[:, lanes], up_ref[...], ((0,), (0,)))
        put_slots(slots, slot_ref, grad, j * CELLS // 4, slice(None))
    for item in send_slots(slots, keep_ref, away_ref, out_sem):
        item.wait()


def down_body(
    sizes, order_ref, active_ref, slope_ref, middle_ref, up_ref, small_ref, *refs
):
    blocks = refs[: len(sizes)]
    out_ref, inner_ref, in_b_ref, weight, sem = refs[len(sizes) :]
    ff, model = weight.shape
    copies = fetch(order_ref, blocks, sizes, ff // CELLS, model, weight, sem)
    for item in copies:
        item.wait()
    out_ref[...] = (
        middle_ref[...]
        + dot(active_ref[...], weight[...])
        + small_row(small_ref, "down_bias")
    ).astype(LOW)
    for j in range(ff // model):
        lanes = slice(j * model, (j + 1) * model)
        grad = dot(up_ref[...], weight[lanes, :], ((1,), (1,)))
        low = (grad * slope_ref[:, lanes].astype(FULL)).astype(LOW)
        inner_ref[:, lanes] = low
        in_b_ref[j : j + 1, :] = jnp.sum(low.astype(FULL), axis=0, keepdims=True)


def middle_back_body(
    sizes, seq, whole, order_ref, slot_ref, lengths_ref, inner_ref, low_ref, mixed_ref,
    middle_ref, cot_ref, small_ref, count_ref, other_ref, *refs,
):
    blocks = refs[: len(sizes)]
    (
        grad_ref, grad_mixed_ref, sums_ref, keep_ref, away_ref, weight, slots, sem, out_sem,
    ) = refs[len(sizes) :]
    model = middle_ref.shape[1]
    ff = inner_ref.shape[1]
    copies = fetch(order_ref, blocks, sizes, model // CELLS, ff + model, weight, sem)
    turned = low_ref[...].T
    for j in range(ff // model):
        lanes = slice(j * model, (j + 1) * model)
        put_slots(slots, slot_ref, dot(turned, inner_ref[:, lanes]), 0, lanes)
    for item in copies:
        item.wait()
    grad_second = dot(inner_ref[...], weight[:, :ff], ((1,), (1,)))
    center, scale = norm_parts(middle_ref[...])
    back, gain_sum, shift_sum = norm_back(
        center, scale, small_row(small_ref, "second_gain"), grad_second
    )
    grad = loss_rows(lengths_ref, count_ref, other_ref, cot_ref, seq, whole) + back
    grad_ref[...] = grad
    grad_low = grad.astype(LOW)
    sums_ref[0:1, :] = jnp.sum(grad_low.astype(FULL), axis=0, keepdims=True)
    sums_ref[1:2, :] = gain_sum
    sums_ref[2:3, :] = shift_sum
    put_slots(
        slots, slot_ref, dot(mixed_ref[...].T, grad_low), 0, slice(ff, ff + model)
    )
    copies = send_slots(slots, keep_ref, away_ref, out_sem)
    grad_mixed_ref[...] = dot(grad_low, weight[:, ff:], ((1,), (1,))).astype(LOW)
    for item in copies:
        item.wait()


def attend_back_body(seq, proj_ref, att_ref, grad_ref, out_ref):
    model = grad_ref.shape[1]
    pairs = model // (2 * HEAD)
    cells = grad_ref.shape[0] // seq
    lane = lax.broadcasted_iota(jnp.int32, (seq, 2 * HEAD), 1)
    scale = HEAD ** (-0.5)

    def step(index, carry):
        s = index // pairs
        p = index % pairs
        rows = pl.ds(pl.multiple_of(s * seq, seq), seq)
        at = pl.multiple_of(p * 2 * HEAD, 2 * HEAD)
        q = proj_ref[rows, pl.ds(at, 2 * HEAD)]
        k_turned = proj_ref[rows, pl.ds(at + model, 2 * HEAD)].T
        v = proj_ref[rows, pl.ds(at + 2 * model, 2 * HEAD)]
        g = grad_ref[rows, pl.ds(at, 2 * HEAD)]
        grad_q = []
        grad_k = []
        grad_v = []
        for i in range(2):
            own = (lane >= i * HEAD) & (lane < (i + 1) * HEAD)
            probs = att_ref[2 * index + i]
            wide = probs.astype(FULL)
            grad_probs = dot(jnp.where(own, v, jnp.zeros_like(v)), g, ((1,), (1,)))
            delta = jnp.sum(wide * grad_probs, axis=0, keepdims=True)
            scores = (wide * (grad_probs - delta)).astype(LOW)
            grad_q.append(dot(k_turned[i * HEAD : (i + 1) * HEAD], scores))
            grad_k.append(dot(scores, q))
            grad_v.append(dot(probs, g))
        first = lane < HEAD
        out_ref[rows, pl.ds(at, 2 * HEAD)] = (
            jnp.concatenate(grad_q, axis=0).T * scale
        ).astype(LOW)
        out_ref[rows, pl.ds(at + model, 2 * HEAD)] = (
            jnp.where(first, grad_k[0], grad_k[1]) * scale
        ).astype(LOW)
        out_ref[rows, pl.ds(at + 2 * model, 2 * HEAD)] = jnp.where(
            first, grad_v[0], grad_v[1]
        ).astype(LOW)
        return carry

    lax.fori_loop(0, cells * pairs, step, 0)


def first_back_body(
    sizes, order_ref, slot_ref, x_ref, low_ref, grad_proj_ref, grad_ref, small_ref, sums_ref,
    in_b_ref, down_b_ref, *refs,
):
    blocks = refs[: len(sizes)]
    out_ref, keep_ref, away_ref, weight, slots, small, sem, out_sem = refs[len(sizes) :]
    model = x_ref.shape[1]
    copies = fetch(order_ref, blocks, sizes, model // CELLS, 3 * model, weight, sem)
    turned = low_ref[...].T
    for j in range(3):
        lanes = slice(j * model, (j + 1) * model)
        put_slots(slots, slot_ref, dot(turned, grad_proj_ref[:, lanes]), 0, lanes)
    for item in copies:
        item.wait()
    grad_first = dot(grad_proj_ref[...], weight[...], ((1,), (1,)))
    center, scale = norm_parts(x_ref[...].astype(FULL))
    back, gain_sum, shift_sum = norm_back(
        center, scale, small_row(small_ref, "first_gain"), grad_first
    )
    out_ref[...] = (grad_ref[...] + back).astype(LOW)

    def put(name, value, offset=0):
        at = ROWS[name] + offset
        small[at : at + value.shape[0], :] = value

    small[...] = jnp.zeros_like(small)
    put("first_gain", gain_sum)
    put("first_shift", shift_sum)
    for i in range(2):
        part = grad_proj_ref[:, 2 * i * model : (2 * i + 1) * model].astype(FULL)
        put("qv_bias", jnp.sum(part, axis=0, keepdims=True), i)
    put("out_bias", sums_ref[0:1, :])
    put("second_gain", sums_ref[1:2, :])
    put("second_shift", sums_ref[2:3, :])
    put("in_bias", in_b_ref[...])
    put("down_bias", down_b_ref[...])
    for i in range(3):
        part = small[:, SMALL_LANES * i : SMALL_LANES * (i + 1)].astype(LOW)
        for device in range(CELLS):
            slots[device, 16 * i : 16 * i + 16, 3 * model :] = part
    for item in send_slots(slots, keep_ref, away_ref, out_sem):
        item.wait()


def finish_body(who_ref, one_ref, two_ref, *refs):
    grad_ref, vectors, small = refs[0], refs[1:-1], refs[-1]
    width = grad_ref.shape[1]
    total = one_ref[...].astype(FULL) + two_ref[...].astype(FULL)
    grad_ref[...] = total[:, :width]
    for i in range(3):
        small[:, SMALL_LANES * i : SMALL_LANES * (i + 1)] = total[16 * i : 16 * i + 16, width:]
    me = who_ref[0]
    model = small.shape[1]
    row = lax.broadcasted_iota(jnp.int32, (SMALL_ROWS, model), 0)
    names = (
        "first_gain", "first_shift", "qv_bias", "out_bias", "second_gain", "second_shift",
        "in_bias", "down_bias",
    )
    for name, ref in zip(names, vectors):
        size = ref.shape[1]
        per_row = model // size
        here_row = jnp.where(row == ROWS[name] + me // per_row, small[...], 0.0)
        values = jnp.sum(here_row, axis=0, keepdims=True)
        picker = one_hot(size, model, size * (me % per_row)).astype(FULL)
        ref[...] = lax.dot_general(
            values, picker, (((1,), (1,)), ((), ())), precision=lax.Precision.HIGHEST,
            preferred_element_type=FULL,
        )


def on_device_ring(
    tokens,
    lengths,
    cotangent,
    first_gain,
    first_shift,
    qkv_weight,
    qv_bias,
    out_weight,
    out_bias,
    second_gain,
    second_shift,
    in_weight,
    in_bias,
    down_weight,
    down_bias,
):
    micro, seq, model = tokens.shape[1:]
    total_rows = micro * seq
    rows = qkv_weight.shape[0]
    down_rows = down_weight.shape[0]
    ff = in_weight.shape[1]
    heads = model // HEAD
    whole = float(lax.axis_size("species") * CELLS * micro * seq)
    index, core, place = here()
    who = jnp.stack([index]).astype(jnp.int32)
    order = jnp.stack(gather_order(core, place)).astype(jnp.int32)
    slot = jnp.stack(scatter_slots(core, place)).astype(jnp.int32)
    lens = lengths.reshape(micro)
    x = tokens.reshape(total_rows, model)
    cot = cotangent.reshape(total_rows, model)
    vectors = (
        first_gain, first_shift, qv_bias, out_bias, second_gain, second_shift, in_bias, down_bias,
    )

    (qkv_block,) = call(
        pack_body,
        [shape((rows, 3 * model + SMALL_LANES))],
        [who] + [item.reshape(1, -1) for item in vectors] + [lens, qkv_weight],
        [SMEM] + [VMEM] * 8 + [SMEM, VMEM],
    )
    qkv_own = both_blocks(qkv_block, core)
    in_own = both_blocks(jnp.concatenate([in_weight, out_weight], axis=1), core)
    down_own = both_blocks(down_weight, core)
    qkv_got = [qkv_own]
    moving = qkv_own
    for step in range(3):
        moving = hop(moving)
        qkv_got += [moving, to_partner(moving)]
    last = hop(half_of(moving, core))
    qkv_got += [last, to_partner(last)]
    in_got = [in_own]
    down_got = [down_own]
    in_moving = hop(after(in_own, moving))
    down_moving = hop(after(down_own, last))
    for step in range(3):
        if step:
            in_moving = hop(in_moving)
            down_moving = hop(down_moving)
        in_got += [in_moving, to_partner(in_moving)]
        down_got += [down_moving, to_partner(down_moving)]
    in_last = hop(half_of(in_moving, core))
    in_got += [in_last, to_partner(in_last)]
    down_last = hop(half_of(down_moving, core))
    down_got += [down_last, to_partner(down_last)]

    dma = pltpu.SemaphoreType.DMA
    sizes = block_sizes(qkv_got)
    low, proj, att, mixed, small, count = call(
        lambda *refs: attend_body(sizes, seq, *refs),
        [
            shape((total_rows, model)),
            shape((total_rows, 3 * model)),
            shape((micro * heads, seq, seq)),
            shape((total_rows, model)),
            shape((SMALL_ROWS, model), FULL),
            shape((8, 128), FULL),
        ],
        [order, lens, x] + qkv_got,
        [SMEM, SMEM, VMEM] + [ANY] * 9,
        scratch=[
            pltpu.VMEM((model, 3 * model), LOW),
            pltpu.VMEM((CELLS, rows, SMALL_LANES), LOW),
            dma((CELLS,)),
            dma((CELLS,)),
        ],
        flops=12 * 10**9,
    )
    other_count = across(count)
    middle, low_two, active, slope, up_low, down_b, down_keep, down_away = call(
        lambda *refs: inner_body(sizes, seq, whole, *refs),
        [
            shape((total_rows, model), FULL),
            shape((total_rows, model)),
            shape((total_rows, ff)),
            shape((total_rows, ff)),
            shape((total_rows, model)),
            shape((1, model), FULL),
            shape((RING_SIZE, down_rows, model)),
            shape((RING_SIZE, down_rows, model)),
        ],
        [order, slot, lens, x, mixed, cot, small, count, other_count] + in_got,
        [SMEM] * 3 + [VMEM] * 6 + [ANY] * 9,
        [VMEM] * 6 + [ANY] * 2,
        scratch=[
            pltpu.VMEM((model, ff + model), LOW),
            pltpu.VMEM((CELLS, down_rows, model), LOW),
            dma((CELLS,)),
            dma((2,)),
        ],
        flops=15 * 10**9,
    )
    down_sum = reduce_blocks(down_keep, down_away, core)
    out_tokens, inner_low, in_b = call(
        lambda *refs: down_body(sizes, *refs),
        [shape((total_rows, model)), shape((total_rows, ff)), shape((ff // model, model), FULL)],
        [order, active, slope, middle, up_low, small] + down_got,
        [SMEM] + [VMEM] * 5 + [ANY] * 9,
        scratch=[pltpu.VMEM((ff, model), LOW), dma((CELLS,))],
        flops=7 * 10**9,
    )
    grad_middle, grad_mixed, sums, in_keep, in_away = call(
        lambda *refs: middle_back_body(sizes, seq, whole, *refs),
        [
            shape((total_rows, model), FULL),
            shape((total_rows, model)),
            shape((3, model), FULL),
            shape((RING_SIZE, rows, ff + model)),
            shape((RING_SIZE, rows, ff + model)),
        ],
        [order, slot, lens, inner_low, low_two, mixed, middle, cot, small, count, other_count]
        + in_got,
        [SMEM] * 3 + [VMEM] * 8 + [ANY] * 9,
        [VMEM] * 3 + [ANY] * 2,
        scratch=[
            pltpu.VMEM((model, ff + model), LOW),
            pltpu.VMEM((CELLS, rows, ff + model), LOW),
            dma((CELLS,)),
            dma((2,)),
        ],
        flops=9 * 10**9,
    )
    in_sum = reduce_blocks(in_keep, in_away, core)
    (grad_proj,) = call(
        lambda *refs: attend_back_body(seq, *refs),
        [shape((total_rows, 3 * model))],
        [proj, att, grad_mixed],
        [VMEM] * 3,
        flops=9 * 10**9,
    )
    grad_tokens, qkv_keep, qkv_away = call(
        lambda *refs: first_back_body(sizes, *refs),
        [
            shape((total_rows, model)),
            shape((RING_SIZE, rows, 3 * model + SMALL_LANES)),
            shape((RING_SIZE, rows, 3 * model + SMALL_LANES)),
        ],
        [order, slot, x, low, grad_proj, grad_middle, small, sums, in_b, down_b] + qkv_got,
        [SMEM] * 2 + [VMEM] * 8 + [ANY] * 9,
        [VMEM] + [ANY] * 2,
        scratch=[
            pltpu.VMEM((model, 3 * model), LOW),
            pltpu.VMEM((CELLS, rows, 3 * model + SMALL_LANES), LOW),
            pltpu.VMEM((SMALL_ROWS, model), FULL),
            dma((CELLS,)),
            dma((2,)),
        ],
        flops=7 * 10**9,
    )
    qkv_sum = reduce_blocks(qkv_keep, qkv_away, core)
    finished = call(
        finish_body,
        [shape((rows, 3 * model), FULL)]
        + [shape((1, item.shape[0]), FULL) for item in vectors],
        [who] + list(qkv_sum),
        [SMEM] + [VMEM] * 2,
        scratch=[pltpu.VMEM((SMALL_ROWS, model), FULL)],
    )
    grad_qkv = finished[0]
    pieces = [item.reshape(-1) for item in finished[1:]]
    in_total = in_sum[0].astype(FULL) + in_sum[1].astype(FULL)
    down_total = down_sum[0].astype(FULL) + down_sum[1].astype(FULL)
    return (
        out_tokens.reshape(tokens.shape),
        grad_tokens.reshape(tokens.shape),
        pieces[0],
        pieces[1],
        grad_qkv,
        pieces[2],
        in_total[:, ff:],
        pieces[3],
        pieces[4],
        pieces[5],
        in_total[:, :ff],
        pieces[6],
        down_total,
        pieces[7],
    )


def on_device(
    tokens,
    lengths,
    cotangent,
    first_gain,
    first_shift,
    qkv_weight,
    qv_bias,
    out_weight,
    out_bias,
    second_gain,
    second_shift,
    in_weight,
    in_bias,
    down_weight,
    down_bias,
):
    local_count = jnp.sum(lengths).astype(jnp.float32)
    count = lax.psum(local_count, ("species", "cells"))
    micro_count = tokens.shape[1]
    seq_rows = tokens.shape[2]
    factor = (
        float(lax.axis_size("species") * lax.axis_size("cells") * micro_count * seq_rows) / count
    )
    output_rows = []
    gradient_rows = []
    summed = None
    for micro_step in range(micro_count):
        gathered = (
            lax.all_gather(first_gain, "cells", axis=0, tiled=True),
            lax.all_gather(first_shift, "cells", axis=0, tiled=True),
            lax.all_gather(qkv_weight, "cells", axis=0, tiled=True),
            lax.all_gather(qv_bias, "cells", axis=0, tiled=True),
            lax.all_gather(out_weight, "cells", axis=0, tiled=True),
            lax.all_gather(out_bias, "cells", axis=0, tiled=True),
            lax.all_gather(second_gain, "cells", axis=0, tiled=True),
            lax.all_gather(second_shift, "cells", axis=0, tiled=True),
            lax.all_gather(in_weight, "cells", axis=0, tiled=True),
            lax.all_gather(in_bias, "cells", axis=0, tiled=True),
            lax.all_gather(down_weight, "cells", axis=0, tiled=True),
            lax.all_gather(down_bias, "cells", axis=0, tiled=True),
        )
        out_seq, grad_seq, grads = sequence_pass(
            gathered,
            tokens[0, micro_step],
            lengths[0, micro_step],
            cotangent[0, micro_step],
            factor,
        )
        output_rows.append(out_seq)
        gradient_rows.append(grad_seq)
        shares = (
            lax.psum_scatter(grads[0], "cells", scatter_dimension=0, tiled=True),
            lax.psum_scatter(grads[1], "cells", scatter_dimension=0, tiled=True),
            lax.psum_scatter(grads[2], "cells", scatter_dimension=0, tiled=True),
            lax.psum_scatter(grads[3], "cells", scatter_dimension=0, tiled=True),
            lax.psum_scatter(grads[4], "cells", scatter_dimension=0, tiled=True),
            lax.psum_scatter(grads[5], "cells", scatter_dimension=0, tiled=True),
            lax.psum_scatter(grads[6], "cells", scatter_dimension=0, tiled=True),
            lax.psum_scatter(grads[7], "cells", scatter_dimension=0, tiled=True),
            lax.psum_scatter(grads[8], "cells", scatter_dimension=0, tiled=True),
            lax.psum_scatter(grads[9], "cells", scatter_dimension=0, tiled=True),
            lax.psum_scatter(grads[10], "cells", scatter_dimension=0, tiled=True),
            lax.psum_scatter(grads[11], "cells", scatter_dimension=0, tiled=True),
        )
        summed = shares if summed is None else jax.tree.map(jnp.add, summed, shares)
    final = (
        lax.psum(summed[0].astype(jnp.bfloat16), "species").astype(jnp.float32),
        lax.psum(summed[1].astype(jnp.bfloat16), "species").astype(jnp.float32),
        lax.psum(summed[2].astype(jnp.bfloat16), "species").astype(jnp.float32),
        lax.psum(summed[3].astype(jnp.bfloat16), "species").astype(jnp.float32),
        lax.psum(summed[4].astype(jnp.bfloat16), "species").astype(jnp.float32),
        lax.psum(summed[5].astype(jnp.bfloat16), "species").astype(jnp.float32),
        lax.psum(summed[6].astype(jnp.bfloat16), "species").astype(jnp.float32),
        lax.psum(summed[7].astype(jnp.bfloat16), "species").astype(jnp.float32),
        lax.psum(summed[8].astype(jnp.bfloat16), "species").astype(jnp.float32),
        lax.psum(summed[9].astype(jnp.bfloat16), "species").astype(jnp.float32),
        lax.psum(summed[10].astype(jnp.bfloat16), "species").astype(jnp.float32),
        lax.psum(summed[11].astype(jnp.bfloat16), "species").astype(jnp.float32),
    )
    out_tokens = jnp.stack(output_rows)[None]
    grad_tokens = jnp.stack(gradient_rows)[None]
    return (out_tokens, grad_tokens) + tuple(final)


def solution(mesh):
    in_specs = (
        P("species", "cells", None, None),
        P("species", "cells"),
        P("species", "cells", None, None),
        P("cells"),
        P("cells"),
        P("cells", None),
        P("cells"),
        P("cells", None),
        P("cells"),
        P("cells"),
        P("cells"),
        P("cells", None),
        P("cells"),
        P("cells", None),
        P("cells"),
    )
    out_specs = (
        P("species", "cells", None, None),
        P("species", "cells", None, None),
        P("cells"),
        P("cells"),
        P("cells", None),
        P("cells"),
        P("cells", None),
        P("cells"),
        P("cells"),
        P("cells"),
        P("cells", None),
        P("cells"),
        P("cells", None),
        P("cells"),
    )
    program = on_device_ring if mesh.shape["cells"] == 2 * RING_SIZE else on_device
    return jax.shard_map(
        program, mesh=mesh, in_specs=in_specs, out_specs=out_specs, check_vma=False
    )
```

```python
import jax
import jax.numpy as jnp
from jax import lax
from jax.experimental import pallas as pl
from jax.experimental.pallas import tpu as pltpu
from jax.sharding import PartitionSpec as P

HEAD = 64


EPSILON = 1e-12
NEGATIVE = -1e30


def normalize(values, gain_vec, shift_vec):
    center = values - jnp.mean(values, axis=-1, keepdims=True)
    spread = jnp.mean(center * center, axis=-1, keepdims=True)
    return center * lax.rsqrt(spread + EPSILON) * gain_vec + shift_vec


def smooth_gate(values):
    return jax.nn.gelu(values, approximate=False)


def times_left(left_side, right_side):
    return lax.dot_general(
        left_side, right_side, (((0,), (0,)), ((), ())), preferred_element_type=jnp.float32
    )


def times_right(left_side, right_side):
    return lax.dot_general(
        left_side, right_side, (((1,), (1,)), ((), ())), preferred_element_type=jnp.float32
    )


def sequence_pass(weights, inputs, length, cot_rows, factor):
    (
        first_gain,
        first_shift,
        qkv_weight,
        qv_bias,
        out_weight,
        out_bias,
        second_gain,
        second_shift,
        in_weight,
        in_bias,
        down_weight,
        down_bias,
    ) = weights
    seq_rows = inputs.shape[0]
    model_width = inputs.shape[1]
    heads_count = model_width // HEAD
    scale_qk = float(HEAD) ** (-0.5)
    as_float = inputs.astype(jnp.float32)
    hidden_one, first_pull = jax.vjp(
        normalize, as_float, first_gain.astype(jnp.float32), first_shift.astype(jnp.float32)
    )
    first_low = hidden_one.astype(jnp.bfloat16)
    bias_float = qv_bias.astype(jnp.float32)
    full_bias = jnp.concatenate(
        [bias_float[:model_width], jnp.zeros((model_width,), jnp.float32), bias_float[model_width:]]
    )
    projected = (
        jnp.dot(first_low, qkv_weight, preferred_element_type=jnp.float32) + full_bias
    ).astype(jnp.bfloat16)
    split_heads = projected.reshape(seq_rows, 3, heads_count, HEAD)
    queries = split_heads[:, 0]
    keys_part = split_heads[:, 1]
    values_part = split_heads[:, 2]
    visible = jnp.arange(seq_rows) < length

    def scores_of():
        raw_scores = (
            jnp.einsum("qhd,khd->hqk", queries, keys_part, preferred_element_type=jnp.float32)
            * scale_qk
        )
        return jnp.where(visible[None, None, :], raw_scores, NEGATIVE)

    scores = scores_of()
    top_score = jnp.max(scores, axis=-1, keepdims=True)
    expo = jnp.exp(scores - top_score)
    total_exp = jnp.sum(expo, axis=-1, keepdims=True)
    log_total = top_score + jnp.log(total_exp)
    attention = (expo / total_exp).astype(jnp.bfloat16)
    mixed = jnp.einsum("hqk,khd->qhd", attention, values_part, preferred_element_type=jnp.float32)
    mixed = mixed.reshape(seq_rows, model_width).astype(jnp.bfloat16)
    middle = (
        as_float
        + jnp.dot(mixed, out_weight, preferred_element_type=jnp.float32)
        + out_bias.astype(jnp.float32)
    )
    hidden_two, second_pull = jax.vjp(
        normalize, middle, second_gain.astype(jnp.float32), second_shift.astype(jnp.float32)
    )
    second_low = hidden_two.astype(jnp.bfloat16)
    inner = jnp.dot(second_low, in_weight, preferred_element_type=jnp.float32) + in_bias.astype(
        jnp.float32
    )
    active, gate_pull = jax.vjp(smooth_gate, inner)
    active_low = active.astype(jnp.bfloat16)
    output = (
        middle
        + jnp.dot(active_low, down_weight, preferred_element_type=jnp.float32)
        + down_bias.astype(jnp.float32)
    )
    upstream = cot_rows.astype(jnp.float32) * visible[:, None].astype(jnp.float32) * factor
    up_low = upstream.astype(jnp.bfloat16)
    grad_down_bias = jnp.sum(up_low.astype(jnp.float32), axis=0)
    grad_down = times_left(active_low, up_low)
    grad_active = times_right(up_low, down_weight)
    (grad_inner,) = gate_pull(grad_active)
    inner_low = grad_inner.astype(jnp.bfloat16)
    grad_in_bias = jnp.sum(inner_low.astype(jnp.float32), axis=0)
    grad_in = times_left(second_low, inner_low)
    grad_second = times_right(inner_low, in_weight)
    grad_middle_norm, grad_second_gain, grad_second_shift = second_pull(grad_second)
    grad_middle = upstream + grad_middle_norm
    middle_low = grad_middle.astype(jnp.bfloat16)
    grad_out_bias = jnp.sum(middle_low.astype(jnp.float32), axis=0)
    grad_out = times_left(mixed, middle_low)
    grad_mixed = (
        times_right(middle_low, out_weight)
        .astype(jnp.bfloat16)
        .reshape(seq_rows, heads_count, HEAD)
    )
    probs_again = jnp.exp(scores_of() - log_total)
    grad_probs = jnp.einsum(
        "qhd,khd->hqk", grad_mixed, values_part, preferred_element_type=jnp.float32
    )
    grad_values = jnp.einsum(
        "hqk,qhd->khd", attention, grad_mixed, preferred_element_type=jnp.float32
    )
    delta = jnp.sum(probs_again * grad_probs, axis=-1, keepdims=True)
    grad_scores = (probs_again * (grad_probs - delta)).astype(jnp.bfloat16)
    grad_queries = (
        jnp.einsum("hqk,khd->qhd", grad_scores, keys_part, preferred_element_type=jnp.float32)
        * scale_qk
    )
    grad_keys = (
        jnp.einsum("hqk,qhd->khd", grad_scores, queries, preferred_element_type=jnp.float32)
        * scale_qk
    )
    grad_projected = jnp.stack([grad_queries, grad_keys, grad_values], axis=1)
    grad_projected = grad_projected.reshape(seq_rows, 3 * model_width).astype(jnp.bfloat16)
    column_sums = jnp.sum(grad_projected.astype(jnp.float32), axis=0)
    grad_qv = jnp.concatenate([column_sums[:model_width], column_sums[2 * model_width :]])
    grad_qkv = times_left(first_low, grad_projected)
    grad_first = times_right(grad_projected, qkv_weight)
    grad_input_norm, grad_first_gain, grad_first_shift = first_pull(grad_first)
    grad_inputs = grad_middle + grad_input_norm
    grads = (
        grad_first_gain,
        grad_first_shift,
        grad_qkv,
        grad_qv,
        grad_out,
        grad_out_bias,
        grad_second_gain,
        grad_second_shift,
        grad_in,
        grad_in_bias,
        grad_down,
        grad_down_bias,
    )
    return (output.astype(jnp.bfloat16), grad_inputs.astype(jnp.bfloat16), grads)


RING = (0, 2, 4, 6, 7, 5, 3, 1)
RING_SIZE = len(RING)
CELLS = 2 * RING_SIZE
ANY = pl.BlockSpec(memory_space=pl.ANY)
VMEM = pl.BlockSpec(memory_space=pltpu.VMEM)
SMEM = pl.BlockSpec(memory_space=pltpu.SMEM)
LOW = jnp.bfloat16
FULL = jnp.float32
ROWS = {
    "first_gain": 0,
    "first_shift": 1,
    "qv_bias": 2,
    "out_bias": 4,
    "second_gain": 5,
    "second_shift": 6,
    "in_bias": 7,
    "down_bias": 11,
    "lengths": 12,
}
NAMES = tuple(ROWS)[:8]
SMALL_ROWS = 16
SMALL_LANES = 256
PIECES = (2, 2, 2, 2, 2, 2, 2, 1, 1)


def ring_pairs():
    pairs = []
    for place in range(RING_SIZE):
        chip = RING[place]
        right = RING[(place + 1) % RING_SIZE]
        left = RING[(place - 1) % RING_SIZE]
        pairs.append((2 * chip, 2 * right))
        pairs.append((2 * chip + 1, 2 * left + 1))
    return pairs


def hop(block):
    return lax.ppermute(block, "cells", ring_pairs())


def to_partner(block):
    return lax.ppermute(block, "cells", [(i, i ^ 1) for i in range(CELLS)])


def across(block):
    return lax.ppermute(block, "species", [(0, 1), (1, 0)])


def after(value, *others):
    return lax.optimization_barrier((value,) + others)[0]


def here():
    index = lax.axis_index("cells")
    core = index % 2
    chip = index // 2
    place = jnp.int32(0)
    for i, ring_chip in enumerate(RING):
        place = jnp.where(chip == ring_chip, i, place)
    return index, core, place


def chip_at(place):
    place = place % RING_SIZE
    chip = jnp.zeros_like(place)
    for i, ring_chip in enumerate(RING):
        chip = jnp.where(place == i, ring_chip, chip)
    return chip


def gather_order(core, place):
    sign = 1 - 2 * core
    order = []

    def pair(at):
        order.append(2 * chip_at(at))
        order.append(2 * chip_at(at) + 1)

    pair(place)
    for step in range(1, 4):
        pair(place - sign * step)
        pair(place + sign * step)
    order.append(2 * chip_at(place + 4) + core)
    order.append(2 * chip_at(place + 4) + 1 - core)
    return order


def scatter_slots(core, place):
    def kept(core_now):
        sign = 1 - 2 * core_now
        order = [2 * chip_at(place + 4) + core_now]
        for step in (3, 2, 1):
            order.append(2 * chip_at(place + sign * step))
            order.append(2 * chip_at(place + sign * step) + 1)
        order.append(2 * chip_at(place) + core_now)
        return order

    order = kept(core) + kept(1 - core)
    slots = []
    for device in range(CELLS):
        slot = jnp.int32(0)
        for i, who in enumerate(order):
            slot = jnp.where(who == device, i, slot)
        slots.append(slot)
    return slots


def both_blocks(block, core):
    other = to_partner(block)
    return jnp.stack([jnp.where(core == 0, block, other), jnp.where(core == 0, other, block)])


def half_of(pair, core):
    return jnp.where(core == 0, pair[0], pair[1])[None]


def add_low(*parts):
    total = parts[0].astype(FULL)
    for part in parts[1:]:
        total = total + part.astype(FULL)
    return total.astype(LOW)


def first_hop(keep, got):
    return hop(add_low(keep[0:1], got[0:1]))


def second_hop(keep, got, moving, core):
    wide = jnp.stack([jnp.where(core == 0, moving[0], 0), jnp.where(core == 0, 0, moving[0])])
    return hop(add_low(keep[1:3], got[1:3], wide))


def later_hop(keep, got, moving, at):
    return hop(add_low(keep[at : at + 2], got[at : at + 2], moving))


def settle(keep, got, moving, core):
    mine = jnp.where(core == 0, moving[0], moving[1])
    other = jnp.where(core == 0, moving[1], moving[0])
    total = add_low(keep[7], got[7], mine, to_partner(other))
    return total, across(total)


def dot(left, right, dims=((1,), (0,))):
    return lax.dot_general(left, right, (dims, ((), ())), preferred_element_type=FULL)


def call(body, out_shape, ins, specs, out_specs=None, scratch=(), vmem=48, flops=0, moved=0):
    return pl.pallas_call(
        body,
        out_shape=out_shape,
        in_specs=specs,
        out_specs=[VMEM] * len(out_shape) if out_specs is None else out_specs,
        scratch_shapes=list(scratch),
        compiler_params=pltpu.CompilerParams(vmem_limit_bytes=vmem * 2**20),
        cost_estimate=pl.CostEstimate(flops=flops, bytes_accessed=moved, transcendentals=0),
    )(*ins)


def shape(dims, kind=LOW):
    return jax.ShapeDtypeStruct(dims, kind)


def fetch(order_ref, refs, sizes, target, first, lanes, sem, extra=None, extra_sem=None):
    rows = target.shape[0] // CELLS
    copies = []
    index = 0
    for source, size in zip(refs, sizes):
        for part in range(size):
            at = order_ref[index]
            copies.append(
                pltpu.make_async_copy(
                    source.at[part, :, pl.ds(0, lanes)],
                    target.at[pl.ds(pl.multiple_of(at * rows, 16), rows), pl.ds(first, lanes)],
                    sem.at[index],
                )
            )
            if extra is not None:
                copies.append(
                    pltpu.make_async_copy(
                        source.at[part, :, pl.ds(lanes, SMALL_LANES)],
                        extra.at[at],
                        extra_sem.at[index],
                    )
                )
            index += 1
    for item in copies:
        item.start()
    return copies


def fetch_qkv(order_ref, blocks, weight, sems, extra=None, extra_sem=None):
    width = weight.shape[1]
    first = (width + SMALL_LANES) // 2
    half = len(blocks) // 2
    copies = fetch(order_ref, blocks[:half], PIECES, weight, 0, first, sems.at[0])
    copies += fetch(
        order_ref, blocks[half:], PIECES, weight, first, width - first, sems.at[1], extra,
        extra_sem,
    )
    return copies


def wait_all(copies):
    for item in copies:
        item.wait()


def one_hot(rows, lanes, offset):
    row = lax.broadcasted_iota(jnp.int32, (rows, lanes), 0)
    lane = lax.broadcasted_iota(jnp.int32, (rows, lanes), 1)
    return lane == row + offset


def pack_body(who_ref, lengths_ref, weight_ref, *refs):
    sources, block_ref, targets, sem = refs[:8], refs[8], refs[9:17], refs[17]
    me = who_ref[0]
    width = block_ref.shape[1] - SMALL_LANES
    copies = [
        pltpu.make_async_copy(source, target, sem.at[i])
        for i, (source, target) in enumerate(zip(sources, targets))
    ]
    weight = pltpu.make_async_copy(
        weight_ref.at[:, pl.ds(weight_ref.shape[1] - width, width)],
        block_ref.at[:, pl.ds(0, width)],
        sem.at[8],
    )
    for item in copies:
        item.start()
    weight.start()
    wait_all(copies)
    model = CELLS * targets[0].shape[1]
    row = lax.broadcasted_iota(jnp.int32, (SMALL_ROWS, model), 0)
    lane = lax.broadcasted_iota(jnp.int32, (SMALL_ROWS, model), 1)
    small = jnp.zeros((SMALL_ROWS, model), FULL)
    for name, ref in zip(NAMES, targets):
        size = ref.shape[1]
        per_row = model // size
        placed = dot(ref[...], one_hot(size, model, size * (me % per_row)).astype(LOW))
        small = small + jnp.where(row == ROWS[name] + me // per_row, placed, 0.0)
    for i in range(2):
        at = (row == ROWS["lengths"]) & (lane == 2 * me + i)
        small = small + jnp.where(at, lengths_ref[i].astype(FULL), 0.0)
    small = small.astype(LOW)
    for i in range(3):
        block_ref[16 * i : 16 * i + 16, width : width + SMALL_LANES] = small[
            :, SMALL_LANES * i : SMALL_LANES * (i + 1)
        ]
    weight.wait()


def norm_parts(values):
    center = values - jnp.mean(values, axis=-1, keepdims=True)
    spread = jnp.mean(center * center, axis=-1, keepdims=True)
    return center, lax.rsqrt(spread + EPSILON)


def norm_back(center, scale, gain, grad):
    weighted = grad * gain
    mean_one = jnp.mean(weighted, axis=-1, keepdims=True)
    mean_two = jnp.mean(weighted * center, axis=-1, keepdims=True)
    back = scale * (weighted - mean_one - center * (scale * scale * mean_two))
    return back, jnp.sum(grad * center * scale, axis=0, keepdims=True), jnp.sum(
        grad, axis=0, keepdims=True
    )


def small_row(small_ref, name, count=1):
    return small_ref[ROWS[name] : ROWS[name] + count, :]


def project_body(seq, order_ref, x_ref, *refs):
    blocks = refs[:18]
    low_ref, proj_ref, small_ref, count_ref, weight, extra, sem, extra_sem = refs[18:]
    model = x_ref.shape[1]
    copies = fetch_qkv(order_ref, blocks, weight, sem, extra, extra_sem)
    center, scale = norm_parts(x_ref[...].astype(FULL))
    wait_all(copies)
    total = extra[0].astype(FULL)
    for i in range(1, CELLS):
        total = total + extra[i].astype(FULL)
    for i in range(3):
        small_ref[:, SMALL_LANES * i : SMALL_LANES * (i + 1)] = total[16 * i : 16 * i + 16]
    count_ref[...] = jnp.broadcast_to(
        jnp.sum(small_row(small_ref, "lengths"), axis=-1, keepdims=True), count_ref.shape
    )
    bias = small_row(small_ref, "qv_bias", 2)
    low_ref[...] = (
        center * scale * small_row(small_ref, "first_gain") + small_row(small_ref, "first_shift")
    ).astype(LOW)
    for j in range(3):
        lanes = slice(j * model, (j + 1) * model)
        part = dot(low_ref[...], weight[:, lanes])
        if j != 1:
            part = part + bias[j // 2 : j // 2 + 1]
        proj_ref[:, lanes] = part.astype(LOW)


def attend_body(seq, lengths_ref, proj_ref, att_ref, mixed_ref):
    model = mixed_ref.shape[1]
    cells = mixed_ref.shape[0] // seq
    pairs = model // (2 * HEAD)
    lane = lax.broadcasted_iota(jnp.int32, (seq, 2 * HEAD), 1)
    key = lax.broadcasted_iota(jnp.int32, (seq, seq), 0)

    def step(index, carry):
        s = index // pairs
        p = index % pairs
        rows = pl.ds(pl.multiple_of(s * seq, seq), seq)
        at = pl.multiple_of(p * 2 * HEAD, 2 * HEAD)
        q = proj_ref[rows, pl.ds(at, 2 * HEAD)] * jnp.asarray(HEAD ** (-0.5), LOW)
        k = proj_ref[rows, pl.ds(at + model, 2 * HEAD)]
        v_turned = proj_ref[rows, pl.ds(at + 2 * model, 2 * HEAD)].T
        visible = key < lengths_ref[s]
        mixed = []
        for i in range(2):
            own = (lane >= i * HEAD) & (lane < (i + 1) * HEAD)
            scores = dot(jnp.where(own, k, jnp.zeros_like(k)), q, ((1,), (1,)))
            scores = jnp.where(visible, scores, NEGATIVE)
            expo = jnp.exp(scores - jnp.max(scores, axis=0, keepdims=True))
            probs = expo * (1.0 / jnp.sum(expo, axis=0, keepdims=True))
            probs = probs.astype(LOW)
            att_ref[2 * index + i] = probs
            mixed.append(dot(v_turned[i * HEAD : (i + 1) * HEAD], probs))
        mixed_ref[rows, pl.ds(at, 2 * HEAD)] = jnp.concatenate(mixed, axis=0).T.astype(LOW)
        return carry

    lax.fori_loop(0, cells * pairs, step, 0, unroll=2)


ERFC_STEP = 0.33
ERFC = (
    0.1863578228018033,
    0.18295566386742124,
    0.2012255082472392,
    0.04721561458875723,
    0.4085089979423051,
    -0.35115900736338407,
    0.4602422572120205,
    -0.13534686486277223,
)


def gelu_parts(inner):
    z = jnp.abs(inner) * (0.5**0.5)
    t = 1.0 / (1.0 + ERFC_STEP * z)
    tail = jnp.full_like(t, 0.5 * ERFC[-1])
    for factor in ERFC[-2::-1]:
        tail = tail * t + 0.5 * factor
    bell = jnp.exp(-(z * z))
    tail = tail * t * bell
    area = jnp.where(inner < 0.0, tail, 1.0 - tail)
    return inner * area, area + inner * bell * (0.5 / 3.141592653589793) ** 0.5


def row_mask(lengths_ref, rows, seq):
    at = lax.broadcasted_iota(jnp.int32, (rows, 1), 0)
    true = (at < lengths_ref[0]).astype(FULL)
    for s in range(1, rows // seq):
        true = jnp.where(at < s * seq, true, (at < lengths_ref[s] + s * seq).astype(FULL))
    return true


def loss_rows(lengths_ref, count_ref, other_ref, cot_ref, seq, whole):
    factor = whole / (count_ref[0:1, 0:1] + other_ref[0:1, 0:1])
    return cot_ref[...].astype(FULL) * (row_mask(lengths_ref, cot_ref.shape[0], seq) * factor)


def put_slots(keep_buf, slot_ref, values, first, lanes):
    rows = keep_buf.shape[1]
    for i in range(values.shape[0] // rows):
        keep_buf[slot_ref[first + i], :, lanes] = values[i * rows : (i + 1) * rows].astype(LOW)


def send_slots(buf, keep_ref, away_ref, sem):
    half = RING_SIZE
    copies = [
        pltpu.make_async_copy(buf.at[pl.ds(half, half)], away_ref, sem.at[0]),
        pltpu.make_async_copy(buf.at[pl.ds(0, half)], keep_ref, sem.at[1]),
    ]
    for item in copies:
        item.start()
    return copies


def inner_body(order_ref, x_ref, mixed_ref, small_ref, *refs):
    blocks = refs[:9]
    middle_ref, low_ref, active_ref, slope_ref, weight, sem = refs[9:]
    model = x_ref.shape[1]
    ff = active_ref.shape[1]
    wait_all(fetch(order_ref, blocks, PIECES, weight, 0, ff + model, sem))
    middle = (
        x_ref[...].astype(FULL)
        + dot(mixed_ref[...], weight[:, ff:])
        + small_row(small_ref, "out_bias")
    )
    middle_ref[...] = middle
    center, scale = norm_parts(middle)
    low = center * scale * small_row(small_ref, "second_gain") + small_row(
        small_ref, "second_shift"
    )
    low_ref[...] = low.astype(LOW)
    step = 2 * (ff // RING_SIZE)
    bias = small_row(small_ref, "in_bias", 4)
    for j in range(ff // step):
        lanes = slice(j * step, (j + 1) * step)
        inner = dot(low_ref[...], weight[:, lanes]) + bias[j : j + 1]
        active, slope = gelu_parts(inner)
        active_ref[:, lanes] = active.astype(LOW)
        slope_ref[:, lanes] = slope.astype(LOW)


def grad_down_body(
    seq, whole, slot_ref, lengths_ref, active_ref, cot_ref, count_ref, other_ref, *refs
):
    up_ref, down_b_ref, keep_ref, away_ref, slots, sem = refs
    up_low = loss_rows(lengths_ref, count_ref, other_ref, cot_ref, seq, whole).astype(LOW)
    up_ref[...] = up_low
    down_b_ref[...] = jnp.sum(up_low.astype(FULL), axis=0, keepdims=True)
    parts = RING_SIZE
    step = active_ref.shape[1] // parts
    for j in range(parts):
        grad = dot(active_ref[:, j * step : (j + 1) * step], up_ref[...], ((0,), (0,)))
        put_slots(slots, slot_ref, grad, j * CELLS // parts, slice(None))
    wait_all(send_slots(slots, keep_ref, away_ref, sem))


def down_body(order_ref, active_ref, slope_ref, middle_ref, up_ref, small_ref, *refs):
    blocks = refs[:9]
    out_ref, inner_ref, in_b_ref, weight, sem = refs[9:]
    ff, model = weight.shape
    wait_all(fetch(order_ref, blocks, PIECES, weight, 0, model, sem))
    for j in range(ff // model):
        lanes = slice(j * model, (j + 1) * model)
        grad = dot(up_ref[...], weight[lanes, :], ((1,), (1,)))
        low = (grad * slope_ref[:, lanes].astype(FULL)).astype(LOW)
        inner_ref[:, lanes] = low
        in_b_ref[j : j + 1, :] = jnp.sum(low.astype(FULL), axis=0, keepdims=True)
    out_ref[...] = (
        middle_ref[...]
        + dot(active_ref[...], weight[...])
        + small_row(small_ref, "down_bias")
    ).astype(LOW)


def grad_in_body(slot_ref, low_ref, inner_ref, keep_ref, away_ref, slots, sem):
    model = low_ref.shape[1]
    turned = low_ref[...].T
    for j in range(inner_ref.shape[1] // model):
        lanes = slice(j * model, (j + 1) * model)
        put_slots(slots, slot_ref, dot(turned, inner_ref[:, lanes]), 0, lanes)
    wait_all(send_slots(slots, keep_ref, away_ref, sem))


def middle_back_body(
    seq, whole, order_ref, lengths_ref, inner_ref, mixed_ref, middle_ref, cot_ref, small_ref,
    count_ref, other_ref, *refs,
):
    blocks = refs[:9]
    grad_ref, grad_mixed_ref, sums_ref, grad_out_ref, weight, sem = refs[9:]
    model = middle_ref.shape[1]
    ff = inner_ref.shape[1]
    wait_all(fetch(order_ref, blocks, PIECES, weight, 0, ff + model, sem))
    grad_second = dot(inner_ref[...], weight[:, :ff], ((1,), (1,)))
    center, scale = norm_parts(middle_ref[...])
    back, gain_sum, shift_sum = norm_back(
        center, scale, small_row(small_ref, "second_gain"), grad_second
    )
    grad = loss_rows(lengths_ref, count_ref, other_ref, cot_ref, seq, whole) + back
    grad_ref[...] = grad
    grad_low = grad.astype(LOW)
    sums_ref[0:1, :] = jnp.sum(grad_low.astype(FULL), axis=0, keepdims=True)
    sums_ref[1:2, :] = gain_sum
    sums_ref[2:3, :] = shift_sum
    grad_mixed_ref[...] = dot(grad_low, weight[:, ff:], ((1,), (1,))).astype(LOW)
    grad_out_ref[...] = dot(mixed_ref[...].T, grad_low).astype(LOW)


def attend_back_body(seq, part, proj_ref, att_ref, grad_ref, out_ref):
    model = grad_ref.shape[1]
    half = model // 2
    all_pairs = model // (2 * HEAD)
    pairs = all_pairs // 2
    cells = grad_ref.shape[0] // seq
    lane = lax.broadcasted_iota(jnp.int32, (seq, 2 * HEAD), 1)
    scale = HEAD ** (-0.5)

    def step(index, carry):
        s = index // pairs
        p = index % pairs
        rows = pl.ds(pl.multiple_of(s * seq, seq), seq)
        to = pl.multiple_of(p * 2 * HEAD, 2 * HEAD)
        at = pl.multiple_of(to + part * half, 2 * HEAD)
        q = proj_ref[rows, pl.ds(at, 2 * HEAD)]
        k_turned = proj_ref[rows, pl.ds(at + model, 2 * HEAD)].T
        v = proj_ref[rows, pl.ds(at + 2 * model, 2 * HEAD)]
        g = grad_ref[rows, pl.ds(at, 2 * HEAD)]
        grad_q = []
        grad_k = []
        grad_v = []
        for i in range(2):
            own = (lane >= i * HEAD) & (lane < (i + 1) * HEAD)
            probs = att_ref[2 * (s * all_pairs + part * pairs + p) + i]
            wide = probs.astype(FULL)
            grad_probs = dot(jnp.where(own, v, jnp.zeros_like(v)), g, ((1,), (1,)))
            delta = jnp.sum(wide * grad_probs, axis=0, keepdims=True)
            scores = (wide * (grad_probs - delta)).astype(LOW)
            grad_q.append(dot(k_turned[i * HEAD : (i + 1) * HEAD], scores))
            grad_k.append(dot(scores, q))
            grad_v.append(dot(probs, g))
        first = lane < HEAD
        out_ref[rows, pl.ds(to, 2 * HEAD)] = (
            jnp.concatenate(grad_q, axis=0).T * scale
        ).astype(LOW)
        out_ref[rows, pl.ds(to + half, 2 * HEAD)] = (
            jnp.where(first, grad_k[0], grad_k[1]) * scale
        ).astype(LOW)
        out_ref[rows, pl.ds(to + 2 * half, 2 * HEAD)] = jnp.where(
            first, grad_v[0], grad_v[1]
        ).astype(LOW)
        return carry

    lax.fori_loop(0, cells * pairs, step, 0, unroll=2)


def grad_qkv_body(slot_ref, low_ref, part_ref, grad_out_ref, keep_ref, away_ref, slots, sem):
    width = part_ref.shape[1]
    put_slots(slots, slot_ref, dot(low_ref[...].T, part_ref[...]), 0, slice(0, width))
    put_slots(slots, slot_ref, grad_out_ref[...], 0, slice(width, slots.shape[2]))
    wait_all(send_slots(slots, keep_ref, away_ref, sem))


def first_back_body(
    order_ref, slot_ref, x_ref, low_ref, one_ref, two_ref, grad_ref, small_ref, sums_ref,
    in_b_ref, down_b_ref, *refs,
):
    blocks = refs[:18]
    out_ref, keep_ref, away_ref, weight, slots, small, sem, out_sem = refs[18:]
    model = x_ref.shape[1]
    half = model // 2
    width = two_ref.shape[1]
    copies = fetch_qkv(order_ref, blocks, weight, sem)
    put_slots(slots, slot_ref, dot(low_ref[...].T, two_ref[...]), 0, slice(0, width))
    wait_all(copies)
    grad_first = jnp.zeros(x_ref.shape, FULL)
    for j in range(3):
        for i, ref in enumerate((one_ref, two_ref)):
            at = j * model + i * half
            grad_first = grad_first + dot(
                ref[:, j * half : (j + 1) * half], weight[:, at : at + half], ((1,), (1,))
            )
    center, scale = norm_parts(x_ref[...].astype(FULL))
    back, gain_sum, shift_sum = norm_back(
        center, scale, small_row(small_ref, "first_gain"), grad_first
    )

    def put(name, value, offset=0):
        at = ROWS[name] + offset
        small[at : at + value.shape[0], :] = value

    small[...] = jnp.zeros_like(small)
    put("first_gain", gain_sum)
    put("first_shift", shift_sum)
    for j in range(2):
        for i, ref in enumerate((one_ref, two_ref)):
            part = ref[:, 2 * j * half : (2 * j + 1) * half].astype(FULL)
            small[ROWS["qv_bias"] + j : ROWS["qv_bias"] + j + 1, i * half : (i + 1) * half] = (
                jnp.sum(part, axis=0, keepdims=True)
            )
    put("out_bias", sums_ref[0:1, :])
    put("second_gain", sums_ref[1:2, :])
    put("second_shift", sums_ref[2:3, :])
    put("in_bias", in_b_ref[...])
    put("down_bias", down_b_ref[...])
    for i in range(3):
        part = small[:, SMALL_LANES * i : SMALL_LANES * (i + 1)].astype(LOW)
        for device in range(CELLS):
            slots[device, 16 * i : 16 * i + 16, width:] = part
    copies = send_slots(slots, keep_ref, away_ref, out_sem)
    out_ref[...] = (grad_ref[...] + back).astype(LOW)
    wait_all(copies)


def finish_body(who_ref, early_ref, early_two_ref, late_ref, late_two_ref, *refs):
    grad_ref, out_ref, vectors, small = refs[0], refs[1], refs[2:-1], refs[-1]
    model = out_ref.shape[1]
    half = model // 2
    early = early_ref[...].astype(FULL) + early_two_ref[...].astype(FULL)
    late = late_ref[...].astype(FULL) + late_two_ref[...].astype(FULL)
    for j in range(3):
        at = j * model
        grad_ref[:, at : at + half] = early[:, j * half : (j + 1) * half]
        grad_ref[:, at + half : at + model] = late[:, j * half : (j + 1) * half]
    out_ref[...] = early[:, 3 * half :]
    for i in range(3):
        small[:, SMALL_LANES * i : SMALL_LANES * (i + 1)] = late[16 * i : 16 * i + 16, 3 * half :]
    me = who_ref[0]
    row = lax.broadcasted_iota(jnp.int32, (SMALL_ROWS, model), 0)
    for name, ref in zip(NAMES, vectors):
        size = ref.shape[1]
        per_row = model // size
        here_row = jnp.where(row == ROWS[name] + me // per_row, small[...], 0.0)
        values = jnp.sum(here_row, axis=0, keepdims=True)
        picker = one_hot(size, model, size * (me % per_row)).astype(FULL)
        ref[...] = lax.dot_general(
            values, picker, (((1,), (1,)), ((), ())), precision=lax.Precision.HIGHEST,
            preferred_element_type=FULL,
        )


def on_device_ring(
    tokens,
    lengths,
    cotangent,
    first_gain,
    first_shift,
    qkv_weight,
    qv_bias,
    out_weight,
    out_bias,
    second_gain,
    second_shift,
    in_weight,
    in_bias,
    down_weight,
    down_bias,
):
    micro, seq, model = tokens.shape[1:]
    total_rows = micro * seq
    rows = qkv_weight.shape[0]
    down_rows = down_weight.shape[0]
    ff = in_weight.shape[1]
    heads = model // HEAD
    whole = float(lax.axis_size("species") * CELLS * micro * seq)
    index, core, place = here()
    who = jnp.stack([index]).astype(jnp.int32)
    order = jnp.stack(gather_order(core, place)).astype(jnp.int32)
    slot = jnp.stack(scatter_slots(core, place)).astype(jnp.int32)
    lens = lengths.reshape(micro)
    x = tokens.reshape(total_rows, model)
    cot = cotangent.reshape(total_rows, model)
    vectors = (
        first_gain, first_shift, qv_bias, out_bias, second_gain, second_shift, in_bias, down_bias,
    )

    dma = pltpu.SemaphoreType.DMA
    qkv_first = (3 * model + SMALL_LANES) // 2

    ones = both_blocks(qkv_weight[:, :qkv_first], core)
    (two_block,) = call(
        pack_body,
        [shape((rows, qkv_first))],
        [who, lens, qkv_weight] + [item.reshape(1, -1) for item in vectors],
        [SMEM, SMEM] + [ANY] * 9,
        scratch=[pltpu.VMEM((1, item.shape[0]), LOW) for item in vectors] + [dma((9,))],
        vmem=4,
    )
    twos = both_blocks(two_block, core)
    in_own = both_blocks(jnp.concatenate([in_weight, out_weight], axis=1), core)
    down_own = both_blocks(down_weight, core)
    one_got = [ones]
    two_got = [twos]
    for step in range(3):
        ones = hop(ones)
        twos = hop(twos)
        one_got += [ones, to_partner(ones)]
        two_got += [twos, to_partner(twos)]
    in_one = hop(after(in_own, ones))
    one_last = hop(half_of(ones, core))
    two_last = hop(half_of(twos, core))
    one_got += [one_last, to_partner(one_last)]
    two_got += [two_last, to_partner(two_last)]
    down_one = hop(after(down_own, two_last))
    qkv_got = one_got + two_got

    low, proj, small, count = call(
        lambda *refs: project_body(seq, *refs),
        [
            shape((total_rows, model)),
            shape((total_rows, 3 * model)),
            shape((SMALL_ROWS, model), FULL),
            shape((8, 128), FULL),
        ],
        [order, x] + qkv_got,
        [SMEM, VMEM] + [ANY] * 18,
        scratch=[
            pltpu.VMEM((model, 3 * model), LOW),
            pltpu.VMEM((CELLS, rows, SMALL_LANES), LOW),
            dma((2, CELLS)),
            dma((CELLS,)),
        ],
        vmem=20,
        flops=5 * 10**9,
    )
    other_count = across(count)
    in_two = hop(after(in_one, proj))
    att, mixed = call(
        lambda *refs: attend_body(seq, *refs),
        [shape((micro * heads, seq, seq)), shape((total_rows, model))],
        [lens, after(proj, in_one)],
        [SMEM, VMEM],
        vmem=16,
        flops=9 * 10**9,
    )
    in_three = hop(after(in_two, mixed))
    down_two = hop(after(down_one, mixed))
    in_last = hop(half_of(in_three, core))
    down_three = hop(after(down_two, in_three))
    in_got = [in_own]
    for item in (in_one, in_two, in_three, in_last):
        in_got += [item, to_partner(item)]
    middle, low_two, active, slope = call(
        inner_body,
        [
            shape((total_rows, model), FULL),
            shape((total_rows, model)),
            shape((total_rows, ff)),
            shape((total_rows, ff)),
        ],
        [order, x, after(mixed, down_two), small] + in_got,
        [SMEM] + [VMEM] * 3 + [ANY] * 9,
        scratch=[pltpu.VMEM((model, ff + model), LOW), dma((CELLS,))],
        vmem=24,
        flops=12 * 10**9,
    )
    down_last = hop(half_of(after(down_three, active), core))
    down_got = [down_own]
    for item in (down_one, down_two, down_three, down_last):
        down_got += [item, to_partner(item)]
    up_low, down_b, down_keep, down_away = call(
        lambda *refs: grad_down_body(seq, whole, *refs),
        [
            shape((total_rows, model)),
            shape((1, model), FULL),
            shape((RING_SIZE, down_rows, model)),
            shape((RING_SIZE, down_rows, model)),
        ],
        [slot, lens, after(active, down_three), cot, count, other_count],
        [SMEM] * 2 + [VMEM] * 4,
        [VMEM] * 2 + [ANY] * 2,
        scratch=[pltpu.VMEM((CELLS, down_rows, model), LOW), dma((2,))],
        vmem=18,
        flops=6 * 10**9,
    )

    down_other = to_partner(down_away)
    out_tokens, inner_low, in_b = call(
        down_body,
        [shape((total_rows, model)), shape((total_rows, ff)), shape((ff // model, model), FULL)],
        [order, active, slope, middle, up_low, small] + down_got,
        [SMEM] + [VMEM] * 5 + [ANY] * 9,
        scratch=[pltpu.VMEM((ff, model), LOW), dma((CELLS,))],
        vmem=24,
        flops=8 * 10**9,
    )
    down_sum = first_hop(down_keep, down_other)
    in_keep, in_away = call(
        grad_in_body,
        [shape((RING_SIZE, rows, ff)), shape((RING_SIZE, rows, ff))],
        [slot, low_two, after(inner_low, down_other)],
        [SMEM] + [VMEM] * 2,
        [ANY] * 2,
        scratch=[pltpu.VMEM((CELLS, rows, ff), LOW), dma((2,))],
        vmem=16,
        flops=6 * 10**9,
    )
    in_other = to_partner(in_away)
    inner_low = after(inner_low, down_sum, in_keep)
    down_sum = second_hop(down_keep, down_other, down_sum, core)
    grad_middle, grad_mixed, sums, grad_out = call(
        lambda *refs: middle_back_body(seq, whole, *refs),
        [
            shape((total_rows, model), FULL),
            shape((total_rows, model)),
            shape((3, model), FULL),
            shape((model, model)),
        ],
        [order, lens, inner_low, mixed, middle, cot, small, count, other_count] + in_got,
        [SMEM] * 2 + [VMEM] * 7 + [ANY] * 9,
        scratch=[pltpu.VMEM((model, ff + model), LOW), dma((CELLS,))],
        vmem=24,
        flops=9 * 10**9,
    )
    in_sum = first_hop(in_keep, in_other)
    grad_mixed = after(grad_mixed, down_sum, in_other)
    down_sum = later_hop(down_keep, down_other, down_sum, 3)

    def attend_back(part, grad):
        return call(
            lambda *refs: attend_back_body(seq, part, *refs),
            [shape((total_rows, 3 * model // 2))],
            [proj, att, grad],
            [VMEM] * 3,
            vmem=14,
            flops=6 * 10**9,
        )[0]

    grad_one = attend_back(0, grad_mixed)
    grad_one = after(grad_one, down_sum, in_sum)
    down_sum = later_hop(down_keep, down_other, down_sum, 5)
    in_sum = second_hop(in_keep, in_other, in_sum, core)
    early_width = 3 * model // 2 + model
    early_keep, early_away = call(
        grad_qkv_body,
        [shape((RING_SIZE, rows, early_width))] * 2,
        [slot, low, grad_one, grad_out],
        [SMEM] + [VMEM] * 3,
        [ANY] * 2,
        scratch=[pltpu.VMEM((CELLS, rows, early_width), LOW), dma((2,))],
        vmem=14,
        flops=4 * 10**9,
    )
    early_other = to_partner(early_away)
    grad_two = attend_back(1, after(grad_mixed, down_sum, in_sum, early_keep))
    down_terms = settle(down_keep, down_other, down_sum, core)
    in_sum = later_hop(in_keep, in_other, in_sum, 3)
    early_sum = first_hop(early_keep, early_other)
    late_width = 3 * model // 2 + SMALL_LANES
    grad_tokens, late_keep, late_away = call(
        first_back_body,
        [
            shape((total_rows, model)),
            shape((RING_SIZE, rows, late_width)),
            shape((RING_SIZE, rows, late_width)),
        ],
        [
            order, slot, x, low, grad_one, after(grad_two, early_other), grad_middle, small, sums,
            in_b, down_b,
        ]
        + qkv_got,
        [SMEM] * 2 + [VMEM] * 9 + [ANY] * 18,
        [VMEM] + [ANY] * 2,
        scratch=[
            pltpu.VMEM((model, 3 * model), LOW),
            pltpu.VMEM((CELLS, rows, late_width), LOW),
            pltpu.VMEM((SMALL_ROWS, model), FULL),
            dma((2, CELLS)),
            dma((2,)),
        ],
        vmem=20,
        flops=7 * 10**9,
    )
    in_sum = later_hop(in_keep, in_other, in_sum, 5)
    late_other = to_partner(late_away)
    early_sum = second_hop(early_keep, early_other, early_sum, core)
    late_sum = first_hop(late_keep, late_other)
    in_terms = settle(in_keep, in_other, in_sum, core)
    early_sum = later_hop(early_keep, early_other, early_sum, 3)
    late_sum = second_hop(late_keep, late_other, late_sum, core)
    early_sum = later_hop(early_keep, early_other, early_sum, 5)
    late_sum = later_hop(late_keep, late_other, late_sum, 3)
    early_terms = settle(early_keep, early_other, early_sum, core)
    late_sum = later_hop(late_keep, late_other, late_sum, 5)
    late_terms = settle(late_keep, late_other, late_sum, core)
    finished = call(
        finish_body,
        [shape((rows, 3 * model), FULL), shape((rows, model), FULL)]
        + [shape((1, item.shape[0]), FULL) for item in vectors],
        [who] + list(early_terms) + list(late_terms),
        [SMEM] + [VMEM] * 4,
        scratch=[pltpu.VMEM((SMALL_ROWS, model), FULL)],
        vmem=6,
    )
    grad_qkv, grad_out = finished[:2]
    pieces = [item.reshape(-1) for item in finished[2:]]
    return (
        out_tokens.reshape(tokens.shape),
        grad_tokens.reshape(tokens.shape),
        pieces[0],
        pieces[1],
        grad_qkv,
        pieces[2],
        grad_out,
        pieces[3],
        pieces[4],
        pieces[5],
        in_terms[0].astype(FULL) + in_terms[1].astype(FULL),
        pieces[6],
        down_terms[0].astype(FULL) + down_terms[1].astype(FULL),
        pieces[7],
    )


def on_device(
    tokens,
    lengths,
    cotangent,
    first_gain,
    first_shift,
    qkv_weight,
    qv_bias,
    out_weight,
    out_bias,
    second_gain,
    second_shift,
    in_weight,
    in_bias,
    down_weight,
    down_bias,
):
    local_count = jnp.sum(lengths).astype(jnp.float32)
    count = lax.psum(local_count, ("species", "cells"))
    micro_count = tokens.shape[1]
    seq_rows = tokens.shape[2]
    factor = (
        float(lax.axis_size("species") * lax.axis_size("cells") * micro_count * seq_rows) / count
    )
    output_rows = []
    gradient_rows = []
    summed = None
    for micro_step in range(micro_count):
        gathered = (
            lax.all_gather(first_gain, "cells", axis=0, tiled=True),
            lax.all_gather(first_shift, "cells", axis=0, tiled=True),
            lax.all_gather(qkv_weight, "cells", axis=0, tiled=True),
            lax.all_gather(qv_bias, "cells", axis=0, tiled=True),
            lax.all_gather(out_weight, "cells", axis=0, tiled=True),
            lax.all_gather(out_bias, "cells", axis=0, tiled=True),
            lax.all_gather(second_gain, "cells", axis=0, tiled=True),
            lax.all_gather(second_shift, "cells", axis=0, tiled=True),
            lax.all_gather(in_weight, "cells", axis=0, tiled=True),
            lax.all_gather(in_bias, "cells", axis=0, tiled=True),
            lax.all_gather(down_weight, "cells", axis=0, tiled=True),
            lax.all_gather(down_bias, "cells", axis=0, tiled=True),
        )
        out_seq, grad_seq, grads = sequence_pass(
            gathered,
            tokens[0, micro_step],
            lengths[0, micro_step],
            cotangent[0, micro_step],
            factor,
        )
        output_rows.append(out_seq)
        gradient_rows.append(grad_seq)
        shares = (
            lax.psum_scatter(grads[0], "cells", scatter_dimension=0, tiled=True),
            lax.psum_scatter(grads[1], "cells", scatter_dimension=0, tiled=True),
            lax.psum_scatter(grads[2], "cells", scatter_dimension=0, tiled=True),
            lax.psum_scatter(grads[3], "cells", scatter_dimension=0, tiled=True),
            lax.psum_scatter(grads[4], "cells", scatter_dimension=0, tiled=True),
            lax.psum_scatter(grads[5], "cells", scatter_dimension=0, tiled=True),
            lax.psum_scatter(grads[6], "cells", scatter_dimension=0, tiled=True),
            lax.psum_scatter(grads[7], "cells", scatter_dimension=0, tiled=True),
            lax.psum_scatter(grads[8], "cells", scatter_dimension=0, tiled=True),
            lax.psum_scatter(grads[9], "cells", scatter_dimension=0, tiled=True),
            lax.psum_scatter(grads[10], "cells", scatter_dimension=0, tiled=True),
            lax.psum_scatter(grads[11], "cells", scatter_dimension=0, tiled=True),
        )
        summed = shares if summed is None else jax.tree.map(jnp.add, summed, shares)
    final = (
        lax.psum(summed[0].astype(jnp.bfloat16), "species").astype(jnp.float32),
        lax.psum(summed[1].astype(jnp.bfloat16), "species").astype(jnp.float32),
        lax.psum(summed[2].astype(jnp.bfloat16), "species").astype(jnp.float32),
        lax.psum(summed[3].astype(jnp.bfloat16), "species").astype(jnp.float32),
        lax.psum(summed[4].astype(jnp.bfloat16), "species").astype(jnp.float32),
        lax.psum(summed[5].astype(jnp.bfloat16), "species").astype(jnp.float32),
        lax.psum(summed[6].astype(jnp.bfloat16), "species").astype(jnp.float32),
        lax.psum(summed[7].astype(jnp.bfloat16), "species").astype(jnp.float32),
        lax.psum(summed[8].astype(jnp.bfloat16), "species").astype(jnp.float32),
        lax.psum(summed[9].astype(jnp.bfloat16), "species").astype(jnp.float32),
        lax.psum(summed[10].astype(jnp.bfloat16), "species").astype(jnp.float32),
        lax.psum(summed[11].astype(jnp.bfloat16), "species").astype(jnp.float32),
    )
    out_tokens = jnp.stack(output_rows)[None]
    grad_tokens = jnp.stack(gradient_rows)[None]
    return (out_tokens, grad_tokens) + tuple(final)


def solution(mesh):
    in_specs = (
        P("species", "cells", None, None),
        P("species", "cells"),
        P("species", "cells", None, None),
        P("cells"),
        P("cells"),
        P("cells", None),
        P("cells"),
        P("cells", None),
        P("cells"),
        P("cells"),
        P("cells"),
        P("cells", None),
        P("cells"),
        P("cells", None),
        P("cells"),
    )
    out_specs = (
        P("species", "cells", None, None),
        P("species", "cells", None, None),
        P("cells"),
        P("cells"),
        P("cells", None),
        P("cells"),
        P("cells", None),
        P("cells"),
        P("cells"),
        P("cells"),
        P("cells", None),
        P("cells"),
        P("cells", None),
        P("cells"),
    )
    program = on_device_ring if mesh.shape["cells"] == 2 * RING_SIZE else on_device
    return jax.shard_map(
        program, mesh=mesh, in_specs=in_specs, out_specs=out_specs, check_vma=False
    )
```

```python
import jax
import jax.numpy as jnp
from jax import lax
from jax.experimental import pallas as pl
from jax.experimental.pallas import tpu as pltpu
from jax.sharding import PartitionSpec as P

HEAD = 64


EPSILON = 1e-12
NEGATIVE = -1e30


def normalize(values, gain_vec, shift_vec):
    center = values - jnp.mean(values, axis=-1, keepdims=True)
    spread = jnp.mean(center * center, axis=-1, keepdims=True)
    return center * lax.rsqrt(spread + EPSILON) * gain_vec + shift_vec


def smooth_gate(values):
    return jax.nn.gelu(values, approximate=False)


def times_left(left_side, right_side):
    return lax.dot_general(
        left_side, right_side, (((0,), (0,)), ((), ())), preferred_element_type=jnp.float32
    )


def times_right(left_side, right_side):
    return lax.dot_general(
        left_side, right_side, (((1,), (1,)), ((), ())), preferred_element_type=jnp.float32
    )


def sequence_pass(weights, inputs, length, cot_rows, factor):
    (
        first_gain,
        first_shift,
        qkv_weight,
        qv_bias,
        out_weight,
        out_bias,
        second_gain,
        second_shift,
        in_weight,
        in_bias,
        down_weight,
        down_bias,
    ) = weights
    seq_rows = inputs.shape[0]
    model_width = inputs.shape[1]
    heads_count = model_width // HEAD
    scale_qk = float(HEAD) ** (-0.5)
    as_float = inputs.astype(jnp.float32)
    hidden_one, first_pull = jax.vjp(
        normalize, as_float, first_gain.astype(jnp.float32), first_shift.astype(jnp.float32)
    )
    first_low = hidden_one.astype(jnp.bfloat16)
    bias_float = qv_bias.astype(jnp.float32)
    full_bias = jnp.concatenate(
        [bias_float[:model_width], jnp.zeros((model_width,), jnp.float32), bias_float[model_width:]]
    )
    projected = (
        jnp.dot(first_low, qkv_weight, preferred_element_type=jnp.float32) + full_bias
    ).astype(jnp.bfloat16)
    split_heads = projected.reshape(seq_rows, 3, heads_count, HEAD)
    queries = split_heads[:, 0]
    keys_part = split_heads[:, 1]
    values_part = split_heads[:, 2]
    visible = jnp.arange(seq_rows) < length

    def scores_of():
        raw_scores = (
            jnp.einsum("qhd,khd->hqk", queries, keys_part, preferred_element_type=jnp.float32)
            * scale_qk
        )
        return jnp.where(visible[None, None, :], raw_scores, NEGATIVE)

    scores = scores_of()
    top_score = jnp.max(scores, axis=-1, keepdims=True)
    expo = jnp.exp(scores - top_score)
    total_exp = jnp.sum(expo, axis=-1, keepdims=True)
    log_total = top_score + jnp.log(total_exp)
    attention = (expo / total_exp).astype(jnp.bfloat16)
    mixed = jnp.einsum("hqk,khd->qhd", attention, values_part, preferred_element_type=jnp.float32)
    mixed = mixed.reshape(seq_rows, model_width).astype(jnp.bfloat16)
    middle = (
        as_float
        + jnp.dot(mixed, out_weight, preferred_element_type=jnp.float32)
        + out_bias.astype(jnp.float32)
    )
    hidden_two, second_pull = jax.vjp(
        normalize, middle, second_gain.astype(jnp.float32), second_shift.astype(jnp.float32)
    )
    second_low = hidden_two.astype(jnp.bfloat16)
    inner = jnp.dot(second_low, in_weight, preferred_element_type=jnp.float32) + in_bias.astype(
        jnp.float32
    )
    active, gate_pull = jax.vjp(smooth_gate, inner)
    active_low = active.astype(jnp.bfloat16)
    output = (
        middle
        + jnp.dot(active_low, down_weight, preferred_element_type=jnp.float32)
        + down_bias.astype(jnp.float32)
    )
    upstream = cot_rows.astype(jnp.float32) * visible[:, None].astype(jnp.float32) * factor
    up_low = upstream.astype(jnp.bfloat16)
    grad_down_bias = jnp.sum(up_low.astype(jnp.float32), axis=0)
    grad_down = times_left(active_low, up_low)
    grad_active = times_right(up_low, down_weight)
    (grad_inner,) = gate_pull(grad_active)
    inner_low = grad_inner.astype(jnp.bfloat16)
    grad_in_bias = jnp.sum(inner_low.astype(jnp.float32), axis=0)
    grad_in = times_left(second_low, inner_low)
    grad_second = times_right(inner_low, in_weight)
    grad_middle_norm, grad_second_gain, grad_second_shift = second_pull(grad_second)
    grad_middle = upstream + grad_middle_norm
    middle_low = grad_middle.astype(jnp.bfloat16)
    grad_out_bias = jnp.sum(middle_low.astype(jnp.float32), axis=0)
    grad_out = times_left(mixed, middle_low)
    grad_mixed = (
        times_right(middle_low, out_weight)
        .astype(jnp.bfloat16)
        .reshape(seq_rows, heads_count, HEAD)
    )
    probs_again = jnp.exp(scores_of() - log_total)
    grad_probs = jnp.einsum(
        "qhd,khd->hqk", grad_mixed, values_part, preferred_element_type=jnp.float32
    )
    grad_values = jnp.einsum(
        "hqk,qhd->khd", attention, grad_mixed, preferred_element_type=jnp.float32
    )
    delta = jnp.sum(probs_again * grad_probs, axis=-1, keepdims=True)
    grad_scores = (probs_again * (grad_probs - delta)).astype(jnp.bfloat16)
    grad_queries = (
        jnp.einsum("hqk,khd->qhd", grad_scores, keys_part, preferred_element_type=jnp.float32)
        * scale_qk
    )
    grad_keys = (
        jnp.einsum("hqk,qhd->khd", grad_scores, queries, preferred_element_type=jnp.float32)
        * scale_qk
    )
    grad_projected = jnp.stack([grad_queries, grad_keys, grad_values], axis=1)
    grad_projected = grad_projected.reshape(seq_rows, 3 * model_width).astype(jnp.bfloat16)
    column_sums = jnp.sum(grad_projected.astype(jnp.float32), axis=0)
    grad_qv = jnp.concatenate([column_sums[:model_width], column_sums[2 * model_width :]])
    grad_qkv = times_left(first_low, grad_projected)
    grad_first = times_right(grad_projected, qkv_weight)
    grad_input_norm, grad_first_gain, grad_first_shift = first_pull(grad_first)
    grad_inputs = grad_middle + grad_input_norm
    grads = (
        grad_first_gain,
        grad_first_shift,
        grad_qkv,
        grad_qv,
        grad_out,
        grad_out_bias,
        grad_second_gain,
        grad_second_shift,
        grad_in,
        grad_in_bias,
        grad_down,
        grad_down_bias,
    )
    return (output.astype(jnp.bfloat16), grad_inputs.astype(jnp.bfloat16), grads)


RING = (0, 2, 4, 6, 7, 5, 3, 1)
RING_SIZE = len(RING)
CELLS = 2 * RING_SIZE
ANY = pl.BlockSpec(memory_space=pl.ANY)
HBM = pl.BlockSpec(memory_space=pltpu.HBM)
VMEM = pl.BlockSpec(memory_space=pltpu.VMEM)
SMEM = pl.BlockSpec(memory_space=pltpu.SMEM)
LOW = jnp.bfloat16
FULL = jnp.float32
ROWS = {
    "first_gain": 0,
    "first_shift": 1,
    "qv_bias": 2,
    "out_bias": 4,
    "second_gain": 5,
    "second_shift": 6,
    "in_bias": 7,
    "down_bias": 11,
    "lengths": 12,
}
NAMES = tuple(ROWS)[:8]
SMALL_ROWS = 16
PIECES = (2, 2, 2, 2, 2, 2, 2, 1, 1)


def ring_pairs():
    pairs = []
    for place in range(RING_SIZE):
        chip = RING[place]
        right = RING[(place + 1) % RING_SIZE]
        left = RING[(place - 1) % RING_SIZE]
        pairs.append((2 * chip, 2 * right))
        pairs.append((2 * chip + 1, 2 * left + 1))
    return pairs


def hop(block):
    return lax.ppermute(block, "cells", ring_pairs())


def to_partner(block):
    return lax.ppermute(block, "cells", [(i, i ^ 1) for i in range(CELLS)])


def across(block):
    return lax.ppermute(block, "species", [(0, 1), (1, 0)])


def sum_cells(values):
    bit = 1
    while bit < CELLS:
        values = values + lax.ppermute(values, "cells", [(i, i ^ bit) for i in range(CELLS)])
        bit *= 2
    return values


def after(value, *others):
    return lax.optimization_barrier((value,) + others)[0]


def here():
    index = lax.axis_index("cells")
    core = index % 2
    chip = index // 2
    place = jnp.int32(0)
    for i, ring_chip in enumerate(RING):
        place = jnp.where(chip == ring_chip, i, place)
    return index, core, place


def chip_at(place):
    place = place % RING_SIZE
    chip = jnp.zeros_like(place)
    for i, ring_chip in enumerate(RING):
        chip = jnp.where(place == i, ring_chip, chip)
    return chip


def gather_order(core, place):
    sign = 1 - 2 * core
    order = []

    def pair(at):
        order.append(2 * chip_at(at))
        order.append(2 * chip_at(at) + 1)

    pair(place)
    for step in range(1, 4):
        pair(place - sign * step)
        pair(place + sign * step)
    order.append(2 * chip_at(place + 4) + core)
    order.append(2 * chip_at(place + 4) + 1 - core)
    return order


def scatter_slots(core, place):
    def kept(core_now):
        sign = 1 - 2 * core_now
        order = [2 * chip_at(place + 4) + core_now]
        for step in (3, 2, 1):
            order.append(2 * chip_at(place + sign * step))
            order.append(2 * chip_at(place + sign * step) + 1)
        order.append(2 * chip_at(place) + core_now)
        return order

    order = kept(core) + kept(1 - core)
    slots = []
    for device in range(CELLS):
        slot = jnp.int32(0)
        for i, who in enumerate(order):
            slot = jnp.where(who == device, i, slot)
        slots.append(slot)
    return slots


def both_blocks(block, core):
    other = to_partner(block)
    return jnp.stack([jnp.where(core == 0, block, other), jnp.where(core == 0, other, block)])


def half_of(pair, core):
    return jnp.where(core == 0, pair[0], pair[1])[None]


def add_low(*parts):
    total = parts[0].astype(FULL)
    for part in parts[1:]:
        total = total + part.astype(FULL)
    return total.astype(LOW)


def first_hop(keep, got):
    return hop(add_low(keep[0:1], got[0:1]))


def second_hop(keep, got, moving, core):
    wide = jnp.stack([jnp.where(core == 0, moving[0], 0), jnp.where(core == 0, 0, moving[0])])
    return hop(add_low(keep[1:3], got[1:3], wide))


def later_hop(keep, got, moving, at):
    return hop(add_low(keep[at : at + 2], got[at : at + 2], moving))


def settle(keep, got, moving, core):
    mine = jnp.where(core == 0, moving[0], moving[1])
    other = jnp.where(core == 0, moving[1], moving[0])
    total = add_low(keep[7], got[7], mine, to_partner(other))
    return total, across(total)


def dot(left, right, dims=((1,), (0,))):
    return lax.dot_general(left, right, (dims, ((), ())), preferred_element_type=FULL)


def call(body, out_shape, ins, specs, out_specs=None, scratch=(), vmem=48):
    return pl.pallas_call(
        body,
        out_shape=out_shape,
        in_specs=specs,
        out_specs=[VMEM] * len(out_shape) if out_specs is None else out_specs,
        scratch_shapes=list(scratch),
        compiler_params=pltpu.CompilerParams(vmem_limit_bytes=vmem * 2**20),
        cost_estimate=pl.CostEstimate(flops=10**6, bytes_accessed=0, transcendentals=0),
    )(*ins)


def shape(dims, kind=LOW):
    return jax.ShapeDtypeStruct(dims, kind)


def fetch(order_ref, refs, target, sem):
    rows = target.shape[0] // CELLS
    copies = []
    index = 0
    for source, size in zip(refs, PIECES):
        for part in range(size):
            at = order_ref[index]
            copies.append(
                pltpu.make_async_copy(
                    source.at[part],
                    target.at[pl.ds(pl.multiple_of(at * rows, 16), rows)],
                    sem.at[index],
                )
            )
            index += 1
    for item in copies:
        item.start()
    return copies


def wait_all(copies):
    for item in copies:
        item.wait()


def one_hot(rows, lanes, offset):
    row = lax.broadcasted_iota(jnp.int32, (rows, lanes), 0)
    lane = lax.broadcasted_iota(jnp.int32, (rows, lanes), 1)
    return lane == row + offset


def pack_body(who_ref, lengths_ref, *refs):
    sources, small_ref = refs[:8], refs[8]
    me = who_ref[0]
    model = small_ref.shape[1]
    row = lax.broadcasted_iota(jnp.int32, (SMALL_ROWS, model), 0)
    lane = lax.broadcasted_iota(jnp.int32, (SMALL_ROWS, model), 1)
    small = jnp.zeros((SMALL_ROWS, model), FULL)
    for name, ref in zip(NAMES, sources):
        size = ref.shape[1]
        per_row = model // size
        placed = dot(ref[...], one_hot(size, model, size * (me % per_row)).astype(LOW))
        small = small + jnp.where(row == ROWS[name] + me // per_row, placed, 0.0)
    for i in range(2):
        at = (row == ROWS["lengths"]) & (lane == 2 * me + i)
        small = small + jnp.where(at, lengths_ref[i].astype(FULL), 0.0)
    small_ref[...] = small.astype(LOW)


def norm_parts(values):
    center = values - jnp.mean(values, axis=-1, keepdims=True)
    spread = jnp.mean(center * center, axis=-1, keepdims=True)
    return center, lax.rsqrt(spread + EPSILON)


def norm_back(center, scale, gain, grad):
    weighted = grad * gain
    mean_one = jnp.mean(weighted, axis=-1, keepdims=True)
    mean_two = jnp.mean(weighted * center, axis=-1, keepdims=True)
    back = scale * (weighted - mean_one - center * (scale * scale * mean_two))
    return back, jnp.sum(grad * center * scale, axis=0, keepdims=True), jnp.sum(
        grad, axis=0, keepdims=True
    )


def small_row(small_ref, name, count=1):
    return small_ref[...].astype(FULL)[ROWS[name] : ROWS[name] + count, :]


def project_body(order_ref, x_ref, small_ref, *refs):
    blocks = refs[:9]
    low_ref, proj_ref, weight, sem = refs[9:]
    model = x_ref.shape[1]
    copies = fetch(order_ref, blocks, weight, sem)
    center, scale = norm_parts(x_ref[...].astype(FULL))
    bias = small_row(small_ref, "qv_bias", 2)
    low_ref[...] = (
        center * scale * small_row(small_ref, "first_gain") + small_row(small_ref, "first_shift")
    ).astype(LOW)
    wait_all(copies)
    for j in range(3):
        lanes = slice(j * model, (j + 1) * model)
        part = dot(low_ref[...], weight[:, lanes])
        if j != 1:
            part = part + bias[j // 2 : j // 2 + 1]
        proj_ref[:, lanes] = part.astype(LOW)


def attend_body(seq, lengths_ref, proj_ref, att_ref, mixed_ref):
    model = mixed_ref.shape[1]
    cells = mixed_ref.shape[0] // seq
    pairs = model // (2 * HEAD)
    lane = lax.broadcasted_iota(jnp.int32, (seq, 2 * HEAD), 1)
    key = lax.broadcasted_iota(jnp.int32, (seq, seq), 0)

    def step(index, carry):
        s = index // pairs
        p = index % pairs
        rows = pl.ds(pl.multiple_of(s * seq, seq), seq)
        at = pl.multiple_of(p * 2 * HEAD, 2 * HEAD)
        q = proj_ref[rows, pl.ds(at, 2 * HEAD)] * jnp.asarray(HEAD ** (-0.5), LOW)
        k = proj_ref[rows, pl.ds(at + model, 2 * HEAD)]
        v_turned = proj_ref[rows, pl.ds(at + 2 * model, 2 * HEAD)].T
        visible = key < lengths_ref[s]
        mixed = []
        for i in range(2):
            own = (lane >= i * HEAD) & (lane < (i + 1) * HEAD)
            scores = dot(jnp.where(own, k, jnp.zeros_like(k)), q, ((1,), (1,)))
            scores = jnp.where(visible, scores, NEGATIVE)
            expo = jnp.exp(scores - jnp.max(scores, axis=0, keepdims=True))
            probs = expo * (1.0 / jnp.sum(expo, axis=0, keepdims=True))
            probs = probs.astype(LOW)
            att_ref[2 * index + i] = probs
            mixed.append(dot(v_turned[i * HEAD : (i + 1) * HEAD], probs))
        mixed_ref[rows, pl.ds(at, 2 * HEAD)] = jnp.concatenate(mixed, axis=0).T.astype(LOW)
        return carry

    lax.fori_loop(0, cells * pairs, step, 0, unroll=2)


ERFC_STEP = 0.33
ERFC = (
    0.1863578228018033,
    0.18295566386742124,
    0.2012255082472392,
    0.04721561458875723,
    0.4085089979423051,
    -0.35115900736338407,
    0.4602422572120205,
    -0.13534686486277223,
)


def gelu_parts(inner):
    z = jnp.abs(inner) * (0.5**0.5)
    t = 1.0 / (1.0 + ERFC_STEP * z)
    tail = jnp.full_like(t, 0.5 * ERFC[-1])
    for factor in ERFC[-2::-1]:
        tail = tail * t + 0.5 * factor
    bell = jnp.exp(-(z * z))
    tail = tail * t * bell
    area = jnp.where(inner < 0.0, tail, 1.0 - tail)
    return inner * area, area + inner * bell * (0.5 / 3.141592653589793) ** 0.5


def row_mask(lengths_ref, rows, seq):
    at = lax.broadcasted_iota(jnp.int32, (rows, 1), 0)
    true = (at < lengths_ref[0]).astype(FULL)
    for s in range(1, rows // seq):
        true = jnp.where(at < s * seq, true, (at < lengths_ref[s] + s * seq).astype(FULL))
    return true


def loss_rows(lengths_ref, small_ref, other_ref, cot_ref, seq, whole):
    count = jnp.sum(
        small_row(small_ref, "lengths") + small_row(other_ref, "lengths"), axis=-1, keepdims=True
    )
    return cot_ref[...].astype(FULL) * (
        row_mask(lengths_ref, cot_ref.shape[0], seq) * (whole / count)
    )


def put_slots(keep_buf, slot_ref, values, first, lanes):
    rows = keep_buf.shape[1]
    for i in range(values.shape[0] // rows):
        keep_buf[slot_ref[first + i], :, lanes] = values[i * rows : (i + 1) * rows].astype(LOW)


def send_slots(buf, keep_ref, away_ref, sem):
    half = RING_SIZE
    copies = [
        pltpu.make_async_copy(buf.at[pl.ds(half, half)], away_ref, sem.at[0]),
        pltpu.make_async_copy(buf.at[pl.ds(0, half)], keep_ref, sem.at[1]),
    ]
    for item in copies:
        item.start()
    return copies


def inner_body(order_ref, x_ref, mixed_ref, small_ref, *refs):
    blocks = refs[:9]
    middle_ref, low_ref, active_ref, slope_ref, weight, sem = refs[9:]
    model = x_ref.shape[1]
    ff = active_ref.shape[1]
    wait_all(fetch(order_ref, blocks, weight, sem))
    middle = (
        x_ref[...].astype(FULL)
        + dot(mixed_ref[...], weight[:, ff:])
        + small_row(small_ref, "out_bias")
    )
    middle_ref[...] = middle
    center, scale = norm_parts(middle)
    low = center * scale * small_row(small_ref, "second_gain") + small_row(
        small_ref, "second_shift"
    )
    low_ref[...] = low.astype(LOW)
    step = 2 * (ff // RING_SIZE)
    bias = small_row(small_ref, "in_bias", 4)
    for j in range(ff // step):
        lanes = slice(j * step, (j + 1) * step)
        inner = dot(low_ref[...], weight[:, lanes]) + bias[j : j + 1]
        active, slope = gelu_parts(inner)
        active_ref[:, lanes] = active.astype(LOW)
        slope_ref[:, lanes] = slope.astype(LOW)


def grad_down_body(
    seq, whole, lengths_ref, active_ref, cot_ref, small_ref, other_ref, up_ref, down_b_ref,
    grad_ref,
):
    up_low = loss_rows(lengths_ref, small_ref, other_ref, cot_ref, seq, whole).astype(LOW)
    up_ref[...] = up_low
    down_b_ref[...] = jnp.sum(up_low.astype(FULL), axis=0, keepdims=True)
    parts = RING_SIZE
    step = active_ref.shape[1] // parts
    rows = grad_ref.shape[2]
    for j in range(parts):
        grad = dot(active_ref[:, j * step : (j + 1) * step], up_ref[...], ((0,), (0,)))
        for i in range(4):
            grad_ref[i % 2, j * CELLS // parts + i // 2] = grad[
                i * rows : (i + 1) * rows
            ].astype(LOW)


def fetch_down(source, target, sem):
    copies = [
        pltpu.make_async_copy(source.at[i], target.at[:, i], sem.at[i]) for i in range(2)
    ]
    for item in copies:
        item.start()
    wait_all(copies)


def inner_back_body(slope_ref, up_ref, blocks, inner_ref, in_b_ref, weight, sem):
    ff = inner_ref.shape[1]
    model = up_ref.shape[1]
    fetch_down(blocks, weight, sem)
    parts = ff // model
    step = CELLS // parts
    for j in range(parts):
        lanes = slice(j * model, (j + 1) * model)
        rows = weight[j * step : (j + 1) * step].reshape(model, model)
        grad = dot(up_ref[...], rows, ((1,), (1,)))
        low = (grad * slope_ref[:, lanes].astype(FULL)).astype(LOW)
        inner_ref[:, lanes] = low
        in_b_ref[j : j + 1, :] = jnp.sum(low.astype(FULL), axis=0, keepdims=True)


def down_body(active_ref, middle_ref, small_ref, blocks, out_ref, weight, sem):
    ff = active_ref.shape[1]
    model = middle_ref.shape[1]
    fetch_down(blocks, weight, sem)
    out_ref[...] = (
        middle_ref[...]
        + dot(active_ref[...], weight[...].reshape(ff, model))
        + small_row(small_ref, "down_bias")
    ).astype(LOW)


def grad_in_body(slot_ref, low_ref, inner_ref, keep_ref, away_ref, slots, sem):
    model = low_ref.shape[1]
    turned = low_ref[...].T
    for j in range(inner_ref.shape[1] // model):
        lanes = slice(j * model, (j + 1) * model)
        put_slots(slots, slot_ref, dot(turned, inner_ref[:, lanes]), 0, lanes)
    wait_all(send_slots(slots, keep_ref, away_ref, sem))


def middle_back_body(
    seq, whole, order_ref, lengths_ref, inner_ref, middle_ref, cot_ref, small_ref, other_ref,
    *refs,
):
    blocks = refs[:9]
    grad_ref, grad_low_ref, grad_mixed_ref, sums_ref, weight, sem = refs[9:]
    model = middle_ref.shape[1]
    ff = inner_ref.shape[1]
    wait_all(fetch(order_ref, blocks, weight, sem))
    grad_second = dot(inner_ref[...], weight[:, :ff], ((1,), (1,)))
    center, scale = norm_parts(middle_ref[...])
    back, gain_sum, shift_sum = norm_back(
        center, scale, small_row(small_ref, "second_gain"), grad_second
    )
    grad = loss_rows(lengths_ref, small_ref, other_ref, cot_ref, seq, whole) + back
    grad_ref[...] = grad
    grad_low = grad.astype(LOW)
    grad_low_ref[...] = grad_low
    grad_mixed_ref[...] = dot(grad_low, weight[:, ff:], ((1,), (1,))).astype(LOW)
    sums_ref[0:1, :] = jnp.sum(grad_low.astype(FULL), axis=0, keepdims=True)
    sums_ref[1:2, :] = gain_sum
    sums_ref[2:3, :] = shift_sum


def attend_back_body(seq, begin, proj_ref, att_ref, grad_ref, out_ref):
    model = grad_ref.shape[1]
    half = out_ref.shape[1] // 3
    all_pairs = model // (2 * HEAD)
    pairs = half // (2 * HEAD)
    cells = grad_ref.shape[0] // seq
    lane = lax.broadcasted_iota(jnp.int32, (seq, 2 * HEAD), 1)
    scale = HEAD ** (-0.5)

    def step(index, carry):
        s = index // pairs
        p = index % pairs
        rows = pl.ds(pl.multiple_of(s * seq, seq), seq)
        to = pl.multiple_of(p * 2 * HEAD, 2 * HEAD)
        at = pl.multiple_of(to + begin * 2 * HEAD, 2 * HEAD)
        q = proj_ref[rows, pl.ds(at, 2 * HEAD)]
        k_turned = proj_ref[rows, pl.ds(at + model, 2 * HEAD)].T
        v = proj_ref[rows, pl.ds(at + 2 * model, 2 * HEAD)]
        g = grad_ref[rows, pl.ds(at, 2 * HEAD)]
        grad_q = []
        grad_k = []
        grad_v = []
        for i in range(2):
            own = (lane >= i * HEAD) & (lane < (i + 1) * HEAD)
            probs = att_ref[2 * (s * all_pairs + begin + p) + i]
            wide = probs.astype(FULL)
            grad_probs = dot(jnp.where(own, v, jnp.zeros_like(v)), g, ((1,), (1,)))
            delta = jnp.sum(wide * grad_probs, axis=0, keepdims=True)
            scores = (wide * (grad_probs - delta)).astype(LOW)
            grad_q.append(dot(k_turned[i * HEAD : (i + 1) * HEAD], scores))
            grad_k.append(dot(scores, q))
            grad_v.append(dot(probs, g))
        first = lane < HEAD
        out_ref[rows, pl.ds(to, 2 * HEAD)] = (
            jnp.concatenate(grad_q, axis=0).T * scale
        ).astype(LOW)
        out_ref[rows, pl.ds(to + half, 2 * HEAD)] = (
            jnp.where(first, grad_k[0], grad_k[1]) * scale
        ).astype(LOW)
        out_ref[rows, pl.ds(to + 2 * half, 2 * HEAD)] = jnp.where(
            first, grad_v[0], grad_v[1]
        ).astype(LOW)
        return carry

    lax.fori_loop(0, cells * pairs, step, 0, unroll=2)


def early_grad_body(
    slot_ref, low_ref, part_ref, mixed_ref, grad_low_ref, keep_ref, away_ref, slots, sem
):
    width = part_ref.shape[1]
    put_slots(slots, slot_ref, dot(low_ref[...].T, part_ref[...]), 0, slice(0, width))
    put_slots(
        slots, slot_ref, dot(mixed_ref[...].T, grad_low_ref[...]), 0,
        slice(width, slots.shape[2]),
    )
    wait_all(send_slots(slots, keep_ref, away_ref, sem))


def late_grad_body(slot_ref, low_ref, part_ref, keep_ref, away_ref, slots, sem):
    put_slots(slots, slot_ref, dot(low_ref[...].T, part_ref[...]), 0, slice(None))
    wait_all(send_slots(slots, keep_ref, away_ref, sem))


def first_back_body(
    order_ref, x_ref, one_ref, two_ref, grad_ref, small_ref, sums_ref, in_b_ref, down_b_ref,
    *refs,
):
    blocks = refs[:9]
    out_ref, sum_ref, weight, sem = refs[9:]
    model = x_ref.shape[1]
    copies = fetch(order_ref, blocks, weight, sem)
    center, scale = norm_parts(x_ref[...].astype(FULL))
    wait_all(copies)
    parts = ((one_ref, 0), (two_ref, one_ref.shape[1] // 3))
    grad_first = jnp.zeros(x_ref.shape, FULL)
    for j in range(3):
        for ref, begin in parts:
            width = ref.shape[1] // 3
            at = j * model + begin
            grad_first = grad_first + dot(
                ref[:, j * width : (j + 1) * width], weight[:, at : at + width], ((1,), (1,))
            )
    back, gain_sum, shift_sum = norm_back(
        center, scale, small_row(small_ref, "first_gain"), grad_first
    )

    def put(name, value, offset=0):
        at = ROWS[name] + offset
        sum_ref[at : at + value.shape[0], :] = value

    sum_ref[...] = jnp.zeros_like(sum_ref)
    put("first_gain", gain_sum)
    put("first_shift", shift_sum)
    for j in range(2):
        at = ROWS["qv_bias"] + j
        for ref, begin in parts:
            width = ref.shape[1] // 3
            part = ref[:, 2 * j * width : (2 * j + 1) * width].astype(FULL)
            sum_ref[at : at + 1, begin : begin + width] = jnp.sum(part, axis=0, keepdims=True)
    put("out_bias", sums_ref[0:1, :])
    put("second_gain", sums_ref[1:2, :])
    put("second_shift", sums_ref[2:3, :])
    put("in_bias", in_b_ref[...])
    put("down_bias", down_b_ref[...])
    out_ref[...] = (grad_ref[...] + back).astype(LOW)


def finish_body(who_ref, early_ref, early_two_ref, late_ref, late_two_ref, small_ref, *refs):
    grad_ref, out_ref, vectors = refs[0], refs[1], refs[2:]
    model = out_ref.shape[1]
    early = early_ref[...].astype(FULL) + early_two_ref[...].astype(FULL)
    late = late_ref[...].astype(FULL) + late_two_ref[...].astype(FULL)
    one = (early.shape[1] - model) // 3
    two = late.shape[1] // 3
    for j in range(3):
        at = j * model
        grad_ref[:, at : at + one] = early[:, j * one : (j + 1) * one]
        grad_ref[:, at + one : at + model] = late[:, j * two : (j + 1) * two]
    out_ref[...] = early[:, 3 * one :]
    me = who_ref[0]
    row = lax.broadcasted_iota(jnp.int32, (SMALL_ROWS, model), 0)
    for name, ref in zip(NAMES, vectors):
        size = ref.shape[1]
        per_row = model // size
        here_row = jnp.where(row == ROWS[name] + me // per_row, small_ref[...], 0.0)
        values = jnp.sum(here_row, axis=0, keepdims=True)
        picker = one_hot(size, model, size * (me % per_row)).astype(FULL)
        ref[...] = lax.dot_general(
            values, picker, (((1,), (1,)), ((), ())), precision=lax.Precision.HIGHEST,
            preferred_element_type=FULL,
        )


def on_device_ring(
    tokens,
    lengths,
    cotangent,
    first_gain,
    first_shift,
    qkv_weight,
    qv_bias,
    out_weight,
    out_bias,
    second_gain,
    second_shift,
    in_weight,
    in_bias,
    down_weight,
    down_bias,
):
    micro, seq, model = tokens.shape[1:]
    total_rows = micro * seq
    rows = qkv_weight.shape[0]
    down_rows = down_weight.shape[0]
    ff = in_weight.shape[1]
    heads = model // HEAD
    whole = float(lax.axis_size("species") * CELLS * micro * seq)
    index, core, place = here()
    who = jnp.stack([index]).astype(jnp.int32)
    order = jnp.stack(gather_order(core, place)).astype(jnp.int32)
    slot = jnp.stack(scatter_slots(core, place)).astype(jnp.int32)
    lens = lengths.reshape(micro)
    x = tokens.reshape(total_rows, model)
    cot = cotangent.reshape(total_rows, model)
    vectors = (
        first_gain, first_shift, qv_bias, out_bias, second_gain, second_shift, in_bias, down_bias,
    )

    dma = pltpu.SemaphoreType.DMA
    both = ("species", "cells")
    species = lax.axis_index("species")
    half_rows = down_rows // 2

    moving = both_blocks(qkv_weight, core)
    pack_lens = after(lens, moving)
    qkv_got = [moving]
    moving = hop(moving)
    qkv_got += [moving, to_partner(moving)]
    (small,) = call(
        pack_body,
        [shape((SMALL_ROWS, model))],
        [who, pack_lens] + [item.reshape(1, -1) for item in vectors],
        [SMEM, SMEM] + [VMEM] * 8,
        vmem=4,
    )
    small = sum_cells(small)
    for step in range(2):
        moving = hop(moving)
        qkv_got += [moving, to_partner(moving)]
    moving, small = lax.optimization_barrier((moving, small))
    other_small = across(small)
    last = hop(half_of(moving, core))
    qkv_got += [last, to_partner(last)]
    in_weight, out_weight = lax.optimization_barrier((in_weight, out_weight, qkv_got[1]))[:2]
    in_own = both_blocks(jnp.concatenate([in_weight, out_weight], axis=1), core)
    in_one = hop(after(in_own, moving))
    down_half = lax.dynamic_slice_in_dim(down_weight, species * half_rows, half_rows)
    down_full = lax.all_gather(after(down_half, moving), both, axis=0, tiled=True)
    down_full = down_full.reshape(2, CELLS, half_rows, model)

    low, proj = call(
        project_body,
        [shape((total_rows, model)), shape((total_rows, 3 * model))],
        [order, x, small] + qkv_got,
        [SMEM, VMEM, VMEM] + [HBM] * 9,
        scratch=[pltpu.VMEM((model, 3 * model), LOW), dma((CELLS,))],
        vmem=20,
    )
    in_two = hop(after(in_one, proj))
    att, mixed = call(
        lambda *refs: attend_body(seq, *refs),
        [shape((micro * heads, seq, seq)), shape((total_rows, model))],
        [lens, after(proj, in_one)],
        [SMEM, VMEM],
        vmem=16,
    )
    in_three = hop(after(in_two, mixed))
    in_last = hop(half_of(in_three, core))
    in_got = [in_own]
    for item in (in_one, in_two, in_three, in_last):
        in_got += [item, to_partner(item)]
    middle, low_two, active, slope = call(
        inner_body,
        [
            shape((total_rows, model), FULL),
            shape((total_rows, model)),
            shape((total_rows, ff)),
            shape((total_rows, ff)),
        ],
        [order, x, mixed, small] + in_got,
        [SMEM] + [VMEM] * 3 + [HBM] * 9,
        scratch=[pltpu.VMEM((model, ff + model), LOW), dma((CELLS,))],
        vmem=24,
    )
    up_low, down_b, down_grad = call(
        lambda *refs: grad_down_body(seq, whole, *refs),
        [
            shape((total_rows, model)),
            shape((1, model), FULL),
            shape((2, CELLS, half_rows, model)),
        ],
        [lens, active, cot, small, other_small],
        [SMEM] + [VMEM] * 4,
        vmem=18,
    )

    down_sum = lax.psum_scatter(
        down_grad.reshape(ff, model), both, scatter_dimension=0, tiled=True
    )
    inner_low, in_b = call(
        inner_back_body,
        [shape((total_rows, ff)), shape((ff // model, model), FULL)],
        [slope, up_low, down_full],
        [VMEM] * 2 + [HBM],
        scratch=[pltpu.VMEM((CELLS, 2, half_rows, model), LOW), dma((2,))],
        vmem=20,
    )
    in_keep, in_away = call(
        grad_in_body,
        [shape((RING_SIZE, rows, ff)), shape((RING_SIZE, rows, ff))],
        [slot, low_two, inner_low],
        [SMEM] + [VMEM] * 2,
        [ANY] * 2,
        scratch=[pltpu.VMEM((CELLS, rows, ff), LOW), dma((2,))],
        vmem=16,
    )
    in_other = to_partner(in_away)
    grad_middle, grad_low, grad_mixed, sums = call(
        lambda *refs: middle_back_body(seq, whole, *refs),
        [
            shape((total_rows, model), FULL),
            shape((total_rows, model)),
            shape((total_rows, model)),
            shape((3, model), FULL),
        ],
        [order, lens, after(inner_low, in_keep), middle, cot, small, other_small]
        + in_got,
        [SMEM] * 2 + [VMEM] * 5 + [HBM] * 9,
        scratch=[pltpu.VMEM((model, ff + model), LOW), dma((CELLS,))],
        vmem=24,
    )
    in_sum = first_hop(in_keep, after(in_other, grad_low))

    def attend_back(begin, pairs, grad):
        return call(
            lambda *refs: attend_back_body(seq, begin, *refs),
            [shape((total_rows, 6 * pairs * HEAD))],
            [proj, att, grad],
            [VMEM] * 3,
            vmem=14,
        )[0]

    pairs = model // (2 * HEAD)
    early_pairs = 2 * pairs // 3
    grad_one = attend_back(0, early_pairs, after(grad_mixed, in_other))
    early_width = 6 * early_pairs * HEAD + model
    early_keep, early_away = call(
        early_grad_body,
        [shape((RING_SIZE, rows, early_width))] * 2,
        [slot, low, after(grad_one, in_sum), mixed, grad_low],
        [SMEM] + [VMEM] * 4,
        [ANY] * 2,
        scratch=[pltpu.VMEM((CELLS, rows, early_width), LOW), dma((2,))],
        vmem=14,
    )
    early_other = to_partner(early_away)
    in_sum = second_hop(in_keep, in_other, after(in_sum, grad_one), core)
    grad_two = attend_back(early_pairs, pairs - early_pairs, after(grad_mixed, early_keep))
    late_width = 6 * (pairs - early_pairs) * HEAD
    late_keep, late_away = call(
        late_grad_body,
        [shape((RING_SIZE, rows, late_width))] * 2,
        [slot, low, after(grad_two, early_other)],
        [SMEM] + [VMEM] * 2,
        [ANY] * 2,
        scratch=[pltpu.VMEM((CELLS, rows, late_width), LOW), dma((2,))],
        vmem=8,
    )
    late_other = to_partner(late_away)
    early_sum = first_hop(early_keep, after(early_other, late_keep))
    in_two_hops = in_sum
    in_sum = later_hop(in_keep, in_other, after(in_sum, late_keep), 3)
    grad_tokens, small_sum = call(
        first_back_body,
        [shape((total_rows, model)), shape((SMALL_ROWS, model), FULL)],
        [order, x, grad_one, after(grad_two, in_two_hops, late_keep), grad_middle, small, sums]
        + [in_b, down_b]
        + qkv_got,
        [SMEM] + [VMEM] * 8 + [HBM] * 9,
        scratch=[pltpu.VMEM((model, 3 * model), LOW), dma((CELLS,))],
        vmem=20,
    )
    small_sum = sum_cells(small_sum)
    small_sum = small_sum + across(small_sum)
    early_sum = second_hop(early_keep, early_other, after(early_sum, grad_tokens), core)
    late_sum = first_hop(late_keep, after(late_other, grad_tokens))
    in_sum = later_hop(in_keep, in_other, after(in_sum, grad_tokens), 5)
    (out_tokens,) = call(
        down_body,
        [shape((total_rows, model))],
        [after(active, grad_tokens), middle, small, down_full],
        [VMEM] * 3 + [HBM],
        scratch=[pltpu.VMEM((CELLS, 2, half_rows, model), LOW), dma((2,))],
        vmem=20,
    )
    in_terms = settle(in_keep, in_other, in_sum, core)
    early_sum = later_hop(early_keep, early_other, after(early_sum, out_tokens), 3)
    late_sum = second_hop(late_keep, late_other, after(late_sum, out_tokens), core)
    early_sum = later_hop(early_keep, early_other, early_sum, 5)
    late_sum = later_hop(late_keep, late_other, late_sum, 3)
    early_terms = settle(early_keep, early_other, early_sum, core)
    late_sum = later_hop(late_keep, late_other, late_sum, 5)
    late_terms = settle(late_keep, late_other, late_sum, core)
    finished = call(
        finish_body,
        [shape((rows, 3 * model), FULL), shape((rows, model), FULL)]
        + [shape((1, item.shape[0]), FULL) for item in vectors],
        [who] + list(early_terms) + list(late_terms) + [small_sum],
        [SMEM] + [VMEM] * 5,
        vmem=6,
    )
    grad_qkv, grad_out = finished[:2]
    pieces = [item.reshape(-1) for item in finished[2:]]
    down_sum = after(down_sum, in_terms[0])
    down_other = across(down_sum)
    down_total = jnp.concatenate(
        [
            jnp.where(species == 0, down_sum, down_other),
            jnp.where(species == 0, down_other, down_sum),
        ]
    ).astype(FULL)
    return (
        out_tokens.reshape(tokens.shape),
        grad_tokens.reshape(tokens.shape),
        pieces[0],
        pieces[1],
        grad_qkv,
        pieces[2],
        grad_out,
        pieces[3],
        pieces[4],
        pieces[5],
        in_terms[0].astype(FULL) + in_terms[1].astype(FULL),
        pieces[6],
        down_total,
        pieces[7],
    )


def on_device(
    tokens,
    lengths,
    cotangent,
    first_gain,
    first_shift,
    qkv_weight,
    qv_bias,
    out_weight,
    out_bias,
    second_gain,
    second_shift,
    in_weight,
    in_bias,
    down_weight,
    down_bias,
):
    local_count = jnp.sum(lengths).astype(jnp.float32)
    count = lax.psum(local_count, ("species", "cells"))
    micro_count = tokens.shape[1]
    seq_rows = tokens.shape[2]
    factor = (
        float(lax.axis_size("species") * lax.axis_size("cells") * micro_count * seq_rows) / count
    )
    output_rows = []
    gradient_rows = []
    summed = None
    for micro_step in range(micro_count):
        gathered = (
            lax.all_gather(first_gain, "cells", axis=0, tiled=True),
            lax.all_gather(first_shift, "cells", axis=0, tiled=True),
            lax.all_gather(qkv_weight, "cells", axis=0, tiled=True),
            lax.all_gather(qv_bias, "cells", axis=0, tiled=True),
            lax.all_gather(out_weight, "cells", axis=0, tiled=True),
            lax.all_gather(out_bias, "cells", axis=0, tiled=True),
            lax.all_gather(second_gain, "cells", axis=0, tiled=True),
            lax.all_gather(second_shift, "cells", axis=0, tiled=True),
            lax.all_gather(in_weight, "cells", axis=0, tiled=True),
            lax.all_gather(in_bias, "cells", axis=0, tiled=True),
            lax.all_gather(down_weight, "cells", axis=0, tiled=True),
            lax.all_gather(down_bias, "cells", axis=0, tiled=True),
        )
        out_seq, grad_seq, grads = sequence_pass(
            gathered,
            tokens[0, micro_step],
            lengths[0, micro_step],
            cotangent[0, micro_step],
            factor,
        )
        output_rows.append(out_seq)
        gradient_rows.append(grad_seq)
        shares = (
            lax.psum_scatter(grads[0], "cells", scatter_dimension=0, tiled=True),
            lax.psum_scatter(grads[1], "cells", scatter_dimension=0, tiled=True),
            lax.psum_scatter(grads[2], "cells", scatter_dimension=0, tiled=True),
            lax.psum_scatter(grads[3], "cells", scatter_dimension=0, tiled=True),
            lax.psum_scatter(grads[4], "cells", scatter_dimension=0, tiled=True),
            lax.psum_scatter(grads[5], "cells", scatter_dimension=0, tiled=True),
            lax.psum_scatter(grads[6], "cells", scatter_dimension=0, tiled=True),
            lax.psum_scatter(grads[7], "cells", scatter_dimension=0, tiled=True),
            lax.psum_scatter(grads[8], "cells", scatter_dimension=0, tiled=True),
            lax.psum_scatter(grads[9], "cells", scatter_dimension=0, tiled=True),
            lax.psum_scatter(grads[10], "cells", scatter_dimension=0, tiled=True),
            lax.psum_scatter(grads[11], "cells", scatter_dimension=0, tiled=True),
        )
        summed = shares if summed is None else jax.tree.map(jnp.add, summed, shares)
    final = (
        lax.psum(summed[0].astype(jnp.bfloat16), "species").astype(jnp.float32),
        lax.psum(summed[1].astype(jnp.bfloat16), "species").astype(jnp.float32),
        lax.psum(summed[2].astype(jnp.bfloat16), "species").astype(jnp.float32),
        lax.psum(summed[3].astype(jnp.bfloat16), "species").astype(jnp.float32),
        lax.psum(summed[4].astype(jnp.bfloat16), "species").astype(jnp.float32),
        lax.psum(summed[5].astype(jnp.bfloat16), "species").astype(jnp.float32),
        lax.psum(summed[6].astype(jnp.bfloat16), "species").astype(jnp.float32),
        lax.psum(summed[7].astype(jnp.bfloat16), "species").astype(jnp.float32),
        lax.psum(summed[8].astype(jnp.bfloat16), "species").astype(jnp.float32),
        lax.psum(summed[9].astype(jnp.bfloat16), "species").astype(jnp.float32),
        lax.psum(summed[10].astype(jnp.bfloat16), "species").astype(jnp.float32),
        lax.psum(summed[11].astype(jnp.bfloat16), "species").astype(jnp.float32),
    )
    out_tokens = jnp.stack(output_rows)[None]
    grad_tokens = jnp.stack(gradient_rows)[None]
    return (out_tokens, grad_tokens) + tuple(final)


def solution(mesh):
    in_specs = (
        P("species", "cells", None, None),
        P("species", "cells"),
        P("species", "cells", None, None),
        P("cells"),
        P("cells"),
        P("cells", None),
        P("cells"),
        P("cells", None),
        P("cells"),
        P("cells"),
        P("cells"),
        P("cells", None),
        P("cells"),
        P("cells", None),
        P("cells"),
    )
    out_specs = (
        P("species", "cells", None, None),
        P("species", "cells", None, None),
        P("cells"),
        P("cells"),
        P("cells", None),
        P("cells"),
        P("cells", None),
        P("cells"),
        P("cells"),
        P("cells"),
        P("cells", None),
        P("cells"),
        P("cells", None),
        P("cells"),
    )
    program = on_device_ring if mesh.shape["cells"] == 2 * RING_SIZE else on_device
    return jax.shard_map(
        program, mesh=mesh, in_specs=in_specs, out_specs=out_specs, check_vma=False
    )
```

```python
import jax
import jax.numpy as jnp
from jax import lax
from jax.experimental import pallas as pl
from jax.experimental.pallas import tpu as pltpu
from jax.sharding import PartitionSpec as P

HEAD = 64


EPSILON = 1e-12
NEGATIVE = -1e30


def normalize(values, gain_vec, shift_vec):
    center = values - jnp.mean(values, axis=-1, keepdims=True)
    spread = jnp.mean(center * center, axis=-1, keepdims=True)
    return center * lax.rsqrt(spread + EPSILON) * gain_vec + shift_vec


def smooth_gate(values):
    return jax.nn.gelu(values, approximate=False)


def times_left(left_side, right_side):
    return lax.dot_general(
        left_side, right_side, (((0,), (0,)), ((), ())), preferred_element_type=jnp.float32
    )


def times_right(left_side, right_side):
    return lax.dot_general(
        left_side, right_side, (((1,), (1,)), ((), ())), preferred_element_type=jnp.float32
    )


def sequence_pass(weights, inputs, length, cot_rows, factor):
    (
        first_gain,
        first_shift,
        qkv_weight,
        qv_bias,
        out_weight,
        out_bias,
        second_gain,
        second_shift,
        in_weight,
        in_bias,
        down_weight,
        down_bias,
    ) = weights
    seq_rows = inputs.shape[0]
    model_width = inputs.shape[1]
    heads_count = model_width // HEAD
    scale_qk = float(HEAD) ** (-0.5)
    as_float = inputs.astype(jnp.float32)
    hidden_one, first_pull = jax.vjp(
        normalize, as_float, first_gain.astype(jnp.float32), first_shift.astype(jnp.float32)
    )
    first_low = hidden_one.astype(jnp.bfloat16)
    bias_float = qv_bias.astype(jnp.float32)
    full_bias = jnp.concatenate(
        [bias_float[:model_width], jnp.zeros((model_width,), jnp.float32), bias_float[model_width:]]
    )
    projected = (
        jnp.dot(first_low, qkv_weight, preferred_element_type=jnp.float32) + full_bias
    ).astype(jnp.bfloat16)
    split_heads = projected.reshape(seq_rows, 3, heads_count, HEAD)
    queries = split_heads[:, 0]
    keys_part = split_heads[:, 1]
    values_part = split_heads[:, 2]
    visible = jnp.arange(seq_rows) < length

    def scores_of():
        raw_scores = (
            jnp.einsum("qhd,khd->hqk", queries, keys_part, preferred_element_type=jnp.float32)
            * scale_qk
        )
        return jnp.where(visible[None, None, :], raw_scores, NEGATIVE)

    scores = scores_of()
    top_score = jnp.max(scores, axis=-1, keepdims=True)
    expo = jnp.exp(scores - top_score)
    total_exp = jnp.sum(expo, axis=-1, keepdims=True)
    log_total = top_score + jnp.log(total_exp)
    attention = (expo / total_exp).astype(jnp.bfloat16)
    mixed = jnp.einsum("hqk,khd->qhd", attention, values_part, preferred_element_type=jnp.float32)
    mixed = mixed.reshape(seq_rows, model_width).astype(jnp.bfloat16)
    middle = (
        as_float
        + jnp.dot(mixed, out_weight, preferred_element_type=jnp.float32)
        + out_bias.astype(jnp.float32)
    )
    hidden_two, second_pull = jax.vjp(
        normalize, middle, second_gain.astype(jnp.float32), second_shift.astype(jnp.float32)
    )
    second_low = hidden_two.astype(jnp.bfloat16)
    inner = jnp.dot(second_low, in_weight, preferred_element_type=jnp.float32) + in_bias.astype(
        jnp.float32
    )
    active, gate_pull = jax.vjp(smooth_gate, inner)
    active_low = active.astype(jnp.bfloat16)
    output = (
        middle
        + jnp.dot(active_low, down_weight, preferred_element_type=jnp.float32)
        + down_bias.astype(jnp.float32)
    )
    upstream = cot_rows.astype(jnp.float32) * visible[:, None].astype(jnp.float32) * factor
    up_low = upstream.astype(jnp.bfloat16)
    grad_down_bias = jnp.sum(up_low.astype(jnp.float32), axis=0)
    grad_down = times_left(active_low, up_low)
    grad_active = times_right(up_low, down_weight)
    (grad_inner,) = gate_pull(grad_active)
    inner_low = grad_inner.astype(jnp.bfloat16)
    grad_in_bias = jnp.sum(inner_low.astype(jnp.float32), axis=0)
    grad_in = times_left(second_low, inner_low)
    grad_second = times_right(inner_low, in_weight)
    grad_middle_norm, grad_second_gain, grad_second_shift = second_pull(grad_second)
    grad_middle = upstream + grad_middle_norm
    middle_low = grad_middle.astype(jnp.bfloat16)
    grad_out_bias = jnp.sum(middle_low.astype(jnp.float32), axis=0)
    grad_out = times_left(mixed, middle_low)
    grad_mixed = (
        times_right(middle_low, out_weight)
        .astype(jnp.bfloat16)
        .reshape(seq_rows, heads_count, HEAD)
    )
    probs_again = jnp.exp(scores_of() - log_total)
    grad_probs = jnp.einsum(
        "qhd,khd->hqk", grad_mixed, values_part, preferred_element_type=jnp.float32
    )
    grad_values = jnp.einsum(
        "hqk,qhd->khd", attention, grad_mixed, preferred_element_type=jnp.float32
    )
    delta = jnp.sum(probs_again * grad_probs, axis=-1, keepdims=True)
    grad_scores = (probs_again * (grad_probs - delta)).astype(jnp.bfloat16)
    grad_queries = (
        jnp.einsum("hqk,khd->qhd", grad_scores, keys_part, preferred_element_type=jnp.float32)
        * scale_qk
    )
    grad_keys = (
        jnp.einsum("hqk,qhd->khd", grad_scores, queries, preferred_element_type=jnp.float32)
        * scale_qk
    )
    grad_projected = jnp.stack([grad_queries, grad_keys, grad_values], axis=1)
    grad_projected = grad_projected.reshape(seq_rows, 3 * model_width).astype(jnp.bfloat16)
    column_sums = jnp.sum(grad_projected.astype(jnp.float32), axis=0)
    grad_qv = jnp.concatenate([column_sums[:model_width], column_sums[2 * model_width :]])
    grad_qkv = times_left(first_low, grad_projected)
    grad_first = times_right(grad_projected, qkv_weight)
    grad_input_norm, grad_first_gain, grad_first_shift = first_pull(grad_first)
    grad_inputs = grad_middle + grad_input_norm
    grads = (
        grad_first_gain,
        grad_first_shift,
        grad_qkv,
        grad_qv,
        grad_out,
        grad_out_bias,
        grad_second_gain,
        grad_second_shift,
        grad_in,
        grad_in_bias,
        grad_down,
        grad_down_bias,
    )
    return (output.astype(jnp.bfloat16), grad_inputs.astype(jnp.bfloat16), grads)


RING = (0, 2, 4, 6, 7, 5, 3, 1)
RING_SIZE = len(RING)
CELLS = 2 * RING_SIZE
ANY = pl.BlockSpec(memory_space=pl.ANY)
HBM = pl.BlockSpec(memory_space=pltpu.HBM)
VMEM = pl.BlockSpec(memory_space=pltpu.VMEM)
SMEM = pl.BlockSpec(memory_space=pltpu.SMEM)
LOW = jnp.bfloat16
FULL = jnp.float32
ROWS = {
    "first_gain": 0,
    "first_shift": 1,
    "qv_bias": 2,
    "out_bias": 4,
    "second_gain": 5,
    "second_shift": 6,
    "in_bias": 7,
    "down_bias": 11,
    "lengths": 12,
}
NAMES = tuple(ROWS)[:8]
SMALL_ROWS = 16
PIECES = (2, 2, 2, 2, 2, 2, 2, 1, 1)


def ring_pairs():
    pairs = []
    for place in range(RING_SIZE):
        chip = RING[place]
        right = RING[(place + 1) % RING_SIZE]
        left = RING[(place - 1) % RING_SIZE]
        pairs.append((2 * chip, 2 * right))
        pairs.append((2 * chip + 1, 2 * left + 1))
    return pairs


def hop(block):
    return lax.ppermute(block, "cells", ring_pairs())


def to_partner(block):
    return lax.ppermute(block, "cells", [(i, i ^ 1) for i in range(CELLS)])


def across(block):
    return lax.ppermute(block, "species", [(0, 1), (1, 0)])


def exchange(values, bit):
    return values + lax.ppermute(values, "cells", [(i, i ^ bit) for i in range(CELLS)])


def after(value, *others):
    return lax.optimization_barrier((value,) + others)[0]


def here():
    index = lax.axis_index("cells")
    core = index % 2
    chip = index // 2
    place = jnp.int32(0)
    for i, ring_chip in enumerate(RING):
        place = jnp.where(chip == ring_chip, i, place)
    return index, core, place


def chip_at(place):
    place = place % RING_SIZE
    chip = jnp.zeros_like(place)
    for i, ring_chip in enumerate(RING):
        chip = jnp.where(place == i, ring_chip, chip)
    return chip


def gather_order(core, place):
    sign = 1 - 2 * core
    order = []

    def pair(at):
        order.append(2 * chip_at(at))
        order.append(2 * chip_at(at) + 1)

    pair(place)
    for step in range(1, 4):
        pair(place - sign * step)
        pair(place + sign * step)
    order.append(2 * chip_at(place + 4) + core)
    order.append(2 * chip_at(place + 4) + 1 - core)
    return order


def scatter_slots(core, place):
    def kept(core_now):
        sign = 1 - 2 * core_now
        order = [2 * chip_at(place + 4) + core_now]
        for step in (3, 2, 1):
            order.append(2 * chip_at(place + sign * step))
            order.append(2 * chip_at(place + sign * step) + 1)
        order.append(2 * chip_at(place) + core_now)
        return order

    order = kept(core) + kept(1 - core)
    slots = []
    for device in range(CELLS):
        slot = jnp.int32(0)
        for i, who in enumerate(order):
            slot = jnp.where(who == device, i, slot)
        slots.append(slot)
    return slots


def both_blocks(block, core):
    other = to_partner(block)
    return jnp.stack([jnp.where(core == 0, block, other), jnp.where(core == 0, other, block)])


def half_of(pair, core):
    return jnp.where(core == 0, pair[0], pair[1])[None]


def add_low(*parts):
    total = parts[0].astype(FULL)
    for part in parts[1:]:
        total = total + part.astype(FULL)
    return total.astype(LOW)


def first_hop(keep, got):
    return hop(add_low(keep[0:1], got[0:1]))


def second_hop(keep, got, moving, core):
    wide = jnp.stack([jnp.where(core == 0, moving[0], 0), jnp.where(core == 0, 0, moving[0])])
    return hop(add_low(keep[1:3], got[1:3], wide))


def later_hop(keep, got, moving, at):
    return hop(add_low(keep[at : at + 2], got[at : at + 2], moving))


def settle(keep, got, moving, core):
    mine = jnp.where(core == 0, moving[0], moving[1])
    other = jnp.where(core == 0, moving[1], moving[0])
    total = add_low(keep[7], got[7], mine, to_partner(other))
    return total, across(total)


def dot(left, right, dims=((1,), (0,))):
    return lax.dot_general(left, right, (dims, ((), ())), preferred_element_type=FULL)


def call(body, out_shape, ins, specs, out_specs=None, scratch=(), vmem=48):
    return pl.pallas_call(
        body,
        out_shape=out_shape,
        in_specs=specs,
        out_specs=[VMEM] * len(out_shape) if out_specs is None else out_specs,
        scratch_shapes=list(scratch),
        compiler_params=pltpu.CompilerParams(vmem_limit_bytes=vmem * 2**20),
        cost_estimate=pl.CostEstimate(flops=10**6, bytes_accessed=0, transcendentals=0),
    )(*ins)


def shape(dims, kind=LOW):
    return jax.ShapeDtypeStruct(dims, kind)


def fetch(order_ref, refs, target, sem):
    rows = target.shape[0] // CELLS
    copies = []
    index = 0
    for source, size in zip(refs, PIECES):
        for part in range(size):
            at = order_ref[index]
            copies.append(
                pltpu.make_async_copy(
                    source.at[part],
                    target.at[pl.ds(pl.multiple_of(at * rows, 16), rows)],
                    sem.at[index],
                )
            )
            index += 1
    for item in copies:
        item.start()
    return copies


def wait_all(copies):
    for item in copies:
        item.wait()


def one_hot(rows, lanes, offset):
    row = lax.broadcasted_iota(jnp.int32, (rows, lanes), 0)
    lane = lax.broadcasted_iota(jnp.int32, (rows, lanes), 1)
    return lane == row + offset


def pack_body(who_ref, lengths_ref, *refs):
    sources, small_ref = refs[:8], refs[8]
    me = who_ref[0]
    model = small_ref.shape[1]
    row = lax.broadcasted_iota(jnp.int32, (SMALL_ROWS, model), 0)
    lane = lax.broadcasted_iota(jnp.int32, (SMALL_ROWS, model), 1)
    small = jnp.zeros((SMALL_ROWS, model), FULL)
    for name, ref in zip(NAMES, sources):
        size = ref.shape[1]
        per_row = model // size
        placed = dot(ref[...], one_hot(size, model, size * (me % per_row)).astype(LOW))
        small = small + jnp.where(row == ROWS[name] + me // per_row, placed, 0.0)
    for i in range(2):
        at = (row == ROWS["lengths"]) & (lane == 2 * me + i)
        small = small + jnp.where(at, lengths_ref[i].astype(FULL), 0.0)
    small_ref[...] = small.astype(LOW)


def norm_parts(values):
    center = values - jnp.mean(values, axis=-1, keepdims=True)
    spread = jnp.mean(center * center, axis=-1, keepdims=True)
    return center, lax.rsqrt(spread + EPSILON)


def norm_back(center, scale, gain, grad):
    weighted = grad * gain
    mean_one = jnp.mean(weighted, axis=-1, keepdims=True)
    mean_two = jnp.mean(weighted * center, axis=-1, keepdims=True)
    back = scale * (weighted - mean_one - center * (scale * scale * mean_two))
    return back, jnp.sum(grad * center * scale, axis=0, keepdims=True), jnp.sum(
        grad, axis=0, keepdims=True
    )


def small_row(small_ref, name, count=1):
    return small_ref[...].astype(FULL)[ROWS[name] : ROWS[name] + count, :]


def project_body(order_ref, x_ref, small_ref, *refs):
    blocks = refs[:9]
    low_ref, proj_ref, weight, sem = refs[9:]
    model = x_ref.shape[1]
    copies = fetch(order_ref, blocks, weight, sem)
    center, scale = norm_parts(x_ref[...].astype(FULL))
    bias = small_row(small_ref, "qv_bias", 2)
    low_ref[...] = (
        center * scale * small_row(small_ref, "first_gain") + small_row(small_ref, "first_shift")
    ).astype(LOW)
    wait_all(copies)
    for j in range(3):
        lanes = slice(j * model, (j + 1) * model)
        part = dot(low_ref[...], weight[:, lanes])
        if j != 1:
            part = part + bias[j // 2 : j // 2 + 1]
        proj_ref[:, lanes] = part.astype(LOW)


def attend_body(seq, lengths_ref, proj_ref, att_ref, mixed_ref):
    model = mixed_ref.shape[1]
    cells = mixed_ref.shape[0] // seq
    pairs = model // (2 * HEAD)
    lane = lax.broadcasted_iota(jnp.int32, (seq, 2 * HEAD), 1)
    key = lax.broadcasted_iota(jnp.int32, (seq, seq), 0)

    def step(index, carry):
        s = index // pairs
        p = index % pairs
        rows = pl.ds(pl.multiple_of(s * seq, seq), seq)
        at = pl.multiple_of(p * 2 * HEAD, 2 * HEAD)
        q = proj_ref[rows, pl.ds(at, 2 * HEAD)] * jnp.asarray(HEAD ** (-0.5), LOW)
        k = proj_ref[rows, pl.ds(at + model, 2 * HEAD)]
        v_turned = proj_ref[rows, pl.ds(at + 2 * model, 2 * HEAD)].T
        visible = key < lengths_ref[s]
        mixed = []
        for i in range(2):
            own = (lane >= i * HEAD) & (lane < (i + 1) * HEAD)
            scores = dot(jnp.where(own, k, jnp.zeros_like(k)), q, ((1,), (1,)))
            scores = jnp.where(visible, scores, NEGATIVE)
            expo = jnp.exp(scores - jnp.max(scores, axis=0, keepdims=True))
            probs = expo * (1.0 / jnp.sum(expo, axis=0, keepdims=True))
            probs = probs.astype(LOW)
            att_ref[2 * index + i] = probs
            mixed.append(dot(v_turned[i * HEAD : (i + 1) * HEAD], probs))
        mixed_ref[rows, pl.ds(at, 2 * HEAD)] = jnp.concatenate(mixed, axis=0).T.astype(LOW)
        return carry

    lax.fori_loop(0, cells * pairs, step, 0, unroll=2)


ERFC_STEP = 0.33
ERFC = (
    0.1863578228018033,
    0.18295566386742124,
    0.2012255082472392,
    0.04721561458875723,
    0.4085089979423051,
    -0.35115900736338407,
    0.4602422572120205,
    -0.13534686486277223,
)


def gelu_parts(inner):
    z = jnp.abs(inner) * (0.5**0.5)
    t = 1.0 / (1.0 + ERFC_STEP * z)
    tail = jnp.full_like(t, 0.5 * ERFC[-1])
    for factor in ERFC[-2::-1]:
        tail = tail * t + 0.5 * factor
    bell = jnp.exp(-(z * z))
    tail = tail * t * bell
    area = jnp.where(inner < 0.0, tail, 1.0 - tail)
    return inner * area, area + inner * bell * (0.5 / 3.141592653589793) ** 0.5


def row_mask(lengths_ref, rows, seq):
    at = lax.broadcasted_iota(jnp.int32, (rows, 1), 0)
    true = (at < lengths_ref[0]).astype(FULL)
    for s in range(1, rows // seq):
        true = jnp.where(at < s * seq, true, (at < lengths_ref[s] + s * seq).astype(FULL))
    return true


def loss_rows(lengths_ref, small_ref, other_ref, cot_ref, seq, whole):
    count = jnp.sum(
        small_row(small_ref, "lengths") + small_row(other_ref, "lengths"), axis=-1, keepdims=True
    )
    return cot_ref[...].astype(FULL) * (
        row_mask(lengths_ref, cot_ref.shape[0], seq) * (whole / count)
    )


def put_slots(keep_buf, slot_ref, values, first, lanes):
    rows = keep_buf.shape[1]
    for i in range(values.shape[0] // rows):
        keep_buf[slot_ref[first + i], :, lanes] = values[i * rows : (i + 1) * rows].astype(LOW)


def send_slots(buf, keep_ref, away_ref, sem):
    half = RING_SIZE
    copies = [
        pltpu.make_async_copy(buf.at[pl.ds(half, half)], away_ref, sem.at[0]),
        pltpu.make_async_copy(buf.at[pl.ds(0, half)], keep_ref, sem.at[1]),
    ]
    for item in copies:
        item.start()
    return copies


def inner_body(order_ref, x_ref, mixed_ref, small_ref, *refs):
    blocks = refs[:9]
    middle_ref, low_ref, active_ref, slope_ref, weight, sem = refs[9:]
    model = x_ref.shape[1]
    ff = active_ref.shape[1]
    wait_all(fetch(order_ref, blocks, weight, sem))
    middle = (
        x_ref[...].astype(FULL)
        + dot(mixed_ref[...], weight[:, ff:])
        + small_row(small_ref, "out_bias")
    )
    middle_ref[...] = middle
    center, scale = norm_parts(middle)
    low = center * scale * small_row(small_ref, "second_gain") + small_row(
        small_ref, "second_shift"
    )
    low_ref[...] = low.astype(LOW)
    step = 2 * (ff // RING_SIZE)
    bias = small_row(small_ref, "in_bias", 4)
    for j in range(ff // step):
        lanes = slice(j * step, (j + 1) * step)
        inner = dot(low_ref[...], weight[:, lanes]) + bias[j : j + 1]
        active, slope = gelu_parts(inner)
        active_ref[:, lanes] = active.astype(LOW)
        slope_ref[:, lanes] = slope.astype(LOW)


def grad_down_body(
    seq, whole, slot_ref, lengths_ref, active_ref, cot_ref, small_ref, other_ref, up_ref,
    down_b_ref, keep_ref, away_ref, slots, sem,
):
    up_low = loss_rows(lengths_ref, small_ref, other_ref, cot_ref, seq, whole).astype(LOW)
    up_ref[...] = up_low
    down_b_ref[...] = jnp.sum(up_low.astype(FULL), axis=0, keepdims=True)
    parts = RING_SIZE
    step = active_ref.shape[1] // parts
    for j in range(parts):
        grad = dot(active_ref[:, j * step : (j + 1) * step], up_ref[...], ((0,), (0,)))
        put_slots(slots, slot_ref, grad, j * CELLS // parts, slice(None))
    wait_all(send_slots(slots, keep_ref, away_ref, sem))


def inner_back_body(order_ref, slope_ref, up_ref, *refs):
    blocks = refs[:9]
    inner_ref, in_b_ref, weight, sem = refs[9:]
    model = up_ref.shape[1]
    wait_all(fetch(order_ref, blocks, weight, sem))
    for j in range(inner_ref.shape[1] // model):
        lanes = slice(j * model, (j + 1) * model)
        grad = dot(up_ref[...], weight[lanes, :], ((1,), (1,)))
        low = (grad * slope_ref[:, lanes].astype(FULL)).astype(LOW)
        inner_ref[:, lanes] = low
        in_b_ref[j : j + 1, :] = jnp.sum(low.astype(FULL), axis=0, keepdims=True)


def down_body(active_ref, middle_ref, small_ref, weight_ref, out_ref):
    out_ref[...] = (
        middle_ref[...]
        + dot(active_ref[...], weight_ref[...])
        + small_row(small_ref, "down_bias")
    ).astype(LOW)


def grad_in_body(slot_ref, low_ref, inner_ref, keep_ref, away_ref, slots, sem):
    model = low_ref.shape[1]
    turned = low_ref[...].T
    for j in range(inner_ref.shape[1] // model):
        lanes = slice(j * model, (j + 1) * model)
        put_slots(slots, slot_ref, dot(turned, inner_ref[:, lanes]), 0, lanes)
    wait_all(send_slots(slots, keep_ref, away_ref, sem))


def middle_back_body(
    seq, whole, lengths_ref, inner_ref, middle_ref, cot_ref, small_ref, other_ref, weight,
    grad_ref, grad_low_ref, grad_mixed_ref, sums_ref,
):
    ff = inner_ref.shape[1]
    grad_second = dot(inner_ref[...], weight[:, :ff], ((1,), (1,)))
    center, scale = norm_parts(middle_ref[...])
    back, gain_sum, shift_sum = norm_back(
        center, scale, small_row(small_ref, "second_gain"), grad_second
    )
    grad = loss_rows(lengths_ref, small_ref, other_ref, cot_ref, seq, whole) + back
    grad_ref[...] = grad
    grad_low = grad.astype(LOW)
    grad_low_ref[...] = grad_low
    grad_mixed_ref[...] = dot(grad_low, weight[:, ff:], ((1,), (1,))).astype(LOW)
    sums_ref[0:1, :] = jnp.sum(grad_low.astype(FULL), axis=0, keepdims=True)
    sums_ref[1:2, :] = gain_sum
    sums_ref[2:3, :] = shift_sum


def attend_back_body(seq, begin, proj_ref, att_ref, grad_ref, out_ref):
    model = grad_ref.shape[1]
    half = out_ref.shape[1] // 3
    all_pairs = model // (2 * HEAD)
    pairs = half // (2 * HEAD)
    cells = grad_ref.shape[0] // seq
    lane = lax.broadcasted_iota(jnp.int32, (seq, 2 * HEAD), 1)
    scale = HEAD ** (-0.5)

    def step(index, carry):
        s = index // pairs
        p = index % pairs
        rows = pl.ds(pl.multiple_of(s * seq, seq), seq)
        to = pl.multiple_of(p * 2 * HEAD, 2 * HEAD)
        at = pl.multiple_of(to + begin * 2 * HEAD, 2 * HEAD)
        q = proj_ref[rows, pl.ds(at, 2 * HEAD)]
        k_turned = proj_ref[rows, pl.ds(at + model, 2 * HEAD)].T
        v = proj_ref[rows, pl.ds(at + 2 * model, 2 * HEAD)]
        g = grad_ref[rows, pl.ds(at, 2 * HEAD)]
        grad_q = []
        grad_k = []
        grad_v = []
        for i in range(2):
            own = (lane >= i * HEAD) & (lane < (i + 1) * HEAD)
            probs = att_ref[2 * (s * all_pairs + begin + p) + i]
            wide = probs.astype(FULL)
            grad_probs = dot(jnp.where(own, v, jnp.zeros_like(v)), g, ((1,), (1,)))
            delta = jnp.sum(wide * grad_probs, axis=0, keepdims=True)
            scores = (wide * (grad_probs - delta)).astype(LOW)
            grad_q.append(dot(k_turned[i * HEAD : (i + 1) * HEAD], scores))
            grad_k.append(dot(scores, q))
            grad_v.append(dot(probs, g))
        first = lane < HEAD
        out_ref[rows, pl.ds(to, 2 * HEAD)] = (
            jnp.concatenate(grad_q, axis=0).T * scale
        ).astype(LOW)
        out_ref[rows, pl.ds(to + half, 2 * HEAD)] = (
            jnp.where(first, grad_k[0], grad_k[1]) * scale
        ).astype(LOW)
        out_ref[rows, pl.ds(to + 2 * half, 2 * HEAD)] = jnp.where(
            first, grad_v[0], grad_v[1]
        ).astype(LOW)
        return carry

    lax.fori_loop(0, cells * pairs, step, 0, unroll=2)


def early_grad_body(
    slot_ref, low_ref, part_ref, mixed_ref, grad_low_ref, keep_ref, away_ref, slots, sem
):
    width = part_ref.shape[1]
    put_slots(slots, slot_ref, dot(low_ref[...].T, part_ref[...]), 0, slice(0, width))
    put_slots(
        slots, slot_ref, dot(mixed_ref[...].T, grad_low_ref[...]), 0,
        slice(width, slots.shape[2]),
    )
    wait_all(send_slots(slots, keep_ref, away_ref, sem))


def late_grad_body(slot_ref, low_ref, part_ref, keep_ref, away_ref, slots, sem):
    put_slots(slots, slot_ref, dot(low_ref[...].T, part_ref[...]), 0, slice(None))
    wait_all(send_slots(slots, keep_ref, away_ref, sem))


def first_back_body(
    x_ref, one_ref, two_ref, grad_ref, small_ref, sums_ref, in_b_ref, down_b_ref, weight,
    out_ref, sum_ref,
):
    model = x_ref.shape[1]
    center, scale = norm_parts(x_ref[...].astype(FULL))
    parts = ((one_ref, 0), (two_ref, one_ref.shape[1] // 3))
    grad_first = jnp.zeros(x_ref.shape, FULL)
    for j in range(3):
        for ref, begin in parts:
            width = ref.shape[1] // 3
            at = j * model + begin
            grad_first = grad_first + dot(
                ref[:, j * width : (j + 1) * width], weight[:, at : at + width], ((1,), (1,))
            )
    back, gain_sum, shift_sum = norm_back(
        center, scale, small_row(small_ref, "first_gain"), grad_first
    )

    def put(name, value, offset=0):
        at = ROWS[name] + offset
        sum_ref[at : at + value.shape[0], :] = value

    sum_ref[...] = jnp.zeros_like(sum_ref)
    put("first_gain", gain_sum)
    put("first_shift", shift_sum)
    for j in range(2):
        at = ROWS["qv_bias"] + j
        for ref, begin in parts:
            width = ref.shape[1] // 3
            part = ref[:, 2 * j * width : (2 * j + 1) * width].astype(FULL)
            sum_ref[at : at + 1, begin : begin + width] = jnp.sum(part, axis=0, keepdims=True)
    put("out_bias", sums_ref[0:1, :])
    put("second_gain", sums_ref[1:2, :])
    put("second_shift", sums_ref[2:3, :])
    put("in_bias", in_b_ref[...])
    put("down_bias", down_b_ref[...])
    out_ref[...] = (grad_ref[...] + back).astype(LOW)


def finish_body(who_ref, early_ref, early_two_ref, late_ref, late_two_ref, small_ref, *refs):
    grad_ref, out_ref, vectors = refs[0], refs[1], refs[2:]
    model = out_ref.shape[1]
    early = early_ref[...].astype(FULL) + early_two_ref[...].astype(FULL)
    late = late_ref[...].astype(FULL) + late_two_ref[...].astype(FULL)
    one = (early.shape[1] - model) // 3
    two = late.shape[1] // 3
    for j in range(3):
        at = j * model
        grad_ref[:, at : at + one] = early[:, j * one : (j + 1) * one]
        grad_ref[:, at + one : at + model] = late[:, j * two : (j + 1) * two]
    out_ref[...] = early[:, 3 * one :]
    me = who_ref[0]
    row = lax.broadcasted_iota(jnp.int32, (SMALL_ROWS, model), 0)
    for name, ref in zip(NAMES, vectors):
        size = ref.shape[1]
        per_row = model // size
        here_row = jnp.where(row == ROWS[name] + me // per_row, small_ref[...], 0.0)
        values = jnp.sum(here_row, axis=0, keepdims=True)
        picker = one_hot(size, model, size * (me % per_row)).astype(FULL)
        ref[...] = lax.dot_general(
            values, picker, (((1,), (1,)), ((), ())), precision=lax.Precision.HIGHEST,
            preferred_element_type=FULL,
        )


def on_device_ring(
    tokens,
    lengths,
    cotangent,
    first_gain,
    first_shift,
    qkv_weight,
    qv_bias,
    out_weight,
    out_bias,
    second_gain,
    second_shift,
    in_weight,
    in_bias,
    down_weight,
    down_bias,
):
    micro, seq, model = tokens.shape[1:]
    total_rows = micro * seq
    rows = qkv_weight.shape[0]
    down_rows = down_weight.shape[0]
    ff = in_weight.shape[1]
    heads = model // HEAD
    whole = float(lax.axis_size("species") * CELLS * micro * seq)
    index, core, place = here()
    who = jnp.stack([index]).astype(jnp.int32)
    order = jnp.stack(gather_order(core, place)).astype(jnp.int32)
    slot = jnp.stack(scatter_slots(core, place)).astype(jnp.int32)
    lens = lengths.reshape(micro)
    x = tokens.reshape(total_rows, model)
    cot = cotangent.reshape(total_rows, model)
    vectors = (
        first_gain, first_shift, qv_bias, out_bias, second_gain, second_shift, in_bias, down_bias,
    )

    dma = pltpu.SemaphoreType.DMA

    def gathered(own, hops):
        got = [own]
        for item in hops:
            got += [item, to_partner(item)]
        return got

    own = both_blocks(qkv_weight, core)
    qkv_one = hop(own)
    (small,) = call(
        pack_body,
        [shape((SMALL_ROWS, model))],
        [who, after(lens, own)] + [item.reshape(1, -1) for item in vectors],
        [SMEM, SMEM] + [VMEM] * 8,
        vmem=4,
    )
    small = exchange(small, 1)
    in_weight, out_weight = lax.optimization_barrier((in_weight, out_weight, own))[:2]
    in_own = both_blocks(jnp.concatenate([in_weight, out_weight], axis=1), core)
    qkv_one, small, in_own = lax.optimization_barrier((qkv_one, small, in_own))
    qkv_two = hop(qkv_one)
    small = exchange(small, 2)
    down_own = both_blocks(after(down_weight, qkv_one), core)
    qkv_two, small, down_own = lax.optimization_barrier((qkv_two, small, down_own))
    qkv_three = hop(qkv_two)
    small = exchange(small, 4)
    qkv_three, small = lax.optimization_barrier((qkv_three, small))
    qkv_last = hop(half_of(qkv_three, core))
    in_one = hop(after(in_own, qkv_three))
    small = exchange(small, 8)
    low, proj, qkv_full = call(
        project_body,
        [
            shape((total_rows, model)),
            shape((total_rows, 3 * model)),
            shape((model, 3 * model)),
        ],
        [order, x, small] + gathered(own, (qkv_one, qkv_two, qkv_three, qkv_last)),
        [SMEM, VMEM, VMEM] + [ANY] * 9,
        scratch=[dma((CELLS,))],
        vmem=20,
    )
    other_small = across(small)
    in_one, proj = lax.optimization_barrier((in_one, proj))
    in_two = hop(in_one)
    down_one = hop(after(down_own, in_one))
    att, mixed = call(
        lambda *refs: attend_body(seq, *refs),
        [shape((micro * heads, seq, seq)), shape((total_rows, model))],
        [lens, proj],
        [SMEM, VMEM],
        vmem=16,
    )
    in_two, mixed = lax.optimization_barrier((in_two, mixed))
    in_three = hop(in_two)
    in_three, down_one = lax.optimization_barrier((in_three, down_one))
    in_last = hop(half_of(in_three, core))
    down_two = hop(down_one)
    in_last, mixed = lax.optimization_barrier((in_last, mixed))
    in_got = gathered(in_own, (in_one, in_two, in_three, in_last))
    middle, low_two, active, slope, in_full = call(
        inner_body,
        [
            shape((total_rows, model), FULL),
            shape((total_rows, model)),
            shape((total_rows, ff)),
            shape((total_rows, ff)),
            shape((model, ff + model)),
        ],
        [order, x, after(mixed, down_two), small] + in_got,
        [SMEM] + [VMEM] * 3 + [ANY] * 9,
        scratch=[dma((CELLS,))],
        vmem=24,
    )
    down_three = hop(down_two)
    down_three, active = lax.optimization_barrier((down_three, active))
    down_last = hop(half_of(down_three, core))
    up_low, down_b, down_keep, down_away = call(
        lambda *refs: grad_down_body(seq, whole, *refs),
        [
            shape((total_rows, model)),
            shape((1, model), FULL),
            shape((RING_SIZE, down_rows, model)),
            shape((RING_SIZE, down_rows, model)),
        ],
        [slot, lens, active, cot, small, other_small],
        [SMEM] * 2 + [VMEM] * 4,
        [VMEM] * 2 + [ANY] * 2,
        scratch=[pltpu.VMEM((CELLS, down_rows, model), LOW), dma((2,))],
        vmem=18,
    )

    down_other = to_partner(down_away)
    inner_low, in_b, down_full = call(
        inner_back_body,
        [
            shape((total_rows, ff)),
            shape((ff // model, model), FULL),
            shape((ff, model)),
        ],
        [order, slope, up_low]
        + gathered(down_own, (down_one, down_two, down_three, down_last)),
        [SMEM] + [VMEM] * 2 + [ANY] * 9,
        scratch=[dma((CELLS,))],
        vmem=20,
    )
    down_other, inner_low = lax.optimization_barrier((down_other, inner_low))
    down_sum = first_hop(down_keep, down_other)
    in_keep, in_away = call(
        grad_in_body,
        [shape((RING_SIZE, rows, ff)), shape((RING_SIZE, rows, ff))],
        [slot, low_two, inner_low],
        [SMEM] + [VMEM] * 2,
        [ANY] * 2,
        scratch=[pltpu.VMEM((CELLS, rows, ff), LOW), dma((2,))],
        vmem=16,
    )
    in_other = to_partner(in_away)
    (out_tokens,) = call(
        down_body,
        [shape((total_rows, model))],
        [after(active, in_keep), middle, small, down_full],
        [VMEM] * 4,
        vmem=14,
    )
    down_sum, out_tokens, inner_low = lax.optimization_barrier((down_sum, out_tokens, inner_low))
    down_sum = second_hop(down_keep, down_other, down_sum, core)
    grad_middle, grad_low, grad_mixed, sums = call(
        lambda *refs: middle_back_body(seq, whole, *refs),
        [
            shape((total_rows, model), FULL),
            shape((total_rows, model)),
            shape((total_rows, model)),
            shape((3, model), FULL),
        ],
        [lens, inner_low, middle, cot, small, other_small, in_full],
        [SMEM] + [VMEM] * 6,
        vmem=24,
    )

    def attend_back(begin, pairs, grad):
        return call(
            lambda *refs: attend_back_body(seq, begin, *refs),
            [shape((total_rows, 6 * pairs * HEAD))],
            [proj, att, grad],
            [VMEM] * 3,
            vmem=14,
        )[0]

    pairs = model // (2 * HEAD)
    early_pairs = 2 * pairs // 3
    down_sum, in_other, grad_mixed = lax.optimization_barrier((down_sum, in_other, grad_mixed))
    down_sum = later_hop(down_keep, down_other, down_sum, 3)
    in_sum = first_hop(in_keep, in_other)
    grad_one = attend_back(0, early_pairs, grad_mixed)
    early_width = 6 * early_pairs * HEAD + model
    early_keep, early_away = call(
        early_grad_body,
        [shape((RING_SIZE, rows, early_width))] * 2,
        [slot, low, grad_one, mixed, grad_low],
        [SMEM] + [VMEM] * 4,
        [ANY] * 2,
        scratch=[pltpu.VMEM((CELLS, rows, early_width), LOW), dma((2,))],
        vmem=14,
    )
    early_other = to_partner(early_away)
    down_sum, in_sum, early_keep, grad_mixed = lax.optimization_barrier(
        (down_sum, in_sum, early_keep, grad_mixed)
    )
    down_sum = later_hop(down_keep, down_other, down_sum, 5)
    in_sum = second_hop(in_keep, in_other, in_sum, core)
    grad_two = attend_back(early_pairs, pairs - early_pairs, grad_mixed)
    late_width = 6 * (pairs - early_pairs) * HEAD
    early_other, grad_two = lax.optimization_barrier((early_other, grad_two))
    early_sum = first_hop(early_keep, early_other)
    late_keep, late_away = call(
        late_grad_body,
        [shape((RING_SIZE, rows, late_width))] * 2,
        [slot, low, grad_two],
        [SMEM] + [VMEM] * 2,
        [ANY] * 2,
        scratch=[pltpu.VMEM((CELLS, rows, late_width), LOW), dma((2,))],
        vmem=8,
    )
    late_other = to_partner(late_away)
    in_sum, grad_two, late_keep = lax.optimization_barrier((in_sum, grad_two, late_keep))
    in_sum = later_hop(in_keep, in_other, in_sum, 3)
    grad_tokens, small_sum = call(
        first_back_body,
        [shape((total_rows, model)), shape((SMALL_ROWS, model), FULL)],
        [x, grad_one, grad_two, grad_middle, small, sums, in_b, down_b, qkv_full],
        [VMEM] * 9,
        vmem=20,
    )
    down_terms = settle(down_keep, down_other, after(down_sum, late_keep), core)
    early_sum, late_other, in_sum, small_sum = lax.optimization_barrier(
        (early_sum, late_other, in_sum, small_sum)
    )
    early_sum = second_hop(early_keep, early_other, early_sum, core)
    small_sum = exchange(small_sum, 1)
    late_sum = first_hop(late_keep, late_other)
    in_sum = later_hop(in_keep, in_other, in_sum, 5)
    small_sum = exchange(small_sum, 2)
    early_sum, late_sum, in_sum = lax.optimization_barrier((early_sum, late_sum, in_sum))
    late_sum = second_hop(late_keep, late_other, late_sum, core)
    early_sum = later_hop(early_keep, early_other, early_sum, 3)
    small_sum = exchange(small_sum, 4)
    late_sum = later_hop(late_keep, late_other, late_sum, 3)
    in_terms = settle(in_keep, in_other, in_sum, core)
    small_sum = exchange(small_sum, 8)
    early_sum = later_hop(early_keep, early_other, early_sum, 5)
    late_sum = later_hop(late_keep, late_other, late_sum, 5)
    small_sum = small_sum + across(small_sum)
    early_terms = settle(early_keep, early_other, early_sum, core)
    late_terms = settle(late_keep, late_other, late_sum, core)
    finished = call(
        finish_body,
        [shape((rows, 3 * model), FULL), shape((rows, model), FULL)]
        + [shape((1, item.shape[0]), FULL) for item in vectors],
        [who] + list(early_terms) + list(late_terms) + [small_sum],
        [SMEM] + [VMEM] * 5,
        vmem=6,
    )
    grad_qkv, grad_out = finished[:2]
    pieces = [item.reshape(-1) for item in finished[2:]]
    return (
        out_tokens.reshape(tokens.shape),
        grad_tokens.reshape(tokens.shape),
        pieces[0],
        pieces[1],
        grad_qkv,
        pieces[2],
        grad_out,
        pieces[3],
        pieces[4],
        pieces[5],
        in_terms[0].astype(FULL) + in_terms[1].astype(FULL),
        pieces[6],
        down_terms[0].astype(FULL) + down_terms[1].astype(FULL),
        pieces[7],
    )


def on_device(
    tokens,
    lengths,
    cotangent,
    first_gain,
    first_shift,
    qkv_weight,
    qv_bias,
    out_weight,
    out_bias,
    second_gain,
    second_shift,
    in_weight,
    in_bias,
    down_weight,
    down_bias,
):
    local_count = jnp.sum(lengths).astype(jnp.float32)
    count = lax.psum(local_count, ("species", "cells"))
    micro_count = tokens.shape[1]
    seq_rows = tokens.shape[2]
    factor = (
        float(lax.axis_size("species") * lax.axis_size("cells") * micro_count * seq_rows) / count
    )
    output_rows = []
    gradient_rows = []
    summed = None
    for micro_step in range(micro_count):
        gathered = (
            lax.all_gather(first_gain, "cells", axis=0, tiled=True),
            lax.all_gather(first_shift, "cells", axis=0, tiled=True),
            lax.all_gather(qkv_weight, "cells", axis=0, tiled=True),
            lax.all_gather(qv_bias, "cells", axis=0, tiled=True),
            lax.all_gather(out_weight, "cells", axis=0, tiled=True),
            lax.all_gather(out_bias, "cells", axis=0, tiled=True),
            lax.all_gather(second_gain, "cells", axis=0, tiled=True),
            lax.all_gather(second_shift, "cells", axis=0, tiled=True),
            lax.all_gather(in_weight, "cells", axis=0, tiled=True),
            lax.all_gather(in_bias, "cells", axis=0, tiled=True),
            lax.all_gather(down_weight, "cells", axis=0, tiled=True),
            lax.all_gather(down_bias, "cells", axis=0, tiled=True),
        )
        out_seq, grad_seq, grads = sequence_pass(
            gathered,
            tokens[0, micro_step],
            lengths[0, micro_step],
            cotangent[0, micro_step],
            factor,
        )
        output_rows.append(out_seq)
        gradient_rows.append(grad_seq)
        shares = (
            lax.psum_scatter(grads[0], "cells", scatter_dimension=0, tiled=True),
            lax.psum_scatter(grads[1], "cells", scatter_dimension=0, tiled=True),
            lax.psum_scatter(grads[2], "cells", scatter_dimension=0, tiled=True),
            lax.psum_scatter(grads[3], "cells", scatter_dimension=0, tiled=True),
            lax.psum_scatter(grads[4], "cells", scatter_dimension=0, tiled=True),
            lax.psum_scatter(grads[5], "cells", scatter_dimension=0, tiled=True),
            lax.psum_scatter(grads[6], "cells", scatter_dimension=0, tiled=True),
            lax.psum_scatter(grads[7], "cells", scatter_dimension=0, tiled=True),
            lax.psum_scatter(grads[8], "cells", scatter_dimension=0, tiled=True),
            lax.psum_scatter(grads[9], "cells", scatter_dimension=0, tiled=True),
            lax.psum_scatter(grads[10], "cells", scatter_dimension=0, tiled=True),
            lax.psum_scatter(grads[11], "cells", scatter_dimension=0, tiled=True),
        )
        summed = shares if summed is None else jax.tree.map(jnp.add, summed, shares)
    final = (
        lax.psum(summed[0].astype(jnp.bfloat16), "species").astype(jnp.float32),
        lax.psum(summed[1].astype(jnp.bfloat16), "species").astype(jnp.float32),
        lax.psum(summed[2].astype(jnp.bfloat16), "species").astype(jnp.float32),
        lax.psum(summed[3].astype(jnp.bfloat16), "species").astype(jnp.float32),
        lax.psum(summed[4].astype(jnp.bfloat16), "species").astype(jnp.float32),
        lax.psum(summed[5].astype(jnp.bfloat16), "species").astype(jnp.float32),
        lax.psum(summed[6].astype(jnp.bfloat16), "species").astype(jnp.float32),
        lax.psum(summed[7].astype(jnp.bfloat16), "species").astype(jnp.float32),
        lax.psum(summed[8].astype(jnp.bfloat16), "species").astype(jnp.float32),
        lax.psum(summed[9].astype(jnp.bfloat16), "species").astype(jnp.float32),
        lax.psum(summed[10].astype(jnp.bfloat16), "species").astype(jnp.float32),
        lax.psum(summed[11].astype(jnp.bfloat16), "species").astype(jnp.float32),
    )
    out_tokens = jnp.stack(output_rows)[None]
    grad_tokens = jnp.stack(gradient_rows)[None]
    return (out_tokens, grad_tokens) + tuple(final)


def solution(mesh):
    in_specs = (
        P("species", "cells", None, None),
        P("species", "cells"),
        P("species", "cells", None, None),
        P("cells"),
        P("cells"),
        P("cells", None),
        P("cells"),
        P("cells", None),
        P("cells"),
        P("cells"),
        P("cells"),
        P("cells", None),
        P("cells"),
        P("cells", None),
        P("cells"),
    )
    out_specs = (
        P("species", "cells", None, None),
        P("species", "cells", None, None),
        P("cells"),
        P("cells"),
        P("cells", None),
        P("cells"),
        P("cells", None),
        P("cells"),
        P("cells"),
        P("cells"),
        P("cells", None),
        P("cells"),
        P("cells", None),
        P("cells"),
    )
    program = on_device_ring if mesh.shape["cells"] == 2 * RING_SIZE else on_device
    return jax.shard_map(
        program, mesh=mesh, in_specs=in_specs, out_specs=out_specs, check_vma=False
    )
```

```python
import jax
import jax.numpy as jnp
from jax import lax
from jax.experimental import pallas as pl
from jax.experimental.pallas import tpu as pltpu
from jax.sharding import PartitionSpec as P

HEAD = 64


EPSILON = 1e-12
NEGATIVE = -1e30


def normalize(values, gain_vec, shift_vec):
    center = values - jnp.mean(values, axis=-1, keepdims=True)
    spread = jnp.mean(center * center, axis=-1, keepdims=True)
    return center * lax.rsqrt(spread + EPSILON) * gain_vec + shift_vec


def smooth_gate(values):
    return jax.nn.gelu(values, approximate=False)


def times_left(left_side, right_side):
    return lax.dot_general(
        left_side, right_side, (((0,), (0,)), ((), ())), preferred_element_type=jnp.float32
    )


def times_right(left_side, right_side):
    return lax.dot_general(
        left_side, right_side, (((1,), (1,)), ((), ())), preferred_element_type=jnp.float32
    )


def sequence_pass(weights, inputs, length, cot_rows, factor):
    (
        first_gain,
        first_shift,
        qkv_weight,
        qv_bias,
        out_weight,
        out_bias,
        second_gain,
        second_shift,
        in_weight,
        in_bias,
        down_weight,
        down_bias,
    ) = weights
    seq_rows = inputs.shape[0]
    model_width = inputs.shape[1]
    heads_count = model_width // HEAD
    scale_qk = float(HEAD) ** (-0.5)
    as_float = inputs.astype(jnp.float32)
    hidden_one, first_pull = jax.vjp(
        normalize, as_float, first_gain.astype(jnp.float32), first_shift.astype(jnp.float32)
    )
    first_low = hidden_one.astype(jnp.bfloat16)
    bias_float = qv_bias.astype(jnp.float32)
    full_bias = jnp.concatenate(
        [bias_float[:model_width], jnp.zeros((model_width,), jnp.float32), bias_float[model_width:]]
    )
    projected = (
        jnp.dot(first_low, qkv_weight, preferred_element_type=jnp.float32) + full_bias
    ).astype(jnp.bfloat16)
    split_heads = projected.reshape(seq_rows, 3, heads_count, HEAD)
    queries = split_heads[:, 0]
    keys_part = split_heads[:, 1]
    values_part = split_heads[:, 2]
    visible = jnp.arange(seq_rows) < length

    def scores_of():
        raw_scores = (
            jnp.einsum("qhd,khd->hqk", queries, keys_part, preferred_element_type=jnp.float32)
            * scale_qk
        )
        return jnp.where(visible[None, None, :], raw_scores, NEGATIVE)

    scores = scores_of()
    top_score = jnp.max(scores, axis=-1, keepdims=True)
    expo = jnp.exp(scores - top_score)
    total_exp = jnp.sum(expo, axis=-1, keepdims=True)
    log_total = top_score + jnp.log(total_exp)
    attention = (expo / total_exp).astype(jnp.bfloat16)
    mixed = jnp.einsum("hqk,khd->qhd", attention, values_part, preferred_element_type=jnp.float32)
    mixed = mixed.reshape(seq_rows, model_width).astype(jnp.bfloat16)
    middle = (
        as_float
        + jnp.dot(mixed, out_weight, preferred_element_type=jnp.float32)
        + out_bias.astype(jnp.float32)
    )
    hidden_two, second_pull = jax.vjp(
        normalize, middle, second_gain.astype(jnp.float32), second_shift.astype(jnp.float32)
    )
    second_low = hidden_two.astype(jnp.bfloat16)
    inner = jnp.dot(second_low, in_weight, preferred_element_type=jnp.float32) + in_bias.astype(
        jnp.float32
    )
    active, gate_pull = jax.vjp(smooth_gate, inner)
    active_low = active.astype(jnp.bfloat16)
    output = (
        middle
        + jnp.dot(active_low, down_weight, preferred_element_type=jnp.float32)
        + down_bias.astype(jnp.float32)
    )
    upstream = cot_rows.astype(jnp.float32) * visible[:, None].astype(jnp.float32) * factor
    up_low = upstream.astype(jnp.bfloat16)
    grad_down_bias = jnp.sum(up_low.astype(jnp.float32), axis=0)
    grad_down = times_left(active_low, up_low)
    grad_active = times_right(up_low, down_weight)
    (grad_inner,) = gate_pull(grad_active)
    inner_low = grad_inner.astype(jnp.bfloat16)
    grad_in_bias = jnp.sum(inner_low.astype(jnp.float32), axis=0)
    grad_in = times_left(second_low, inner_low)
    grad_second = times_right(inner_low, in_weight)
    grad_middle_norm, grad_second_gain, grad_second_shift = second_pull(grad_second)
    grad_middle = upstream + grad_middle_norm
    middle_low = grad_middle.astype(jnp.bfloat16)
    grad_out_bias = jnp.sum(middle_low.astype(jnp.float32), axis=0)
    grad_out = times_left(mixed, middle_low)
    grad_mixed = (
        times_right(middle_low, out_weight)
        .astype(jnp.bfloat16)
        .reshape(seq_rows, heads_count, HEAD)
    )
    probs_again = jnp.exp(scores_of() - log_total)
    grad_probs = jnp.einsum(
        "qhd,khd->hqk", grad_mixed, values_part, preferred_element_type=jnp.float32
    )
    grad_values = jnp.einsum(
        "hqk,qhd->khd", attention, grad_mixed, preferred_element_type=jnp.float32
    )
    delta = jnp.sum(probs_again * grad_probs, axis=-1, keepdims=True)
    grad_scores = (probs_again * (grad_probs - delta)).astype(jnp.bfloat16)
    grad_queries = (
        jnp.einsum("hqk,khd->qhd", grad_scores, keys_part, preferred_element_type=jnp.float32)
        * scale_qk
    )
    grad_keys = (
        jnp.einsum("hqk,qhd->khd", grad_scores, queries, preferred_element_type=jnp.float32)
        * scale_qk
    )
    grad_projected = jnp.stack([grad_queries, grad_keys, grad_values], axis=1)
    grad_projected = grad_projected.reshape(seq_rows, 3 * model_width).astype(jnp.bfloat16)
    column_sums = jnp.sum(grad_projected.astype(jnp.float32), axis=0)
    grad_qv = jnp.concatenate([column_sums[:model_width], column_sums[2 * model_width :]])
    grad_qkv = times_left(first_low, grad_projected)
    grad_first = times_right(grad_projected, qkv_weight)
    grad_input_norm, grad_first_gain, grad_first_shift = first_pull(grad_first)
    grad_inputs = grad_middle + grad_input_norm
    grads = (
        grad_first_gain,
        grad_first_shift,
        grad_qkv,
        grad_qv,
        grad_out,
        grad_out_bias,
        grad_second_gain,
        grad_second_shift,
        grad_in,
        grad_in_bias,
        grad_down,
        grad_down_bias,
    )
    return (output.astype(jnp.bfloat16), grad_inputs.astype(jnp.bfloat16), grads)


RING = (0, 2, 4, 6, 7, 5, 3, 1)
RING_SIZE = len(RING)
CELLS = 2 * RING_SIZE
ANY = pl.BlockSpec(memory_space=pl.ANY)
HBM = pl.BlockSpec(memory_space=pltpu.HBM)
VMEM = pl.BlockSpec(memory_space=pltpu.VMEM)
SMEM = pl.BlockSpec(memory_space=pltpu.SMEM)
LOW = jnp.bfloat16
FULL = jnp.float32
COST = 10**10
ROWS = {
    "first_gain": 0,
    "first_shift": 1,
    "qv_bias": 2,
    "out_bias": 4,
    "second_gain": 5,
    "second_shift": 6,
    "in_bias": 7,
    "down_bias": 11,
    "lengths": 12,
}
NAMES = tuple(ROWS)[:8]
SMALL_ROWS = 16
SMALL_LANES = 256
PIECES = (2, 2, 2, 2, 2, 2, 2, 1, 1)


def ring_pairs():
    pairs = []
    for place in range(RING_SIZE):
        chip = RING[place]
        right = RING[(place + 1) % RING_SIZE]
        left = RING[(place - 1) % RING_SIZE]
        pairs.append((2 * chip, 2 * right))
        pairs.append((2 * chip + 1, 2 * left + 1))
    return pairs


def hop(block):
    return lax.ppermute(block, "cells", ring_pairs())


def to_partner(block):
    return lax.ppermute(block, "cells", [(i, i ^ 1) for i in range(CELLS)])


def across(block):
    return lax.ppermute(block, "species", [(0, 1), (1, 0)])


def exchange(values, bit):
    return values + lax.ppermute(values, "cells", [(i, i ^ bit) for i in range(CELLS)])


def after(value, *others):
    return lax.optimization_barrier((value,) + others)[0]


def here():
    index = lax.axis_index("cells")
    core = index % 2
    chip = index // 2
    place = jnp.int32(0)
    for i, ring_chip in enumerate(RING):
        place = jnp.where(chip == ring_chip, i, place)
    return index, core, place


def chip_at(place):
    place = place % RING_SIZE
    chip = jnp.zeros_like(place)
    for i, ring_chip in enumerate(RING):
        chip = jnp.where(place == i, ring_chip, chip)
    return chip


def gather_order(core, place):
    sign = 1 - 2 * core
    order = []

    def pair(at):
        order.append(2 * chip_at(at))
        order.append(2 * chip_at(at) + 1)

    pair(place)
    for step in range(1, 4):
        pair(place - sign * step)
        pair(place + sign * step)
    order.append(2 * chip_at(place + 4) + core)
    order.append(2 * chip_at(place + 4) + 1 - core)
    return order


def scatter_slots(core, place):
    def kept(core_now):
        sign = 1 - 2 * core_now
        order = [2 * chip_at(place + 4) + core_now]
        for step in (3, 2, 1):
            order.append(2 * chip_at(place + sign * step))
            order.append(2 * chip_at(place + sign * step) + 1)
        order.append(2 * chip_at(place) + core_now)
        return order

    order = kept(core) + kept(1 - core)
    slots = []
    for device in range(CELLS):
        slot = jnp.int32(0)
        for i, who in enumerate(order):
            slot = jnp.where(who == device, i, slot)
        slots.append(slot)
    return slots


def both_blocks(block, core):
    other = to_partner(block)
    return jnp.stack([jnp.where(core == 0, block, other), jnp.where(core == 0, other, block)])


def half_of(pair, core):
    return jnp.where(core == 0, pair[0], pair[1])[None]


def add_low(*parts):
    total = parts[0].astype(FULL)
    for part in parts[1:]:
        total = total + part.astype(FULL)
    return total.astype(LOW)


def first_hop(keep, got):
    return hop(add_low(keep[0:1], got[0:1]))


def second_hop(keep, got, moving, core):
    wide = jnp.stack([jnp.where(core == 0, moving[0], 0), jnp.where(core == 0, 0, moving[0])])
    return hop(add_low(keep[1:3], got[1:3], wide))


def later_hop(keep, got, moving, at):
    return hop(add_low(keep[at : at + 2], got[at : at + 2], moving))


def settle(keep, got, moving, core):
    mine = jnp.where(core == 0, moving[0], moving[1])
    other = jnp.where(core == 0, moving[1], moving[0])
    total = add_low(keep[7], got[7], mine, to_partner(other))
    return total, across(total)


def dot(left, right, dims=((1,), (0,))):
    return lax.dot_general(left, right, (dims, ((), ())), preferred_element_type=FULL)


def call(body, out_shape, ins, specs, out_specs=None, scratch=(), vmem=48):
    return pl.pallas_call(
        body,
        out_shape=out_shape,
        in_specs=specs,
        out_specs=[VMEM] * len(out_shape) if out_specs is None else out_specs,
        scratch_shapes=list(scratch),
        compiler_params=pltpu.CompilerParams(vmem_limit_bytes=vmem * 2**20),
        cost_estimate=pl.CostEstimate(flops=COST, bytes_accessed=0, transcendentals=0),
    )(*ins)


def shape(dims, kind=LOW):
    return jax.ShapeDtypeStruct(dims, kind)


def fetch(order_ref, refs, target, sem):
    rows = target.shape[0] // CELLS
    copies = []
    index = 0
    for source, size in zip(refs, PIECES):
        for part in range(size):
            at = order_ref[index]
            copies.append(
                pltpu.make_async_copy(
                    source.at[part],
                    target.at[pl.ds(pl.multiple_of(at * rows, 16), rows)],
                    sem.at[index],
                )
            )
            index += 1
    for item in copies:
        item.start()
    return copies


def wait_all(copies):
    for item in copies:
        item.wait()


def one_hot(rows, lanes, offset):
    row = lax.broadcasted_iota(jnp.int32, (rows, lanes), 0)
    lane = lax.broadcasted_iota(jnp.int32, (rows, lanes), 1)
    return lane == row + offset


def pack_body(who_ref, lengths_ref, *refs):
    sources, small_ref = refs[:8], refs[8]
    me = who_ref[0]
    model = small_ref.shape[1]
    row = lax.broadcasted_iota(jnp.int32, (SMALL_ROWS, model), 0)
    lane = lax.broadcasted_iota(jnp.int32, (SMALL_ROWS, model), 1)
    small = jnp.zeros((SMALL_ROWS, model), FULL)
    for name, ref in zip(NAMES, sources):
        size = ref.shape[1]
        per_row = model // size
        placed = dot(ref[...], one_hot(size, model, size * (me % per_row)).astype(LOW))
        small = small + jnp.where(row == ROWS[name] + me // per_row, placed, 0.0)
    for i in range(2):
        at = (row == ROWS["lengths"]) & (lane == 2 * me + i)
        small = small + jnp.where(at, lengths_ref[i].astype(FULL), 0.0)
    small_ref[...] = small.astype(LOW)


def norm_parts(values):
    center = values - jnp.mean(values, axis=-1, keepdims=True)
    spread = jnp.mean(center * center, axis=-1, keepdims=True)
    return center, lax.rsqrt(spread + EPSILON)


def norm_back(center, scale, gain, grad):
    weighted = grad * gain
    mean_one = jnp.mean(weighted, axis=-1, keepdims=True)
    mean_two = jnp.mean(weighted * center, axis=-1, keepdims=True)
    back = scale * (weighted - mean_one - center * (scale * scale * mean_two))
    return back, jnp.sum(grad * center * scale, axis=0, keepdims=True), jnp.sum(
        grad, axis=0, keepdims=True
    )


def small_row(small_ref, name, count=1):
    return small_ref[...].astype(FULL)[ROWS[name] : ROWS[name] + count, :]


def project_body(order_ref, x_ref, small_ref, *refs):
    blocks = refs[:9]
    low_ref, proj_ref, weight, sem = refs[9:]
    model = x_ref.shape[1]
    copies = fetch(order_ref, blocks, weight, sem)
    center, scale = norm_parts(x_ref[...].astype(FULL))
    bias = small_row(small_ref, "qv_bias", 2)
    low_ref[...] = (
        center * scale * small_row(small_ref, "first_gain") + small_row(small_ref, "first_shift")
    ).astype(LOW)
    wait_all(copies)
    for j in range(3):
        lanes = slice(j * model, (j + 1) * model)
        part = dot(low_ref[...], weight[:, lanes])
        if j != 1:
            part = part + bias[j // 2 : j // 2 + 1]
        proj_ref[:, lanes] = part.astype(LOW)


def attend_body(seq, lengths_ref, proj_ref, att_ref, mixed_ref):
    model = mixed_ref.shape[1]
    cells = mixed_ref.shape[0] // seq
    pairs = model // (2 * HEAD)
    lane = lax.broadcasted_iota(jnp.int32, (seq, 2 * HEAD), 1)
    key = lax.broadcasted_iota(jnp.int32, (seq, seq), 0)

    def step(index, carry):
        s = index // pairs
        p = index % pairs
        rows = pl.ds(pl.multiple_of(s * seq, seq), seq)
        at = pl.multiple_of(p * 2 * HEAD, 2 * HEAD)
        q = proj_ref[rows, pl.ds(at, 2 * HEAD)] * jnp.asarray(HEAD ** (-0.5), LOW)
        k = proj_ref[rows, pl.ds(at + model, 2 * HEAD)]
        v_turned = proj_ref[rows, pl.ds(at + 2 * model, 2 * HEAD)].T
        visible = key < lengths_ref[s]
        mixed = []
        for i in range(2):
            own = (lane >= i * HEAD) & (lane < (i + 1) * HEAD)
            scores = dot(jnp.where(own, k, jnp.zeros_like(k)), q, ((1,), (1,)))
            scores = jnp.where(visible, scores, NEGATIVE)
            expo = jnp.exp(scores - jnp.max(scores, axis=0, keepdims=True))
            probs = expo * (1.0 / jnp.sum(expo, axis=0, keepdims=True))
            probs = probs.astype(LOW)
            att_ref[2 * index + i] = probs
            mixed.append(dot(v_turned[i * HEAD : (i + 1) * HEAD], probs))
        mixed_ref[rows, pl.ds(at, 2 * HEAD)] = jnp.concatenate(mixed, axis=0).T.astype(LOW)
        return carry

    lax.fori_loop(0, cells * pairs, step, 0, unroll=2)


ERFC_STEP = 0.33
ERFC = (
    0.1863578228018033,
    0.18295566386742124,
    0.2012255082472392,
    0.04721561458875723,
    0.4085089979423051,
    -0.35115900736338407,
    0.4602422572120205,
    -0.13534686486277223,
)


def gelu_parts(inner):
    z = jnp.abs(inner) * (0.5**0.5)
    t = 1.0 / (1.0 + ERFC_STEP * z)
    tail = jnp.full_like(t, 0.5 * ERFC[-1])
    for factor in ERFC[-2::-1]:
        tail = tail * t + 0.5 * factor
    bell = jnp.exp(-(z * z))
    tail = tail * t * bell
    area = jnp.where(inner < 0.0, tail, 1.0 - tail)
    return inner * area, area + inner * bell * (0.5 / 3.141592653589793) ** 0.5


def row_mask(lengths_ref, rows, seq):
    at = lax.broadcasted_iota(jnp.int32, (rows, 1), 0)
    true = (at < lengths_ref[0]).astype(FULL)
    for s in range(1, rows // seq):
        true = jnp.where(at < s * seq, true, (at < lengths_ref[s] + s * seq).astype(FULL))
    return true


def loss_rows(lengths_ref, small_ref, other_ref, cot_ref, seq, whole):
    count = jnp.sum(
        small_row(small_ref, "lengths") + small_row(other_ref, "lengths"), axis=-1, keepdims=True
    )
    return cot_ref[...].astype(FULL) * (
        row_mask(lengths_ref, cot_ref.shape[0], seq) * (whole / count)
    )


def put_slots(keep_buf, slot_ref, values, first, lanes):
    rows = keep_buf.shape[1]
    for i in range(values.shape[0] // rows):
        keep_buf[slot_ref[first + i], :, lanes] = values[i * rows : (i + 1) * rows].astype(LOW)


def send_slots(buf, keep_ref, away_ref, sem):
    half = RING_SIZE
    copies = [
        pltpu.make_async_copy(buf.at[pl.ds(half, half)], away_ref, sem.at[0]),
        pltpu.make_async_copy(buf.at[pl.ds(0, half)], keep_ref, sem.at[1]),
    ]
    for item in copies:
        item.start()
    return copies


def inner_body(order_ref, x_ref, mixed_ref, small_ref, *refs):
    blocks = refs[:9]
    middle_ref, low_ref, active_ref, slope_ref, weight, sem = refs[9:]
    model = x_ref.shape[1]
    ff = active_ref.shape[1]
    wait_all(fetch(order_ref, blocks, weight, sem))
    middle = (
        x_ref[...].astype(FULL)
        + dot(mixed_ref[...], weight[:, ff:])
        + small_row(small_ref, "out_bias")
    )
    middle_ref[...] = middle
    center, scale = norm_parts(middle)
    low = center * scale * small_row(small_ref, "second_gain") + small_row(
        small_ref, "second_shift"
    )
    low_ref[...] = low.astype(LOW)
    step = 2 * (ff // RING_SIZE)
    bias = small_row(small_ref, "in_bias", 4)
    for j in range(ff // step):
        lanes = slice(j * step, (j + 1) * step)
        inner = dot(low_ref[...], weight[:, lanes]) + bias[j : j + 1]
        active, slope = gelu_parts(inner)
        active_ref[:, lanes] = active.astype(LOW)
        slope_ref[:, lanes] = slope.astype(LOW)


def grad_down_body(
    seq, whole, slot_ref, lengths_ref, active_ref, cot_ref, small_ref, other_ref, up_ref,
    down_b_ref, keep_ref, away_ref, slots, sem,
):
    up_low = loss_rows(lengths_ref, small_ref, other_ref, cot_ref, seq, whole).astype(LOW)
    up_ref[...] = up_low
    down_b_ref[...] = jnp.sum(up_low.astype(FULL), axis=0, keepdims=True)
    parts = RING_SIZE
    step = active_ref.shape[1] // parts
    for j in range(parts):
        grad = dot(active_ref[:, j * step : (j + 1) * step], up_ref[...], ((0,), (0,)))
        put_slots(slots, slot_ref, grad, j * CELLS // parts, slice(None))
    wait_all(send_slots(slots, keep_ref, away_ref, sem))


def inner_back_body(order_ref, slope_ref, up_ref, *refs):
    blocks = refs[:9]
    inner_ref, in_b_ref, weight, sem = refs[9:]
    model = up_ref.shape[1]
    wait_all(fetch(order_ref, blocks, weight, sem))
    for j in range(inner_ref.shape[1] // model):
        lanes = slice(j * model, (j + 1) * model)
        grad = dot(up_ref[...], weight[lanes, :], ((1,), (1,)))
        low = (grad * slope_ref[:, lanes].astype(FULL)).astype(LOW)
        inner_ref[:, lanes] = low
        in_b_ref[j : j + 1, :] = jnp.sum(low.astype(FULL), axis=0, keepdims=True)


def down_body(active_ref, middle_ref, small_ref, weight_ref, out_ref):
    out_ref[...] = (
        middle_ref[...]
        + dot(active_ref[...], weight_ref[...])
        + small_row(small_ref, "down_bias")
    ).astype(LOW)


def grad_in_body(slot_ref, low_ref, inner_ref, keep_ref, away_ref, slots, sem):
    model = low_ref.shape[1]
    turned = low_ref[...].T
    for j in range(inner_ref.shape[1] // model):
        lanes = slice(j * model, (j + 1) * model)
        put_slots(slots, slot_ref, dot(turned, inner_ref[:, lanes]), 0, lanes)
    wait_all(send_slots(slots, keep_ref, away_ref, sem))


def middle_back_body(
    seq, whole, lengths_ref, inner_ref, middle_ref, cot_ref, small_ref, other_ref, weight,
    grad_ref, grad_low_ref, grad_mixed_ref, sums_ref,
):
    ff = inner_ref.shape[1]
    grad_second = dot(inner_ref[...], weight[:, :ff], ((1,), (1,)))
    center, scale = norm_parts(middle_ref[...])
    back, gain_sum, shift_sum = norm_back(
        center, scale, small_row(small_ref, "second_gain"), grad_second
    )
    grad = loss_rows(lengths_ref, small_ref, other_ref, cot_ref, seq, whole) + back
    grad_ref[...] = grad
    grad_low = grad.astype(LOW)
    grad_low_ref[...] = grad_low
    grad_mixed_ref[...] = dot(grad_low, weight[:, ff:], ((1,), (1,))).astype(LOW)
    sums_ref[0:1, :] = jnp.sum(grad_low.astype(FULL), axis=0, keepdims=True)
    sums_ref[1:2, :] = gain_sum
    sums_ref[2:3, :] = shift_sum


def attend_back_body(seq, begin, proj_ref, att_ref, grad_ref, out_ref):
    model = grad_ref.shape[1]
    half = out_ref.shape[1] // 3
    all_pairs = model // (2 * HEAD)
    pairs = half // (2 * HEAD)
    cells = grad_ref.shape[0] // seq
    lane = lax.broadcasted_iota(jnp.int32, (seq, 2 * HEAD), 1)
    scale = HEAD ** (-0.5)

    def step(index, carry):
        s = index // pairs
        p = index % pairs
        rows = pl.ds(pl.multiple_of(s * seq, seq), seq)
        to = pl.multiple_of(p * 2 * HEAD, 2 * HEAD)
        at = pl.multiple_of(to + begin * 2 * HEAD, 2 * HEAD)
        q = proj_ref[rows, pl.ds(at, 2 * HEAD)]
        k_turned = proj_ref[rows, pl.ds(at + model, 2 * HEAD)].T
        v = proj_ref[rows, pl.ds(at + 2 * model, 2 * HEAD)]
        g = grad_ref[rows, pl.ds(at, 2 * HEAD)]
        grad_q = []
        grad_k = []
        grad_v = []
        for i in range(2):
            own = (lane >= i * HEAD) & (lane < (i + 1) * HEAD)
            probs = att_ref[2 * (s * all_pairs + begin + p) + i]
            wide = probs.astype(FULL)
            grad_probs = dot(jnp.where(own, v, jnp.zeros_like(v)), g, ((1,), (1,)))
            delta = jnp.sum(wide * grad_probs, axis=0, keepdims=True)
            scores = (wide * (grad_probs - delta)).astype(LOW)
            grad_q.append(dot(k_turned[i * HEAD : (i + 1) * HEAD], scores))
            grad_k.append(dot(scores, q))
            grad_v.append(dot(probs, g))
        first = lane < HEAD
        out_ref[rows, pl.ds(to, 2 * HEAD)] = (
            jnp.concatenate(grad_q, axis=0).T * scale
        ).astype(LOW)
        out_ref[rows, pl.ds(to + half, 2 * HEAD)] = (
            jnp.where(first, grad_k[0], grad_k[1]) * scale
        ).astype(LOW)
        out_ref[rows, pl.ds(to + 2 * half, 2 * HEAD)] = jnp.where(
            first, grad_v[0], grad_v[1]
        ).astype(LOW)
        return carry

    lax.fori_loop(0, cells * pairs, step, 0, unroll=2)


def early_grad_body(
    slot_ref, low_ref, part_ref, mixed_ref, grad_low_ref, keep_ref, away_ref, slots, sem
):
    width = part_ref.shape[1]
    put_slots(slots, slot_ref, dot(low_ref[...].T, part_ref[...]), 0, slice(0, width))
    put_slots(
        slots, slot_ref, dot(mixed_ref[...].T, grad_low_ref[...]), 0,
        slice(width, slots.shape[2]),
    )
    wait_all(send_slots(slots, keep_ref, away_ref, sem))


def first_back_body(
    slot_ref, x_ref, low_ref, one_ref, two_ref, grad_ref, small_ref, sums_ref, in_b_ref,
    down_b_ref, weight, out_ref, keep_ref, away_ref, sum_ref, slots, sem,
):
    model = x_ref.shape[1]
    late = two_ref.shape[1]
    center, scale = norm_parts(x_ref[...].astype(FULL))
    parts = ((one_ref, 0), (two_ref, one_ref.shape[1] // 3))
    grad_first = jnp.zeros(x_ref.shape, FULL)
    for j in range(3):
        for ref, begin in parts:
            width = ref.shape[1] // 3
            at = j * model + begin
            grad_first = grad_first + dot(
                ref[:, j * width : (j + 1) * width], weight[:, at : at + width], ((1,), (1,))
            )
    put_slots(slots, slot_ref, dot(low_ref[...].T, two_ref[...]), 0, slice(0, late))
    back, gain_sum, shift_sum = norm_back(
        center, scale, small_row(small_ref, "first_gain"), grad_first
    )

    def put(name, value, offset=0):
        at = ROWS[name] + offset
        sum_ref[at : at + value.shape[0], :] = value

    sum_ref[...] = jnp.zeros_like(sum_ref)
    put("first_gain", gain_sum)
    put("first_shift", shift_sum)
    for j in range(2):
        at = ROWS["qv_bias"] + j
        for ref, begin in parts:
            width = ref.shape[1] // 3
            part = ref[:, 2 * j * width : (2 * j + 1) * width].astype(FULL)
            sum_ref[at : at + 1, begin : begin + width] = jnp.sum(part, axis=0, keepdims=True)
    put("out_bias", sums_ref[0:1, :])
    put("second_gain", sums_ref[1:2, :])
    put("second_shift", sums_ref[2:3, :])
    put("in_bias", in_b_ref[...])
    put("down_bias", down_b_ref[...])
    for i in range(3):
        part = sum_ref[:, SMALL_LANES * i : SMALL_LANES * (i + 1)].astype(LOW)
        for device in range(CELLS):
            slots[device, 16 * i : 16 * i + 16, late:] = part
    copies = send_slots(slots, keep_ref, away_ref, sem)
    out_ref[...] = (grad_ref[...] + back).astype(LOW)
    wait_all(copies)


def finish_body(who_ref, early_ref, early_two_ref, late_ref, late_two_ref, *refs):
    grad_ref, out_ref, vectors, small_ref = refs[0], refs[1], refs[2:-1], refs[-1]
    model = out_ref.shape[1]
    early = early_ref[...].astype(FULL) + early_two_ref[...].astype(FULL)
    late = late_ref[...].astype(FULL) + late_two_ref[...].astype(FULL)
    one = (early.shape[1] - model) // 3
    two = (late.shape[1] - SMALL_LANES) // 3
    for j in range(3):
        at = j * model
        grad_ref[:, at : at + one] = early[:, j * one : (j + 1) * one]
        grad_ref[:, at + one : at + model] = late[:, j * two : (j + 1) * two]
    out_ref[...] = early[:, 3 * one :]
    for i in range(3):
        small_ref[:, SMALL_LANES * i : SMALL_LANES * (i + 1)] = late[
            16 * i : 16 * i + 16, 3 * two :
        ]
    me = who_ref[0]
    row = lax.broadcasted_iota(jnp.int32, (SMALL_ROWS, model), 0)
    for name, ref in zip(NAMES, vectors):
        size = ref.shape[1]
        per_row = model // size
        here_row = jnp.where(row == ROWS[name] + me // per_row, small_ref[...], 0.0)
        values = jnp.sum(here_row, axis=0, keepdims=True)
        picker = one_hot(size, model, size * (me % per_row)).astype(FULL)
        ref[...] = lax.dot_general(
            values, picker, (((1,), (1,)), ((), ())), precision=lax.Precision.HIGHEST,
            preferred_element_type=FULL,
        )


def on_device_ring(
    tokens,
    lengths,
    cotangent,
    first_gain,
    first_shift,
    qkv_weight,
    qv_bias,
    out_weight,
    out_bias,
    second_gain,
    second_shift,
    in_weight,
    in_bias,
    down_weight,
    down_bias,
):
    micro, seq, model = tokens.shape[1:]
    total_rows = micro * seq
    rows = qkv_weight.shape[0]
    down_rows = down_weight.shape[0]
    ff = in_weight.shape[1]
    heads = model // HEAD
    whole = float(lax.axis_size("species") * CELLS * micro * seq)
    index, core, place = here()
    who = jnp.stack([index]).astype(jnp.int32)
    order = jnp.stack(gather_order(core, place)).astype(jnp.int32)
    slot = jnp.stack(scatter_slots(core, place)).astype(jnp.int32)
    lens = lengths.reshape(micro)
    x = tokens.reshape(total_rows, model)
    cot = cotangent.reshape(total_rows, model)
    vectors = (
        first_gain, first_shift, qv_bias, out_bias, second_gain, second_shift, in_bias, down_bias,
    )

    dma = pltpu.SemaphoreType.DMA

    def gathered(own, hops):
        got = [own]
        for item in hops:
            got += [item, to_partner(item)]
        return got

    own = both_blocks(qkv_weight, core)
    qkv_one = hop(own)
    (small,) = call(
        pack_body,
        [shape((SMALL_ROWS, model))],
        [who, after(lens, own)] + [item.reshape(1, -1) for item in vectors],
        [SMEM, SMEM] + [VMEM] * 8,
        vmem=4,
    )
    small = exchange(small, 1)
    in_weight, out_weight = lax.optimization_barrier((in_weight, out_weight, own))[:2]
    in_own = both_blocks(jnp.concatenate([in_weight, out_weight], axis=1), core)
    qkv_one, small, in_own = lax.optimization_barrier((qkv_one, small, in_own))
    qkv_two = hop(qkv_one)
    small = exchange(small, 2)
    down_own = both_blocks(after(down_weight, qkv_one), core)
    qkv_two, small, down_own = lax.optimization_barrier((qkv_two, small, down_own))
    qkv_three = hop(qkv_two)
    small = exchange(small, 4)
    qkv_three, small = lax.optimization_barrier((qkv_three, small))
    qkv_last = hop(half_of(qkv_three, core))
    in_one = hop(after(in_own, qkv_three))
    small = exchange(small, 8)
    low, proj, qkv_full = call(
        project_body,
        [
            shape((total_rows, model)),
            shape((total_rows, 3 * model)),
            shape((model, 3 * model)),
        ],
        [order, x, small] + gathered(own, (qkv_one, qkv_two, qkv_three, qkv_last)),
        [SMEM, VMEM, VMEM] + [ANY] * 9,
        scratch=[dma((CELLS,))],
        vmem=20,
    )
    other_small = across(small)
    in_one, proj = lax.optimization_barrier((in_one, proj))
    in_two = hop(in_one)
    down_one = hop(after(down_own, in_one))
    att, mixed = call(
        lambda *refs: attend_body(seq, *refs),
        [shape((micro * heads, seq, seq)), shape((total_rows, model))],
        [lens, proj],
        [SMEM, VMEM],
        vmem=16,
    )
    in_two, mixed = lax.optimization_barrier((in_two, mixed))
    in_three = hop(in_two)
    down_two = hop(after(down_one, in_two))
    in_last = hop(half_of(in_three, core))
    down_three = hop(after(down_two, in_three))
    in_got = gathered(in_own, (in_one, in_two, in_three, in_last))
    middle, low_two, active, slope, in_full = call(
        inner_body,
        [
            shape((total_rows, model), FULL),
            shape((total_rows, model)),
            shape((total_rows, ff)),
            shape((total_rows, ff)),
            shape((model, ff + model)),
        ],
        [order, x, after(mixed, down_two), small] + in_got,
        [SMEM] + [VMEM] * 3 + [ANY] * 9,
        scratch=[dma((CELLS,))],
        vmem=24,
    )
    down_three, active = lax.optimization_barrier((down_three, active))
    down_last = hop(half_of(down_three, core))
    up_low, down_b, down_keep, down_away = call(
        lambda *refs: grad_down_body(seq, whole, *refs),
        [
            shape((total_rows, model)),
            shape((1, model), FULL),
            shape((RING_SIZE, down_rows, model)),
            shape((RING_SIZE, down_rows, model)),
        ],
        [slot, lens, active, cot, small, other_small],
        [SMEM] * 2 + [VMEM] * 4,
        [VMEM] * 2 + [ANY] * 2,
        scratch=[pltpu.VMEM((CELLS, down_rows, model), LOW), dma((2,))],
        vmem=18,
    )

    down_other = to_partner(down_away)
    inner_low, in_b, down_full = call(
        inner_back_body,
        [
            shape((total_rows, ff)),
            shape((ff // model, model), FULL),
            shape((ff, model)),
        ],
        [order, slope, up_low]
        + gathered(down_own, (down_one, down_two, down_three, down_last)),
        [SMEM] + [VMEM] * 2 + [ANY] * 9,
        scratch=[dma((CELLS,))],
        vmem=20,
    )
    down_other, inner_low = lax.optimization_barrier((down_other, inner_low))
    down_sum = first_hop(down_keep, down_other)
    in_keep, in_away = call(
        grad_in_body,
        [shape((RING_SIZE, rows, ff)), shape((RING_SIZE, rows, ff))],
        [slot, low_two, inner_low],
        [SMEM] + [VMEM] * 2,
        [ANY] * 2,
        scratch=[pltpu.VMEM((CELLS, rows, ff), LOW), dma((2,))],
        vmem=16,
    )
    in_other = to_partner(in_away)
    (out_tokens,) = call(
        down_body,
        [shape((total_rows, model))],
        [after(active, in_keep), middle, small, down_full],
        [VMEM] * 4,
        vmem=14,
    )
    down_sum, in_other, out_tokens, inner_low = lax.optimization_barrier(
        (down_sum, in_other, out_tokens, inner_low)
    )
    down_sum = second_hop(down_keep, down_other, down_sum, core)
    in_sum = first_hop(in_keep, in_other)
    grad_middle, grad_low, grad_mixed, sums = call(
        lambda *refs: middle_back_body(seq, whole, *refs),
        [
            shape((total_rows, model), FULL),
            shape((total_rows, model)),
            shape((total_rows, model)),
            shape((3, model), FULL),
        ],
        [lens, inner_low, middle, cot, small, other_small, in_full],
        [SMEM] + [VMEM] * 6,
        vmem=24,
    )

    def attend_back(begin, pairs, grad):
        return call(
            lambda *refs: attend_back_body(seq, begin, *refs),
            [shape((total_rows, 6 * pairs * HEAD))],
            [proj, att, grad],
            [VMEM] * 3,
            vmem=14,
        )[0]

    pairs = model // (2 * HEAD)
    early_pairs = 2 * pairs // 3
    down_sum, grad_mixed = lax.optimization_barrier((down_sum, grad_mixed))
    down_sum = later_hop(down_keep, down_other, down_sum, 3)
    grad_one = attend_back(0, early_pairs, grad_mixed)
    in_sum, grad_one = lax.optimization_barrier((in_sum, grad_one))
    in_sum = second_hop(in_keep, in_other, in_sum, core)
    early_width = 6 * early_pairs * HEAD + model
    early_keep, early_away = call(
        early_grad_body,
        [shape((RING_SIZE, rows, early_width))] * 2,
        [slot, low, grad_one, mixed, grad_low],
        [SMEM] + [VMEM] * 4,
        [ANY] * 2,
        scratch=[pltpu.VMEM((CELLS, rows, early_width), LOW), dma((2,))],
        vmem=14,
    )
    early_other = to_partner(early_away)
    grad_two = attend_back(early_pairs, pairs - early_pairs, after(grad_mixed, early_keep))
    down_sum, early_other, grad_two = lax.optimization_barrier(
        (down_sum, early_other, grad_two)
    )
    down_sum = later_hop(down_keep, down_other, down_sum, 5)
    late_width = 6 * (pairs - early_pairs) * HEAD + SMALL_LANES
    grad_tokens, late_keep, late_away = call(
        first_back_body,
        [
            shape((total_rows, model)),
            shape((RING_SIZE, rows, late_width)),
            shape((RING_SIZE, rows, late_width)),
        ],
        [slot, x, low, grad_one, grad_two, grad_middle, small, sums, in_b, down_b, qkv_full],
        [SMEM] + [VMEM] * 10,
        [VMEM] + [ANY] * 2,
        scratch=[
            pltpu.VMEM((SMALL_ROWS, model), FULL),
            pltpu.VMEM((CELLS, rows, late_width), LOW),
            dma((2,)),
        ],
        vmem=20,
    )
    late_other = to_partner(late_away)
    in_sum, early_other, late_keep, down_sum = lax.optimization_barrier(
        (in_sum, early_other, late_keep, down_sum)
    )
    in_sum = later_hop(in_keep, in_other, in_sum, 3)
    early_sum = first_hop(early_keep, early_other)
    down_terms = settle(down_keep, down_other, down_sum, core)
    early_sum = second_hop(early_keep, early_other, early_sum, core)
    in_sum = later_hop(in_keep, in_other, in_sum, 5)
    late_sum = first_hop(late_keep, late_other)
    early_sum = later_hop(early_keep, early_other, early_sum, 3)
    late_sum = second_hop(late_keep, late_other, late_sum, core)
    in_terms = settle(in_keep, in_other, in_sum, core)
    early_sum = later_hop(early_keep, early_other, early_sum, 5)
    late_sum = later_hop(late_keep, late_other, late_sum, 3)
    early_terms = settle(early_keep, early_other, early_sum, core)
    late_sum = later_hop(late_keep, late_other, late_sum, 5)
    late_terms = settle(late_keep, late_other, late_sum, core)
    finished = call(
        finish_body,
        [shape((rows, 3 * model), FULL), shape((rows, model), FULL)]
        + [shape((1, item.shape[0]), FULL) for item in vectors],
        [who] + list(early_terms) + list(late_terms),
        [SMEM] + [VMEM] * 4,
        scratch=[pltpu.VMEM((SMALL_ROWS, model), FULL)],
        vmem=6,
    )
    grad_qkv, grad_out = finished[:2]
    pieces = [item.reshape(-1) for item in finished[2:]]
    return (
        out_tokens.reshape(tokens.shape),
        grad_tokens.reshape(tokens.shape),
        pieces[0],
        pieces[1],
        grad_qkv,
        pieces[2],
        grad_out,
        pieces[3],
        pieces[4],
        pieces[5],
        in_terms[0].astype(FULL) + in_terms[1].astype(FULL),
        pieces[6],
        down_terms[0].astype(FULL) + down_terms[1].astype(FULL),
        pieces[7],
    )


def on_device(
    tokens,
    lengths,
    cotangent,
    first_gain,
    first_shift,
    qkv_weight,
    qv_bias,
    out_weight,
    out_bias,
    second_gain,
    second_shift,
    in_weight,
    in_bias,
    down_weight,
    down_bias,
):
    local_count = jnp.sum(lengths).astype(jnp.float32)
    count = lax.psum(local_count, ("species", "cells"))
    micro_count = tokens.shape[1]
    seq_rows = tokens.shape[2]
    factor = (
        float(lax.axis_size("species") * lax.axis_size("cells") * micro_count * seq_rows) / count
    )
    output_rows = []
    gradient_rows = []
    summed = None
    for micro_step in range(micro_count):
        gathered = (
            lax.all_gather(first_gain, "cells", axis=0, tiled=True),
            lax.all_gather(first_shift, "cells", axis=0, tiled=True),
            lax.all_gather(qkv_weight, "cells", axis=0, tiled=True),
            lax.all_gather(qv_bias, "cells", axis=0, tiled=True),
            lax.all_gather(out_weight, "cells", axis=0, tiled=True),
            lax.all_gather(out_bias, "cells", axis=0, tiled=True),
            lax.all_gather(second_gain, "cells", axis=0, tiled=True),
            lax.all_gather(second_shift, "cells", axis=0, tiled=True),
            lax.all_gather(in_weight, "cells", axis=0, tiled=True),
            lax.all_gather(in_bias, "cells", axis=0, tiled=True),
            lax.all_gather(down_weight, "cells", axis=0, tiled=True),
            lax.all_gather(down_bias, "cells", axis=0, tiled=True),
        )
        out_seq, grad_seq, grads = sequence_pass(
            gathered,
            tokens[0, micro_step],
            lengths[0, micro_step],
            cotangent[0, micro_step],
            factor,
        )
        output_rows.append(out_seq)
        gradient_rows.append(grad_seq)
        shares = (
            lax.psum_scatter(grads[0], "cells", scatter_dimension=0, tiled=True),
            lax.psum_scatter(grads[1], "cells", scatter_dimension=0, tiled=True),
            lax.psum_scatter(grads[2], "cells", scatter_dimension=0, tiled=True),
            lax.psum_scatter(grads[3], "cells", scatter_dimension=0, tiled=True),
            lax.psum_scatter(grads[4], "cells", scatter_dimension=0, tiled=True),
            lax.psum_scatter(grads[5], "cells", scatter_dimension=0, tiled=True),
            lax.psum_scatter(grads[6], "cells", scatter_dimension=0, tiled=True),
            lax.psum_scatter(grads[7], "cells", scatter_dimension=0, tiled=True),
            lax.psum_scatter(grads[8], "cells", scatter_dimension=0, tiled=True),
            lax.psum_scatter(grads[9], "cells", scatter_dimension=0, tiled=True),
            lax.psum_scatter(grads[10], "cells", scatter_dimension=0, tiled=True),
            lax.psum_scatter(grads[11], "cells", scatter_dimension=0, tiled=True),
        )
        summed = shares if summed is None else jax.tree.map(jnp.add, summed, shares)
    final = (
        lax.psum(summed[0].astype(jnp.bfloat16), "species").astype(jnp.float32),
        lax.psum(summed[1].astype(jnp.bfloat16), "species").astype(jnp.float32),
        lax.psum(summed[2].astype(jnp.bfloat16), "species").astype(jnp.float32),
        lax.psum(summed[3].astype(jnp.bfloat16), "species").astype(jnp.float32),
        lax.psum(summed[4].astype(jnp.bfloat16), "species").astype(jnp.float32),
        lax.psum(summed[5].astype(jnp.bfloat16), "species").astype(jnp.float32),
        lax.psum(summed[6].astype(jnp.bfloat16), "species").astype(jnp.float32),
        lax.psum(summed[7].astype(jnp.bfloat16), "species").astype(jnp.float32),
        lax.psum(summed[8].astype(jnp.bfloat16), "species").astype(jnp.float32),
        lax.psum(summed[9].astype(jnp.bfloat16), "species").astype(jnp.float32),
        lax.psum(summed[10].astype(jnp.bfloat16), "species").astype(jnp.float32),
        lax.psum(summed[11].astype(jnp.bfloat16), "species").astype(jnp.float32),
    )
    out_tokens = jnp.stack(output_rows)[None]
    grad_tokens = jnp.stack(gradient_rows)[None]
    return (out_tokens, grad_tokens) + tuple(final)


def solution(mesh):
    in_specs = (
        P("species", "cells", None, None),
        P("species", "cells"),
        P("species", "cells", None, None),
        P("cells"),
        P("cells"),
        P("cells", None),
        P("cells"),
        P("cells", None),
        P("cells"),
        P("cells"),
        P("cells"),
        P("cells", None),
        P("cells"),
        P("cells", None),
        P("cells"),
    )
    out_specs = (
        P("species", "cells", None, None),
        P("species", "cells", None, None),
        P("cells"),
        P("cells"),
        P("cells", None),
        P("cells"),
        P("cells", None),
        P("cells"),
        P("cells"),
        P("cells"),
        P("cells", None),
        P("cells"),
        P("cells", None),
        P("cells"),
    )
    program = on_device_ring if mesh.shape["cells"] == 2 * RING_SIZE else on_device
    return jax.shard_map(
        program, mesh=mesh, in_specs=in_specs, out_specs=out_specs, check_vma=False
    )
```

```python
import jax
import jax.numpy as jnp
from jax import lax
from jax.experimental import pallas as pl
from jax.experimental.pallas import tpu as pltpu
from jax.sharding import PartitionSpec as P

HEAD = 64


EPSILON = 1e-12
NEGATIVE = -1e30


def normalize(values, gain_vec, shift_vec):
    center = values - jnp.mean(values, axis=-1, keepdims=True)
    spread = jnp.mean(center * center, axis=-1, keepdims=True)
    return center * lax.rsqrt(spread + EPSILON) * gain_vec + shift_vec


def smooth_gate(values):
    return jax.nn.gelu(values, approximate=False)


def times_left(left_side, right_side):
    return lax.dot_general(
        left_side, right_side, (((0,), (0,)), ((), ())), preferred_element_type=jnp.float32
    )


def times_right(left_side, right_side):
    return lax.dot_general(
        left_side, right_side, (((1,), (1,)), ((), ())), preferred_element_type=jnp.float32
    )


def sequence_pass(weights, inputs, length, cot_rows, factor):
    (
        first_gain,
        first_shift,
        qkv_weight,
        qv_bias,
        out_weight,
        out_bias,
        second_gain,
        second_shift,
        in_weight,
        in_bias,
        down_weight,
        down_bias,
    ) = weights
    seq_rows = inputs.shape[0]
    model_width = inputs.shape[1]
    heads_count = model_width // HEAD
    scale_qk = float(HEAD) ** (-0.5)
    as_float = inputs.astype(jnp.float32)
    hidden_one, first_pull = jax.vjp(
        normalize, as_float, first_gain.astype(jnp.float32), first_shift.astype(jnp.float32)
    )
    first_low = hidden_one.astype(jnp.bfloat16)
    bias_float = qv_bias.astype(jnp.float32)
    full_bias = jnp.concatenate(
        [bias_float[:model_width], jnp.zeros((model_width,), jnp.float32), bias_float[model_width:]]
    )
    projected = (
        jnp.dot(first_low, qkv_weight, preferred_element_type=jnp.float32) + full_bias
    ).astype(jnp.bfloat16)
    split_heads = projected.reshape(seq_rows, 3, heads_count, HEAD)
    queries = split_heads[:, 0]
    keys_part = split_heads[:, 1]
    values_part = split_heads[:, 2]
    visible = jnp.arange(seq_rows) < length

    def scores_of():
        raw_scores = (
            jnp.einsum("qhd,khd->hqk", queries, keys_part, preferred_element_type=jnp.float32)
            * scale_qk
        )
        return jnp.where(visible[None, None, :], raw_scores, NEGATIVE)

    scores = scores_of()
    top_score = jnp.max(scores, axis=-1, keepdims=True)
    expo = jnp.exp(scores - top_score)
    total_exp = jnp.sum(expo, axis=-1, keepdims=True)
    log_total = top_score + jnp.log(total_exp)
    attention = (expo / total_exp).astype(jnp.bfloat16)
    mixed = jnp.einsum("hqk,khd->qhd", attention, values_part, preferred_element_type=jnp.float32)
    mixed = mixed.reshape(seq_rows, model_width).astype(jnp.bfloat16)
    middle = (
        as_float
        + jnp.dot(mixed, out_weight, preferred_element_type=jnp.float32)
        + out_bias.astype(jnp.float32)
    )
    hidden_two, second_pull = jax.vjp(
        normalize, middle, second_gain.astype(jnp.float32), second_shift.astype(jnp.float32)
    )
    second_low = hidden_two.astype(jnp.bfloat16)
    inner = jnp.dot(second_low, in_weight, preferred_element_type=jnp.float32) + in_bias.astype(
        jnp.float32
    )
    active, gate_pull = jax.vjp(smooth_gate, inner)
    active_low = active.astype(jnp.bfloat16)
    output = (
        middle
        + jnp.dot(active_low, down_weight, preferred_element_type=jnp.float32)
        + down_bias.astype(jnp.float32)
    )
    upstream = cot_rows.astype(jnp.float32) * visible[:, None].astype(jnp.float32) * factor
    up_low = upstream.astype(jnp.bfloat16)
    grad_down_bias = jnp.sum(up_low.astype(jnp.float32), axis=0)
    grad_down = times_left(active_low, up_low)
    grad_active = times_right(up_low, down_weight)
    (grad_inner,) = gate_pull(grad_active)
    inner_low = grad_inner.astype(jnp.bfloat16)
    grad_in_bias = jnp.sum(inner_low.astype(jnp.float32), axis=0)
    grad_in = times_left(second_low, inner_low)
    grad_second = times_right(inner_low, in_weight)
    grad_middle_norm, grad_second_gain, grad_second_shift = second_pull(grad_second)
    grad_middle = upstream + grad_middle_norm
    middle_low = grad_middle.astype(jnp.bfloat16)
    grad_out_bias = jnp.sum(middle_low.astype(jnp.float32), axis=0)
    grad_out = times_left(mixed, middle_low)
    grad_mixed = (
        times_right(middle_low, out_weight)
        .astype(jnp.bfloat16)
        .reshape(seq_rows, heads_count, HEAD)
    )
    probs_again = jnp.exp(scores_of() - log_total)
    grad_probs = jnp.einsum(
        "qhd,khd->hqk", grad_mixed, values_part, preferred_element_type=jnp.float32
    )
    grad_values = jnp.einsum(
        "hqk,qhd->khd", attention, grad_mixed, preferred_element_type=jnp.float32
    )
    delta = jnp.sum(probs_again * grad_probs, axis=-1, keepdims=True)
    grad_scores = (probs_again * (grad_probs - delta)).astype(jnp.bfloat16)
    grad_queries = (
        jnp.einsum("hqk,khd->qhd", grad_scores, keys_part, preferred_element_type=jnp.float32)
        * scale_qk
    )
    grad_keys = (
        jnp.einsum("hqk,qhd->khd", grad_scores, queries, preferred_element_type=jnp.float32)
        * scale_qk
    )
    grad_projected = jnp.stack([grad_queries, grad_keys, grad_values], axis=1)
    grad_projected = grad_projected.reshape(seq_rows, 3 * model_width).astype(jnp.bfloat16)
    column_sums = jnp.sum(grad_projected.astype(jnp.float32), axis=0)
    grad_qv = jnp.concatenate([column_sums[:model_width], column_sums[2 * model_width :]])
    grad_qkv = times_left(first_low, grad_projected)
    grad_first = times_right(grad_projected, qkv_weight)
    grad_input_norm, grad_first_gain, grad_first_shift = first_pull(grad_first)
    grad_inputs = grad_middle + grad_input_norm
    grads = (
        grad_first_gain,
        grad_first_shift,
        grad_qkv,
        grad_qv,
        grad_out,
        grad_out_bias,
        grad_second_gain,
        grad_second_shift,
        grad_in,
        grad_in_bias,
        grad_down,
        grad_down_bias,
    )
    return (output.astype(jnp.bfloat16), grad_inputs.astype(jnp.bfloat16), grads)


RING = (0, 2, 4, 6, 7, 5, 3, 1)
RING_SIZE = len(RING)
CELLS = 2 * RING_SIZE
ANY = pl.BlockSpec(memory_space=pl.ANY)
HBM = pl.BlockSpec(memory_space=pltpu.HBM)
VMEM = pl.BlockSpec(memory_space=pltpu.VMEM)
SMEM = pl.BlockSpec(memory_space=pltpu.SMEM)
LOW = jnp.bfloat16
FULL = jnp.float32
COST = 10**10
ROWS = {
    "first_gain": 0,
    "first_shift": 1,
    "qv_bias": 2,
    "out_bias": 4,
    "second_gain": 5,
    "second_shift": 6,
    "in_bias": 7,
    "down_bias": 11,
    "lengths": 12,
}
NAMES = tuple(ROWS)[:8]
SMALL_ROWS = 16
SMALL_LANES = 256
PIECES = (2, 2, 2, 2, 2, 2, 2, 1, 1)


def ring_pairs():
    pairs = []
    for place in range(RING_SIZE):
        chip = RING[place]
        right = RING[(place + 1) % RING_SIZE]
        left = RING[(place - 1) % RING_SIZE]
        pairs.append((2 * chip, 2 * right))
        pairs.append((2 * chip + 1, 2 * left + 1))
    return pairs


def hop(block):
    return lax.ppermute(block, "cells", ring_pairs())


def to_partner(block):
    return lax.ppermute(block, "cells", [(i, i ^ 1) for i in range(CELLS)])


def across(block):
    return lax.ppermute(block, "species", [(0, 1), (1, 0)])


def exchange(values, bit):
    return values + lax.ppermute(values, "cells", [(i, i ^ bit) for i in range(CELLS)])


def after(value, *others):
    return lax.optimization_barrier((value,) + others)[0]


def here():
    index = lax.axis_index("cells")
    core = index % 2
    chip = index // 2
    place = jnp.int32(0)
    for i, ring_chip in enumerate(RING):
        place = jnp.where(chip == ring_chip, i, place)
    return index, core, place


def chip_at(place):
    place = place % RING_SIZE
    chip = jnp.zeros_like(place)
    for i, ring_chip in enumerate(RING):
        chip = jnp.where(place == i, ring_chip, chip)
    return chip


def gather_order(core, place):
    sign = 1 - 2 * core
    order = []

    def pair(at):
        order.append(2 * chip_at(at))
        order.append(2 * chip_at(at) + 1)

    pair(place)
    for step in range(1, 4):
        pair(place - sign * step)
        pair(place + sign * step)
    order.append(2 * chip_at(place + 4) + core)
    order.append(2 * chip_at(place + 4) + 1 - core)
    return order


def scatter_slots(core, place):
    def kept(core_now):
        sign = 1 - 2 * core_now
        order = [2 * chip_at(place + 4) + core_now]
        for step in (3, 2, 1):
            order.append(2 * chip_at(place + sign * step))
            order.append(2 * chip_at(place + sign * step) + 1)
        order.append(2 * chip_at(place) + core_now)
        return order

    order = kept(core) + kept(1 - core)
    slots = []
    for device in range(CELLS):
        slot = jnp.int32(0)
        for i, who in enumerate(order):
            slot = jnp.where(who == device, i, slot)
        slots.append(slot)
    return slots


def both_blocks(block, core):
    other = to_partner(block)
    return jnp.stack([jnp.where(core == 0, block, other), jnp.where(core == 0, other, block)])


def half_of(pair, core):
    return jnp.where(core == 0, pair[0], pair[1])[None]


def add_low(*parts):
    total = parts[0].astype(FULL)
    for part in parts[1:]:
        total = total + part.astype(FULL)
    return total.astype(LOW)


def first_hop(*parts):
    return hop(add_low(*[part[0:1] for part in parts]))


def second_hop(moving, core, *parts):
    wide = jnp.stack([jnp.where(core == 0, moving[0], 0), jnp.where(core == 0, 0, moving[0])])
    return hop(add_low(wide, *[part[1:3] for part in parts]))


def later_hop(moving, at, *parts):
    return hop(add_low(moving, *[part[at : at + 2] for part in parts]))


def settle(moving, core, *parts):
    mine = jnp.where(core == 0, moving[0], moving[1])
    other = jnp.where(core == 0, moving[1], moving[0])
    return add_low(mine, to_partner(other), *[part[7] for part in parts])


def dot(left, right, dims=((1,), (0,))):
    return lax.dot_general(left, right, (dims, ((), ())), preferred_element_type=FULL)


def call(body, out_shape, ins, specs, out_specs=None, scratch=(), vmem=48):
    return pl.pallas_call(
        body,
        out_shape=out_shape,
        in_specs=specs,
        out_specs=[VMEM] * len(out_shape) if out_specs is None else out_specs,
        scratch_shapes=list(scratch),
        compiler_params=pltpu.CompilerParams(vmem_limit_bytes=vmem * 2**20),
        cost_estimate=pl.CostEstimate(flops=COST, bytes_accessed=0, transcendentals=0),
    )(*ins)


def shape(dims, kind=LOW):
    return jax.ShapeDtypeStruct(dims, kind)


def fetch(order_ref, refs, target, sem):
    rows = target.shape[0] // CELLS
    copies = []
    index = 0
    for source, size in zip(refs, PIECES):
        for part in range(size):
            at = order_ref[index]
            copies.append(
                pltpu.make_async_copy(
                    source.at[part],
                    target.at[pl.ds(pl.multiple_of(at * rows, 16), rows)],
                    sem.at[index],
                )
            )
            index += 1
    for item in copies:
        item.start()
    return copies


def wait_all(copies):
    for item in copies:
        item.wait()


def one_hot(rows, lanes, offset):
    row = lax.broadcasted_iota(jnp.int32, (rows, lanes), 0)
    lane = lax.broadcasted_iota(jnp.int32, (rows, lanes), 1)
    return lane == row + offset


def pack_body(who_ref, lengths_ref, *refs):
    sources, small_ref = refs[:8], refs[8]
    me = who_ref[0]
    model = small_ref.shape[1]
    row = lax.broadcasted_iota(jnp.int32, (SMALL_ROWS, model), 0)
    lane = lax.broadcasted_iota(jnp.int32, (SMALL_ROWS, model), 1)
    small = jnp.zeros((SMALL_ROWS, model), FULL)
    for name, ref in zip(NAMES, sources):
        size = ref.shape[1]
        per_row = model // size
        placed = dot(ref[...], one_hot(size, model, size * (me % per_row)).astype(LOW))
        small = small + jnp.where(row == ROWS[name] + me // per_row, placed, 0.0)
    for i in range(2):
        at = (row == ROWS["lengths"]) & (lane == 2 * me + i)
        small = small + jnp.where(at, lengths_ref[i].astype(FULL), 0.0)
    small_ref[...] = small.astype(LOW)


def norm_parts(values):
    center = values - jnp.mean(values, axis=-1, keepdims=True)
    spread = jnp.mean(center * center, axis=-1, keepdims=True)
    return center, lax.rsqrt(spread + EPSILON)


def norm_back(center, scale, gain, grad):
    weighted = grad * gain
    mean_one = jnp.mean(weighted, axis=-1, keepdims=True)
    mean_two = jnp.mean(weighted * center, axis=-1, keepdims=True)
    back = scale * (weighted - mean_one - center * (scale * scale * mean_two))
    return back, jnp.sum(grad * center * scale, axis=0, keepdims=True), jnp.sum(
        grad, axis=0, keepdims=True
    )


def small_row(small_ref, name, count=1):
    return small_ref[...].astype(FULL)[ROWS[name] : ROWS[name] + count, :]


def project_body(order_ref, x_ref, small_ref, *refs):
    blocks = refs[:9]
    low_ref, proj_ref, weight, sem = refs[9:]
    model = x_ref.shape[1]
    copies = fetch(order_ref, blocks, weight, sem)
    center, scale = norm_parts(x_ref[...].astype(FULL))
    bias = small_row(small_ref, "qv_bias", 2)
    low_ref[...] = (
        center * scale * small_row(small_ref, "first_gain") + small_row(small_ref, "first_shift")
    ).astype(LOW)
    wait_all(copies)
    for j in range(3):
        lanes = slice(j * model, (j + 1) * model)
        part = dot(low_ref[...], weight[:, lanes])
        if j != 1:
            part = part + bias[j // 2 : j // 2 + 1]
        proj_ref[:, lanes] = part.astype(LOW)


def attend_body(seq, lengths_ref, proj_ref, att_ref, mixed_ref):
    model = mixed_ref.shape[1]
    cells = mixed_ref.shape[0] // seq
    pairs = model // (2 * HEAD)
    lane = lax.broadcasted_iota(jnp.int32, (seq, 2 * HEAD), 1)
    key = lax.broadcasted_iota(jnp.int32, (seq, seq), 0)

    def step(index, carry):
        s = index // pairs
        p = index % pairs
        rows = pl.ds(pl.multiple_of(s * seq, seq), seq)
        at = pl.multiple_of(p * 2 * HEAD, 2 * HEAD)
        q = proj_ref[rows, pl.ds(at, 2 * HEAD)] * jnp.asarray(HEAD ** (-0.5), LOW)
        k = proj_ref[rows, pl.ds(at + model, 2 * HEAD)]
        v_turned = proj_ref[rows, pl.ds(at + 2 * model, 2 * HEAD)].T
        visible = key < lengths_ref[s]
        mixed = []
        for i in range(2):
            own = (lane >= i * HEAD) & (lane < (i + 1) * HEAD)
            scores = dot(jnp.where(own, k, jnp.zeros_like(k)), q, ((1,), (1,)))
            scores = jnp.where(visible, scores, NEGATIVE)
            expo = jnp.exp(scores - jnp.max(scores, axis=0, keepdims=True))
            probs = expo * (1.0 / jnp.sum(expo, axis=0, keepdims=True))
            probs = probs.astype(LOW)
            att_ref[2 * index + i] = probs
            mixed.append(dot(v_turned[i * HEAD : (i + 1) * HEAD], probs))
        mixed_ref[rows, pl.ds(at, 2 * HEAD)] = jnp.concatenate(mixed, axis=0).T.astype(LOW)
        return carry

    lax.fori_loop(0, cells * pairs, step, 0, unroll=2)


ERFC_STEP = 0.33
ERFC = (
    0.1863578228018033,
    0.18295566386742124,
    0.2012255082472392,
    0.04721561458875723,
    0.4085089979423051,
    -0.35115900736338407,
    0.4602422572120205,
    -0.13534686486277223,
)


def gelu_parts(inner):
    z = jnp.abs(inner) * (0.5**0.5)
    t = 1.0 / (1.0 + ERFC_STEP * z)
    tail = jnp.full_like(t, 0.5 * ERFC[-1])
    for factor in ERFC[-2::-1]:
        tail = tail * t + 0.5 * factor
    bell = jnp.exp(-(z * z))
    tail = tail * t * bell
    area = jnp.where(inner < 0.0, tail, 1.0 - tail)
    return inner * area, area + inner * bell * (0.5 / 3.141592653589793) ** 0.5


def row_mask(lengths_ref, rows, seq):
    at = lax.broadcasted_iota(jnp.int32, (rows, 1), 0)
    true = (at < lengths_ref[0]).astype(FULL)
    for s in range(1, rows // seq):
        true = jnp.where(at < s * seq, true, (at < lengths_ref[s] + s * seq).astype(FULL))
    return true


def loss_rows(lengths_ref, small_ref, other_ref, cot_ref, seq, whole):
    count = jnp.sum(
        small_row(small_ref, "lengths") + small_row(other_ref, "lengths"), axis=-1, keepdims=True
    )
    return cot_ref[...].astype(FULL) * (
        row_mask(lengths_ref, cot_ref.shape[0], seq) * (whole / count)
    )


def put_slots(keep_buf, slot_ref, values, first, lanes):
    rows = keep_buf.shape[1]
    for i in range(values.shape[0] // rows):
        keep_buf[slot_ref[first + i], :, lanes] = values[i * rows : (i + 1) * rows].astype(LOW)


def send_slots(buf, keep_ref, away_ref, sem):
    half = RING_SIZE
    copies = [
        pltpu.make_async_copy(buf.at[pl.ds(half, half)], away_ref, sem.at[0]),
        pltpu.make_async_copy(buf.at[pl.ds(0, half)], keep_ref, sem.at[1]),
    ]
    for item in copies:
        item.start()
    return copies


def inner_body(order_ref, x_ref, mixed_ref, small_ref, *refs):
    blocks = refs[:9]
    middle_ref, low_ref, active_ref, slope_ref, weight, sem = refs[9:]
    model = x_ref.shape[1]
    ff = active_ref.shape[1]
    wait_all(fetch(order_ref, blocks, weight, sem))
    middle = (
        x_ref[...].astype(FULL)
        + dot(mixed_ref[...], weight[:, ff:])
        + small_row(small_ref, "out_bias")
    )
    middle_ref[...] = middle
    center, scale = norm_parts(middle)
    low = center * scale * small_row(small_ref, "second_gain") + small_row(
        small_ref, "second_shift"
    )
    low_ref[...] = low.astype(LOW)
    step = 2 * (ff // RING_SIZE)
    bias = small_row(small_ref, "in_bias", 4)
    for j in range(ff // step):
        lanes = slice(j * step, (j + 1) * step)
        inner = dot(low_ref[...], weight[:, lanes]) + bias[j : j + 1]
        active, slope = gelu_parts(inner)
        active_ref[:, lanes] = active.astype(LOW)
        slope_ref[:, lanes] = slope.astype(LOW)


def grad_down_body(
    seq, whole, who_ref, slot_ref, lengths_ref, active_ref, cot_ref, small_ref, other_ref,
    up_ref, down_b_ref, keep_ref, away_ref, keep_two_ref, away_two_ref, slots, sem,
):
    up_low = loss_rows(lengths_ref, small_ref, other_ref, cot_ref, seq, whole).astype(LOW)
    up_ref[...] = up_low
    down_b_ref[...] = jnp.sum(up_low.astype(FULL), axis=0, keepdims=True)
    parts = RING_SIZE
    step = active_ref.shape[1] // parts
    rows = slots.shape[2]
    side = who_ref[1]
    for j in range(parts):
        grad = dot(active_ref[:, j * step : (j + 1) * step], up_ref[...], ((0,), (0,)))
        for i in range(4):
            slots[(i + side) % 2, slot_ref[j * CELLS // parts + i // 2]] = grad[
                i * rows : (i + 1) * rows
            ].astype(LOW)
    copies = send_slots(slots.at[1], keep_two_ref, away_two_ref, sem.at[1])
    copies += send_slots(slots.at[0], keep_ref, away_ref, sem.at[0])
    wait_all(copies)


def inner_back_body(order_ref, slope_ref, up_ref, *refs):
    blocks = refs[:9]
    inner_ref, in_b_ref, weight, sem = refs[9:]
    model = up_ref.shape[1]
    wait_all(fetch(order_ref, blocks, weight, sem))
    for j in range(inner_ref.shape[1] // model):
        lanes = slice(j * model, (j + 1) * model)
        grad = dot(up_ref[...], weight[lanes, :], ((1,), (1,)))
        low = (grad * slope_ref[:, lanes].astype(FULL)).astype(LOW)
        inner_ref[:, lanes] = low
        in_b_ref[j : j + 1, :] = jnp.sum(low.astype(FULL), axis=0, keepdims=True)


def down_body(active_ref, middle_ref, small_ref, weight_ref, out_ref):
    out_ref[...] = (
        middle_ref[...]
        + dot(active_ref[...], weight_ref[...])
        + small_row(small_ref, "down_bias")
    ).astype(LOW)


def grad_in_body(slot_ref, low_ref, inner_ref, keep_ref, away_ref, slots, sem):
    model = low_ref.shape[1]
    turned = low_ref[...].T
    for j in range(inner_ref.shape[1] // model):
        lanes = slice(j * model, (j + 1) * model)
        put_slots(slots, slot_ref, dot(turned, inner_ref[:, lanes]), 0, lanes)
    wait_all(send_slots(slots, keep_ref, away_ref, sem))


def middle_back_body(
    seq, whole, lengths_ref, inner_ref, middle_ref, cot_ref, small_ref, other_ref, weight,
    grad_ref, grad_low_ref, grad_mixed_ref, sums_ref,
):
    ff = inner_ref.shape[1]
    grad_second = dot(inner_ref[...], weight[:, :ff], ((1,), (1,)))
    center, scale = norm_parts(middle_ref[...])
    back, gain_sum, shift_sum = norm_back(
        center, scale, small_row(small_ref, "second_gain"), grad_second
    )
    grad = loss_rows(lengths_ref, small_ref, other_ref, cot_ref, seq, whole) + back
    grad_ref[...] = grad
    grad_low = grad.astype(LOW)
    grad_low_ref[...] = grad_low
    grad_mixed_ref[...] = dot(grad_low, weight[:, ff:], ((1,), (1,))).astype(LOW)
    sums_ref[0:1, :] = jnp.sum(grad_low.astype(FULL), axis=0, keepdims=True)
    sums_ref[1:2, :] = gain_sum
    sums_ref[2:3, :] = shift_sum


def attend_back_body(seq, begin, proj_ref, att_ref, grad_ref, out_ref):
    model = grad_ref.shape[1]
    half = out_ref.shape[1] // 3
    all_pairs = model // (2 * HEAD)
    pairs = half // (2 * HEAD)
    cells = grad_ref.shape[0] // seq
    lane = lax.broadcasted_iota(jnp.int32, (seq, 2 * HEAD), 1)
    scale = HEAD ** (-0.5)

    def step(index, carry):
        s = index // pairs
        p = index % pairs
        rows = pl.ds(pl.multiple_of(s * seq, seq), seq)
        to = pl.multiple_of(p * 2 * HEAD, 2 * HEAD)
        at = pl.multiple_of(to + begin * 2 * HEAD, 2 * HEAD)
        q = proj_ref[rows, pl.ds(at, 2 * HEAD)]
        k_turned = proj_ref[rows, pl.ds(at + model, 2 * HEAD)].T
        v = proj_ref[rows, pl.ds(at + 2 * model, 2 * HEAD)]
        g = grad_ref[rows, pl.ds(at, 2 * HEAD)]
        grad_q = []
        grad_k = []
        grad_v = []
        for i in range(2):
            own = (lane >= i * HEAD) & (lane < (i + 1) * HEAD)
            probs = att_ref[2 * (s * all_pairs + begin + p) + i]
            wide = probs.astype(FULL)
            grad_probs = dot(jnp.where(own, v, jnp.zeros_like(v)), g, ((1,), (1,)))
            delta = jnp.sum(wide * grad_probs, axis=0, keepdims=True)
            scores = (wide * (grad_probs - delta)).astype(LOW)
            grad_q.append(dot(k_turned[i * HEAD : (i + 1) * HEAD], scores))
            grad_k.append(dot(scores, q))
            grad_v.append(dot(probs, g))
        first = lane < HEAD
        out_ref[rows, pl.ds(to, 2 * HEAD)] = (
            jnp.concatenate(grad_q, axis=0).T * scale
        ).astype(LOW)
        out_ref[rows, pl.ds(to + half, 2 * HEAD)] = (
            jnp.where(first, grad_k[0], grad_k[1]) * scale
        ).astype(LOW)
        out_ref[rows, pl.ds(to + 2 * half, 2 * HEAD)] = jnp.where(
            first, grad_v[0], grad_v[1]
        ).astype(LOW)
        return carry

    lax.fori_loop(0, cells * pairs, step, 0, unroll=2)


def early_grad_body(
    slot_ref, low_ref, part_ref, mixed_ref, grad_low_ref, keep_ref, away_ref, slots, sem
):
    width = part_ref.shape[1]
    put_slots(slots, slot_ref, dot(low_ref[...].T, part_ref[...]), 0, slice(0, width))
    put_slots(
        slots, slot_ref, dot(mixed_ref[...].T, grad_low_ref[...]), 0,
        slice(width, slots.shape[2]),
    )
    wait_all(send_slots(slots, keep_ref, away_ref, sem))


def first_back_body(
    slot_ref, x_ref, low_ref, one_ref, two_ref, grad_ref, small_ref, sums_ref, in_b_ref,
    down_b_ref, weight, out_ref, keep_ref, away_ref, sum_ref, slots, sem,
):
    model = x_ref.shape[1]
    late = two_ref.shape[1]
    center, scale = norm_parts(x_ref[...].astype(FULL))
    parts = ((one_ref, 0), (two_ref, one_ref.shape[1] // 3))
    grad_first = jnp.zeros(x_ref.shape, FULL)
    for j in range(3):
        for ref, begin in parts:
            width = ref.shape[1] // 3
            at = j * model + begin
            grad_first = grad_first + dot(
                ref[:, j * width : (j + 1) * width], weight[:, at : at + width], ((1,), (1,))
            )
    put_slots(slots, slot_ref, dot(low_ref[...].T, two_ref[...]), 0, slice(0, late))
    back, gain_sum, shift_sum = norm_back(
        center, scale, small_row(small_ref, "first_gain"), grad_first
    )

    def put(name, value, offset=0):
        at = ROWS[name] + offset
        sum_ref[at : at + value.shape[0], :] = value

    sum_ref[...] = jnp.zeros_like(sum_ref)
    put("first_gain", gain_sum)
    put("first_shift", shift_sum)
    for j in range(2):
        at = ROWS["qv_bias"] + j
        for ref, begin in parts:
            width = ref.shape[1] // 3
            part = ref[:, 2 * j * width : (2 * j + 1) * width].astype(FULL)
            sum_ref[at : at + 1, begin : begin + width] = jnp.sum(part, axis=0, keepdims=True)
    put("out_bias", sums_ref[0:1, :])
    put("second_gain", sums_ref[1:2, :])
    put("second_shift", sums_ref[2:3, :])
    put("in_bias", in_b_ref[...])
    put("down_bias", down_b_ref[...])
    for i in range(3):
        part = sum_ref[:, SMALL_LANES * i : SMALL_LANES * (i + 1)].astype(LOW)
        for device in range(CELLS):
            slots[device, 16 * i : 16 * i + 16, late:] = part
    copies = send_slots(slots, keep_ref, away_ref, sem)
    out_ref[...] = (grad_ref[...] + back).astype(LOW)
    wait_all(copies)


def finish_body(who_ref, early_ref, early_two_ref, late_ref, late_two_ref, *refs):
    grad_ref, out_ref, vectors, small_ref = refs[0], refs[1], refs[2:-1], refs[-1]
    model = out_ref.shape[1]
    early = early_ref[...].astype(FULL) + early_two_ref[...].astype(FULL)
    late = late_ref[...].astype(FULL) + late_two_ref[...].astype(FULL)
    one = (early.shape[1] - model) // 3
    two = (late.shape[1] - SMALL_LANES) // 3
    for j in range(3):
        at = j * model
        grad_ref[:, at : at + one] = early[:, j * one : (j + 1) * one]
        grad_ref[:, at + one : at + model] = late[:, j * two : (j + 1) * two]
    out_ref[...] = early[:, 3 * one :]
    for i in range(3):
        small_ref[:, SMALL_LANES * i : SMALL_LANES * (i + 1)] = late[
            16 * i : 16 * i + 16, 3 * two :
        ]
    me = who_ref[0]
    row = lax.broadcasted_iota(jnp.int32, (SMALL_ROWS, model), 0)
    for name, ref in zip(NAMES, vectors):
        size = ref.shape[1]
        per_row = model // size
        here_row = jnp.where(row == ROWS[name] + me // per_row, small_ref[...], 0.0)
        values = jnp.sum(here_row, axis=0, keepdims=True)
        picker = one_hot(size, model, size * (me % per_row)).astype(FULL)
        ref[...] = lax.dot_general(
            values, picker, (((1,), (1,)), ((), ())), precision=lax.Precision.HIGHEST,
            preferred_element_type=FULL,
        )


def on_device_ring(
    tokens,
    lengths,
    cotangent,
    first_gain,
    first_shift,
    qkv_weight,
    qv_bias,
    out_weight,
    out_bias,
    second_gain,
    second_shift,
    in_weight,
    in_bias,
    down_weight,
    down_bias,
):
    micro, seq, model = tokens.shape[1:]
    total_rows = micro * seq
    rows = qkv_weight.shape[0]
    down_rows = down_weight.shape[0]
    ff = in_weight.shape[1]
    heads = model // HEAD
    whole = float(lax.axis_size("species") * CELLS * micro * seq)
    index, core, place = here()
    species = lax.axis_index("species")
    who = jnp.stack([index, species]).astype(jnp.int32)
    order = jnp.stack(gather_order(core, place)).astype(jnp.int32)
    slot = jnp.stack(scatter_slots(core, place)).astype(jnp.int32)
    lens = lengths.reshape(micro)
    x = tokens.reshape(total_rows, model)
    cot = cotangent.reshape(total_rows, model)
    vectors = (
        first_gain, first_shift, qv_bias, out_bias, second_gain, second_shift, in_bias, down_bias,
    )

    dma = pltpu.SemaphoreType.DMA

    def gathered(own, hops):
        got = [own]
        for item in hops:
            got += [item, to_partner(item)]
        return got

    own = both_blocks(qkv_weight, core)
    qkv_one = hop(own)
    (small,) = call(
        pack_body,
        [shape((SMALL_ROWS, model))],
        [who, after(lens, own)] + [item.reshape(1, -1) for item in vectors],
        [SMEM, SMEM] + [VMEM] * 8,
        vmem=4,
    )
    small = exchange(small, 1)
    small = exchange(small, 2)
    in_weight, out_weight = lax.optimization_barrier((in_weight, out_weight, own))[:2]
    in_own = both_blocks(jnp.concatenate([in_weight, out_weight], axis=1), core)
    qkv_one, small, in_own = lax.optimization_barrier((qkv_one, small, in_own))
    qkv_two = hop(qkv_one)
    small = exchange(small, 4)
    down_own = both_blocks(after(down_weight, qkv_one), core)
    qkv_two, small, down_own = lax.optimization_barrier((qkv_two, small, down_own))
    qkv_three = hop(qkv_two)
    small = exchange(small, 8)
    qkv_three, small = lax.optimization_barrier((qkv_three, small))
    qkv_last = hop(half_of(qkv_three, core))
    in_one = hop(after(in_own, qkv_three))
    low, proj, qkv_full = call(
        project_body,
        [
            shape((total_rows, model)),
            shape((total_rows, 3 * model)),
            shape((model, 3 * model)),
        ],
        [order, x, small] + gathered(own, (qkv_one, qkv_two, qkv_three, qkv_last)),
        [SMEM, VMEM, VMEM] + [ANY] * 9,
        scratch=[dma((CELLS,))],
        vmem=20,
    )
    other_small = across(small)
    in_one, proj = lax.optimization_barrier((in_one, proj))
    in_two = hop(in_one)
    down_one = hop(after(down_own, in_one))
    att, mixed = call(
        lambda *refs: attend_body(seq, *refs),
        [shape((micro * heads, seq, seq)), shape((total_rows, model))],
        [lens, proj],
        [SMEM, VMEM],
        vmem=16,
    )
    in_two, mixed, down_one = lax.optimization_barrier((in_two, mixed, down_one))
    in_three = hop(in_two)
    down_two = hop(after(down_one, in_two))
    in_last = hop(half_of(in_three, core))
    down_three = hop(after(down_two, in_three))
    in_got = gathered(in_own, (in_one, in_two, in_three, in_last))
    middle, low_two, active, slope, in_full = call(
        inner_body,
        [
            shape((total_rows, model), FULL),
            shape((total_rows, model)),
            shape((total_rows, ff)),
            shape((total_rows, ff)),
            shape((model, ff + model)),
        ],
        [order, x, after(mixed, down_two), small] + in_got,
        [SMEM] + [VMEM] * 3 + [ANY] * 9,
        scratch=[dma((CELLS,))],
        vmem=24,
    )
    down_three, active = lax.optimization_barrier((down_three, active))
    down_last = hop(half_of(down_three, core))
    up_low, down_b, down_keep, down_away, down_keep_two, down_away_two = call(
        lambda *refs: grad_down_body(seq, whole, *refs),
        [
            shape((total_rows, model)),
            shape((1, model), FULL),
        ]
        + [shape((RING_SIZE, down_rows // 2, model))] * 4,
        [who, slot, lens, active, cot, small, other_small],
        [SMEM] * 3 + [VMEM] * 4,
        [VMEM] * 2 + [ANY] * 4,
        scratch=[pltpu.VMEM((2, CELLS, down_rows // 2, model), LOW), dma((2, 2))],
        vmem=18,
    )

    down_away, down_away_two, down_last = lax.optimization_barrier(
        (down_away, down_away_two, down_last)
    )
    down_other_two = to_partner(down_away_two)
    down_other = to_partner(down_away)
    inner_low, in_b, down_full = call(
        inner_back_body,
        [
            shape((total_rows, ff)),
            shape((ff // model, model), FULL),
            shape((ff, model)),
        ],
        [order, slope, up_low]
        + gathered(down_own, (down_one, down_two, down_three, down_last)),
        [SMEM] + [VMEM] * 2 + [ANY] * 9,
        scratch=[dma((CELLS,))],
        vmem=20,
    )
    down_other_two, inner_low = lax.optimization_barrier((down_other_two, inner_low))
    down_x = across(add_low(down_keep_two[0:3], down_other_two[0:3]))
    down_x_two = across(add_low(down_keep_two[3:8], down_other_two[3:8]))
    in_keep, in_away = call(
        grad_in_body,
        [shape((RING_SIZE, rows, ff)), shape((RING_SIZE, rows, ff))],
        [slot, low_two, inner_low],
        [SMEM] + [VMEM] * 2,
        [ANY] * 2,
        scratch=[pltpu.VMEM((CELLS, rows, ff), LOW), dma((2,))],
        vmem=16,
    )
    in_other = to_partner(in_away)
    (out_tokens,) = call(
        down_body,
        [shape((total_rows, model))],
        [after(active, in_keep), middle, small, down_full],
        [VMEM] * 4,
        vmem=14,
    )
    in_other, out_tokens, inner_low = lax.optimization_barrier((in_other, out_tokens, inner_low))
    in_sum = first_hop(in_keep, in_other)
    grad_middle, grad_low, grad_mixed, sums = call(
        lambda *refs: middle_back_body(seq, whole, *refs),
        [
            shape((total_rows, model), FULL),
            shape((total_rows, model)),
            shape((total_rows, model)),
            shape((3, model), FULL),
        ],
        [lens, inner_low, middle, cot, small, other_small, in_full],
        [SMEM] + [VMEM] * 6,
        vmem=24,
    )

    def attend_back(begin, pairs, grad):
        return call(
            lambda *refs: attend_back_body(seq, begin, *refs),
            [shape((total_rows, 6 * pairs * HEAD))],
            [proj, att, grad],
            [VMEM] * 3,
            vmem=14,
        )[0]

    pairs = model // (2 * HEAD)
    early_pairs = 2 * pairs // 3
    in_sum, grad_mixed = lax.optimization_barrier((in_sum, grad_mixed))
    in_sum = second_hop(in_sum, core, in_keep, in_other)
    grad_one = attend_back(0, early_pairs, grad_mixed)
    early_width = 6 * early_pairs * HEAD + model
    early_keep, early_away = call(
        early_grad_body,
        [shape((RING_SIZE, rows, early_width))] * 2,
        [slot, low, grad_one, mixed, grad_low],
        [SMEM] + [VMEM] * 4,
        [ANY] * 2,
        scratch=[pltpu.VMEM((CELLS, rows, early_width), LOW), dma((2,))],
        vmem=14,
    )
    early_other = to_partner(early_away)
    in_sum, down_x, down_other, early_keep, grad_mixed = lax.optimization_barrier(
        (in_sum, down_x, down_other, early_keep, grad_mixed)
    )
    in_sum = later_hop(in_sum, 3, in_keep, in_other)
    down_sum = first_hop(down_keep, down_other, down_x)
    grad_two = attend_back(early_pairs, pairs - early_pairs, grad_mixed)
    down_sum, early_other, grad_two = lax.optimization_barrier((down_sum, early_other, grad_two))
    down_sum = second_hop(down_sum, core, down_keep, down_other, down_x)
    early_sum = first_hop(early_keep, early_other)
    late_width = 6 * (pairs - early_pairs) * HEAD + SMALL_LANES
    grad_tokens, late_keep, late_away = call(
        first_back_body,
        [
            shape((total_rows, model)),
            shape((RING_SIZE, rows, late_width)),
            shape((RING_SIZE, rows, late_width)),
        ],
        [slot, x, low, grad_one, grad_two, grad_middle, small, sums, in_b, down_b, qkv_full],
        [SMEM] + [VMEM] * 10,
        [VMEM] + [ANY] * 2,
        scratch=[
            pltpu.VMEM((SMALL_ROWS, model), FULL),
            pltpu.VMEM((CELLS, rows, late_width), LOW),
            dma((2,)),
        ],
        vmem=20,
    )
    late_other = to_partner(late_away)
    in_sum, early_sum, late_keep, down_sum, down_x_two = lax.optimization_barrier(
        (in_sum, early_sum, late_keep, down_sum, down_x_two)
    )
    in_sum = later_hop(in_sum, 5, in_keep, in_other)
    early_sum = second_hop(early_sum, core, early_keep, early_other)
    down_sum = hop(
        add_low(down_sum, down_keep[3:5], down_other[3:5], down_x_two[0:2])
    )
    late_sum = first_hop(late_keep, late_other)
    late_sum, early_sum, in_sum, down_sum = lax.optimization_barrier(
        (late_sum, early_sum, in_sum, down_sum)
    )
    late_sum = second_hop(late_sum, core, late_keep, late_other)
    early_sum = later_hop(early_sum, 3, early_keep, early_other)
    down_sum = hop(
        add_low(down_sum, down_keep[5:7], down_other[5:7], down_x_two[2:4])
    )
    in_sum = settle(in_sum, core, in_keep, in_other)
    late_sum, early_sum, down_sum, in_sum = lax.optimization_barrier(
        (late_sum, early_sum, down_sum, in_sum)
    )
    late_sum = later_hop(late_sum, 3, late_keep, late_other)
    early_sum = later_hop(early_sum, 5, early_keep, early_other)
    in_terms = (in_sum, across(in_sum))
    mine = jnp.where(core == 0, down_sum[0], down_sum[1])
    other = to_partner(jnp.where(core == 0, down_sum[1], down_sum[0]))
    down_sum = add_low(mine, other, down_keep[7], down_other[7], down_x_two[4])
    down_terms = (down_sum, across(down_sum))
    late_sum = later_hop(late_sum, 5, late_keep, late_other)
    early_sum = settle(early_sum, core, early_keep, early_other)
    early_terms = (early_sum, across(early_sum))
    late_sum = settle(late_sum, core, late_keep, late_other)
    late_terms = (late_sum, across(late_sum))
    finished = call(
        finish_body,
        [shape((rows, 3 * model), FULL), shape((rows, model), FULL)]
        + [shape((1, item.shape[0]), FULL) for item in vectors],
        [who] + list(early_terms) + list(late_terms),
        [SMEM] + [VMEM] * 4,
        scratch=[pltpu.VMEM((SMALL_ROWS, model), FULL)],
        vmem=6,
    )
    grad_qkv, grad_out = finished[:2]
    pieces = [item.reshape(-1) for item in finished[2:]]
    return (
        out_tokens.reshape(tokens.shape),
        grad_tokens.reshape(tokens.shape),
        pieces[0],
        pieces[1],
        grad_qkv,
        pieces[2],
        grad_out,
        pieces[3],
        pieces[4],
        pieces[5],
        in_terms[0].astype(FULL) + in_terms[1].astype(FULL),
        pieces[6],
        jnp.concatenate(
            [
                jnp.where(species == 0, down_terms[0], down_terms[1]),
                jnp.where(species == 0, down_terms[1], down_terms[0]),
            ]
        ).astype(FULL),
        pieces[7],
    )


def on_device(
    tokens,
    lengths,
    cotangent,
    first_gain,
    first_shift,
    qkv_weight,
    qv_bias,
    out_weight,
    out_bias,
    second_gain,
    second_shift,
    in_weight,
    in_bias,
    down_weight,
    down_bias,
):
    local_count = jnp.sum(lengths).astype(jnp.float32)
    count = lax.psum(local_count, ("species", "cells"))
    micro_count = tokens.shape[1]
    seq_rows = tokens.shape[2]
    factor = (
        float(lax.axis_size("species") * lax.axis_size("cells") * micro_count * seq_rows) / count
    )
    output_rows = []
    gradient_rows = []
    summed = None
    for micro_step in range(micro_count):
        gathered = (
            lax.all_gather(first_gain, "cells", axis=0, tiled=True),
            lax.all_gather(first_shift, "cells", axis=0, tiled=True),
            lax.all_gather(qkv_weight, "cells", axis=0, tiled=True),
            lax.all_gather(qv_bias, "cells", axis=0, tiled=True),
            lax.all_gather(out_weight, "cells", axis=0, tiled=True),
            lax.all_gather(out_bias, "cells", axis=0, tiled=True),
            lax.all_gather(second_gain, "cells", axis=0, tiled=True),
            lax.all_gather(second_shift, "cells", axis=0, tiled=True),
            lax.all_gather(in_weight, "cells", axis=0, tiled=True),
            lax.all_gather(in_bias, "cells", axis=0, tiled=True),
            lax.all_gather(down_weight, "cells", axis=0, tiled=True),
            lax.all_gather(down_bias, "cells", axis=0, tiled=True),
        )
        out_seq, grad_seq, grads = sequence_pass(
            gathered,
            tokens[0, micro_step],
            lengths[0, micro_step],
            cotangent[0, micro_step],
            factor,
        )
        output_rows.append(out_seq)
        gradient_rows.append(grad_seq)
        shares = (
            lax.psum_scatter(grads[0], "cells", scatter_dimension=0, tiled=True),
            lax.psum_scatter(grads[1], "cells", scatter_dimension=0, tiled=True),
            lax.psum_scatter(grads[2], "cells", scatter_dimension=0, tiled=True),
            lax.psum_scatter(grads[3], "cells", scatter_dimension=0, tiled=True),
            lax.psum_scatter(grads[4], "cells", scatter_dimension=0, tiled=True),
            lax.psum_scatter(grads[5], "cells", scatter_dimension=0, tiled=True),
            lax.psum_scatter(grads[6], "cells", scatter_dimension=0, tiled=True),
            lax.psum_scatter(grads[7], "cells", scatter_dimension=0, tiled=True),
            lax.psum_scatter(grads[8], "cells", scatter_dimension=0, tiled=True),
            lax.psum_scatter(grads[9], "cells", scatter_dimension=0, tiled=True),
            lax.psum_scatter(grads[10], "cells", scatter_dimension=0, tiled=True),
            lax.psum_scatter(grads[11], "cells", scatter_dimension=0, tiled=True),
        )
        summed = shares if summed is None else jax.tree.map(jnp.add, summed, shares)
    final = (
        lax.psum(summed[0].astype(jnp.bfloat16), "species").astype(jnp.float32),
        lax.psum(summed[1].astype(jnp.bfloat16), "species").astype(jnp.float32),
        lax.psum(summed[2].astype(jnp.bfloat16), "species").astype(jnp.float32),
        lax.psum(summed[3].astype(jnp.bfloat16), "species").astype(jnp.float32),
        lax.psum(summed[4].astype(jnp.bfloat16), "species").astype(jnp.float32),
        lax.psum(summed[5].astype(jnp.bfloat16), "species").astype(jnp.float32),
        lax.psum(summed[6].astype(jnp.bfloat16), "species").astype(jnp.float32),
        lax.psum(summed[7].astype(jnp.bfloat16), "species").astype(jnp.float32),
        lax.psum(summed[8].astype(jnp.bfloat16), "species").astype(jnp.float32),
        lax.psum(summed[9].astype(jnp.bfloat16), "species").astype(jnp.float32),
        lax.psum(summed[10].astype(jnp.bfloat16), "species").astype(jnp.float32),
        lax.psum(summed[11].astype(jnp.bfloat16), "species").astype(jnp.float32),
    )
    out_tokens = jnp.stack(output_rows)[None]
    grad_tokens = jnp.stack(gradient_rows)[None]
    return (out_tokens, grad_tokens) + tuple(final)


def solution(mesh):
    in_specs = (
        P("species", "cells", None, None),
        P("species", "cells"),
        P("species", "cells", None, None),
        P("cells"),
        P("cells"),
        P("cells", None),
        P("cells"),
        P("cells", None),
        P("cells"),
        P("cells"),
        P("cells"),
        P("cells", None),
        P("cells"),
        P("cells", None),
        P("cells"),
    )
    out_specs = (
        P("species", "cells", None, None),
        P("species", "cells", None, None),
        P("cells"),
        P("cells"),
        P("cells", None),
        P("cells"),
        P("cells", None),
        P("cells"),
        P("cells"),
        P("cells"),
        P("cells", None),
        P("cells"),
        P("cells", None),
        P("cells"),
    )
    program = on_device_ring if mesh.shape["cells"] == 2 * RING_SIZE else on_device
    return jax.shard_map(
        program, mesh=mesh, in_specs=in_specs, out_specs=out_specs, check_vma=False
    )
```

```python
import jax
import jax.numpy as jnp
from jax import lax
from jax.experimental import pallas as pl
from jax.experimental.pallas import tpu as pltpu
from jax.sharding import PartitionSpec as P

HEAD = 64


EPSILON = 1e-12
NEGATIVE = -1e30


def normalize(values, gain_vec, shift_vec):
    center = values - jnp.mean(values, axis=-1, keepdims=True)
    spread = jnp.mean(center * center, axis=-1, keepdims=True)
    return center * lax.rsqrt(spread + EPSILON) * gain_vec + shift_vec


def smooth_gate(values):
    return jax.nn.gelu(values, approximate=False)


def times_left(left_side, right_side):
    return lax.dot_general(
        left_side, right_side, (((0,), (0,)), ((), ())), preferred_element_type=jnp.float32
    )


def times_right(left_side, right_side):
    return lax.dot_general(
        left_side, right_side, (((1,), (1,)), ((), ())), preferred_element_type=jnp.float32
    )


def sequence_pass(weights, inputs, length, cot_rows, factor):
    (
        first_gain,
        first_shift,
        qkv_weight,
        qv_bias,
        out_weight,
        out_bias,
        second_gain,
        second_shift,
        in_weight,
        in_bias,
        down_weight,
        down_bias,
    ) = weights
    seq_rows = inputs.shape[0]
    model_width = inputs.shape[1]
    heads_count = model_width // HEAD
    scale_qk = float(HEAD) ** (-0.5)
    as_float = inputs.astype(jnp.float32)
    hidden_one, first_pull = jax.vjp(
        normalize, as_float, first_gain.astype(jnp.float32), first_shift.astype(jnp.float32)
    )
    first_low = hidden_one.astype(jnp.bfloat16)
    bias_float = qv_bias.astype(jnp.float32)
    full_bias = jnp.concatenate(
        [bias_float[:model_width], jnp.zeros((model_width,), jnp.float32), bias_float[model_width:]]
    )
    projected = (
        jnp.dot(first_low, qkv_weight, preferred_element_type=jnp.float32) + full_bias
    ).astype(jnp.bfloat16)
    split_heads = projected.reshape(seq_rows, 3, heads_count, HEAD)
    queries = split_heads[:, 0]
    keys_part = split_heads[:, 1]
    values_part = split_heads[:, 2]
    visible = jnp.arange(seq_rows) < length

    def scores_of():
        raw_scores = (
            jnp.einsum("qhd,khd->hqk", queries, keys_part, preferred_element_type=jnp.float32)
            * scale_qk
        )
        return jnp.where(visible[None, None, :], raw_scores, NEGATIVE)

    scores = scores_of()
    top_score = jnp.max(scores, axis=-1, keepdims=True)
    expo = jnp.exp(scores - top_score)
    total_exp = jnp.sum(expo, axis=-1, keepdims=True)
    log_total = top_score + jnp.log(total_exp)
    attention = (expo / total_exp).astype(jnp.bfloat16)
    mixed = jnp.einsum("hqk,khd->qhd", attention, values_part, preferred_element_type=jnp.float32)
    mixed = mixed.reshape(seq_rows, model_width).astype(jnp.bfloat16)
    middle = (
        as_float
        + jnp.dot(mixed, out_weight, preferred_element_type=jnp.float32)
        + out_bias.astype(jnp.float32)
    )
    hidden_two, second_pull = jax.vjp(
        normalize, middle, second_gain.astype(jnp.float32), second_shift.astype(jnp.float32)
    )
    second_low = hidden_two.astype(jnp.bfloat16)
    inner = jnp.dot(second_low, in_weight, preferred_element_type=jnp.float32) + in_bias.astype(
        jnp.float32
    )
    active, gate_pull = jax.vjp(smooth_gate, inner)
    active_low = active.astype(jnp.bfloat16)
    output = (
        middle
        + jnp.dot(active_low, down_weight, preferred_element_type=jnp.float32)
        + down_bias.astype(jnp.float32)
    )
    upstream = cot_rows.astype(jnp.float32) * visible[:, None].astype(jnp.float32) * factor
    up_low = upstream.astype(jnp.bfloat16)
    grad_down_bias = jnp.sum(up_low.astype(jnp.float32), axis=0)
    grad_down = times_left(active_low, up_low)
    grad_active = times_right(up_low, down_weight)
    (grad_inner,) = gate_pull(grad_active)
    inner_low = grad_inner.astype(jnp.bfloat16)
    grad_in_bias = jnp.sum(inner_low.astype(jnp.float32), axis=0)
    grad_in = times_left(second_low, inner_low)
    grad_second = times_right(inner_low, in_weight)
    grad_middle_norm, grad_second_gain, grad_second_shift = second_pull(grad_second)
    grad_middle = upstream + grad_middle_norm
    middle_low = grad_middle.astype(jnp.bfloat16)
    grad_out_bias = jnp.sum(middle_low.astype(jnp.float32), axis=0)
    grad_out = times_left(mixed, middle_low)
    grad_mixed = (
        times_right(middle_low, out_weight)
        .astype(jnp.bfloat16)
        .reshape(seq_rows, heads_count, HEAD)
    )
    probs_again = jnp.exp(scores_of() - log_total)
    grad_probs = jnp.einsum(
        "qhd,khd->hqk", grad_mixed, values_part, preferred_element_type=jnp.float32
    )
    grad_values = jnp.einsum(
        "hqk,qhd->khd", attention, grad_mixed, preferred_element_type=jnp.float32
    )
    delta = jnp.sum(probs_again * grad_probs, axis=-1, keepdims=True)
    grad_scores = (probs_again * (grad_probs - delta)).astype(jnp.bfloat16)
    grad_queries = (
        jnp.einsum("hqk,khd->qhd", grad_scores, keys_part, preferred_element_type=jnp.float32)
        * scale_qk
    )
    grad_keys = (
        jnp.einsum("hqk,qhd->khd", grad_scores, queries, preferred_element_type=jnp.float32)
        * scale_qk
    )
    grad_projected = jnp.stack([grad_queries, grad_keys, grad_values], axis=1)
    grad_projected = grad_projected.reshape(seq_rows, 3 * model_width).astype(jnp.bfloat16)
    column_sums = jnp.sum(grad_projected.astype(jnp.float32), axis=0)
    grad_qv = jnp.concatenate([column_sums[:model_width], column_sums[2 * model_width :]])
    grad_qkv = times_left(first_low, grad_projected)
    grad_first = times_right(grad_projected, qkv_weight)
    grad_input_norm, grad_first_gain, grad_first_shift = first_pull(grad_first)
    grad_inputs = grad_middle + grad_input_norm
    grads = (
        grad_first_gain,
        grad_first_shift,
        grad_qkv,
        grad_qv,
        grad_out,
        grad_out_bias,
        grad_second_gain,
        grad_second_shift,
        grad_in,
        grad_in_bias,
        grad_down,
        grad_down_bias,
    )
    return (output.astype(jnp.bfloat16), grad_inputs.astype(jnp.bfloat16), grads)


RING = (0, 2, 4, 6, 7, 5, 3, 1)
RING_SIZE = len(RING)
CELLS = 2 * RING_SIZE
ANY = pl.BlockSpec(memory_space=pl.ANY)
HBM = pl.BlockSpec(memory_space=pltpu.HBM)
VMEM = pl.BlockSpec(memory_space=pltpu.VMEM)
SMEM = pl.BlockSpec(memory_space=pltpu.SMEM)
LOW = jnp.bfloat16
FULL = jnp.float32
HEAVY = 10**10
UNIT = 10**8
ROWS = {
    "first_gain": 0,
    "first_shift": 1,
    "qv_bias": 2,
    "out_bias": 4,
    "second_gain": 5,
    "second_shift": 6,
    "in_bias": 7,
    "down_bias": 11,
    "lengths": 12,
}
NAMES = tuple(ROWS)[:8]
SMALL_ROWS = 16
SMALL_LANES = 256
PIECES = (2, 2, 2, 2, 2, 2, 2, 1, 1)


def ring_pairs():
    pairs = []
    for place in range(RING_SIZE):
        chip = RING[place]
        right = RING[(place + 1) % RING_SIZE]
        left = RING[(place - 1) % RING_SIZE]
        pairs.append((2 * chip, 2 * right))
        pairs.append((2 * chip + 1, 2 * left + 1))
    return pairs


def hop(block):
    return lax.ppermute(block, "cells", ring_pairs())


def to_partner(block):
    return lax.ppermute(block, "cells", [(i, i ^ 1) for i in range(CELLS)])


def across(block):
    return lax.ppermute(block, "species", [(0, 1), (1, 0)])


def exchange(values, bit):
    return values + lax.ppermute(values, "cells", [(i, i ^ bit) for i in range(CELLS)])


def after(value, *others):
    return lax.optimization_barrier((value,) + others)[0]


def here():
    index = lax.axis_index("cells")
    core = index % 2
    chip = index // 2
    place = jnp.int32(0)
    for i, ring_chip in enumerate(RING):
        place = jnp.where(chip == ring_chip, i, place)
    return index, core, place


def chip_at(place):
    place = place % RING_SIZE
    chip = jnp.zeros_like(place)
    for i, ring_chip in enumerate(RING):
        chip = jnp.where(place == i, ring_chip, chip)
    return chip


def gather_order(core, place):
    sign = 1 - 2 * core
    order = []

    def pair(at):
        order.append(2 * chip_at(at))
        order.append(2 * chip_at(at) + 1)

    pair(place)
    for step in range(1, 4):
        pair(place - sign * step)
        pair(place + sign * step)
    order.append(2 * chip_at(place + 4) + core)
    order.append(2 * chip_at(place + 4) + 1 - core)
    return order


def scatter_slots(core, place):
    def kept(core_now):
        sign = 1 - 2 * core_now
        order = [2 * chip_at(place + 4) + core_now]
        for step in (3, 2, 1):
            order.append(2 * chip_at(place + sign * step))
            order.append(2 * chip_at(place + sign * step) + 1)
        order.append(2 * chip_at(place) + core_now)
        return order

    order = kept(core) + kept(1 - core)
    slots = []
    for device in range(CELLS):
        slot = jnp.int32(0)
        for i, who in enumerate(order):
            slot = jnp.where(who == device, i, slot)
        slots.append(slot)
    return slots


def both_blocks(block, core):
    other = to_partner(block)
    return jnp.stack([jnp.where(core == 0, block, other), jnp.where(core == 0, other, block)])


def half_of(pair, core):
    return jnp.where(core == 0, pair[0], pair[1])[None]


def add_low(*parts):
    total = parts[0].astype(FULL)
    for part in parts[1:]:
        total = total + part.astype(FULL)
    return total.astype(LOW)


def first_hop(*parts):
    return hop(add_low(*[part[0:1] for part in parts]))


def second_hop(moving, core, *parts):
    wide = jnp.stack([jnp.where(core == 0, moving[0], 0), jnp.where(core == 0, 0, moving[0])])
    return hop(add_low(wide, *[part[1:3] for part in parts]))


def later_hop(moving, at, *parts):
    return hop(add_low(moving, *[part[at : at + 2] for part in parts]))


def settle(moving, core, *parts):
    mine = jnp.where(core == 0, moving[0], moving[1])
    other = jnp.where(core == 0, moving[1], moving[0])
    return add_low(mine, to_partner(other), *[part[7] for part in parts])


def dot(left, right, dims=((1,), (0,))):
    return lax.dot_general(left, right, (dims, ((), ())), preferred_element_type=FULL)


def call(body, out_shape, ins, specs, out_specs=None, scratch=(), vmem=48, cost=HEAVY):
    return pl.pallas_call(
        body,
        out_shape=out_shape,
        in_specs=specs,
        out_specs=[VMEM] * len(out_shape) if out_specs is None else out_specs,
        scratch_shapes=list(scratch),
        compiler_params=pltpu.CompilerParams(vmem_limit_bytes=vmem * 2**20),
        cost_estimate=pl.CostEstimate(flops=cost, bytes_accessed=0, transcendentals=0),
    )(*ins)


def shape(dims, kind=LOW):
    return jax.ShapeDtypeStruct(dims, kind)


def fetch(order_ref, refs, target, sem):
    rows = target.shape[0] // CELLS
    copies = []
    index = 0
    for source, size in zip(refs, PIECES):
        for part in range(size):
            at = order_ref[index]
            copies.append(
                pltpu.make_async_copy(
                    source.at[part],
                    target.at[pl.ds(pl.multiple_of(at * rows, 16), rows)],
                    sem.at[index],
                )
            )
            index += 1
    for item in copies:
        item.start()
    return copies


def wait_all(copies):
    for item in copies:
        item.wait()


def one_hot(rows, lanes, offset):
    row = lax.broadcasted_iota(jnp.int32, (rows, lanes), 0)
    lane = lax.broadcasted_iota(jnp.int32, (rows, lanes), 1)
    return lane == row + offset


def pack_body(who_ref, lengths_ref, *refs):
    sources, small_ref = refs[:8], refs[8]
    me = who_ref[0]
    model = small_ref.shape[1]
    row = lax.broadcasted_iota(jnp.int32, (SMALL_ROWS, model), 0)
    lane = lax.broadcasted_iota(jnp.int32, (SMALL_ROWS, model), 1)
    small = jnp.zeros((SMALL_ROWS, model), FULL)
    for name, ref in zip(NAMES, sources):
        size = ref.shape[1]
        per_row = model // size
        placed = dot(ref[...], one_hot(size, model, size * (me % per_row)).astype(LOW))
        small = small + jnp.where(row == ROWS[name] + me // per_row, placed, 0.0)
    for i in range(2):
        at = (row == ROWS["lengths"]) & (lane == 2 * me + i)
        small = small + jnp.where(at, lengths_ref[i].astype(FULL), 0.0)
    small_ref[...] = small.astype(LOW)


def norm_parts(values):
    center = values - jnp.mean(values, axis=-1, keepdims=True)
    spread = jnp.mean(center * center, axis=-1, keepdims=True)
    return center, lax.rsqrt(spread + EPSILON)


def norm_back(center, scale, gain, grad):
    weighted = grad * gain
    mean_one = jnp.mean(weighted, axis=-1, keepdims=True)
    mean_two = jnp.mean(weighted * center, axis=-1, keepdims=True)
    back = scale * (weighted - mean_one - center * (scale * scale * mean_two))
    return back, jnp.sum(grad * center * scale, axis=0, keepdims=True), jnp.sum(
        grad, axis=0, keepdims=True
    )


def small_row(small_ref, name, count=1):
    return small_ref[...].astype(FULL)[ROWS[name] : ROWS[name] + count, :]


def project_body(order_ref, x_ref, small_ref, *refs):
    blocks = refs[:9]
    low_ref, proj_ref, weight, sem = refs[9:]
    model = x_ref.shape[1]
    copies = fetch(order_ref, blocks, weight, sem)
    center, scale = norm_parts(x_ref[...].astype(FULL))
    bias = small_row(small_ref, "qv_bias", 2)
    low_ref[...] = (
        center * scale * small_row(small_ref, "first_gain") + small_row(small_ref, "first_shift")
    ).astype(LOW)
    wait_all(copies)
    for j in range(3):
        lanes = slice(j * model, (j + 1) * model)
        part = dot(low_ref[...], weight[:, lanes])
        if j != 1:
            part = part + bias[j // 2 : j // 2 + 1]
        proj_ref[:, lanes] = part.astype(LOW)


def attend_body(seq, lengths_ref, proj_ref, att_ref, mixed_ref):
    model = mixed_ref.shape[1]
    cells = mixed_ref.shape[0] // seq
    pairs = model // (2 * HEAD)
    lane = lax.broadcasted_iota(jnp.int32, (seq, 2 * HEAD), 1)
    key = lax.broadcasted_iota(jnp.int32, (seq, seq), 0)

    def step(index, carry):
        s = index // pairs
        p = index % pairs
        rows = pl.ds(pl.multiple_of(s * seq, seq), seq)
        at = pl.multiple_of(p * 2 * HEAD, 2 * HEAD)
        q = proj_ref[rows, pl.ds(at, 2 * HEAD)] * jnp.asarray(HEAD ** (-0.5), LOW)
        k = proj_ref[rows, pl.ds(at + model, 2 * HEAD)]
        v_turned = proj_ref[rows, pl.ds(at + 2 * model, 2 * HEAD)].T
        visible = key < lengths_ref[s]
        mixed = []
        for i in range(2):
            own = (lane >= i * HEAD) & (lane < (i + 1) * HEAD)
            scores = dot(jnp.where(own, k, jnp.zeros_like(k)), q, ((1,), (1,)))
            scores = jnp.where(visible, scores, NEGATIVE)
            expo = jnp.exp(scores - jnp.max(scores, axis=0, keepdims=True))
            probs = expo * (1.0 / jnp.sum(expo, axis=0, keepdims=True))
            probs = probs.astype(LOW)
            att_ref[2 * index + i] = probs
            mixed.append(dot(v_turned[i * HEAD : (i + 1) * HEAD], probs))
        mixed_ref[rows, pl.ds(at, 2 * HEAD)] = jnp.concatenate(mixed, axis=0).T.astype(LOW)
        return carry

    lax.fori_loop(0, cells * pairs, step, 0, unroll=2)


ERFC_STEP = 0.33
ERFC = (
    0.1863578228018033,
    0.18295566386742124,
    0.2012255082472392,
    0.04721561458875723,
    0.4085089979423051,
    -0.35115900736338407,
    0.4602422572120205,
    -0.13534686486277223,
)


def gelu_parts(inner):
    z = jnp.abs(inner) * (0.5**0.5)
    t = 1.0 / (1.0 + ERFC_STEP * z)
    tail = jnp.full_like(t, 0.5 * ERFC[-1])
    for factor in ERFC[-2::-1]:
        tail = tail * t + 0.5 * factor
    bell = jnp.exp(-(z * z))
    tail = tail * t * bell
    area = jnp.where(inner < 0.0, tail, 1.0 - tail)
    return inner * area, area + inner * bell * (0.5 / 3.141592653589793) ** 0.5


def row_mask(lengths_ref, rows, seq):
    at = lax.broadcasted_iota(jnp.int32, (rows, 1), 0)
    true = (at < lengths_ref[0]).astype(FULL)
    for s in range(1, rows // seq):
        true = jnp.where(at < s * seq, true, (at < lengths_ref[s] + s * seq).astype(FULL))
    return true


def loss_rows(lengths_ref, small_ref, other_ref, cot_ref, seq, whole):
    count = jnp.sum(
        small_row(small_ref, "lengths") + small_row(other_ref, "lengths"), axis=-1, keepdims=True
    )
    return cot_ref[...].astype(FULL) * (
        row_mask(lengths_ref, cot_ref.shape[0], seq) * (whole / count)
    )


def put_slots(keep_buf, slot_ref, values, first, lanes):
    rows = keep_buf.shape[1]
    for i in range(values.shape[0] // rows):
        keep_buf[slot_ref[first + i], :, lanes] = values[i * rows : (i + 1) * rows].astype(LOW)


def send_slots(buf, keep_ref, away_ref, sem):
    half = RING_SIZE
    copies = [
        pltpu.make_async_copy(buf.at[pl.ds(half, half)], away_ref, sem.at[0]),
        pltpu.make_async_copy(buf.at[pl.ds(0, half)], keep_ref, sem.at[1]),
    ]
    for item in copies:
        item.start()
    return copies


def inner_body(order_ref, x_ref, mixed_ref, small_ref, *refs):
    blocks = refs[:9]
    middle_ref, low_ref, active_ref, slope_ref, weight, sem = refs[9:]
    model = x_ref.shape[1]
    ff = active_ref.shape[1]
    wait_all(fetch(order_ref, blocks, weight, sem))
    middle = (
        x_ref[...].astype(FULL)
        + dot(mixed_ref[...], weight[:, ff:])
        + small_row(small_ref, "out_bias")
    )
    middle_ref[...] = middle
    center, scale = norm_parts(middle)
    low = center * scale * small_row(small_ref, "second_gain") + small_row(
        small_ref, "second_shift"
    )
    low_ref[...] = low.astype(LOW)
    step = 2 * (ff // RING_SIZE)
    bias = small_row(small_ref, "in_bias", 4)
    for j in range(ff // step):
        lanes = slice(j * step, (j + 1) * step)
        inner = dot(low_ref[...], weight[:, lanes]) + bias[j : j + 1]
        active, slope = gelu_parts(inner)
        active_ref[:, lanes] = active.astype(LOW)
        slope_ref[:, lanes] = slope.astype(LOW)


def grad_down_body(
    seq, whole, who_ref, slot_ref, lengths_ref, active_ref, cot_ref, small_ref, other_ref,
    up_ref, down_b_ref, keep_ref, away_ref, keep_two_ref, away_two_ref, slots, sem,
):
    up_low = loss_rows(lengths_ref, small_ref, other_ref, cot_ref, seq, whole).astype(LOW)
    up_ref[...] = up_low
    down_b_ref[...] = jnp.sum(up_low.astype(FULL), axis=0, keepdims=True)
    parts = RING_SIZE
    step = active_ref.shape[1] // parts
    rows = slots.shape[2]
    side = who_ref[1]
    for j in range(parts):
        grad = dot(active_ref[:, j * step : (j + 1) * step], up_ref[...], ((0,), (0,)))
        for i in range(4):
            slots[(i + side) % 2, slot_ref[j * CELLS // parts + i // 2]] = grad[
                i * rows : (i + 1) * rows
            ].astype(LOW)
    copies = send_slots(slots.at[1], keep_two_ref, away_two_ref, sem.at[1])
    copies += send_slots(slots.at[0], keep_ref, away_ref, sem.at[0])
    wait_all(copies)


def inner_back_body(order_ref, slope_ref, up_ref, *refs):
    blocks = refs[:9]
    inner_ref, in_b_ref, weight, sem = refs[9:]
    model = up_ref.shape[1]
    wait_all(fetch(order_ref, blocks, weight, sem))
    for j in range(inner_ref.shape[1] // model):
        lanes = slice(j * model, (j + 1) * model)
        grad = dot(up_ref[...], weight[lanes, :], ((1,), (1,)))
        low = (grad * slope_ref[:, lanes].astype(FULL)).astype(LOW)
        inner_ref[:, lanes] = low
        in_b_ref[j : j + 1, :] = jnp.sum(low.astype(FULL), axis=0, keepdims=True)


def down_body(active_ref, middle_ref, small_ref, weight_ref, out_ref):
    out_ref[...] = (
        middle_ref[...]
        + dot(active_ref[...], weight_ref[...])
        + small_row(small_ref, "down_bias")
    ).astype(LOW)


def grad_in_body(slot_ref, low_ref, inner_ref, keep_ref, away_ref, slots, sem):
    model = low_ref.shape[1]
    turned = low_ref[...].T
    for j in range(inner_ref.shape[1] // model):
        lanes = slice(j * model, (j + 1) * model)
        put_slots(slots, slot_ref, dot(turned, inner_ref[:, lanes]), 0, lanes)
    wait_all(send_slots(slots, keep_ref, away_ref, sem))


def middle_back_body(
    seq, whole, lengths_ref, inner_ref, middle_ref, cot_ref, small_ref, other_ref, weight,
    grad_ref, grad_low_ref, grad_mixed_ref, sums_ref,
):
    ff = inner_ref.shape[1]
    grad_second = dot(inner_ref[...], weight[:, :ff], ((1,), (1,)))
    center, scale = norm_parts(middle_ref[...])
    back, gain_sum, shift_sum = norm_back(
        center, scale, small_row(small_ref, "second_gain"), grad_second
    )
    grad = loss_rows(lengths_ref, small_ref, other_ref, cot_ref, seq, whole) + back
    grad_ref[...] = grad
    grad_low = grad.astype(LOW)
    grad_low_ref[...] = grad_low
    grad_mixed_ref[...] = dot(grad_low, weight[:, ff:], ((1,), (1,))).astype(LOW)
    sums_ref[0:1, :] = jnp.sum(grad_low.astype(FULL), axis=0, keepdims=True)
    sums_ref[1:2, :] = gain_sum
    sums_ref[2:3, :] = shift_sum


def attend_back_body(seq, begin, proj_ref, att_ref, grad_ref, out_ref):
    model = grad_ref.shape[1]
    half = out_ref.shape[1] // 3
    all_pairs = model // (2 * HEAD)
    pairs = half // (2 * HEAD)
    cells = grad_ref.shape[0] // seq
    lane = lax.broadcasted_iota(jnp.int32, (seq, 2 * HEAD), 1)
    scale = HEAD ** (-0.5)

    def step(index, carry):
        s = index // pairs
        p = index % pairs
        rows = pl.ds(pl.multiple_of(s * seq, seq), seq)
        to = pl.multiple_of(p * 2 * HEAD, 2 * HEAD)
        at = pl.multiple_of(to + begin * 2 * HEAD, 2 * HEAD)
        q = proj_ref[rows, pl.ds(at, 2 * HEAD)]
        k_turned = proj_ref[rows, pl.ds(at + model, 2 * HEAD)].T
        v = proj_ref[rows, pl.ds(at + 2 * model, 2 * HEAD)]
        g = grad_ref[rows, pl.ds(at, 2 * HEAD)]
        grad_q = []
        grad_k = []
        grad_v = []
        for i in range(2):
            own = (lane >= i * HEAD) & (lane < (i + 1) * HEAD)
            probs = att_ref[2 * (s * all_pairs + begin + p) + i]
            wide = probs.astype(FULL)
            grad_probs = dot(jnp.where(own, v, jnp.zeros_like(v)), g, ((1,), (1,)))
            delta = jnp.sum(wide * grad_probs, axis=0, keepdims=True)
            scores = (wide * (grad_probs - delta)).astype(LOW)
            grad_q.append(dot(k_turned[i * HEAD : (i + 1) * HEAD], scores))
            grad_k.append(dot(scores, q))
            grad_v.append(dot(probs, g))
        first = lane < HEAD
        out_ref[rows, pl.ds(to, 2 * HEAD)] = (
            jnp.concatenate(grad_q, axis=0).T * scale
        ).astype(LOW)
        out_ref[rows, pl.ds(to + half, 2 * HEAD)] = (
            jnp.where(first, grad_k[0], grad_k[1]) * scale
        ).astype(LOW)
        out_ref[rows, pl.ds(to + 2 * half, 2 * HEAD)] = jnp.where(
            first, grad_v[0], grad_v[1]
        ).astype(LOW)
        return carry

    lax.fori_loop(0, cells * pairs, step, 0, unroll=2)


def early_grad_body(
    slot_ref, low_ref, part_ref, mixed_ref, grad_low_ref, keep_ref, away_ref, slots, sem
):
    width = part_ref.shape[1]
    put_slots(slots, slot_ref, dot(low_ref[...].T, part_ref[...]), 0, slice(0, width))
    put_slots(
        slots, slot_ref, dot(mixed_ref[...].T, grad_low_ref[...]), 0,
        slice(width, slots.shape[2]),
    )
    wait_all(send_slots(slots, keep_ref, away_ref, sem))


def first_back_body(
    slot_ref, x_ref, low_ref, one_ref, two_ref, grad_ref, small_ref, sums_ref, in_b_ref,
    down_b_ref, weight, out_ref, keep_ref, away_ref, sum_ref, slots, sem,
):
    model = x_ref.shape[1]
    late = two_ref.shape[1]
    center, scale = norm_parts(x_ref[...].astype(FULL))
    parts = ((one_ref, 0), (two_ref, one_ref.shape[1] // 3))
    grad_first = jnp.zeros(x_ref.shape, FULL)
    for j in range(3):
        for ref, begin in parts:
            width = ref.shape[1] // 3
            at = j * model + begin
            grad_first = grad_first + dot(
                ref[:, j * width : (j + 1) * width], weight[:, at : at + width], ((1,), (1,))
            )
    put_slots(slots, slot_ref, dot(low_ref[...].T, two_ref[...]), 0, slice(0, late))
    back, gain_sum, shift_sum = norm_back(
        center, scale, small_row(small_ref, "first_gain"), grad_first
    )

    def put(name, value, offset=0):
        at = ROWS[name] + offset
        sum_ref[at : at + value.shape[0], :] = value

    sum_ref[...] = jnp.zeros_like(sum_ref)
    put("first_gain", gain_sum)
    put("first_shift", shift_sum)
    for j in range(2):
        at = ROWS["qv_bias"] + j
        for ref, begin in parts:
            width = ref.shape[1] // 3
            part = ref[:, 2 * j * width : (2 * j + 1) * width].astype(FULL)
            sum_ref[at : at + 1, begin : begin + width] = jnp.sum(part, axis=0, keepdims=True)
    put("out_bias", sums_ref[0:1, :])
    put("second_gain", sums_ref[1:2, :])
    put("second_shift", sums_ref[2:3, :])
    put("in_bias", in_b_ref[...])
    put("down_bias", down_b_ref[...])
    for i in range(3):
        part = sum_ref[:, SMALL_LANES * i : SMALL_LANES * (i + 1)].astype(LOW)
        for device in range(CELLS):
            slots[device, 16 * i : 16 * i + 16, late:] = part
    copies = send_slots(slots, keep_ref, away_ref, sem)
    out_ref[...] = (grad_ref[...] + back).astype(LOW)
    wait_all(copies)


def finish_body(who_ref, early_ref, early_two_ref, late_ref, late_two_ref, *refs):
    grad_ref, out_ref, vectors, small_ref = refs[0], refs[1], refs[2:-1], refs[-1]
    model = out_ref.shape[1]
    early = early_ref[...].astype(FULL) + early_two_ref[...].astype(FULL)
    late = late_ref[...].astype(FULL) + late_two_ref[...].astype(FULL)
    one = (early.shape[1] - model) // 3
    two = (late.shape[1] - SMALL_LANES) // 3
    for j in range(3):
        at = j * model
        grad_ref[:, at : at + one] = early[:, j * one : (j + 1) * one]
        grad_ref[:, at + one : at + model] = late[:, j * two : (j + 1) * two]
    out_ref[...] = early[:, 3 * one :]
    for i in range(3):
        small_ref[:, SMALL_LANES * i : SMALL_LANES * (i + 1)] = late[
            16 * i : 16 * i + 16, 3 * two :
        ]
    me = who_ref[0]
    row = lax.broadcasted_iota(jnp.int32, (SMALL_ROWS, model), 0)
    for name, ref in zip(NAMES, vectors):
        size = ref.shape[1]
        per_row = model // size
        here_row = jnp.where(row == ROWS[name] + me // per_row, small_ref[...], 0.0)
        values = jnp.sum(here_row, axis=0, keepdims=True)
        picker = one_hot(size, model, size * (me % per_row)).astype(FULL)
        ref[...] = lax.dot_general(
            values, picker, (((1,), (1,)), ((), ())), precision=lax.Precision.HIGHEST,
            preferred_element_type=FULL,
        )


def on_device_ring(
    tokens,
    lengths,
    cotangent,
    first_gain,
    first_shift,
    qkv_weight,
    qv_bias,
    out_weight,
    out_bias,
    second_gain,
    second_shift,
    in_weight,
    in_bias,
    down_weight,
    down_bias,
):
    micro, seq, model = tokens.shape[1:]
    total_rows = micro * seq
    rows = qkv_weight.shape[0]
    down_rows = down_weight.shape[0]
    ff = in_weight.shape[1]
    heads = model // HEAD
    whole = float(lax.axis_size("species") * CELLS * micro * seq)
    index, core, place = here()
    species = lax.axis_index("species")
    who = jnp.stack([index, species]).astype(jnp.int32)
    order = jnp.stack(gather_order(core, place)).astype(jnp.int32)
    slot = jnp.stack(scatter_slots(core, place)).astype(jnp.int32)
    lens = lengths.reshape(micro)
    x = tokens.reshape(total_rows, model)
    cot = cotangent.reshape(total_rows, model)
    vectors = (
        first_gain, first_shift, qv_bias, out_bias, second_gain, second_shift, in_bias, down_bias,
    )

    dma = pltpu.SemaphoreType.DMA

    def gathered(own, hops):
        got = [own]
        for item in hops:
            got += [item, to_partner(item)]
        return got

    own = both_blocks(qkv_weight, core)
    qkv_one = hop(own)
    (small,) = call(
        pack_body,
        [shape((SMALL_ROWS, model))],
        [who, after(lens, own)] + [item.reshape(1, -1) for item in vectors],
        [SMEM, SMEM] + [VMEM] * 8,
        vmem=4,
    )
    small = exchange(small, 1)
    in_weight, out_weight = lax.optimization_barrier((in_weight, out_weight, own))[:2]
    in_own = both_blocks(jnp.concatenate([in_weight, out_weight], axis=1), core)
    qkv_one, small, in_own = lax.optimization_barrier((qkv_one, small, in_own))
    qkv_two = hop(qkv_one)
    small = exchange(small, 2)
    down_own = both_blocks(after(down_weight, qkv_one), core)
    qkv_two, small, down_own = lax.optimization_barrier((qkv_two, small, down_own))
    qkv_three = hop(qkv_two)
    small = exchange(small, 4)
    qkv_three, small = lax.optimization_barrier((qkv_three, small))
    qkv_last = hop(half_of(qkv_three, core))
    small = exchange(small, 8)
    in_one = hop(after(in_own, qkv_three))
    low, proj, qkv_full = call(
        project_body,
        [
            shape((total_rows, model)),
            shape((total_rows, 3 * model)),
            shape((model, 3 * model)),
        ],
        [order, after(x, in_one), small] + gathered(own, (qkv_one, qkv_two, qkv_three, qkv_last)),
        [SMEM, VMEM, VMEM] + [ANY] * 9,
        scratch=[dma((CELLS,))],
        vmem=20,
    )
    other_small = across(small)
    in_two = hop(in_one)
    down_one = hop(after(down_own, in_one))
    att, mixed = call(
        lambda *refs: attend_body(seq, *refs),
        [shape((micro * heads, seq, seq)), shape((total_rows, model))],
        [lens, proj],
        [SMEM, VMEM],
        vmem=12,
    )
    in_two, mixed, down_one = lax.optimization_barrier((in_two, mixed, down_one))
    in_three = hop(in_two)
    down_two = hop(after(down_one, in_two))
    in_last = hop(half_of(after(in_three, down_two), core))
    down_three = hop(after(down_two, in_three))
    in_got = gathered(in_own, (in_one, in_two, in_three, in_last))
    middle, low_two, active, slope, in_full = call(
        inner_body,
        [
            shape((total_rows, model), FULL),
            shape((total_rows, model)),
            shape((total_rows, ff)),
            shape((total_rows, ff)),
            shape((model, ff + model)),
        ],
        [order, x, after(mixed, down_two), small] + in_got,
        [SMEM] + [VMEM] * 3 + [ANY] * 9,
        scratch=[dma((CELLS,))],
        vmem=24,
    )
    down_three, active = lax.optimization_barrier((down_three, active))
    down_last = hop(half_of(down_three, core))
    up_low, down_b, down_keep, down_away, down_keep_two, down_away_two = call(
        lambda *refs: grad_down_body(seq, whole, *refs),
        [
            shape((total_rows, model)),
            shape((1, model), FULL),
        ]
        + [shape((RING_SIZE, down_rows // 2, model))] * 4,
        [who, slot, lens, active, cot, small, other_small],
        [SMEM] * 3 + [VMEM] * 4,
        [VMEM] * 2 + [ANY] * 4,
        scratch=[pltpu.VMEM((2, CELLS, down_rows // 2, model), LOW), dma((2, 2))],
        vmem=15,
    )

    down_away, down_away_two, down_last = lax.optimization_barrier(
        (down_away, down_away_two, down_last)
    )
    down_other_two = to_partner(down_away_two)
    down_other = to_partner(down_away)
    inner_low, in_b, down_full = call(
        inner_back_body,
        [
            shape((total_rows, ff)),
            shape((ff // model, model), FULL),
            shape((ff, model)),
        ],
        [order, slope, up_low]
        + gathered(down_own, (down_one, down_two, down_three, down_last)),
        [SMEM] + [VMEM] * 2 + [ANY] * 9,
        scratch=[dma((CELLS,))],
        vmem=20,
    )
    down_other_two, inner_low = lax.optimization_barrier((down_other_two, inner_low))
    down_x = across(add_low(down_keep_two[0:3], down_other_two[0:3]))
    down_x_two = across(add_low(down_keep_two[3:8], down_other_two[3:8]))
    in_keep, in_away = call(
        grad_in_body,
        [shape((RING_SIZE, rows, ff)), shape((RING_SIZE, rows, ff))],
        [slot, low_two, inner_low],
        [SMEM] + [VMEM] * 2,
        [ANY] * 2,
        scratch=[pltpu.VMEM((CELLS, rows, ff), LOW), dma((2,))],
        vmem=13,
    )
    in_other = to_partner(in_away)
    (out_tokens,) = call(
        down_body,
        [shape((total_rows, model))],
        [after(active, in_keep), middle, small, down_full],
        [VMEM] * 4,
        vmem=13,
    )
    in_other, out_tokens, inner_low = lax.optimization_barrier((in_other, out_tokens, inner_low))
    in_sum = first_hop(in_keep, in_other)
    grad_middle, grad_low, grad_mixed, sums = call(
        lambda *refs: middle_back_body(seq, whole, *refs),
        [
            shape((total_rows, model), FULL),
            shape((total_rows, model)),
            shape((total_rows, model)),
            shape((3, model), FULL),
        ],
        [lens, inner_low, middle, cot, small, other_small, in_full],
        [SMEM] + [VMEM] * 6,
        vmem=19,
    )

    def attend_back(begin, pairs, grad):
        return call(
            lambda *refs: attend_back_body(seq, begin, *refs),
            [shape((total_rows, 6 * pairs * HEAD))],
            [proj, att, grad],
            [VMEM] * 3,
            vmem=11,

        )[0]

    pairs = model // (2 * HEAD)
    early_pairs = 2 * pairs // 3
    in_sum, down_x, down_other, grad_mixed = lax.optimization_barrier(
        (in_sum, down_x, down_other, grad_mixed)
    )
    down_sum = first_hop(down_keep, down_other, down_x)
    in_sum = second_hop(in_sum, core, in_keep, in_other)
    grad_one = attend_back(0, early_pairs, grad_mixed)
    down_sum, grad_one = lax.optimization_barrier((down_sum, grad_one))
    down_sum = second_hop(down_sum, core, down_keep, down_other, down_x)
    early_width = 6 * early_pairs * HEAD + model
    early_keep, early_away = call(
        early_grad_body,
        [shape((RING_SIZE, rows, early_width))] * 2,
        [slot, low, grad_one, mixed, grad_low],
        [SMEM] + [VMEM] * 4,
        [ANY] * 2,
        scratch=[pltpu.VMEM((CELLS, rows, early_width), LOW), dma((2,))],
        vmem=12,
    )
    early_other = to_partner(early_away)
    in_sum, early_keep, grad_mixed = lax.optimization_barrier((in_sum, early_keep, grad_mixed))
    in_sum = later_hop(in_sum, 3, in_keep, in_other)
    grad_two = attend_back(early_pairs, pairs - early_pairs, grad_mixed)
    early_other, grad_two = lax.optimization_barrier((early_other, grad_two))
    early_sum = first_hop(early_keep, early_other)
    late_width = 6 * (pairs - early_pairs) * HEAD + SMALL_LANES
    grad_tokens, late_keep, late_away = call(
        first_back_body,
        [
            shape((total_rows, model)),
            shape((RING_SIZE, rows, late_width)),
            shape((RING_SIZE, rows, late_width)),
        ],
        [slot, x, low, grad_one, grad_two, grad_middle, small, sums, in_b, down_b, qkv_full],
        [SMEM] + [VMEM] * 10,
        [VMEM] + [ANY] * 2,
        scratch=[
            pltpu.VMEM((SMALL_ROWS, model), FULL),
            pltpu.VMEM((CELLS, rows, late_width), LOW),
            dma((2,)),
        ],
        vmem=16,

    )
    late_other = to_partner(late_away)
    in_sum, early_sum, late_keep, down_sum, down_x_two = lax.optimization_barrier(
        (in_sum, early_sum, late_keep, down_sum, down_x_two)
    )
    in_sum = later_hop(in_sum, 5, in_keep, in_other)
    early_sum = second_hop(early_sum, core, early_keep, early_other)
    down_sum = hop(add_low(down_sum, down_keep[3:5], down_other[3:5], down_x_two[0:2]))
    late_sum = first_hop(late_keep, late_other)
    late_sum, early_sum, down_sum = lax.optimization_barrier((late_sum, early_sum, down_sum))
    down_sum = hop(add_low(down_sum, down_keep[5:7], down_other[5:7], down_x_two[2:4]))
    late_sum = second_hop(late_sum, core, late_keep, late_other)
    early_sum = later_hop(early_sum, 3, early_keep, early_other)
    late_sum, early_sum, down_sum, in_sum = lax.optimization_barrier(
        (late_sum, early_sum, down_sum, in_sum)
    )
    late_sum = later_hop(late_sum, 3, late_keep, late_other)
    early_sum = later_hop(early_sum, 5, early_keep, early_other)
    in_sum = settle(in_sum, core, in_keep, in_other)
    in_terms = (in_sum, across(in_sum))
    mine = jnp.where(core == 0, down_sum[0], down_sum[1])
    other = to_partner(jnp.where(core == 0, down_sum[1], down_sum[0]))
    down_sum = add_low(mine, other, down_keep[7], down_other[7], down_x_two[4])
    down_terms = (down_sum, across(down_sum))
    late_sum = later_hop(late_sum, 5, late_keep, late_other)
    early_sum = settle(early_sum, core, early_keep, early_other)
    early_terms = (early_sum, across(early_sum))
    late_sum = settle(late_sum, core, late_keep, late_other)
    late_terms = (late_sum, across(late_sum))
    finished = call(
        finish_body,
        [shape((rows, 3 * model), FULL), shape((rows, model), FULL)]
        + [shape((1, item.shape[0]), FULL) for item in vectors],
        [who] + list(early_terms) + list(late_terms),
        [SMEM] + [VMEM] * 4,
        scratch=[pltpu.VMEM((SMALL_ROWS, model), FULL)],
        vmem=6,
    )
    grad_qkv, grad_out = finished[:2]
    pieces = [item.reshape(-1) for item in finished[2:]]
    return (
        out_tokens.reshape(tokens.shape),
        grad_tokens.reshape(tokens.shape),
        pieces[0],
        pieces[1],
        grad_qkv,
        pieces[2],
        grad_out,
        pieces[3],
        pieces[4],
        pieces[5],
        in_terms[0].astype(FULL) + in_terms[1].astype(FULL),
        pieces[6],
        jnp.concatenate(
            [
                jnp.where(species == 0, down_terms[0], down_terms[1]),
                jnp.where(species == 0, down_terms[1], down_terms[0]),
            ]
        ).astype(FULL),
        pieces[7],
    )


def on_device(
    tokens,
    lengths,
    cotangent,
    first_gain,
    first_shift,
    qkv_weight,
    qv_bias,
    out_weight,
    out_bias,
    second_gain,
    second_shift,
    in_weight,
    in_bias,
    down_weight,
    down_bias,
):
    local_count = jnp.sum(lengths).astype(jnp.float32)
    count = lax.psum(local_count, ("species", "cells"))
    micro_count = tokens.shape[1]
    seq_rows = tokens.shape[2]
    factor = (
        float(lax.axis_size("species") * lax.axis_size("cells") * micro_count * seq_rows) / count
    )
    output_rows = []
    gradient_rows = []
    summed = None
    for micro_step in range(micro_count):
        gathered = (
            lax.all_gather(first_gain, "cells", axis=0, tiled=True),
            lax.all_gather(first_shift, "cells", axis=0, tiled=True),
            lax.all_gather(qkv_weight, "cells", axis=0, tiled=True),
            lax.all_gather(qv_bias, "cells", axis=0, tiled=True),
            lax.all_gather(out_weight, "cells", axis=0, tiled=True),
            lax.all_gather(out_bias, "cells", axis=0, tiled=True),
            lax.all_gather(second_gain, "cells", axis=0, tiled=True),
            lax.all_gather(second_shift, "cells", axis=0, tiled=True),
            lax.all_gather(in_weight, "cells", axis=0, tiled=True),
            lax.all_gather(in_bias, "cells", axis=0, tiled=True),
            lax.all_gather(down_weight, "cells", axis=0, tiled=True),
            lax.all_gather(down_bias, "cells", axis=0, tiled=True),
        )
        out_seq, grad_seq, grads = sequence_pass(
            gathered,
            tokens[0, micro_step],
            lengths[0, micro_step],
            cotangent[0, micro_step],
            factor,
        )
        output_rows.append(out_seq)
        gradient_rows.append(grad_seq)
        shares = (
            lax.psum_scatter(grads[0], "cells", scatter_dimension=0, tiled=True),
            lax.psum_scatter(grads[1], "cells", scatter_dimension=0, tiled=True),
            lax.psum_scatter(grads[2], "cells", scatter_dimension=0, tiled=True),
            lax.psum_scatter(grads[3], "cells", scatter_dimension=0, tiled=True),
            lax.psum_scatter(grads[4], "cells", scatter_dimension=0, tiled=True),
            lax.psum_scatter(grads[5], "cells", scatter_dimension=0, tiled=True),
            lax.psum_scatter(grads[6], "cells", scatter_dimension=0, tiled=True),
            lax.psum_scatter(grads[7], "cells", scatter_dimension=0, tiled=True),
            lax.psum_scatter(grads[8], "cells", scatter_dimension=0, tiled=True),
            lax.psum_scatter(grads[9], "cells", scatter_dimension=0, tiled=True),
            lax.psum_scatter(grads[10], "cells", scatter_dimension=0, tiled=True),
            lax.psum_scatter(grads[11], "cells", scatter_dimension=0, tiled=True),
        )
        summed = shares if summed is None else jax.tree.map(jnp.add, summed, shares)
    final = (
        lax.psum(summed[0].astype(jnp.bfloat16), "species").astype(jnp.float32),
        lax.psum(summed[1].astype(jnp.bfloat16), "species").astype(jnp.float32),
        lax.psum(summed[2].astype(jnp.bfloat16), "species").astype(jnp.float32),
        lax.psum(summed[3].astype(jnp.bfloat16), "species").astype(jnp.float32),
        lax.psum(summed[4].astype(jnp.bfloat16), "species").astype(jnp.float32),
        lax.psum(summed[5].astype(jnp.bfloat16), "species").astype(jnp.float32),
        lax.psum(summed[6].astype(jnp.bfloat16), "species").astype(jnp.float32),
        lax.psum(summed[7].astype(jnp.bfloat16), "species").astype(jnp.float32),
        lax.psum(summed[8].astype(jnp.bfloat16), "species").astype(jnp.float32),
        lax.psum(summed[9].astype(jnp.bfloat16), "species").astype(jnp.float32),
        lax.psum(summed[10].astype(jnp.bfloat16), "species").astype(jnp.float32),
        lax.psum(summed[11].astype(jnp.bfloat16), "species").astype(jnp.float32),
    )
    out_tokens = jnp.stack(output_rows)[None]
    grad_tokens = jnp.stack(gradient_rows)[None]
    return (out_tokens, grad_tokens) + tuple(final)


def solution(mesh):
    in_specs = (
        P("species", "cells", None, None),
        P("species", "cells"),
        P("species", "cells", None, None),
        P("cells"),
        P("cells"),
        P("cells", None),
        P("cells"),
        P("cells", None),
        P("cells"),
        P("cells"),
        P("cells"),
        P("cells", None),
        P("cells"),
        P("cells", None),
        P("cells"),
    )
    out_specs = (
        P("species", "cells", None, None),
        P("species", "cells", None, None),
        P("cells"),
        P("cells"),
        P("cells", None),
        P("cells"),
        P("cells", None),
        P("cells"),
        P("cells"),
        P("cells"),
        P("cells", None),
        P("cells"),
        P("cells", None),
        P("cells"),
    )
    program = on_device_ring if mesh.shape["cells"] == 2 * RING_SIZE else on_device
    return jax.shard_map(
        program, mesh=mesh, in_specs=in_specs, out_specs=out_specs, check_vma=False
    )
```

```python
import jax
import jax.numpy as jnp
from jax import lax
from jax.experimental import pallas as pl
from jax.experimental.pallas import tpu as pltpu
from jax.sharding import PartitionSpec as P

HEAD = 64


EPSILON = 1e-12
NEGATIVE = -1e30


def normalize(values, gain_vec, shift_vec):
    center = values - jnp.mean(values, axis=-1, keepdims=True)
    spread = jnp.mean(center * center, axis=-1, keepdims=True)
    return center * lax.rsqrt(spread + EPSILON) * gain_vec + shift_vec


def smooth_gate(values):
    return jax.nn.gelu(values, approximate=False)


def times_left(left_side, right_side):
    return lax.dot_general(
        left_side, right_side, (((0,), (0,)), ((), ())), preferred_element_type=jnp.float32
    )


def times_right(left_side, right_side):
    return lax.dot_general(
        left_side, right_side, (((1,), (1,)), ((), ())), preferred_element_type=jnp.float32
    )


def sequence_pass(weights, inputs, length, cot_rows, factor):
    (
        first_gain,
        first_shift,
        qkv_weight,
        qv_bias,
        out_weight,
        out_bias,
        second_gain,
        second_shift,
        in_weight,
        in_bias,
        down_weight,
        down_bias,
    ) = weights
    seq_rows = inputs.shape[0]
    model_width = inputs.shape[1]
    heads_count = model_width // HEAD
    scale_qk = float(HEAD) ** (-0.5)
    as_float = inputs.astype(jnp.float32)
    hidden_one, first_pull = jax.vjp(
        normalize, as_float, first_gain.astype(jnp.float32), first_shift.astype(jnp.float32)
    )
    first_low = hidden_one.astype(jnp.bfloat16)
    bias_float = qv_bias.astype(jnp.float32)
    full_bias = jnp.concatenate(
        [bias_float[:model_width], jnp.zeros((model_width,), jnp.float32), bias_float[model_width:]]
    )
    projected = (
        jnp.dot(first_low, qkv_weight, preferred_element_type=jnp.float32) + full_bias
    ).astype(jnp.bfloat16)
    split_heads = projected.reshape(seq_rows, 3, heads_count, HEAD)
    queries = split_heads[:, 0]
    keys_part = split_heads[:, 1]
    values_part = split_heads[:, 2]
    visible = jnp.arange(seq_rows) < length

    def scores_of():
        raw_scores = (
            jnp.einsum("qhd,khd->hqk", queries, keys_part, preferred_element_type=jnp.float32)
            * scale_qk
        )
        return jnp.where(visible[None, None, :], raw_scores, NEGATIVE)

    scores = scores_of()
    top_score = jnp.max(scores, axis=-1, keepdims=True)
    expo = jnp.exp(scores - top_score)
    total_exp = jnp.sum(expo, axis=-1, keepdims=True)
    log_total = top_score + jnp.log(total_exp)
    attention = (expo / total_exp).astype(jnp.bfloat16)
    mixed = jnp.einsum("hqk,khd->qhd", attention, values_part, preferred_element_type=jnp.float32)
    mixed = mixed.reshape(seq_rows, model_width).astype(jnp.bfloat16)
    middle = (
        as_float
        + jnp.dot(mixed, out_weight, preferred_element_type=jnp.float32)
        + out_bias.astype(jnp.float32)
    )
    hidden_two, second_pull = jax.vjp(
        normalize, middle, second_gain.astype(jnp.float32), second_shift.astype(jnp.float32)
    )
    second_low = hidden_two.astype(jnp.bfloat16)
    inner = jnp.dot(second_low, in_weight, preferred_element_type=jnp.float32) + in_bias.astype(
        jnp.float32
    )
    active, gate_pull = jax.vjp(smooth_gate, inner)
    active_low = active.astype(jnp.bfloat16)
    output = (
        middle
        + jnp.dot(active_low, down_weight, preferred_element_type=jnp.float32)
        + down_bias.astype(jnp.float32)
    )
    upstream = cot_rows.astype(jnp.float32) * visible[:, None].astype(jnp.float32) * factor
    up_low = upstream.astype(jnp.bfloat16)
    grad_down_bias = jnp.sum(up_low.astype(jnp.float32), axis=0)
    grad_down = times_left(active_low, up_low)
    grad_active = times_right(up_low, down_weight)
    (grad_inner,) = gate_pull(grad_active)
    inner_low = grad_inner.astype(jnp.bfloat16)
    grad_in_bias = jnp.sum(inner_low.astype(jnp.float32), axis=0)
    grad_in = times_left(second_low, inner_low)
    grad_second = times_right(inner_low, in_weight)
    grad_middle_norm, grad_second_gain, grad_second_shift = second_pull(grad_second)
    grad_middle = upstream + grad_middle_norm
    middle_low = grad_middle.astype(jnp.bfloat16)
    grad_out_bias = jnp.sum(middle_low.astype(jnp.float32), axis=0)
    grad_out = times_left(mixed, middle_low)
    grad_mixed = (
        times_right(middle_low, out_weight)
        .astype(jnp.bfloat16)
        .reshape(seq_rows, heads_count, HEAD)
    )
    probs_again = jnp.exp(scores_of() - log_total)
    grad_probs = jnp.einsum(
        "qhd,khd->hqk", grad_mixed, values_part, preferred_element_type=jnp.float32
    )
    grad_values = jnp.einsum(
        "hqk,qhd->khd", attention, grad_mixed, preferred_element_type=jnp.float32
    )
    delta = jnp.sum(probs_again * grad_probs, axis=-1, keepdims=True)
    grad_scores = (probs_again * (grad_probs - delta)).astype(jnp.bfloat16)
    grad_queries = (
        jnp.einsum("hqk,khd->qhd", grad_scores, keys_part, preferred_element_type=jnp.float32)
        * scale_qk
    )
    grad_keys = (
        jnp.einsum("hqk,qhd->khd", grad_scores, queries, preferred_element_type=jnp.float32)
        * scale_qk
    )
    grad_projected = jnp.stack([grad_queries, grad_keys, grad_values], axis=1)
    grad_projected = grad_projected.reshape(seq_rows, 3 * model_width).astype(jnp.bfloat16)
    column_sums = jnp.sum(grad_projected.astype(jnp.float32), axis=0)
    grad_qv = jnp.concatenate([column_sums[:model_width], column_sums[2 * model_width :]])
    grad_qkv = times_left(first_low, grad_projected)
    grad_first = times_right(grad_projected, qkv_weight)
    grad_input_norm, grad_first_gain, grad_first_shift = first_pull(grad_first)
    grad_inputs = grad_middle + grad_input_norm
    grads = (
        grad_first_gain,
        grad_first_shift,
        grad_qkv,
        grad_qv,
        grad_out,
        grad_out_bias,
        grad_second_gain,
        grad_second_shift,
        grad_in,
        grad_in_bias,
        grad_down,
        grad_down_bias,
    )
    return (output.astype(jnp.bfloat16), grad_inputs.astype(jnp.bfloat16), grads)


RING = (0, 2, 4, 6, 7, 5, 3, 1)
RING_SIZE = len(RING)
CELLS = 2 * RING_SIZE
ANY = pl.BlockSpec(memory_space=pl.ANY)
HBM = pl.BlockSpec(memory_space=pltpu.HBM)
VMEM = pl.BlockSpec(memory_space=pltpu.VMEM)
SMEM = pl.BlockSpec(memory_space=pltpu.SMEM)
LOW = jnp.bfloat16
FULL = jnp.float32
HEAVY = 10**10
UNIT = 10**8
ROWS = {
    "first_gain": 0,
    "first_shift": 1,
    "qv_bias": 2,
    "out_bias": 4,
    "second_gain": 5,
    "second_shift": 6,
    "in_bias": 7,
    "down_bias": 11,
    "lengths": 12,
}
NAMES = tuple(ROWS)[:8]
SMALL_ROWS = 16
SMALL_LANES = 256
PIECES = (2, 2, 2, 2, 2, 2, 2, 1, 1)


def ring_pairs():
    pairs = []
    for place in range(RING_SIZE):
        chip = RING[place]
        right = RING[(place + 1) % RING_SIZE]
        left = RING[(place - 1) % RING_SIZE]
        pairs.append((2 * chip, 2 * right))
        pairs.append((2 * chip + 1, 2 * left + 1))
    return pairs


def hop(block):
    return lax.ppermute(block, "cells", ring_pairs())


def to_partner(block):
    return lax.ppermute(block, "cells", [(i, i ^ 1) for i in range(CELLS)])


def across(block):
    return lax.ppermute(block, "species", [(0, 1), (1, 0)])


def exchange(values, bit):
    return values + lax.ppermute(values, "cells", [(i, i ^ bit) for i in range(CELLS)])


def after(value, *others):
    return lax.optimization_barrier((value,) + others)[0]


def here():
    index = lax.axis_index("cells")
    core = index % 2
    chip = index // 2
    place = jnp.int32(0)
    for i, ring_chip in enumerate(RING):
        place = jnp.where(chip == ring_chip, i, place)
    return index, core, place


def chip_at(place):
    place = place % RING_SIZE
    chip = jnp.zeros_like(place)
    for i, ring_chip in enumerate(RING):
        chip = jnp.where(place == i, ring_chip, chip)
    return chip


def gather_order(core, place):
    sign = 1 - 2 * core
    order = []

    def pair(at):
        order.append(2 * chip_at(at))
        order.append(2 * chip_at(at) + 1)

    pair(place)
    for step in range(1, 4):
        pair(place - sign * step)
        pair(place + sign * step)
    order.append(2 * chip_at(place + 4) + core)
    order.append(2 * chip_at(place + 4) + 1 - core)
    return order


def scatter_slots(core, place):
    def kept(core_now):
        sign = 1 - 2 * core_now
        order = [2 * chip_at(place + 4) + core_now]
        for step in (3, 2, 1):
            order.append(2 * chip_at(place + sign * step))
            order.append(2 * chip_at(place + sign * step) + 1)
        order.append(2 * chip_at(place) + core_now)
        return order

    order = kept(core) + kept(1 - core)
    slots = []
    for device in range(CELLS):
        slot = jnp.int32(0)
        for i, who in enumerate(order):
            slot = jnp.where(who == device, i, slot)
        slots.append(slot)
    return slots


def both_blocks(block, core):
    other = to_partner(block)
    return jnp.stack([jnp.where(core == 0, block, other), jnp.where(core == 0, other, block)])


def half_of(pair, core):
    return jnp.where(core == 0, pair[0], pair[1])[None]


def add_low(*parts):
    total = parts[0].astype(FULL)
    for part in parts[1:]:
        total = total + part.astype(FULL)
    return total.astype(LOW)


def first_hop(*parts):
    return hop(add_low(*[part[0:1] for part in parts]))


def second_hop(moving, core, *parts):
    wide = jnp.stack([jnp.where(core == 0, moving[0], 0), jnp.where(core == 0, 0, moving[0])])
    return hop(add_low(wide, *[part[1:3] for part in parts]))


def later_hop(moving, at, *parts):
    return hop(add_low(moving, *[part[at : at + 2] for part in parts]))


def settle(moving, core, *parts):
    mine = jnp.where(core == 0, moving[0], moving[1])
    other = jnp.where(core == 0, moving[1], moving[0])
    return add_low(mine, to_partner(other), *[part[7] for part in parts])


def dot(left, right, dims=((1,), (0,))):
    return lax.dot_general(left, right, (dims, ((), ())), preferred_element_type=FULL)


def call(body, out_shape, ins, specs, out_specs=None, scratch=(), vmem=48, cost=HEAVY):
    return pl.pallas_call(
        body,
        out_shape=out_shape,
        in_specs=specs,
        out_specs=[VMEM] * len(out_shape) if out_specs is None else out_specs,
        scratch_shapes=list(scratch),
        compiler_params=pltpu.CompilerParams(vmem_limit_bytes=vmem * 2**20),
        cost_estimate=pl.CostEstimate(flops=cost, bytes_accessed=0, transcendentals=0),
    )(*ins)


def shape(dims, kind=LOW):
    return jax.ShapeDtypeStruct(dims, kind)


def fetch(order_ref, refs, target, sem):
    rows = target.shape[0] // CELLS
    copies = []
    index = 0
    for source, size in zip(refs, PIECES):
        for part in range(size):
            at = order_ref[index]
            copies.append(
                pltpu.make_async_copy(
                    source.at[part],
                    target.at[pl.ds(pl.multiple_of(at * rows, 16), rows)],
                    sem.at[index],
                )
            )
            index += 1
    for item in copies:
        item.start()
    return copies


def fetch_halves(order_ref, side, refs, target, sem):
    rows = target.shape[0] // CELLS
    half = rows // 2
    copies = []

    def add(source, at, first, count):
        start = pl.multiple_of(at * rows + first, 16)
        copies.append(
            pltpu.make_async_copy(source, target.at[pl.ds(start, count)], sem.at[len(copies)])
        )

    for part in range(2):
        add(refs[0].at[part], order_ref[part], 0, rows)
    index = 2
    for step in range(4):
        for side_now, group in ((side, refs[1 + 4 * step : 3 + 4 * step]),
                                (1 - side, refs[3 + 4 * step : 5 + 4 * step])):
            at = index
            for source in group:
                for part in range(source.shape[0]):
                    add(source.at[part], order_ref[at], side_now * half, half)
                    at += 1
        index = at
    for item in copies:
        item.start()
    return copies


def wait_all(copies):
    for item in copies:
        item.wait()


def one_hot(rows, lanes, offset):
    row = lax.broadcasted_iota(jnp.int32, (rows, lanes), 0)
    lane = lax.broadcasted_iota(jnp.int32, (rows, lanes), 1)
    return lane == row + offset


def pack_body(who_ref, lengths_ref, *refs):
    sources, small_ref = refs[:8], refs[8]
    me = who_ref[0]
    model = small_ref.shape[1]
    row = lax.broadcasted_iota(jnp.int32, (SMALL_ROWS, model), 0)
    lane = lax.broadcasted_iota(jnp.int32, (SMALL_ROWS, model), 1)
    small = jnp.zeros((SMALL_ROWS, model), FULL)
    for name, ref in zip(NAMES, sources):
        size = ref.shape[1]
        per_row = model // size
        placed = dot(ref[...], one_hot(size, model, size * (me % per_row)).astype(LOW))
        small = small + jnp.where(row == ROWS[name] + me // per_row, placed, 0.0)
    for i in range(2):
        at = (row == ROWS["lengths"]) & (lane == 2 * me + i)
        small = small + jnp.where(at, lengths_ref[i].astype(FULL), 0.0)
    small_ref[...] = small.astype(LOW)


def norm_parts(values):
    center = values - jnp.mean(values, axis=-1, keepdims=True)
    spread = jnp.mean(center * center, axis=-1, keepdims=True)
    return center, lax.rsqrt(spread + EPSILON)


def norm_back(center, scale, gain, grad):
    weighted = grad * gain
    mean_one = jnp.mean(weighted, axis=-1, keepdims=True)
    mean_two = jnp.mean(weighted * center, axis=-1, keepdims=True)
    back = scale * (weighted - mean_one - center * (scale * scale * mean_two))
    return back, jnp.sum(grad * center * scale, axis=0, keepdims=True), jnp.sum(
        grad, axis=0, keepdims=True
    )


def small_row(small_ref, name, count=1):
    return small_ref[...].astype(FULL)[ROWS[name] : ROWS[name] + count, :]


def project_body(order_ref, x_ref, small_ref, *refs):
    blocks = refs[:9]
    low_ref, proj_ref, weight, sem = refs[9:]
    model = x_ref.shape[1]
    copies = fetch(order_ref, blocks, weight, sem)
    center, scale = norm_parts(x_ref[...].astype(FULL))
    bias = small_row(small_ref, "qv_bias", 2)
    low_ref[...] = (
        center * scale * small_row(small_ref, "first_gain") + small_row(small_ref, "first_shift")
    ).astype(LOW)
    wait_all(copies)
    for j in range(3):
        lanes = slice(j * model, (j + 1) * model)
        part = dot(low_ref[...], weight[:, lanes])
        if j != 1:
            part = part + bias[j // 2 : j // 2 + 1]
        proj_ref[:, lanes] = part.astype(LOW)


def attend_body(seq, lengths_ref, proj_ref, att_ref, mixed_ref):
    model = mixed_ref.shape[1]
    cells = mixed_ref.shape[0] // seq
    pairs = model // (2 * HEAD)
    lane = lax.broadcasted_iota(jnp.int32, (seq, 2 * HEAD), 1)
    key = lax.broadcasted_iota(jnp.int32, (seq, seq), 0)

    def step(index, carry):
        s = index // pairs
        p = index % pairs
        rows = pl.ds(pl.multiple_of(s * seq, seq), seq)
        at = pl.multiple_of(p * 2 * HEAD, 2 * HEAD)
        q = proj_ref[rows, pl.ds(at, 2 * HEAD)] * jnp.asarray(HEAD ** (-0.5), LOW)
        k = proj_ref[rows, pl.ds(at + model, 2 * HEAD)]
        v_turned = proj_ref[rows, pl.ds(at + 2 * model, 2 * HEAD)].T
        visible = key < lengths_ref[s]
        mixed = []
        for i in range(2):
            own = (lane >= i * HEAD) & (lane < (i + 1) * HEAD)
            scores = dot(jnp.where(own, k, jnp.zeros_like(k)), q, ((1,), (1,)))
            scores = jnp.where(visible, scores, NEGATIVE)
            expo = jnp.exp(scores - jnp.max(scores, axis=0, keepdims=True))
            probs = expo * (1.0 / jnp.sum(expo, axis=0, keepdims=True))
            probs = probs.astype(LOW)
            att_ref[2 * index + i] = probs
            mixed.append(dot(v_turned[i * HEAD : (i + 1) * HEAD], probs))
        mixed_ref[rows, pl.ds(at, 2 * HEAD)] = jnp.concatenate(mixed, axis=0).T.astype(LOW)
        return carry

    lax.fori_loop(0, cells * pairs, step, 0, unroll=2)


ERFC_STEP = 0.33
ERFC = (
    0.1863578228018033,
    0.18295566386742124,
    0.2012255082472392,
    0.04721561458875723,
    0.4085089979423051,
    -0.35115900736338407,
    0.4602422572120205,
    -0.13534686486277223,
)


def gelu_parts(inner):
    z = jnp.abs(inner) * (0.5**0.5)
    t = 1.0 / (1.0 + ERFC_STEP * z)
    tail = jnp.full_like(t, 0.5 * ERFC[-1])
    for factor in ERFC[-2::-1]:
        tail = tail * t + 0.5 * factor
    bell = jnp.exp(-(z * z))
    tail = tail * t * bell
    area = jnp.where(inner < 0.0, tail, 1.0 - tail)
    return inner * area, area + inner * bell * (0.5 / 3.141592653589793) ** 0.5


def row_mask(lengths_ref, rows, seq):
    at = lax.broadcasted_iota(jnp.int32, (rows, 1), 0)
    true = (at < lengths_ref[0]).astype(FULL)
    for s in range(1, rows // seq):
        true = jnp.where(at < s * seq, true, (at < lengths_ref[s] + s * seq).astype(FULL))
    return true


def loss_rows(lengths_ref, small_ref, other_ref, cot_ref, seq, whole):
    count = jnp.sum(
        small_row(small_ref, "lengths") + small_row(other_ref, "lengths"), axis=-1, keepdims=True
    )
    return cot_ref[...].astype(FULL) * (
        row_mask(lengths_ref, cot_ref.shape[0], seq) * (whole / count)
    )


def put_slots(keep_buf, slot_ref, values, first, lanes):
    rows = keep_buf.shape[1]
    for i in range(values.shape[0] // rows):
        keep_buf[slot_ref[first + i], :, lanes] = values[i * rows : (i + 1) * rows].astype(LOW)


def send_slots(buf, keep_ref, away_ref, sem):
    half = RING_SIZE
    copies = [
        pltpu.make_async_copy(buf.at[pl.ds(half, half)], away_ref, sem.at[0]),
        pltpu.make_async_copy(buf.at[pl.ds(0, half)], keep_ref, sem.at[1]),
    ]
    for item in copies:
        item.start()
    return copies


def inner_body(order_ref, x_ref, mixed_ref, small_ref, *refs):
    blocks = refs[:9]
    middle_ref, low_ref, active_ref, slope_ref, weight, sem = refs[9:]
    model = x_ref.shape[1]
    ff = active_ref.shape[1]
    wait_all(fetch(order_ref, blocks, weight, sem))
    middle = (
        x_ref[...].astype(FULL)
        + dot(mixed_ref[...], weight[:, ff:])
        + small_row(small_ref, "out_bias")
    )
    middle_ref[...] = middle
    center, scale = norm_parts(middle)
    low = center * scale * small_row(small_ref, "second_gain") + small_row(
        small_ref, "second_shift"
    )
    low_ref[...] = low.astype(LOW)
    step = 2 * (ff // RING_SIZE)
    bias = small_row(small_ref, "in_bias", 4)
    for j in range(ff // step):
        lanes = slice(j * step, (j + 1) * step)
        inner = dot(low_ref[...], weight[:, lanes]) + bias[j : j + 1]
        active, slope = gelu_parts(inner)
        active_ref[:, lanes] = active.astype(LOW)
        slope_ref[:, lanes] = slope.astype(LOW)


def grad_down_body(
    seq, whole, who_ref, slot_ref, lengths_ref, active_ref, cot_ref, small_ref, other_ref,
    up_ref, down_b_ref, keep_ref, away_ref, keep_two_ref, away_two_ref, slots, sem,
):
    up_low = loss_rows(lengths_ref, small_ref, other_ref, cot_ref, seq, whole).astype(LOW)
    up_ref[...] = up_low
    down_b_ref[...] = jnp.sum(up_low.astype(FULL), axis=0, keepdims=True)
    parts = RING_SIZE
    step = active_ref.shape[1] // parts
    rows = slots.shape[2]
    side = who_ref[1]
    for j in range(parts):
        grad = dot(active_ref[:, j * step : (j + 1) * step], up_ref[...], ((0,), (0,)))
        for i in range(4):
            slots[(i + side) % 2, slot_ref[j * CELLS // parts + i // 2]] = grad[
                i * rows : (i + 1) * rows
            ].astype(LOW)
    copies = send_slots(slots.at[1], keep_two_ref, away_two_ref, sem.at[1])
    copies += send_slots(slots.at[0], keep_ref, away_ref, sem.at[0])
    wait_all(copies)


def inner_back_body(who_ref, order_ref, slope_ref, up_ref, *refs):
    blocks = refs[:17]
    inner_ref, in_b_ref, weight, sem = refs[17:]
    model = up_ref.shape[1]
    wait_all(fetch_halves(order_ref, who_ref[1], blocks, weight, sem))
    for j in range(inner_ref.shape[1] // model):
        lanes = slice(j * model, (j + 1) * model)
        grad = dot(up_ref[...], weight[lanes, :], ((1,), (1,)))
        low = (grad * slope_ref[:, lanes].astype(FULL)).astype(LOW)
        inner_ref[:, lanes] = low
        in_b_ref[j : j + 1, :] = jnp.sum(low.astype(FULL), axis=0, keepdims=True)


def down_body(active_ref, middle_ref, small_ref, weight_ref, out_ref):
    out_ref[...] = (
        middle_ref[...]
        + dot(active_ref[...], weight_ref[...])
        + small_row(small_ref, "down_bias")
    ).astype(LOW)


def grad_in_body(slot_ref, low_ref, inner_ref, keep_ref, away_ref, slots, sem):
    model = low_ref.shape[1]
    turned = low_ref[...].T
    for j in range(inner_ref.shape[1] // model):
        lanes = slice(j * model, (j + 1) * model)
        put_slots(slots, slot_ref, dot(turned, inner_ref[:, lanes]), 0, lanes)
    wait_all(send_slots(slots, keep_ref, away_ref, sem))


def middle_back_body(
    seq, whole, lengths_ref, inner_ref, middle_ref, cot_ref, small_ref, other_ref, weight,
    grad_ref, grad_low_ref, grad_mixed_ref, sums_ref,
):
    ff = inner_ref.shape[1]
    grad_second = dot(inner_ref[...], weight[:, :ff], ((1,), (1,)))
    center, scale = norm_parts(middle_ref[...])
    back, gain_sum, shift_sum = norm_back(
        center, scale, small_row(small_ref, "second_gain"), grad_second
    )
    grad = loss_rows(lengths_ref, small_ref, other_ref, cot_ref, seq, whole) + back
    grad_ref[...] = grad
    grad_low = grad.astype(LOW)
    grad_low_ref[...] = grad_low
    grad_mixed_ref[...] = dot(grad_low, weight[:, ff:], ((1,), (1,))).astype(LOW)
    sums_ref[0:1, :] = jnp.sum(grad_low.astype(FULL), axis=0, keepdims=True)
    sums_ref[1:2, :] = gain_sum
    sums_ref[2:3, :] = shift_sum


def attend_back_body(seq, begin, proj_ref, att_ref, grad_ref, out_ref):
    model = grad_ref.shape[1]
    half = out_ref.shape[1] // 3
    all_pairs = model // (2 * HEAD)
    pairs = half // (2 * HEAD)
    cells = grad_ref.shape[0] // seq
    lane = lax.broadcasted_iota(jnp.int32, (seq, 2 * HEAD), 1)
    scale = HEAD ** (-0.5)

    def step(index, carry):
        s = index // pairs
        p = index % pairs
        rows = pl.ds(pl.multiple_of(s * seq, seq), seq)
        to = pl.multiple_of(p * 2 * HEAD, 2 * HEAD)
        at = pl.multiple_of(to + begin * 2 * HEAD, 2 * HEAD)
        q = proj_ref[rows, pl.ds(at, 2 * HEAD)]
        k_turned = proj_ref[rows, pl.ds(at + model, 2 * HEAD)].T
        v = proj_ref[rows, pl.ds(at + 2 * model, 2 * HEAD)]
        g = grad_ref[rows, pl.ds(at, 2 * HEAD)]
        grad_q = []
        grad_k = []
        grad_v = []
        for i in range(2):
            own = (lane >= i * HEAD) & (lane < (i + 1) * HEAD)
            probs = att_ref[2 * (s * all_pairs + begin + p) + i]
            wide = probs.astype(FULL)
            grad_probs = dot(jnp.where(own, v, jnp.zeros_like(v)), g, ((1,), (1,)))
            delta = jnp.sum(wide * grad_probs, axis=0, keepdims=True)
            scores = (wide * (grad_probs - delta)).astype(LOW)
            grad_q.append(dot(k_turned[i * HEAD : (i + 1) * HEAD], scores))
            grad_k.append(dot(scores, q))
            grad_v.append(dot(probs, g))
        first = lane < HEAD
        out_ref[rows, pl.ds(to, 2 * HEAD)] = (
            jnp.concatenate(grad_q, axis=0).T * scale
        ).astype(LOW)
        out_ref[rows, pl.ds(to + half, 2 * HEAD)] = (
            jnp.where(first, grad_k[0], grad_k[1]) * scale
        ).astype(LOW)
        out_ref[rows, pl.ds(to + 2 * half, 2 * HEAD)] = jnp.where(
            first, grad_v[0], grad_v[1]
        ).astype(LOW)
        return carry

    lax.fori_loop(0, cells * pairs, step, 0, unroll=2)


def early_grad_body(
    slot_ref, low_ref, part_ref, mixed_ref, grad_low_ref, keep_ref, away_ref, slots, sem
):
    width = part_ref.shape[1]
    put_slots(slots, slot_ref, dot(low_ref[...].T, part_ref[...]), 0, slice(0, width))
    put_slots(
        slots, slot_ref, dot(mixed_ref[...].T, grad_low_ref[...]), 0,
        slice(width, slots.shape[2]),
    )
    wait_all(send_slots(slots, keep_ref, away_ref, sem))


def first_back_body(
    slot_ref, x_ref, low_ref, one_ref, two_ref, grad_ref, small_ref, sums_ref, in_b_ref,
    down_b_ref, weight, out_ref, keep_ref, away_ref, sum_ref, slots, sem,
):
    model = x_ref.shape[1]
    late = two_ref.shape[1]
    center, scale = norm_parts(x_ref[...].astype(FULL))
    parts = ((one_ref, 0), (two_ref, one_ref.shape[1] // 3))
    grad_first = jnp.zeros(x_ref.shape, FULL)
    for j in range(3):
        for ref, begin in parts:
            width = ref.shape[1] // 3
            at = j * model + begin
            grad_first = grad_first + dot(
                ref[:, j * width : (j + 1) * width], weight[:, at : at + width], ((1,), (1,))
            )
    put_slots(slots, slot_ref, dot(low_ref[...].T, two_ref[...]), 0, slice(0, late))
    back, gain_sum, shift_sum = norm_back(
        center, scale, small_row(small_ref, "first_gain"), grad_first
    )

    def put(name, value, offset=0):
        at = ROWS[name] + offset
        sum_ref[at : at + value.shape[0], :] = value

    sum_ref[...] = jnp.zeros_like(sum_ref)
    put("first_gain", gain_sum)
    put("first_shift", shift_sum)
    for j in range(2):
        at = ROWS["qv_bias"] + j
        for ref, begin in parts:
            width = ref.shape[1] // 3
            part = ref[:, 2 * j * width : (2 * j + 1) * width].astype(FULL)
            sum_ref[at : at + 1, begin : begin + width] = jnp.sum(part, axis=0, keepdims=True)
    put("out_bias", sums_ref[0:1, :])
    put("second_gain", sums_ref[1:2, :])
    put("second_shift", sums_ref[2:3, :])
    put("in_bias", in_b_ref[...])
    put("down_bias", down_b_ref[...])
    for i in range(3):
        part = sum_ref[:, SMALL_LANES * i : SMALL_LANES * (i + 1)].astype(LOW)
        for device in range(CELLS):
            slots[device, 16 * i : 16 * i + 16, late:] = part
    copies = send_slots(slots, keep_ref, away_ref, sem)
    out_ref[...] = (grad_ref[...] + back).astype(LOW)
    wait_all(copies)


def finish_body(who_ref, early_ref, early_two_ref, late_ref, late_two_ref, *refs):
    grad_ref, out_ref, vectors, small_ref = refs[0], refs[1], refs[2:-1], refs[-1]
    model = out_ref.shape[1]
    early = early_ref[...].astype(FULL) + early_two_ref[...].astype(FULL)
    late = late_ref[...].astype(FULL) + late_two_ref[...].astype(FULL)
    one = (early.shape[1] - model) // 3
    two = (late.shape[1] - SMALL_LANES) // 3
    for j in range(3):
        at = j * model
        grad_ref[:, at : at + one] = early[:, j * one : (j + 1) * one]
        grad_ref[:, at + one : at + model] = late[:, j * two : (j + 1) * two]
    out_ref[...] = early[:, 3 * one :]
    for i in range(3):
        small_ref[:, SMALL_LANES * i : SMALL_LANES * (i + 1)] = late[
            16 * i : 16 * i + 16, 3 * two :
        ]
    me = who_ref[0]
    row = lax.broadcasted_iota(jnp.int32, (SMALL_ROWS, model), 0)
    for name, ref in zip(NAMES, vectors):
        size = ref.shape[1]
        per_row = model // size
        here_row = jnp.where(row == ROWS[name] + me // per_row, small_ref[...], 0.0)
        values = jnp.sum(here_row, axis=0, keepdims=True)
        picker = one_hot(size, model, size * (me % per_row)).astype(FULL)
        ref[...] = lax.dot_general(
            values, picker, (((1,), (1,)), ((), ())), precision=lax.Precision.HIGHEST,
            preferred_element_type=FULL,
        )


def on_device_ring(
    tokens,
    lengths,
    cotangent,
    first_gain,
    first_shift,
    qkv_weight,
    qv_bias,
    out_weight,
    out_bias,
    second_gain,
    second_shift,
    in_weight,
    in_bias,
    down_weight,
    down_bias,
):
    micro, seq, model = tokens.shape[1:]
    total_rows = micro * seq
    rows = qkv_weight.shape[0]
    down_rows = down_weight.shape[0]
    ff = in_weight.shape[1]
    heads = model // HEAD
    whole = float(lax.axis_size("species") * CELLS * micro * seq)
    index, core, place = here()
    species = lax.axis_index("species")
    who = jnp.stack([index, species]).astype(jnp.int32)
    order = jnp.stack(gather_order(core, place)).astype(jnp.int32)
    slot = jnp.stack(scatter_slots(core, place)).astype(jnp.int32)
    lens = lengths.reshape(micro)
    x = tokens.reshape(total_rows, model)
    cot = cotangent.reshape(total_rows, model)
    vectors = (
        first_gain, first_shift, qv_bias, out_bias, second_gain, second_shift, in_bias, down_bias,
    )

    dma = pltpu.SemaphoreType.DMA

    def gathered(own, hops):
        got = [own]
        for item in hops:
            got += [item, to_partner(item)]
        return got

    own = both_blocks(qkv_weight, core)
    qkv_one = hop(own)
    (small,) = call(
        pack_body,
        [shape((SMALL_ROWS, model))],
        [who, after(lens, own)] + [item.reshape(1, -1) for item in vectors],
        [SMEM, SMEM] + [VMEM] * 8,
        vmem=4,
    )
    small = exchange(small, 2)
    in_weight, out_weight = lax.optimization_barrier((in_weight, out_weight, own))[:2]
    in_own = both_blocks(jnp.concatenate([in_weight, out_weight], axis=1), core)
    qkv_one, small, in_own = lax.optimization_barrier((qkv_one, small, in_own))
    qkv_two = hop(qkv_one)
    small = exchange(small, 4)
    down_own = both_blocks(after(down_weight, qkv_one), core)
    qkv_two, small, down_own = lax.optimization_barrier((qkv_two, small, down_own))
    qkv_three = hop(qkv_two)
    small = exchange(small, 8)
    qkv_three, small = lax.optimization_barrier((qkv_three, small))
    qkv_last = hop(half_of(qkv_three, core))
    small = exchange(small, 1)
    in_one = hop(after(in_own, qkv_three))
    low, proj, qkv_full = call(
        project_body,
        [
            shape((total_rows, model)),
            shape((total_rows, 3 * model)),
            shape((model, 3 * model)),
        ],
        [order, x, small] + gathered(own, (qkv_one, qkv_two, qkv_three, qkv_last)),
        [SMEM, VMEM, VMEM] + [ANY] * 9,
        scratch=[dma((CELLS,))],
        vmem=20,
    )
    other_small = across(small)
    in_one, proj = lax.optimization_barrier((in_one, proj))
    in_two = hop(in_one)
    down_half = jnp.where(species == 0, down_own[:, : down_rows // 2], down_own[:, down_rows // 2 :])
    down_one = hop(after(down_half, in_one))
    att, mixed = call(
        lambda *refs: attend_body(seq, *refs),
        [shape((micro * heads, seq, seq)), shape((total_rows, model))],
        [lens, proj],
        [SMEM, VMEM],
        vmem=12,
    )
    in_two, mixed, down_one = lax.optimization_barrier((in_two, mixed, down_one))
    in_three = hop(in_two)
    down_two = hop(after(down_one, in_two))
    swap_one = across(down_one)
    in_three, down_two, swap_one = lax.optimization_barrier((in_three, down_two, swap_one))
    in_last = hop(half_of(in_three, core))
    down_three = hop(down_two)
    swap_two = across(down_two)
    in_last, down_three, mixed = lax.optimization_barrier((in_last, down_three, mixed))
    down_last = hop(half_of(down_three, core))
    swap_three = across(down_three)
    in_got = gathered(in_own, (in_one, in_two, in_three, in_last))
    middle, low_two, active, slope, in_full = call(
        inner_body,
        [
            shape((total_rows, model), FULL),
            shape((total_rows, model)),
            shape((total_rows, ff)),
            shape((total_rows, ff)),
            shape((model, ff + model)),
        ],
        [order, x, mixed, small] + in_got,
        [SMEM] + [VMEM] * 3 + [ANY] * 9,
        scratch=[dma((CELLS,))],
        vmem=24,
    )
    down_last, active = lax.optimization_barrier((down_last, active))
    swap_last = across(down_last)
    up_low, down_b, down_keep, down_away, down_keep_two, down_away_two = call(
        lambda *refs: grad_down_body(seq, whole, *refs),
        [
            shape((total_rows, model)),
            shape((1, model), FULL),
        ]
        + [shape((RING_SIZE, down_rows // 2, model))] * 4,
        [who, slot, lens, active, cot, small, other_small],
        [SMEM] * 3 + [VMEM] * 4,
        [VMEM] * 2 + [ANY] * 4,
        scratch=[pltpu.VMEM((2, CELLS, down_rows // 2, model), LOW), dma((2, 2))],
        vmem=15,
    )

    swap_last, up_low = lax.optimization_barrier((swap_last, up_low))
    down_got = [down_own]
    for item, swapped in (
        (down_one, swap_one), (down_two, swap_two), (down_three, swap_three),
        (down_last, swap_last),
    ):
        down_got += [item, to_partner(item), swapped, to_partner(swapped)]
    down_other_two = to_partner(down_away_two)
    down_other = to_partner(down_away)
    inner_low, in_b, down_full = call(
        inner_back_body,
        [
            shape((total_rows, ff)),
            shape((ff // model, model), FULL),
            shape((ff, model)),
        ],
        [who, order, slope, up_low] + down_got,
        [SMEM] * 2 + [VMEM] * 2 + [ANY] * 17,
        scratch=[dma((2 * CELLS,))],
        vmem=20,
    )
    down_other_two, inner_low = lax.optimization_barrier((down_other_two, inner_low))
    down_x = across(add_low(down_keep_two[0:3], down_other_two[0:3]))
    down_x_two = across(add_low(down_keep_two[3:8], down_other_two[3:8]))
    in_keep, in_away = call(
        grad_in_body,
        [shape((RING_SIZE, rows, ff)), shape((RING_SIZE, rows, ff))],
        [slot, low_two, inner_low],
        [SMEM] + [VMEM] * 2,
        [ANY] * 2,
        scratch=[pltpu.VMEM((CELLS, rows, ff), LOW), dma((2,))],
        vmem=13,
    )
    in_other = to_partner(in_away)
    inner_low = after(inner_low, in_keep)
    grad_middle, grad_low, grad_mixed, sums = call(
        lambda *refs: middle_back_body(seq, whole, *refs),
        [
            shape((total_rows, model), FULL),
            shape((total_rows, model)),
            shape((total_rows, model)),
            shape((3, model), FULL),
        ],
        [lens, inner_low, middle, cot, small, other_small, in_full],
        [SMEM] + [VMEM] * 6,
        vmem=19,
    )

    def attend_back(begin, pairs, grad):
        return call(
            lambda *refs: attend_back_body(seq, begin, *refs),
            [shape((total_rows, 6 * pairs * HEAD))],
            [proj, att, grad],
            [VMEM] * 3,
            vmem=11,

        )[0]

    pairs = model // (2 * HEAD)
    early_pairs = 2 * pairs // 3
    in_other, grad_mixed = lax.optimization_barrier((in_other, grad_mixed))
    in_sum = first_hop(in_keep, in_other)
    grad_one = attend_back(0, early_pairs, grad_mixed)
    in_sum, down_x, down_other, grad_one = lax.optimization_barrier(
        (in_sum, down_x, down_other, grad_one)
    )
    in_sum = second_hop(in_sum, core, in_keep, in_other)
    down_sum = first_hop(down_keep, down_other, down_x)
    early_width = 6 * early_pairs * HEAD + model
    early_keep, early_away = call(
        early_grad_body,
        [shape((RING_SIZE, rows, early_width))] * 2,
        [slot, low, grad_one, mixed, grad_low],
        [SMEM] + [VMEM] * 4,
        [ANY] * 2,
        scratch=[pltpu.VMEM((CELLS, rows, early_width), LOW), dma((2,))],
        vmem=12,
    )
    early_other = to_partner(early_away)
    early_keep, grad_mixed = lax.optimization_barrier((early_keep, grad_mixed))
    grad_two = attend_back(early_pairs, pairs - early_pairs, grad_mixed)
    early_other, in_sum, down_sum, grad_two = lax.optimization_barrier(
        (early_other, in_sum, down_sum, grad_two)
    )
    in_sum = later_hop(in_sum, 3, in_keep, in_other)
    down_sum = second_hop(down_sum, core, down_keep, down_other, down_x)
    early_sum = first_hop(early_keep, early_other)
    late_width = 6 * (pairs - early_pairs) * HEAD + SMALL_LANES
    grad_tokens, late_keep, late_away = call(
        first_back_body,
        [
            shape((total_rows, model)),
            shape((RING_SIZE, rows, late_width)),
            shape((RING_SIZE, rows, late_width)),
        ],
        [slot, x, low, grad_one, grad_two, grad_middle, small, sums, in_b, down_b, qkv_full],
        [SMEM] + [VMEM] * 10,
        [VMEM] + [ANY] * 2,
        scratch=[
            pltpu.VMEM((SMALL_ROWS, model), FULL),
            pltpu.VMEM((CELLS, rows, late_width), LOW),
            dma((2,)),
        ],
        vmem=16,

    )
    late_other = to_partner(late_away)
    in_sum, early_sum, late_keep, down_sum, down_x_two = lax.optimization_barrier(
        (in_sum, early_sum, late_keep, down_sum, down_x_two)
    )
    in_sum = later_hop(in_sum, 5, in_keep, in_other)
    early_sum = second_hop(early_sum, core, early_keep, early_other)
    down_sum = hop(add_low(down_sum, down_keep[3:5], down_other[3:5], down_x_two[0:2]))
    late_sum = first_hop(late_keep, late_other)
    late_sum, early_sum, down_sum = lax.optimization_barrier((late_sum, early_sum, down_sum))
    late_ready = late_sum
    down_sum = hop(add_low(down_sum, down_keep[5:7], down_other[5:7], down_x_two[2:4]))
    late_sum = second_hop(late_sum, core, late_keep, late_other)
    early_sum = later_hop(early_sum, 3, early_keep, early_other)
    (out_tokens,) = call(
        down_body,
        [shape((total_rows, model))],
        [after(active, late_ready), middle, small, down_full],
        [VMEM] * 4,
        vmem=13,
    )
    late_sum, early_sum, down_sum, in_sum, out_tokens = lax.optimization_barrier(
        (late_sum, early_sum, down_sum, in_sum, out_tokens)
    )
    late_sum = later_hop(late_sum, 3, late_keep, late_other)
    early_sum = later_hop(early_sum, 5, early_keep, early_other)
    in_sum = settle(in_sum, core, in_keep, in_other)
    in_terms = (in_sum, across(in_sum))
    mine = jnp.where(core == 0, down_sum[0], down_sum[1])
    other = to_partner(jnp.where(core == 0, down_sum[1], down_sum[0]))
    down_sum = add_low(mine, other, down_keep[7], down_other[7], down_x_two[4])
    down_terms = (down_sum, across(down_sum))
    late_sum = later_hop(late_sum, 5, late_keep, late_other)
    early_sum = settle(early_sum, core, early_keep, early_other)
    early_terms = (early_sum, across(early_sum))
    late_sum = settle(late_sum, core, late_keep, late_other)
    late_terms = (late_sum, across(late_sum))
    finished = call(
        finish_body,
        [shape((rows, 3 * model), FULL), shape((rows, model), FULL)]
        + [shape((1, item.shape[0]), FULL) for item in vectors],
        [who] + list(early_terms) + list(late_terms),
        [SMEM] + [VMEM] * 4,
        scratch=[pltpu.VMEM((SMALL_ROWS, model), FULL)],
        vmem=6,
    )
    grad_qkv, grad_out = finished[:2]
    pieces = [item.reshape(-1) for item in finished[2:]]
    return (
        out_tokens.reshape(tokens.shape),
        grad_tokens.reshape(tokens.shape),
        pieces[0],
        pieces[1],
        grad_qkv,
        pieces[2],
        grad_out,
        pieces[3],
        pieces[4],
        pieces[5],
        in_terms[0].astype(FULL) + in_terms[1].astype(FULL),
        pieces[6],
        jnp.concatenate(
            [
                jnp.where(species == 0, down_terms[0], down_terms[1]),
                jnp.where(species == 0, down_terms[1], down_terms[0]),
            ]
        ).astype(FULL),
        pieces[7],
    )


def on_device(
    tokens,
    lengths,
    cotangent,
    first_gain,
    first_shift,
    qkv_weight,
    qv_bias,
    out_weight,
    out_bias,
    second_gain,
    second_shift,
    in_weight,
    in_bias,
    down_weight,
    down_bias,
):
    local_count = jnp.sum(lengths).astype(jnp.float32)
    count = lax.psum(local_count, ("species", "cells"))
    micro_count = tokens.shape[1]
    seq_rows = tokens.shape[2]
    factor = (
        float(lax.axis_size("species") * lax.axis_size("cells") * micro_count * seq_rows) / count
    )
    output_rows = []
    gradient_rows = []
    summed = None
    for micro_step in range(micro_count):
        gathered = (
            lax.all_gather(first_gain, "cells", axis=0, tiled=True),
            lax.all_gather(first_shift, "cells", axis=0, tiled=True),
            lax.all_gather(qkv_weight, "cells", axis=0, tiled=True),
            lax.all_gather(qv_bias, "cells", axis=0, tiled=True),
            lax.all_gather(out_weight, "cells", axis=0, tiled=True),
            lax.all_gather(out_bias, "cells", axis=0, tiled=True),
            lax.all_gather(second_gain, "cells", axis=0, tiled=True),
            lax.all_gather(second_shift, "cells", axis=0, tiled=True),
            lax.all_gather(in_weight, "cells", axis=0, tiled=True),
            lax.all_gather(in_bias, "cells", axis=0, tiled=True),
            lax.all_gather(down_weight, "cells", axis=0, tiled=True),
            lax.all_gather(down_bias, "cells", axis=0, tiled=True),
        )
        out_seq, grad_seq, grads = sequence_pass(
            gathered,
            tokens[0, micro_step],
            lengths[0, micro_step],
            cotangent[0, micro_step],
            factor,
        )
        output_rows.append(out_seq)
        gradient_rows.append(grad_seq)
        shares = (
            lax.psum_scatter(grads[0], "cells", scatter_dimension=0, tiled=True),
            lax.psum_scatter(grads[1], "cells", scatter_dimension=0, tiled=True),
            lax.psum_scatter(grads[2], "cells", scatter_dimension=0, tiled=True),
            lax.psum_scatter(grads[3], "cells", scatter_dimension=0, tiled=True),
            lax.psum_scatter(grads[4], "cells", scatter_dimension=0, tiled=True),
            lax.psum_scatter(grads[5], "cells", scatter_dimension=0, tiled=True),
            lax.psum_scatter(grads[6], "cells", scatter_dimension=0, tiled=True),
            lax.psum_scatter(grads[7], "cells", scatter_dimension=0, tiled=True),
            lax.psum_scatter(grads[8], "cells", scatter_dimension=0, tiled=True),
            lax.psum_scatter(grads[9], "cells", scatter_dimension=0, tiled=True),
            lax.psum_scatter(grads[10], "cells", scatter_dimension=0, tiled=True),
            lax.psum_scatter(grads[11], "cells", scatter_dimension=0, tiled=True),
        )
        summed = shares if summed is None else jax.tree.map(jnp.add, summed, shares)
    final = (
        lax.psum(summed[0].astype(jnp.bfloat16), "species").astype(jnp.float32),
        lax.psum(summed[1].astype(jnp.bfloat16), "species").astype(jnp.float32),
        lax.psum(summed[2].astype(jnp.bfloat16), "species").astype(jnp.float32),
        lax.psum(summed[3].astype(jnp.bfloat16), "species").astype(jnp.float32),
        lax.psum(summed[4].astype(jnp.bfloat16), "species").astype(jnp.float32),
        lax.psum(summed[5].astype(jnp.bfloat16), "species").astype(jnp.float32),
        lax.psum(summed[6].astype(jnp.bfloat16), "species").astype(jnp.float32),
        lax.psum(summed[7].astype(jnp.bfloat16), "species").astype(jnp.float32),
        lax.psum(summed[8].astype(jnp.bfloat16), "species").astype(jnp.float32),
        lax.psum(summed[9].astype(jnp.bfloat16), "species").astype(jnp.float32),
        lax.psum(summed[10].astype(jnp.bfloat16), "species").astype(jnp.float32),
        lax.psum(summed[11].astype(jnp.bfloat16), "species").astype(jnp.float32),
    )
    out_tokens = jnp.stack(output_rows)[None]
    grad_tokens = jnp.stack(gradient_rows)[None]
    return (out_tokens, grad_tokens) + tuple(final)


def solution(mesh):
    in_specs = (
        P("species", "cells", None, None),
        P("species", "cells"),
        P("species", "cells", None, None),
        P("cells"),
        P("cells"),
        P("cells", None),
        P("cells"),
        P("cells", None),
        P("cells"),
        P("cells"),
        P("cells"),
        P("cells", None),
        P("cells"),
        P("cells", None),
        P("cells"),
    )
    out_specs = (
        P("species", "cells", None, None),
        P("species", "cells", None, None),
        P("cells"),
        P("cells"),
        P("cells", None),
        P("cells"),
        P("cells", None),
        P("cells"),
        P("cells"),
        P("cells"),
        P("cells", None),
        P("cells"),
        P("cells", None),
        P("cells"),
    )
    program = on_device_ring if mesh.shape["cells"] == 2 * RING_SIZE else on_device
    return jax.shard_map(
        program, mesh=mesh, in_specs=in_specs, out_specs=out_specs, check_vma=False
    )
```

```python
import jax
import jax.numpy as jnp
from jax import lax
from jax.experimental import pallas as pl
from jax.experimental.pallas import tpu as pltpu
from jax.sharding import PartitionSpec as P

HEAD = 64


EPSILON = 1e-12
NEGATIVE = -1e30


def normalize(values, gain_vec, shift_vec):
    center = values - jnp.mean(values, axis=-1, keepdims=True)
    spread = jnp.mean(center * center, axis=-1, keepdims=True)
    return center * lax.rsqrt(spread + EPSILON) * gain_vec + shift_vec


def smooth_gate(values):
    return jax.nn.gelu(values, approximate=False)


def times_left(left_side, right_side):
    return lax.dot_general(
        left_side, right_side, (((0,), (0,)), ((), ())), preferred_element_type=jnp.float32
    )


def times_right(left_side, right_side):
    return lax.dot_general(
        left_side, right_side, (((1,), (1,)), ((), ())), preferred_element_type=jnp.float32
    )


def sequence_pass(weights, inputs, length, cot_rows, factor):
    (
        first_gain,
        first_shift,
        qkv_weight,
        qv_bias,
        out_weight,
        out_bias,
        second_gain,
        second_shift,
        in_weight,
        in_bias,
        down_weight,
        down_bias,
    ) = weights
    seq_rows = inputs.shape[0]
    model_width = inputs.shape[1]
    heads_count = model_width // HEAD
    scale_qk = float(HEAD) ** (-0.5)
    as_float = inputs.astype(jnp.float32)
    hidden_one, first_pull = jax.vjp(
        normalize, as_float, first_gain.astype(jnp.float32), first_shift.astype(jnp.float32)
    )
    first_low = hidden_one.astype(jnp.bfloat16)
    bias_float = qv_bias.astype(jnp.float32)
    full_bias = jnp.concatenate(
        [bias_float[:model_width], jnp.zeros((model_width,), jnp.float32), bias_float[model_width:]]
    )
    projected = (
        jnp.dot(first_low, qkv_weight, preferred_element_type=jnp.float32) + full_bias
    ).astype(jnp.bfloat16)
    split_heads = projected.reshape(seq_rows, 3, heads_count, HEAD)
    queries = split_heads[:, 0]
    keys_part = split_heads[:, 1]
    values_part = split_heads[:, 2]
    visible = jnp.arange(seq_rows) < length

    def scores_of():
        raw_scores = (
            jnp.einsum("qhd,khd->hqk", queries, keys_part, preferred_element_type=jnp.float32)
            * scale_qk
        )
        return jnp.where(visible[None, None, :], raw_scores, NEGATIVE)

    scores = scores_of()
    top_score = jnp.max(scores, axis=-1, keepdims=True)
    expo = jnp.exp(scores - top_score)
    total_exp = jnp.sum(expo, axis=-1, keepdims=True)
    log_total = top_score + jnp.log(total_exp)
    attention = (expo / total_exp).astype(jnp.bfloat16)
    mixed = jnp.einsum("hqk,khd->qhd", attention, values_part, preferred_element_type=jnp.float32)
    mixed = mixed.reshape(seq_rows, model_width).astype(jnp.bfloat16)
    middle = (
        as_float
        + jnp.dot(mixed, out_weight, preferred_element_type=jnp.float32)
        + out_bias.astype(jnp.float32)
    )
    hidden_two, second_pull = jax.vjp(
        normalize, middle, second_gain.astype(jnp.float32), second_shift.astype(jnp.float32)
    )
    second_low = hidden_two.astype(jnp.bfloat16)
    inner = jnp.dot(second_low, in_weight, preferred_element_type=jnp.float32) + in_bias.astype(
        jnp.float32
    )
    active, gate_pull = jax.vjp(smooth_gate, inner)
    active_low = active.astype(jnp.bfloat16)
    output = (
        middle
        + jnp.dot(active_low, down_weight, preferred_element_type=jnp.float32)
        + down_bias.astype(jnp.float32)
    )
    upstream = cot_rows.astype(jnp.float32) * visible[:, None].astype(jnp.float32) * factor
    up_low = upstream.astype(jnp.bfloat16)
    grad_down_bias = jnp.sum(up_low.astype(jnp.float32), axis=0)
    grad_down = times_left(active_low, up_low)
    grad_active = times_right(up_low, down_weight)
    (grad_inner,) = gate_pull(grad_active)
    inner_low = grad_inner.astype(jnp.bfloat16)
    grad_in_bias = jnp.sum(inner_low.astype(jnp.float32), axis=0)
    grad_in = times_left(second_low, inner_low)
    grad_second = times_right(inner_low, in_weight)
    grad_middle_norm, grad_second_gain, grad_second_shift = second_pull(grad_second)
    grad_middle = upstream + grad_middle_norm
    middle_low = grad_middle.astype(jnp.bfloat16)
    grad_out_bias = jnp.sum(middle_low.astype(jnp.float32), axis=0)
    grad_out = times_left(mixed, middle_low)
    grad_mixed = (
        times_right(middle_low, out_weight)
        .astype(jnp.bfloat16)
        .reshape(seq_rows, heads_count, HEAD)
    )
    probs_again = jnp.exp(scores_of() - log_total)
    grad_probs = jnp.einsum(
        "qhd,khd->hqk", grad_mixed, values_part, preferred_element_type=jnp.float32
    )
    grad_values = jnp.einsum(
        "hqk,qhd->khd", attention, grad_mixed, preferred_element_type=jnp.float32
    )
    delta = jnp.sum(probs_again * grad_probs, axis=-1, keepdims=True)
    grad_scores = (probs_again * (grad_probs - delta)).astype(jnp.bfloat16)
    grad_queries = (
        jnp.einsum("hqk,khd->qhd", grad_scores, keys_part, preferred_element_type=jnp.float32)
        * scale_qk
    )
    grad_keys = (
        jnp.einsum("hqk,qhd->khd", grad_scores, queries, preferred_element_type=jnp.float32)
        * scale_qk
    )
    grad_projected = jnp.stack([grad_queries, grad_keys, grad_values], axis=1)
    grad_projected = grad_projected.reshape(seq_rows, 3 * model_width).astype(jnp.bfloat16)
    column_sums = jnp.sum(grad_projected.astype(jnp.float32), axis=0)
    grad_qv = jnp.concatenate([column_sums[:model_width], column_sums[2 * model_width :]])
    grad_qkv = times_left(first_low, grad_projected)
    grad_first = times_right(grad_projected, qkv_weight)
    grad_input_norm, grad_first_gain, grad_first_shift = first_pull(grad_first)
    grad_inputs = grad_middle + grad_input_norm
    grads = (
        grad_first_gain,
        grad_first_shift,
        grad_qkv,
        grad_qv,
        grad_out,
        grad_out_bias,
        grad_second_gain,
        grad_second_shift,
        grad_in,
        grad_in_bias,
        grad_down,
        grad_down_bias,
    )
    return (output.astype(jnp.bfloat16), grad_inputs.astype(jnp.bfloat16), grads)


RING = (0, 2, 4, 6, 7, 5, 3, 1)
RING_SIZE = len(RING)
CELLS = 2 * RING_SIZE
ANY = pl.BlockSpec(memory_space=pl.ANY)
HBM = pl.BlockSpec(memory_space=pltpu.HBM)
VMEM = pl.BlockSpec(memory_space=pltpu.VMEM)
SMEM = pl.BlockSpec(memory_space=pltpu.SMEM)
LOW = jnp.bfloat16
FULL = jnp.float32
HEAVY = 10**10
UNIT = 10**8
K1 = 50
K4 = 100
ROWS = {
    "first_gain": 0,
    "first_shift": 1,
    "qv_bias": 2,
    "out_bias": 4,
    "second_gain": 5,
    "second_shift": 6,
    "in_bias": 7,
    "down_bias": 11,
    "lengths": 12,
}
NAMES = tuple(ROWS)[:8]
SMALL_ROWS = 16
SMALL_LANES = 256
PIECES = (2, 2, 2, 2, 2, 2, 2, 1, 1)


def ring_pairs():
    pairs = []
    for place in range(RING_SIZE):
        chip = RING[place]
        right = RING[(place + 1) % RING_SIZE]
        left = RING[(place - 1) % RING_SIZE]
        pairs.append((2 * chip, 2 * right))
        pairs.append((2 * chip + 1, 2 * left + 1))
    return pairs


def hop(block):
    return lax.ppermute(block, "cells", ring_pairs())


def to_partner(block):
    return lax.ppermute(block, "cells", [(i, i ^ 1) for i in range(CELLS)])


def across(block):
    return lax.ppermute(block, "species", [(0, 1), (1, 0)])


def exchange(values, bit):
    return values + lax.ppermute(values, "cells", [(i, i ^ bit) for i in range(CELLS)])


def after(value, *others):
    return lax.optimization_barrier((value,) + others)[0]


def here():
    index = lax.axis_index("cells")
    core = index % 2
    chip = index // 2
    place = jnp.int32(0)
    for i, ring_chip in enumerate(RING):
        place = jnp.where(chip == ring_chip, i, place)
    return index, core, place


def chip_at(place):
    place = place % RING_SIZE
    chip = jnp.zeros_like(place)
    for i, ring_chip in enumerate(RING):
        chip = jnp.where(place == i, ring_chip, chip)
    return chip


def gather_order(core, place):
    sign = 1 - 2 * core
    order = []

    def pair(at):
        order.append(2 * chip_at(at))
        order.append(2 * chip_at(at) + 1)

    pair(place)
    for step in range(1, 4):
        pair(place - sign * step)
        pair(place + sign * step)
    order.append(2 * chip_at(place + 4) + core)
    order.append(2 * chip_at(place + 4) + 1 - core)
    return order


def scatter_slots(core, place):
    def kept(core_now):
        sign = 1 - 2 * core_now
        order = [2 * chip_at(place + 4) + core_now]
        for step in (3, 2, 1):
            order.append(2 * chip_at(place + sign * step))
            order.append(2 * chip_at(place + sign * step) + 1)
        order.append(2 * chip_at(place) + core_now)
        return order

    order = kept(core) + kept(1 - core)
    slots = []
    for device in range(CELLS):
        slot = jnp.int32(0)
        for i, who in enumerate(order):
            slot = jnp.where(who == device, i, slot)
        slots.append(slot)
    return slots


def both_blocks(block, core):
    other = to_partner(block)
    return jnp.stack([jnp.where(core == 0, block, other), jnp.where(core == 0, other, block)])


def half_of(pair, core):
    return jnp.where(core == 0, pair[0], pair[1])[None]


def add_low(*parts):
    total = parts[0].astype(FULL)
    for part in parts[1:]:
        total = total + part.astype(FULL)
    return total.astype(LOW)


def first_hop(*parts):
    return hop(add_low(*[part[0:1] for part in parts]))


def second_hop(moving, core, *parts):
    wide = jnp.stack([jnp.where(core == 0, moving[0], 0), jnp.where(core == 0, 0, moving[0])])
    return hop(add_low(wide, *[part[1:3] for part in parts]))


def later_hop(moving, at, *parts):
    return hop(add_low(moving, *[part[at : at + 2] for part in parts]))


def settle(moving, core, *parts):
    mine = jnp.where(core == 0, moving[0], moving[1])
    other = jnp.where(core == 0, moving[1], moving[0])
    return add_low(mine, to_partner(other), *[part[7] for part in parts])


def dot(left, right, dims=((1,), (0,))):
    return lax.dot_general(left, right, (dims, ((), ())), preferred_element_type=FULL)


def call(body, out_shape, ins, specs, out_specs=None, scratch=(), vmem=48, cost=HEAVY):
    return pl.pallas_call(
        body,
        out_shape=out_shape,
        in_specs=specs,
        out_specs=[VMEM] * len(out_shape) if out_specs is None else out_specs,
        scratch_shapes=list(scratch),
        compiler_params=pltpu.CompilerParams(vmem_limit_bytes=vmem * 2**20),
        cost_estimate=pl.CostEstimate(flops=cost, bytes_accessed=0, transcendentals=0),
    )(*ins)


def shape(dims, kind=LOW):
    return jax.ShapeDtypeStruct(dims, kind)


def fetch(order_ref, refs, target, sem):
    rows = target.shape[0] // CELLS
    copies = []
    index = 0
    for source, size in zip(refs, PIECES):
        for part in range(size):
            at = order_ref[index]
            copies.append(
                pltpu.make_async_copy(
                    source.at[part],
                    target.at[pl.ds(pl.multiple_of(at * rows, 16), rows)],
                    sem.at[index],
                )
            )
            index += 1
    for item in copies:
        item.start()
    return copies


def wait_all(copies):
    for item in copies:
        item.wait()


def one_hot(rows, lanes, offset):
    row = lax.broadcasted_iota(jnp.int32, (rows, lanes), 0)
    lane = lax.broadcasted_iota(jnp.int32, (rows, lanes), 1)
    return lane == row + offset


def pack_body(who_ref, lengths_ref, *refs):
    sources, small_ref = refs[:8], refs[8]
    me = who_ref[0]
    model = small_ref.shape[1]
    row = lax.broadcasted_iota(jnp.int32, (SMALL_ROWS, model), 0)
    lane = lax.broadcasted_iota(jnp.int32, (SMALL_ROWS, model), 1)
    small = jnp.zeros((SMALL_ROWS, model), FULL)
    for name, ref in zip(NAMES, sources):
        size = ref.shape[1]
        per_row = model // size
        placed = dot(ref[...], one_hot(size, model, size * (me % per_row)).astype(LOW))
        small = small + jnp.where(row == ROWS[name] + me // per_row, placed, 0.0)
    for i in range(2):
        at = (row == ROWS["lengths"]) & (lane == 2 * me + i)
        small = small + jnp.where(at, lengths_ref[i].astype(FULL), 0.0)
    small_ref[...] = small.astype(LOW)


def norm_parts(values):
    center = values - jnp.mean(values, axis=-1, keepdims=True)
    spread = jnp.mean(center * center, axis=-1, keepdims=True)
    return center, lax.rsqrt(spread + EPSILON)


def norm_back(center, scale, gain, grad):
    weighted = grad * gain
    mean_one = jnp.mean(weighted, axis=-1, keepdims=True)
    mean_two = jnp.mean(weighted * center, axis=-1, keepdims=True)
    back = scale * (weighted - mean_one - center * (scale * scale * mean_two))
    return back, jnp.sum(grad * center * scale, axis=0, keepdims=True), jnp.sum(
        grad, axis=0, keepdims=True
    )


def small_row(small_ref, name, count=1):
    return small_ref[...].astype(FULL)[ROWS[name] : ROWS[name] + count, :]


def project_body(order_ref, x_ref, small_ref, *refs):
    blocks = refs[:9]
    low_ref, proj_ref, weight, sem = refs[9:]
    model = x_ref.shape[1]
    copies = fetch(order_ref, blocks, weight, sem)
    center, scale = norm_parts(x_ref[...].astype(FULL))
    bias = small_row(small_ref, "qv_bias", 2)
    low_ref[...] = (
        center * scale * small_row(small_ref, "first_gain") + small_row(small_ref, "first_shift")
    ).astype(LOW)
    wait_all(copies)
    for j in range(3):
        lanes = slice(j * model, (j + 1) * model)
        part = dot(low_ref[...], weight[:, lanes])
        if j != 1:
            part = part + bias[j // 2 : j // 2 + 1]
        proj_ref[:, lanes] = part.astype(LOW)


def attend_body(seq, lengths_ref, proj_ref, att_out_ref, mixed_ref, att_ref, sem):
    model = mixed_ref.shape[1]
    cells = mixed_ref.shape[0] // seq
    pairs = model // (2 * HEAD)
    lane = lax.broadcasted_iota(jnp.int32, (seq, 2 * HEAD), 1)
    key = lax.broadcasted_iota(jnp.int32, (seq, seq), 0)

    def step(index, carry):
        s = index // pairs
        p = index % pairs
        rows = pl.ds(pl.multiple_of(s * seq, seq), seq)
        at = pl.multiple_of(p * 2 * HEAD, 2 * HEAD)
        q = proj_ref[rows, pl.ds(at, 2 * HEAD)] * jnp.asarray(HEAD ** (-0.5), LOW)
        k = proj_ref[rows, pl.ds(at + model, 2 * HEAD)]
        v_turned = proj_ref[rows, pl.ds(at + 2 * model, 2 * HEAD)].T
        visible = key < lengths_ref[s]
        mixed = []
        for i in range(2):
            own = (lane >= i * HEAD) & (lane < (i + 1) * HEAD)
            scores = dot(jnp.where(own, k, jnp.zeros_like(k)), q, ((1,), (1,)))
            scores = jnp.where(visible, scores, NEGATIVE)
            expo = jnp.exp(scores - jnp.max(scores, axis=0, keepdims=True))
            probs = expo * (1.0 / jnp.sum(expo, axis=0, keepdims=True))
            probs = probs.astype(LOW)
            att_ref[2 * index + i] = probs
            mixed.append(dot(v_turned[i * HEAD : (i + 1) * HEAD], probs))
        mixed_ref[rows, pl.ds(at, 2 * HEAD)] = jnp.concatenate(mixed, axis=0).T.astype(LOW)
        done = pl.ds(2 * index, 2)
        pltpu.make_async_copy(att_ref.at[done], att_out_ref.at[done], sem.at[index]).start()
        return carry

    lax.fori_loop(0, cells * pairs, step, 0, unroll=2)
    for index in range(cells * pairs):
        done = pl.ds(2 * index, 2)
        pltpu.make_async_copy(att_ref.at[done], att_out_ref.at[done], sem.at[index]).wait()


ERFC_STEP = 0.33
ERFC = (
    0.1863578228018033,
    0.18295566386742124,
    0.2012255082472392,
    0.04721561458875723,
    0.4085089979423051,
    -0.35115900736338407,
    0.4602422572120205,
    -0.13534686486277223,
)


def gelu_parts(inner):
    z = jnp.abs(inner) * (0.5**0.5)
    t = 1.0 / (1.0 + ERFC_STEP * z)
    tail = jnp.full_like(t, 0.5 * ERFC[-1])
    for factor in ERFC[-2::-1]:
        tail = tail * t + 0.5 * factor
    bell = jnp.exp(-(z * z))
    tail = tail * t * bell
    area = jnp.where(inner < 0.0, tail, 1.0 - tail)
    return inner * area, area + inner * bell * (0.5 / 3.141592653589793) ** 0.5


def row_mask(lengths_ref, rows, seq):
    at = lax.broadcasted_iota(jnp.int32, (rows, 1), 0)
    true = (at < lengths_ref[0]).astype(FULL)
    for s in range(1, rows // seq):
        true = jnp.where(at < s * seq, true, (at < lengths_ref[s] + s * seq).astype(FULL))
    return true


def loss_rows(lengths_ref, small_ref, other_ref, cot_ref, seq, whole):
    count = jnp.sum(
        small_row(small_ref, "lengths") + small_row(other_ref, "lengths"), axis=-1, keepdims=True
    )
    return cot_ref[...].astype(FULL) * (
        row_mask(lengths_ref, cot_ref.shape[0], seq) * (whole / count)
    )


def put_slots(keep_buf, slot_ref, values, first, lanes):
    rows = keep_buf.shape[1]
    for i in range(values.shape[0] // rows):
        keep_buf[slot_ref[first + i], :, lanes] = values[i * rows : (i + 1) * rows].astype(LOW)


def send_slots(buf, keep_ref, away_ref, sem):
    half = RING_SIZE
    copies = [
        pltpu.make_async_copy(buf.at[pl.ds(half, half)], away_ref, sem.at[0]),
        pltpu.make_async_copy(buf.at[pl.ds(0, half)], keep_ref, sem.at[1]),
    ]
    for item in copies:
        item.start()
    return copies


def inner_body(order_ref, x_ref, mixed_ref, small_ref, *refs):
    blocks = refs[:9]
    middle_ref, low_ref, active_ref, slope_ref, weight, sem = refs[9:]
    model = x_ref.shape[1]
    ff = active_ref.shape[1]
    wait_all(fetch(order_ref, blocks, weight, sem))
    middle = (
        x_ref[...].astype(FULL)
        + dot(mixed_ref[...], weight[:, ff:])
        + small_row(small_ref, "out_bias")
    )
    middle_ref[...] = middle
    center, scale = norm_parts(middle)
    low = center * scale * small_row(small_ref, "second_gain") + small_row(
        small_ref, "second_shift"
    )
    low_ref[...] = low.astype(LOW)
    step = 2 * (ff // RING_SIZE)
    bias = small_row(small_ref, "in_bias", 4)
    for j in range(ff // step):
        lanes = slice(j * step, (j + 1) * step)
        inner = dot(low_ref[...], weight[:, lanes]) + bias[j : j + 1]
        active, slope = gelu_parts(inner)
        active_ref[:, lanes] = active.astype(LOW)
        slope_ref[:, lanes] = slope.astype(LOW)


def grad_down_body(
    seq, whole, who_ref, slot_ref, lengths_ref, active_ref, cot_ref, small_ref, other_ref,
    up_ref, down_b_ref, keep_ref, away_ref, keep_two_ref, away_two_ref, slots, sem,
):
    up_low = loss_rows(lengths_ref, small_ref, other_ref, cot_ref, seq, whole).astype(LOW)
    up_ref[...] = up_low
    down_b_ref[...] = jnp.sum(up_low.astype(FULL), axis=0, keepdims=True)
    parts = RING_SIZE
    step = active_ref.shape[1] // parts
    rows = slots.shape[2]
    side = who_ref[1]
    for j in range(parts):
        grad = dot(active_ref[:, j * step : (j + 1) * step], up_ref[...], ((0,), (0,)))
        for i in range(4):
            slots[(i + side) % 2, slot_ref[j * CELLS // parts + i // 2]] = grad[
                i * rows : (i + 1) * rows
            ].astype(LOW)
    copies = send_slots(slots.at[1], keep_two_ref, away_two_ref, sem.at[1])
    copies += send_slots(slots.at[0], keep_ref, away_ref, sem.at[0])
    wait_all(copies)


def inner_back_body(order_ref, slope_ref, up_ref, *refs):
    blocks = refs[:9]
    inner_ref, in_b_ref, weight, sem = refs[9:]
    model = up_ref.shape[1]
    wait_all(fetch(order_ref, blocks, weight, sem))
    for j in range(inner_ref.shape[1] // model):
        lanes = slice(j * model, (j + 1) * model)
        grad = dot(up_ref[...], weight[lanes, :], ((1,), (1,)))
        low = (grad * slope_ref[:, lanes].astype(FULL)).astype(LOW)
        inner_ref[:, lanes] = low
        in_b_ref[j : j + 1, :] = jnp.sum(low.astype(FULL), axis=0, keepdims=True)


def down_body(active_ref, middle_ref, small_ref, weight_ref, out_ref):
    out_ref[...] = (
        middle_ref[...]
        + dot(active_ref[...], weight_ref[...])
        + small_row(small_ref, "down_bias")
    ).astype(LOW)


def grad_in_body(slot_ref, low_ref, inner_ref, keep_ref, away_ref, slots, sem):
    model = low_ref.shape[1]
    turned = low_ref[...].T
    for j in range(inner_ref.shape[1] // model):
        lanes = slice(j * model, (j + 1) * model)
        put_slots(slots, slot_ref, dot(turned, inner_ref[:, lanes]), 0, lanes)
    wait_all(send_slots(slots, keep_ref, away_ref, sem))


def middle_back_body(
    seq, whole, lengths_ref, inner_ref, middle_ref, cot_ref, small_ref, other_ref, weight,
    grad_ref, grad_low_ref, grad_mixed_ref, sums_ref,
):
    ff = inner_ref.shape[1]
    grad_second = dot(inner_ref[...], weight[:, :ff], ((1,), (1,)))
    center, scale = norm_parts(middle_ref[...])
    back, gain_sum, shift_sum = norm_back(
        center, scale, small_row(small_ref, "second_gain"), grad_second
    )
    grad = loss_rows(lengths_ref, small_ref, other_ref, cot_ref, seq, whole) + back
    grad_ref[...] = grad
    grad_low = grad.astype(LOW)
    grad_low_ref[...] = grad_low
    grad_mixed_ref[...] = dot(grad_low, weight[:, ff:], ((1,), (1,))).astype(LOW)
    sums_ref[0:1, :] = jnp.sum(grad_low.astype(FULL), axis=0, keepdims=True)
    sums_ref[1:2, :] = gain_sum
    sums_ref[2:3, :] = shift_sum


def attend_back_body(seq, begin, proj_ref, att_ref, grad_ref, out_ref):
    model = grad_ref.shape[1]
    half = out_ref.shape[1] // 3
    all_pairs = model // (2 * HEAD)
    pairs = half // (2 * HEAD)
    cells = grad_ref.shape[0] // seq
    lane = lax.broadcasted_iota(jnp.int32, (seq, 2 * HEAD), 1)
    scale = HEAD ** (-0.5)

    def step(index, carry):
        s = index // pairs
        p = index % pairs
        rows = pl.ds(pl.multiple_of(s * seq, seq), seq)
        to = pl.multiple_of(p * 2 * HEAD, 2 * HEAD)
        at = pl.multiple_of(to + begin * 2 * HEAD, 2 * HEAD)
        q = proj_ref[rows, pl.ds(at, 2 * HEAD)]
        k_turned = proj_ref[rows, pl.ds(at + model, 2 * HEAD)].T
        v = proj_ref[rows, pl.ds(at + 2 * model, 2 * HEAD)]
        g = grad_ref[rows, pl.ds(at, 2 * HEAD)]
        grad_q = []
        grad_k = []
        grad_v = []
        for i in range(2):
            own = (lane >= i * HEAD) & (lane < (i + 1) * HEAD)
            probs = att_ref[2 * (s * all_pairs + begin + p) + i]
            wide = probs.astype(FULL)
            grad_probs = dot(jnp.where(own, v, jnp.zeros_like(v)), g, ((1,), (1,)))
            delta = jnp.sum(wide * grad_probs, axis=0, keepdims=True)
            scores = (wide * (grad_probs - delta)).astype(LOW)
            grad_q.append(dot(k_turned[i * HEAD : (i + 1) * HEAD], scores))
            grad_k.append(dot(scores, q))
            grad_v.append(dot(probs, g))
        first = lane < HEAD
        out_ref[rows, pl.ds(to, 2 * HEAD)] = (
            jnp.concatenate(grad_q, axis=0).T * scale
        ).astype(LOW)
        out_ref[rows, pl.ds(to + half, 2 * HEAD)] = (
            jnp.where(first, grad_k[0], grad_k[1]) * scale
        ).astype(LOW)
        out_ref[rows, pl.ds(to + 2 * half, 2 * HEAD)] = jnp.where(
            first, grad_v[0], grad_v[1]
        ).astype(LOW)
        return carry

    lax.fori_loop(0, cells * pairs, step, 0, unroll=2)


def early_grad_body(
    slot_ref, low_ref, part_ref, mixed_ref, grad_low_ref, keep_ref, away_ref, slots, sem
):
    width = part_ref.shape[1]
    put_slots(slots, slot_ref, dot(low_ref[...].T, part_ref[...]), 0, slice(0, width))
    put_slots(
        slots, slot_ref, dot(mixed_ref[...].T, grad_low_ref[...]), 0,
        slice(width, slots.shape[2]),
    )
    wait_all(send_slots(slots, keep_ref, away_ref, sem))


def first_back_body(
    slot_ref, x_ref, low_ref, one_ref, two_ref, grad_ref, small_ref, sums_ref, in_b_ref,
    down_b_ref, weight, out_ref, keep_ref, away_ref, sum_ref, slots, sem,
):
    model = x_ref.shape[1]
    late = two_ref.shape[1]
    center, scale = norm_parts(x_ref[...].astype(FULL))
    parts = ((one_ref, 0), (two_ref, one_ref.shape[1] // 3))
    grad_first = jnp.zeros(x_ref.shape, FULL)
    for j in range(3):
        for ref, begin in parts:
            width = ref.shape[1] // 3
            at = j * model + begin
            grad_first = grad_first + dot(
                ref[:, j * width : (j + 1) * width], weight[:, at : at + width], ((1,), (1,))
            )
    put_slots(slots, slot_ref, dot(low_ref[...].T, two_ref[...]), 0, slice(0, late))
    back, gain_sum, shift_sum = norm_back(
        center, scale, small_row(small_ref, "first_gain"), grad_first
    )

    def put(name, value, offset=0):
        at = ROWS[name] + offset
        sum_ref[at : at + value.shape[0], :] = value

    sum_ref[...] = jnp.zeros_like(sum_ref)
    put("first_gain", gain_sum)
    put("first_shift", shift_sum)
    for j in range(2):
        at = ROWS["qv_bias"] + j
        for ref, begin in parts:
            width = ref.shape[1] // 3
            part = ref[:, 2 * j * width : (2 * j + 1) * width].astype(FULL)
            sum_ref[at : at + 1, begin : begin + width] = jnp.sum(part, axis=0, keepdims=True)
    put("out_bias", sums_ref[0:1, :])
    put("second_gain", sums_ref[1:2, :])
    put("second_shift", sums_ref[2:3, :])
    put("in_bias", in_b_ref[...])
    put("down_bias", down_b_ref[...])
    for i in range(3):
        part = sum_ref[:, SMALL_LANES * i : SMALL_LANES * (i + 1)].astype(LOW)
        for device in range(CELLS):
            slots[device, 16 * i : 16 * i + 16, late:] = part
    copies = send_slots(slots, keep_ref, away_ref, sem)
    out_ref[...] = (grad_ref[...] + back).astype(LOW)
    wait_all(copies)


def finish_body(who_ref, early_ref, early_two_ref, late_ref, late_two_ref, *refs):
    grad_ref, out_ref, vectors, small_ref = refs[0], refs[1], refs[2:-1], refs[-1]
    model = out_ref.shape[1]
    early = early_ref[...].astype(FULL) + early_two_ref[...].astype(FULL)
    late = late_ref[...].astype(FULL) + late_two_ref[...].astype(FULL)
    one = (early.shape[1] - model) // 3
    two = (late.shape[1] - SMALL_LANES) // 3
    for j in range(3):
        at = j * model
        grad_ref[:, at : at + one] = early[:, j * one : (j + 1) * one]
        grad_ref[:, at + one : at + model] = late[:, j * two : (j + 1) * two]
    out_ref[...] = early[:, 3 * one :]
    for i in range(3):
        small_ref[:, SMALL_LANES * i : SMALL_LANES * (i + 1)] = late[
            16 * i : 16 * i + 16, 3 * two :
        ]
    me = who_ref[0]
    row = lax.broadcasted_iota(jnp.int32, (SMALL_ROWS, model), 0)
    for name, ref in zip(NAMES, vectors):
        size = ref.shape[1]
        per_row = model // size
        here_row = jnp.where(row == ROWS[name] + me // per_row, small_ref[...], 0.0)
        values = jnp.sum(here_row, axis=0, keepdims=True)
        picker = one_hot(size, model, size * (me % per_row)).astype(FULL)
        ref[...] = lax.dot_general(
            values, picker, (((1,), (1,)), ((), ())), precision=lax.Precision.HIGHEST,
            preferred_element_type=FULL,
        )


def on_device_ring(
    tokens,
    lengths,
    cotangent,
    first_gain,
    first_shift,
    qkv_weight,
    qv_bias,
    out_weight,
    out_bias,
    second_gain,
    second_shift,
    in_weight,
    in_bias,
    down_weight,
    down_bias,
):
    micro, seq, model = tokens.shape[1:]
    total_rows = micro * seq
    rows = qkv_weight.shape[0]
    down_rows = down_weight.shape[0]
    ff = in_weight.shape[1]
    heads = model // HEAD
    whole = float(lax.axis_size("species") * CELLS * micro * seq)
    index, core, place = here()
    species = lax.axis_index("species")
    who = jnp.stack([index, species]).astype(jnp.int32)
    order = jnp.stack(gather_order(core, place)).astype(jnp.int32)
    slot = jnp.stack(scatter_slots(core, place)).astype(jnp.int32)
    lens = lengths.reshape(micro)
    x = tokens.reshape(total_rows, model)
    cot = cotangent.reshape(total_rows, model)
    vectors = (
        first_gain, first_shift, qv_bias, out_bias, second_gain, second_shift, in_bias, down_bias,
    )

    dma = pltpu.SemaphoreType.DMA

    def gathered(own, hops):
        got = [own]
        for item in hops:
            got += [item, to_partner(item)]
        return got

    own = both_blocks(qkv_weight, core)
    qkv_one = hop(own)
    (small,) = call(
        pack_body,
        [shape((SMALL_ROWS, model))],
        [who, after(lens, own)] + [item.reshape(1, -1) for item in vectors],
        [SMEM, SMEM] + [VMEM] * 8,
        vmem=4,
    )
    small = exchange(small, 1)
    in_weight, out_weight = lax.optimization_barrier((in_weight, out_weight, own))[:2]
    in_own = both_blocks(jnp.concatenate([in_weight, out_weight], axis=1), core)
    qkv_one, small, in_own = lax.optimization_barrier((qkv_one, small, in_own))
    qkv_two = hop(qkv_one)
    small = exchange(small, 2)
    down_own = both_blocks(after(down_weight, qkv_one), core)
    qkv_two, small, down_own = lax.optimization_barrier((qkv_two, small, down_own))
    qkv_three = hop(qkv_two)
    small = exchange(small, 4)
    qkv_three, small = lax.optimization_barrier((qkv_three, small))
    qkv_last = hop(half_of(qkv_three, core))
    small = exchange(small, 8)
    in_one = hop(after(in_own, qkv_three))
    low, proj, qkv_full = call(
        project_body,
        [
            shape((total_rows, model)),
            shape((total_rows, 3 * model)),
            shape((model, 3 * model)),
        ],
        [order, x, small] + gathered(own, (qkv_one, qkv_two, qkv_three, qkv_last)),
        [SMEM, VMEM, VMEM] + [ANY] * 9,
        scratch=[dma((CELLS,))],
        vmem=20,
        cost=K1 * UNIT,
    )
    other_small = across(small)
    in_one, proj = lax.optimization_barrier((in_one, proj))
    in_two = hop(in_one)
    down_one = hop(after(down_own, in_one))
    att, mixed = call(
        lambda *refs: attend_body(seq, *refs),
        [shape((micro * heads, seq, seq)), shape((total_rows, model))],
        [lens, proj],
        [SMEM, VMEM],
        [ANY, VMEM],
        scratch=[
            pltpu.VMEM((micro * heads, seq, seq), LOW),
            dma((micro * heads // 2,)),
        ],
        vmem=14,
    )
    in_two, mixed, down_one = lax.optimization_barrier((in_two, mixed, down_one))
    in_three = hop(in_two)
    down_two = hop(after(down_one, in_two))
    in_three, down_two, other_small = lax.optimization_barrier(
        (in_three, down_two, other_small)
    )
    in_last = hop(half_of(in_three, core))
    down_three = hop(after(down_two, in_three))
    in_got = gathered(in_own, (in_one, in_two, in_three, in_last))
    middle, low_two, active, slope, in_full = call(
        inner_body,
        [
            shape((total_rows, model), FULL),
            shape((total_rows, model)),
            shape((total_rows, ff)),
            shape((total_rows, ff)),
            shape((model, ff + model)),
        ],
        [order, x, after(mixed, down_two), small] + in_got,
        [SMEM] + [VMEM] * 3 + [ANY] * 9,
        scratch=[dma((CELLS,))],
        vmem=24,
    )
    down_three, active = lax.optimization_barrier((down_three, active))
    down_last = hop(half_of(down_three, core))
    up_low, down_b, down_keep, down_away, down_keep_two, down_away_two = call(
        lambda *refs: grad_down_body(seq, whole, *refs),
        [
            shape((total_rows, model)),
            shape((1, model), FULL),
        ]
        + [shape((RING_SIZE, down_rows // 2, model))] * 4,
        [who, slot, lens, active, cot, small, other_small],
        [SMEM] * 3 + [VMEM] * 4,
        [VMEM] * 2 + [ANY] * 4,
        scratch=[pltpu.VMEM((2, CELLS, down_rows // 2, model), LOW), dma((2, 2))],
        vmem=15,
    )

    down_away, down_away_two, down_last = lax.optimization_barrier(
        (down_away, down_away_two, down_last)
    )
    down_other_two = to_partner(down_away_two)
    down_other = to_partner(down_away)
    inner_low, in_b, down_full = call(
        inner_back_body,
        [
            shape((total_rows, ff)),
            shape((ff // model, model), FULL),
            shape((ff, model)),
        ],
        [order, slope, up_low]
        + gathered(down_own, (down_one, down_two, down_three, down_last)),
        [SMEM] + [VMEM] * 2 + [ANY] * 9,
        scratch=[dma((CELLS,))],
        vmem=20,
    )
    down_other_two, inner_low = lax.optimization_barrier((down_other_two, inner_low))
    down_x = across(add_low(down_keep_two[0:3], down_other_two[0:3]))
    down_x_two = across(add_low(down_keep_two[3:8], down_other_two[3:8]))
    in_keep, in_away = call(
        grad_in_body,
        [shape((RING_SIZE, rows, ff)), shape((RING_SIZE, rows, ff))],
        [slot, low_two, inner_low],
        [SMEM] + [VMEM] * 2,
        [ANY] * 2,
        scratch=[pltpu.VMEM((CELLS, rows, ff), LOW), dma((2,))],
        vmem=13,
    )
    in_other = to_partner(in_away)
    in_other, inner_low = lax.optimization_barrier((in_other, inner_low))
    in_sum = first_hop(in_keep, in_other)
    grad_middle, grad_low, grad_mixed, sums = call(
        lambda *refs: middle_back_body(seq, whole, *refs),
        [
            shape((total_rows, model), FULL),
            shape((total_rows, model)),
            shape((total_rows, model)),
            shape((3, model), FULL),
        ],
        [lens, inner_low, middle, cot, small, other_small, in_full],
        [SMEM] + [VMEM] * 6,
        vmem=19,
    )

    def attend_back(begin, pairs, grad):
        return call(
            lambda *refs: attend_back_body(seq, begin, *refs),
            [shape((total_rows, 6 * pairs * HEAD))],
            [proj, att, grad],
            [VMEM] * 3,
            vmem=11,
            cost=HEAVY if begin == 0 else K4 * UNIT,

        )[0]

    pairs = model // (2 * HEAD)
    early_pairs = 2 * pairs // 3
    in_sum, down_x, down_other, grad_mixed = lax.optimization_barrier(
        (in_sum, down_x, down_other, grad_mixed)
    )
    down_sum = first_hop(down_keep, down_other, down_x)
    in_sum = second_hop(in_sum, core, in_keep, in_other)
    grad_one = attend_back(0, early_pairs, grad_mixed)
    down_sum, grad_one = lax.optimization_barrier((down_sum, grad_one))
    down_sum = second_hop(down_sum, core, down_keep, down_other, down_x)
    early_width = 6 * early_pairs * HEAD + model
    early_keep, early_away = call(
        early_grad_body,
        [shape((RING_SIZE, rows, early_width))] * 2,
        [slot, low, grad_one, mixed, grad_low],
        [SMEM] + [VMEM] * 4,
        [ANY] * 2,
        scratch=[pltpu.VMEM((CELLS, rows, early_width), LOW), dma((2,))],
        vmem=12,
    )
    early_other = to_partner(early_away)
    in_sum, early_keep, grad_mixed = lax.optimization_barrier((in_sum, early_keep, grad_mixed))
    in_sum = later_hop(in_sum, 3, in_keep, in_other)
    grad_two = attend_back(early_pairs, pairs - early_pairs, grad_mixed)
    early_other, grad_two = lax.optimization_barrier((early_other, grad_two))
    early_sum = first_hop(early_keep, early_other)
    late_width = 6 * (pairs - early_pairs) * HEAD + SMALL_LANES
    grad_tokens, late_keep, late_away = call(
        first_back_body,
        [
            shape((total_rows, model)),
            shape((RING_SIZE, rows, late_width)),
            shape((RING_SIZE, rows, late_width)),
        ],
        [slot, x, low, grad_one, grad_two, grad_middle, small, sums, in_b, down_b, qkv_full],
        [SMEM] + [VMEM] * 10,
        [VMEM] + [ANY] * 2,
        scratch=[
            pltpu.VMEM((SMALL_ROWS, model), FULL),
            pltpu.VMEM((CELLS, rows, late_width), LOW),
            dma((2,)),
        ],
        vmem=16,

    )
    late_other = to_partner(late_away)
    in_sum, early_sum, late_keep, down_sum, down_x_two = lax.optimization_barrier(
        (in_sum, early_sum, late_keep, down_sum, down_x_two)
    )
    in_sum = later_hop(in_sum, 5, in_keep, in_other)
    early_sum = second_hop(early_sum, core, early_keep, early_other)
    down_sum = hop(add_low(down_sum, down_keep[3:5], down_other[3:5], down_x_two[0:2]))
    late_sum = first_hop(late_keep, late_other)
    late_sum, early_sum, down_sum = lax.optimization_barrier((late_sum, early_sum, down_sum))
    late_ready = late_sum
    down_sum = hop(add_low(down_sum, down_keep[5:7], down_other[5:7], down_x_two[2:4]))
    late_sum = second_hop(late_sum, core, late_keep, late_other)
    early_sum = later_hop(early_sum, 3, early_keep, early_other)
    (out_tokens,) = call(
        down_body,
        [shape((total_rows, model))],
        [after(active, late_ready), middle, small, down_full],
        [VMEM] * 4,
        vmem=13,
    )
    late_sum, early_sum, down_sum, in_sum, out_tokens = lax.optimization_barrier(
        (late_sum, early_sum, down_sum, in_sum, out_tokens)
    )
    late_sum = later_hop(late_sum, 3, late_keep, late_other)
    early_sum = later_hop(early_sum, 5, early_keep, early_other)
    in_sum = settle(in_sum, core, in_keep, in_other)
    in_terms = (in_sum, across(in_sum))
    mine = jnp.where(core == 0, down_sum[0], down_sum[1])
    other = to_partner(jnp.where(core == 0, down_sum[1], down_sum[0]))
    down_sum = add_low(mine, other, down_keep[7], down_other[7], down_x_two[4])
    down_terms = (down_sum, across(down_sum))
    late_sum = later_hop(late_sum, 5, late_keep, late_other)
    early_sum = settle(early_sum, core, early_keep, early_other)
    early_terms = (early_sum, across(early_sum))
    late_sum = settle(late_sum, core, late_keep, late_other)
    late_terms = (late_sum, across(late_sum))
    finished = call(
        finish_body,
        [shape((rows, 3 * model), FULL), shape((rows, model), FULL)]
        + [shape((1, item.shape[0]), FULL) for item in vectors],
        [who] + list(early_terms) + list(late_terms),
        [SMEM] + [VMEM] * 4,
        scratch=[pltpu.VMEM((SMALL_ROWS, model), FULL)],
        vmem=6,
    )
    grad_qkv, grad_out = finished[:2]
    pieces = [item.reshape(-1) for item in finished[2:]]
    return (
        out_tokens.reshape(tokens.shape),
        grad_tokens.reshape(tokens.shape),
        pieces[0],
        pieces[1],
        grad_qkv,
        pieces[2],
        grad_out,
        pieces[3],
        pieces[4],
        pieces[5],
        in_terms[0].astype(FULL) + in_terms[1].astype(FULL),
        pieces[6],
        jnp.concatenate(
            [
                jnp.where(species == 0, down_terms[0], down_terms[1]),
                jnp.where(species == 0, down_terms[1], down_terms[0]),
            ]
        ).astype(FULL),
        pieces[7],
    )


def on_device(
    tokens,
    lengths,
    cotangent,
    first_gain,
    first_shift,
    qkv_weight,
    qv_bias,
    out_weight,
    out_bias,
    second_gain,
    second_shift,
    in_weight,
    in_bias,
    down_weight,
    down_bias,
):
    local_count = jnp.sum(lengths).astype(jnp.float32)
    count = lax.psum(local_count, ("species", "cells"))
    micro_count = tokens.shape[1]
    seq_rows = tokens.shape[2]
    factor = (
        float(lax.axis_size("species") * lax.axis_size("cells") * micro_count * seq_rows) / count
    )
    output_rows = []
    gradient_rows = []
    summed = None
    for micro_step in range(micro_count):
        gathered = (
            lax.all_gather(first_gain, "cells", axis=0, tiled=True),
            lax.all_gather(first_shift, "cells", axis=0, tiled=True),
            lax.all_gather(qkv_weight, "cells", axis=0, tiled=True),
            lax.all_gather(qv_bias, "cells", axis=0, tiled=True),
            lax.all_gather(out_weight, "cells", axis=0, tiled=True),
            lax.all_gather(out_bias, "cells", axis=0, tiled=True),
            lax.all_gather(second_gain, "cells", axis=0, tiled=True),
            lax.all_gather(second_shift, "cells", axis=0, tiled=True),
            lax.all_gather(in_weight, "cells", axis=0, tiled=True),
            lax.all_gather(in_bias, "cells", axis=0, tiled=True),
            lax.all_gather(down_weight, "cells", axis=0, tiled=True),
            lax.all_gather(down_bias, "cells", axis=0, tiled=True),
        )
        out_seq, grad_seq, grads = sequence_pass(
            gathered,
            tokens[0, micro_step],
            lengths[0, micro_step],
            cotangent[0, micro_step],
            factor,
        )
        output_rows.append(out_seq)
        gradient_rows.append(grad_seq)
        shares = (
            lax.psum_scatter(grads[0], "cells", scatter_dimension=0, tiled=True),
            lax.psum_scatter(grads[1], "cells", scatter_dimension=0, tiled=True),
            lax.psum_scatter(grads[2], "cells", scatter_dimension=0, tiled=True),
            lax.psum_scatter(grads[3], "cells", scatter_dimension=0, tiled=True),
            lax.psum_scatter(grads[4], "cells", scatter_dimension=0, tiled=True),
            lax.psum_scatter(grads[5], "cells", scatter_dimension=0, tiled=True),
            lax.psum_scatter(grads[6], "cells", scatter_dimension=0, tiled=True),
            lax.psum_scatter(grads[7], "cells", scatter_dimension=0, tiled=True),
            lax.psum_scatter(grads[8], "cells", scatter_dimension=0, tiled=True),
            lax.psum_scatter(grads[9], "cells", scatter_dimension=0, tiled=True),
            lax.psum_scatter(grads[10], "cells", scatter_dimension=0, tiled=True),
            lax.psum_scatter(grads[11], "cells", scatter_dimension=0, tiled=True),
        )
        summed = shares if summed is None else jax.tree.map(jnp.add, summed, shares)
    final = (
        lax.psum(summed[0].astype(jnp.bfloat16), "species").astype(jnp.float32),
        lax.psum(summed[1].astype(jnp.bfloat16), "species").astype(jnp.float32),
        lax.psum(summed[2].astype(jnp.bfloat16), "species").astype(jnp.float32),
        lax.psum(summed[3].astype(jnp.bfloat16), "species").astype(jnp.float32),
        lax.psum(summed[4].astype(jnp.bfloat16), "species").astype(jnp.float32),
        lax.psum(summed[5].astype(jnp.bfloat16), "species").astype(jnp.float32),
        lax.psum(summed[6].astype(jnp.bfloat16), "species").astype(jnp.float32),
        lax.psum(summed[7].astype(jnp.bfloat16), "species").astype(jnp.float32),
        lax.psum(summed[8].astype(jnp.bfloat16), "species").astype(jnp.float32),
        lax.psum(summed[9].astype(jnp.bfloat16), "species").astype(jnp.float32),
        lax.psum(summed[10].astype(jnp.bfloat16), "species").astype(jnp.float32),
        lax.psum(summed[11].astype(jnp.bfloat16), "species").astype(jnp.float32),
    )
    out_tokens = jnp.stack(output_rows)[None]
    grad_tokens = jnp.stack(gradient_rows)[None]
    return (out_tokens, grad_tokens) + tuple(final)


def solution(mesh):
    in_specs = (
        P("species", "cells", None, None),
        P("species", "cells"),
        P("species", "cells", None, None),
        P("cells"),
        P("cells"),
        P("cells", None),
        P("cells"),
        P("cells", None),
        P("cells"),
        P("cells"),
        P("cells"),
        P("cells", None),
        P("cells"),
        P("cells", None),
        P("cells"),
    )
    out_specs = (
        P("species", "cells", None, None),
        P("species", "cells", None, None),
        P("cells"),
        P("cells"),
        P("cells", None),
        P("cells"),
        P("cells", None),
        P("cells"),
        P("cells"),
        P("cells"),
        P("cells", None),
        P("cells"),
        P("cells", None),
        P("cells"),
    )
    program = on_device_ring if mesh.shape["cells"] == 2 * RING_SIZE else on_device
    return jax.shard_map(
        program, mesh=mesh, in_specs=in_specs, out_specs=out_specs, check_vma=False
    )
```

```python
import jax
import jax.numpy as jnp
from jax import lax
from jax.experimental import pallas as pl
from jax.experimental.pallas import tpu as pltpu
from jax.sharding import PartitionSpec as P

HEAD = 64


EPSILON = 1e-12
NEGATIVE = -1e30


def normalize(values, gain_vec, shift_vec):
    center = values - jnp.mean(values, axis=-1, keepdims=True)
    spread = jnp.mean(center * center, axis=-1, keepdims=True)
    return center * lax.rsqrt(spread + EPSILON) * gain_vec + shift_vec


def smooth_gate(values):
    return jax.nn.gelu(values, approximate=False)


def times_left(left_side, right_side):
    return lax.dot_general(
        left_side, right_side, (((0,), (0,)), ((), ())), preferred_element_type=jnp.float32
    )


def times_right(left_side, right_side):
    return lax.dot_general(
        left_side, right_side, (((1,), (1,)), ((), ())), preferred_element_type=jnp.float32
    )


def sequence_pass(weights, inputs, length, cot_rows, factor):
    (
        first_gain,
        first_shift,
        qkv_weight,
        qv_bias,
        out_weight,
        out_bias,
        second_gain,
        second_shift,
        in_weight,
        in_bias,
        down_weight,
        down_bias,
    ) = weights
    seq_rows = inputs.shape[0]
    model_width = inputs.shape[1]
    heads_count = model_width // HEAD
    scale_qk = float(HEAD) ** (-0.5)
    as_float = inputs.astype(jnp.float32)
    hidden_one, first_pull = jax.vjp(
        normalize, as_float, first_gain.astype(jnp.float32), first_shift.astype(jnp.float32)
    )
    first_low = hidden_one.astype(jnp.bfloat16)
    bias_float = qv_bias.astype(jnp.float32)
    full_bias = jnp.concatenate(
        [bias_float[:model_width], jnp.zeros((model_width,), jnp.float32), bias_float[model_width:]]
    )
    projected = (
        jnp.dot(first_low, qkv_weight, preferred_element_type=jnp.float32) + full_bias
    ).astype(jnp.bfloat16)
    split_heads = projected.reshape(seq_rows, 3, heads_count, HEAD)
    queries = split_heads[:, 0]
    keys_part = split_heads[:, 1]
    values_part = split_heads[:, 2]
    visible = jnp.arange(seq_rows) < length

    def scores_of():
        raw_scores = (
            jnp.einsum("qhd,khd->hqk", queries, keys_part, preferred_element_type=jnp.float32)
            * scale_qk
        )
        return jnp.where(visible[None, None, :], raw_scores, NEGATIVE)

    scores = scores_of()
    top_score = jnp.max(scores, axis=-1, keepdims=True)
    expo = jnp.exp(scores - top_score)
    total_exp = jnp.sum(expo, axis=-1, keepdims=True)
    log_total = top_score + jnp.log(total_exp)
    attention = (expo / total_exp).astype(jnp.bfloat16)
    mixed = jnp.einsum("hqk,khd->qhd", attention, values_part, preferred_element_type=jnp.float32)
    mixed = mixed.reshape(seq_rows, model_width).astype(jnp.bfloat16)
    middle = (
        as_float
        + jnp.dot(mixed, out_weight, preferred_element_type=jnp.float32)
        + out_bias.astype(jnp.float32)
    )
    hidden_two, second_pull = jax.vjp(
        normalize, middle, second_gain.astype(jnp.float32), second_shift.astype(jnp.float32)
    )
    second_low = hidden_two.astype(jnp.bfloat16)
    inner = jnp.dot(second_low, in_weight, preferred_element_type=jnp.float32) + in_bias.astype(
        jnp.float32
    )
    active, gate_pull = jax.vjp(smooth_gate, inner)
    active_low = active.astype(jnp.bfloat16)
    output = (
        middle
        + jnp.dot(active_low, down_weight, preferred_element_type=jnp.float32)
        + down_bias.astype(jnp.float32)
    )
    upstream = cot_rows.astype(jnp.float32) * visible[:, None].astype(jnp.float32) * factor
    up_low = upstream.astype(jnp.bfloat16)
    grad_down_bias = jnp.sum(up_low.astype(jnp.float32), axis=0)
    grad_down = times_left(active_low, up_low)
    grad_active = times_right(up_low, down_weight)
    (grad_inner,) = gate_pull(grad_active)
    inner_low = grad_inner.astype(jnp.bfloat16)
    grad_in_bias = jnp.sum(inner_low.astype(jnp.float32), axis=0)
    grad_in = times_left(second_low, inner_low)
    grad_second = times_right(inner_low, in_weight)
    grad_middle_norm, grad_second_gain, grad_second_shift = second_pull(grad_second)
    grad_middle = upstream + grad_middle_norm
    middle_low = grad_middle.astype(jnp.bfloat16)
    grad_out_bias = jnp.sum(middle_low.astype(jnp.float32), axis=0)
    grad_out = times_left(mixed, middle_low)
    grad_mixed = (
        times_right(middle_low, out_weight)
        .astype(jnp.bfloat16)
        .reshape(seq_rows, heads_count, HEAD)
    )
    probs_again = jnp.exp(scores_of() - log_total)
    grad_probs = jnp.einsum(
        "qhd,khd->hqk", grad_mixed, values_part, preferred_element_type=jnp.float32
    )
    grad_values = jnp.einsum(
        "hqk,qhd->khd", attention, grad_mixed, preferred_element_type=jnp.float32
    )
    delta = jnp.sum(probs_again * grad_probs, axis=-1, keepdims=True)
    grad_scores = (probs_again * (grad_probs - delta)).astype(jnp.bfloat16)
    grad_queries = (
        jnp.einsum("hqk,khd->qhd", grad_scores, keys_part, preferred_element_type=jnp.float32)
        * scale_qk
    )
    grad_keys = (
        jnp.einsum("hqk,qhd->khd", grad_scores, queries, preferred_element_type=jnp.float32)
        * scale_qk
    )
    grad_projected = jnp.stack([grad_queries, grad_keys, grad_values], axis=1)
    grad_projected = grad_projected.reshape(seq_rows, 3 * model_width).astype(jnp.bfloat16)
    column_sums = jnp.sum(grad_projected.astype(jnp.float32), axis=0)
    grad_qv = jnp.concatenate([column_sums[:model_width], column_sums[2 * model_width :]])
    grad_qkv = times_left(first_low, grad_projected)
    grad_first = times_right(grad_projected, qkv_weight)
    grad_input_norm, grad_first_gain, grad_first_shift = first_pull(grad_first)
    grad_inputs = grad_middle + grad_input_norm
    grads = (
        grad_first_gain,
        grad_first_shift,
        grad_qkv,
        grad_qv,
        grad_out,
        grad_out_bias,
        grad_second_gain,
        grad_second_shift,
        grad_in,
        grad_in_bias,
        grad_down,
        grad_down_bias,
    )
    return (output.astype(jnp.bfloat16), grad_inputs.astype(jnp.bfloat16), grads)


RING = (0, 2, 4, 6, 7, 5, 3, 1)
RING_SIZE = len(RING)
CELLS = 2 * RING_SIZE
ANY = pl.BlockSpec(memory_space=pl.ANY)
HBM = pl.BlockSpec(memory_space=pltpu.HBM)
VMEM = pl.BlockSpec(memory_space=pltpu.VMEM)
SMEM = pl.BlockSpec(memory_space=pltpu.SMEM)
LOW = jnp.bfloat16
FULL = jnp.float32
HEAVY = 10**10
UNIT = 10**8
ROWS = {
    "first_gain": 0,
    "first_shift": 1,
    "qv_bias": 2,
    "out_bias": 4,
    "second_gain": 5,
    "second_shift": 6,
    "in_bias": 7,
    "down_bias": 11,
    "lengths": 12,
}
NAMES = tuple(ROWS)[:8]
SMALL_ROWS = 16
SMALL_LANES = 256
PIECES = (2, 2, 2, 2, 2, 2, 2, 1, 1)


def ring_pairs():
    pairs = []
    for place in range(RING_SIZE):
        chip = RING[place]
        right = RING[(place + 1) % RING_SIZE]
        left = RING[(place - 1) % RING_SIZE]
        pairs.append((2 * chip, 2 * right))
        pairs.append((2 * chip + 1, 2 * left + 1))
    return pairs


def hop(block):
    return lax.ppermute(block, "cells", ring_pairs())


def to_partner(block):
    return lax.ppermute(block, "cells", [(i, i ^ 1) for i in range(CELLS)])


def across(block):
    return lax.ppermute(block, "species", [(0, 1), (1, 0)])


def exchange(values, bit):
    return values + lax.ppermute(values, "cells", [(i, i ^ bit) for i in range(CELLS)])


def after(value, *others):
    return lax.optimization_barrier((value,) + others)[0]


def here():
    index = lax.axis_index("cells")
    core = index % 2
    chip = index // 2
    place = jnp.int32(0)
    for i, ring_chip in enumerate(RING):
        place = jnp.where(chip == ring_chip, i, place)
    return index, core, place


def chip_at(place):
    place = place % RING_SIZE
    chip = jnp.zeros_like(place)
    for i, ring_chip in enumerate(RING):
        chip = jnp.where(place == i, ring_chip, chip)
    return chip


def gather_order(core, place):
    sign = 1 - 2 * core
    order = []

    def pair(at):
        order.append(2 * chip_at(at))
        order.append(2 * chip_at(at) + 1)

    pair(place)
    for step in range(1, 4):
        pair(place - sign * step)
        pair(place + sign * step)
    order.append(2 * chip_at(place + 4) + core)
    order.append(2 * chip_at(place + 4) + 1 - core)
    return order


def scatter_slots(core, place):
    def kept(core_now):
        sign = 1 - 2 * core_now
        order = [2 * chip_at(place + 4) + core_now]
        for step in (3, 2, 1):
            order.append(2 * chip_at(place + sign * step))
            order.append(2 * chip_at(place + sign * step) + 1)
        order.append(2 * chip_at(place) + core_now)
        return order

    order = kept(core) + kept(1 - core)
    slots = []
    for device in range(CELLS):
        slot = jnp.int32(0)
        for i, who in enumerate(order):
            slot = jnp.where(who == device, i, slot)
        slots.append(slot)
    return slots


def both_blocks(block, core):
    other = to_partner(block)
    return jnp.stack([jnp.where(core == 0, block, other), jnp.where(core == 0, other, block)])


def half_of(pair, core):
    return jnp.where(core == 0, pair[0], pair[1])[None]


def add_low(*parts):
    total = parts[0].astype(FULL)
    for part in parts[1:]:
        total = total + part.astype(FULL)
    return total.astype(LOW)


def first_hop(*parts):
    return hop(add_low(*[part[0:1] for part in parts]))


def second_hop(moving, core, *parts):
    wide = jnp.stack([jnp.where(core == 0, moving[0], 0), jnp.where(core == 0, 0, moving[0])])
    return hop(add_low(wide, *[part[1:3] for part in parts]))


def later_hop(moving, at, *parts):
    return hop(add_low(moving, *[part[at : at + 2] for part in parts]))


def settle(moving, core, *parts):
    mine = jnp.where(core == 0, moving[0], moving[1])
    other = jnp.where(core == 0, moving[1], moving[0])
    return add_low(mine, to_partner(other), *[part[7] for part in parts])


def dot(left, right, dims=((1,), (0,))):
    return lax.dot_general(left, right, (dims, ((), ())), preferred_element_type=FULL)


def call(body, out_shape, ins, specs, out_specs=None, scratch=(), vmem=48, cost=HEAVY):
    return pl.pallas_call(
        body,
        out_shape=out_shape,
        in_specs=specs,
        out_specs=[VMEM] * len(out_shape) if out_specs is None else out_specs,
        scratch_shapes=list(scratch),
        compiler_params=pltpu.CompilerParams(vmem_limit_bytes=vmem * 2**20),
        cost_estimate=pl.CostEstimate(flops=cost, bytes_accessed=0, transcendentals=0),
    )(*ins)


def shape(dims, kind=LOW):
    return jax.ShapeDtypeStruct(dims, kind)


def fetch(order_ref, refs, target, sem):
    rows = target.shape[0] // CELLS
    copies = []
    index = 0
    for source, size in zip(refs, PIECES):
        for part in range(size):
            at = order_ref[index]
            copies.append(
                pltpu.make_async_copy(
                    source.at[part],
                    target.at[pl.ds(pl.multiple_of(at * rows, 16), rows)],
                    sem.at[index],
                )
            )
            index += 1
    for item in copies:
        item.start()
    return copies


def wait_all(copies):
    for item in copies:
        item.wait()


def one_hot(rows, lanes, offset):
    row = lax.broadcasted_iota(jnp.int32, (rows, lanes), 0)
    lane = lax.broadcasted_iota(jnp.int32, (rows, lanes), 1)
    return lane == row + offset


def pack_body(who_ref, lengths_ref, *refs):
    sources, small_ref = refs[:8], refs[8]
    me = who_ref[0]
    model = small_ref.shape[1]
    row = lax.broadcasted_iota(jnp.int32, (SMALL_ROWS, model), 0)
    lane = lax.broadcasted_iota(jnp.int32, (SMALL_ROWS, model), 1)
    small = jnp.zeros((SMALL_ROWS, model), FULL)
    for name, ref in zip(NAMES, sources):
        size = ref.shape[1]
        per_row = model // size
        placed = dot(ref[...], one_hot(size, model, size * (me % per_row)).astype(LOW))
        small = small + jnp.where(row == ROWS[name] + me // per_row, placed, 0.0)
    for i in range(2):
        at = (row == ROWS["lengths"]) & (lane == 2 * me + i)
        small = small + jnp.where(at, lengths_ref[i].astype(FULL), 0.0)
    small_ref[...] = small.astype(LOW)


def norm_parts(values):
    center = values - jnp.mean(values, axis=-1, keepdims=True)
    spread = jnp.mean(center * center, axis=-1, keepdims=True)
    return center, lax.rsqrt(spread + EPSILON)


def norm_back(center, scale, gain, grad):
    weighted = grad * gain
    mean_one = jnp.mean(weighted, axis=-1, keepdims=True)
    mean_two = jnp.mean(weighted * center, axis=-1, keepdims=True)
    back = scale * (weighted - mean_one - center * (scale * scale * mean_two))
    return back, jnp.sum(grad * center * scale, axis=0, keepdims=True), jnp.sum(
        grad, axis=0, keepdims=True
    )


def small_row(small_ref, name, count=1):
    return small_ref[...].astype(FULL)[ROWS[name] : ROWS[name] + count, :]


def project_body(order_ref, x_ref, small_ref, *refs):
    blocks = refs[:9]
    low_ref, proj_ref, weight, sem = refs[9:]
    model = x_ref.shape[1]
    copies = fetch(order_ref, blocks, weight, sem)
    center, scale = norm_parts(x_ref[...].astype(FULL))
    bias = small_row(small_ref, "qv_bias", 2)
    low_ref[...] = (
        center * scale * small_row(small_ref, "first_gain") + small_row(small_ref, "first_shift")
    ).astype(LOW)
    wait_all(copies)
    for j in range(3):
        lanes = slice(j * model, (j + 1) * model)
        part = dot(low_ref[...], weight[:, lanes])
        if j != 1:
            part = part + bias[j // 2 : j // 2 + 1]
        proj_ref[:, lanes] = part.astype(LOW)


def attend_body(seq, lengths_ref, proj_ref, att_ref, mixed_ref):
    model = mixed_ref.shape[1]
    cells = mixed_ref.shape[0] // seq
    pairs = model // (2 * HEAD)
    lane = lax.broadcasted_iota(jnp.int32, (seq, 2 * HEAD), 1)
    key = lax.broadcasted_iota(jnp.int32, (seq, seq), 0)

    def step(index, carry):
        s = index // pairs
        p = index % pairs
        rows = pl.ds(pl.multiple_of(s * seq, seq), seq)
        at = pl.multiple_of(p * 2 * HEAD, 2 * HEAD)
        q = proj_ref[rows, pl.ds(at, 2 * HEAD)] * jnp.asarray(HEAD ** (-0.5), LOW)
        k = proj_ref[rows, pl.ds(at + model, 2 * HEAD)]
        v_turned = proj_ref[rows, pl.ds(at + 2 * model, 2 * HEAD)].T
        visible = key < lengths_ref[s]
        mixed = []
        for i in range(2):
            own = (lane >= i * HEAD) & (lane < (i + 1) * HEAD)
            scores = dot(jnp.where(own, k, jnp.zeros_like(k)), q, ((1,), (1,)))
            scores = jnp.where(visible, scores, NEGATIVE)
            expo = jnp.exp(scores - jnp.max(scores, axis=0, keepdims=True))
            probs = expo * (1.0 / jnp.sum(expo, axis=0, keepdims=True))
            probs = probs.astype(LOW)
            att_ref[2 * index + i] = probs
            mixed.append(dot(v_turned[i * HEAD : (i + 1) * HEAD], probs))
        mixed_ref[rows, pl.ds(at, 2 * HEAD)] = jnp.concatenate(mixed, axis=0).T.astype(LOW)
        return carry

    lax.fori_loop(0, cells * pairs, step, 0, unroll=2)


ERFC_STEP = 0.33
ERFC = (
    0.1863578228018033,
    0.18295566386742124,
    0.2012255082472392,
    0.04721561458875723,
    0.4085089979423051,
    -0.35115900736338407,
    0.4602422572120205,
    -0.13534686486277223,
)


def gelu_parts(inner):
    z = jnp.abs(inner) * (0.5**0.5)
    t = 1.0 / (1.0 + ERFC_STEP * z)
    tail = jnp.full_like(t, 0.5 * ERFC[-1])
    for factor in ERFC[-2::-1]:
        tail = tail * t + 0.5 * factor
    bell = jnp.exp(-(z * z))
    tail = tail * t * bell
    area = jnp.where(inner < 0.0, tail, 1.0 - tail)
    return inner * area, area + inner * bell * (0.5 / 3.141592653589793) ** 0.5


def row_mask(lengths_ref, rows, seq):
    at = lax.broadcasted_iota(jnp.int32, (rows, 1), 0)
    true = (at < lengths_ref[0]).astype(FULL)
    for s in range(1, rows // seq):
        true = jnp.where(at < s * seq, true, (at < lengths_ref[s] + s * seq).astype(FULL))
    return true


def loss_rows(lengths_ref, small_ref, other_ref, cot_ref, seq, whole):
    count = jnp.sum(
        small_row(small_ref, "lengths") + small_row(other_ref, "lengths"), axis=-1, keepdims=True
    )
    return cot_ref[...].astype(FULL) * (
        row_mask(lengths_ref, cot_ref.shape[0], seq) * (whole / count)
    )


def put_slots(keep_buf, slot_ref, values, first, lanes):
    rows = keep_buf.shape[1]
    for i in range(values.shape[0] // rows):
        keep_buf[slot_ref[first + i], :, lanes] = values[i * rows : (i + 1) * rows].astype(LOW)


def send_slots(buf, keep_ref, away_ref, sem):
    half = RING_SIZE
    copies = [
        pltpu.make_async_copy(buf.at[pl.ds(half, half)], away_ref, sem.at[0]),
        pltpu.make_async_copy(buf.at[pl.ds(0, half)], keep_ref, sem.at[1]),
    ]
    for item in copies:
        item.start()
    return copies


def inner_body(order_ref, x_ref, mixed_ref, small_ref, *refs):
    blocks = refs[:9]
    middle_ref, low_ref, active_ref, slope_ref, weight, sem = refs[9:]
    model = x_ref.shape[1]
    ff = active_ref.shape[1]
    wait_all(fetch(order_ref, blocks, weight, sem))
    middle = (
        x_ref[...].astype(FULL)
        + dot(mixed_ref[...], weight[:, ff:])
        + small_row(small_ref, "out_bias")
    )
    middle_ref[...] = middle
    center, scale = norm_parts(middle)
    low = center * scale * small_row(small_ref, "second_gain") + small_row(
        small_ref, "second_shift"
    )
    low_ref[...] = low.astype(LOW)
    step = 2 * (ff // RING_SIZE)
    bias = small_row(small_ref, "in_bias", 4)
    for j in range(ff // step):
        lanes = slice(j * step, (j + 1) * step)
        inner = dot(low_ref[...], weight[:, lanes]) + bias[j : j + 1]
        active, slope = gelu_parts(inner)
        active_ref[:, lanes] = active.astype(LOW)
        slope_ref[:, lanes] = slope.astype(LOW)


def grad_down_body(
    seq, whole, who_ref, slot_ref, lengths_ref, active_ref, cot_ref, small_ref, other_ref,
    up_ref, down_b_ref, keep_ref, away_ref, keep_two_ref, away_two_ref, slots, sem,
):
    up_low = loss_rows(lengths_ref, small_ref, other_ref, cot_ref, seq, whole).astype(LOW)
    up_ref[...] = up_low
    down_b_ref[...] = jnp.sum(up_low.astype(FULL), axis=0, keepdims=True)
    parts = RING_SIZE
    step = active_ref.shape[1] // parts
    rows = slots.shape[2]
    side = who_ref[1]
    for j in range(parts):
        grad = dot(active_ref[:, j * step : (j + 1) * step], up_ref[...], ((0,), (0,)))
        for i in range(4):
            slots[(i + side) % 2, slot_ref[j * CELLS // parts + i // 2]] = grad[
                i * rows : (i + 1) * rows
            ].astype(LOW)
    copies = send_slots(slots.at[1], keep_two_ref, away_two_ref, sem.at[1])
    copies += send_slots(slots.at[0], keep_ref, away_ref, sem.at[0])
    wait_all(copies)


def inner_back_body(order_ref, slope_ref, up_ref, *refs):
    blocks = refs[:9]
    inner_ref, in_b_ref, weight, sem = refs[9:]
    model = up_ref.shape[1]
    wait_all(fetch(order_ref, blocks, weight, sem))
    for j in range(inner_ref.shape[1] // model):
        lanes = slice(j * model, (j + 1) * model)
        grad = dot(up_ref[...], weight[lanes, :], ((1,), (1,)))
        low = (grad * slope_ref[:, lanes].astype(FULL)).astype(LOW)
        inner_ref[:, lanes] = low
        in_b_ref[j : j + 1, :] = jnp.sum(low.astype(FULL), axis=0, keepdims=True)


def down_body(active_ref, middle_ref, small_ref, weight_ref, out_ref):
    out_ref[...] = (
        middle_ref[...]
        + dot(active_ref[...], weight_ref[...])
        + small_row(small_ref, "down_bias")
    ).astype(LOW)


def grad_in_body(slot_ref, low_ref, inner_ref, keep_ref, away_ref, slots, sem):
    model = low_ref.shape[1]
    turned = low_ref[...].T
    for j in range(inner_ref.shape[1] // model):
        lanes = slice(j * model, (j + 1) * model)
        put_slots(slots, slot_ref, dot(turned, inner_ref[:, lanes]), 0, lanes)
    wait_all(send_slots(slots, keep_ref, away_ref, sem))


def middle_back_body(
    seq, whole, lengths_ref, inner_ref, middle_ref, cot_ref, small_ref, other_ref, weight,
    grad_ref, grad_low_ref, grad_mixed_ref, sums_ref,
):
    ff = inner_ref.shape[1]
    grad_second = dot(inner_ref[...], weight[:, :ff], ((1,), (1,)))
    center, scale = norm_parts(middle_ref[...])
    back, gain_sum, shift_sum = norm_back(
        center, scale, small_row(small_ref, "second_gain"), grad_second
    )
    grad = loss_rows(lengths_ref, small_ref, other_ref, cot_ref, seq, whole) + back
    grad_ref[...] = grad
    grad_low = grad.astype(LOW)
    grad_low_ref[...] = grad_low
    grad_mixed_ref[...] = dot(grad_low, weight[:, ff:], ((1,), (1,))).astype(LOW)
    sums_ref[0:1, :] = jnp.sum(grad_low.astype(FULL), axis=0, keepdims=True)
    sums_ref[1:2, :] = gain_sum
    sums_ref[2:3, :] = shift_sum


def attend_back_body(seq, begin, proj_ref, att_ref, grad_ref, out_ref):
    model = grad_ref.shape[1]
    half = out_ref.shape[1] // 3
    all_pairs = model // (2 * HEAD)
    pairs = half // (2 * HEAD)
    cells = grad_ref.shape[0] // seq
    lane = lax.broadcasted_iota(jnp.int32, (seq, 2 * HEAD), 1)
    scale = HEAD ** (-0.5)

    def step(index, carry):
        s = index // pairs
        p = index % pairs
        rows = pl.ds(pl.multiple_of(s * seq, seq), seq)
        to = pl.multiple_of(p * 2 * HEAD, 2 * HEAD)
        at = pl.multiple_of(to + begin * 2 * HEAD, 2 * HEAD)
        q = proj_ref[rows, pl.ds(at, 2 * HEAD)]
        k_turned = proj_ref[rows, pl.ds(at + model, 2 * HEAD)].T
        v = proj_ref[rows, pl.ds(at + 2 * model, 2 * HEAD)]
        g = grad_ref[rows, pl.ds(at, 2 * HEAD)]
        grad_q = []
        grad_k = []
        grad_v = []
        for i in range(2):
            own = (lane >= i * HEAD) & (lane < (i + 1) * HEAD)
            probs = att_ref[2 * (s * all_pairs + begin + p) + i]
            wide = probs.astype(FULL)
            grad_probs = dot(jnp.where(own, v, jnp.zeros_like(v)), g, ((1,), (1,)))
            delta = jnp.sum(wide * grad_probs, axis=0, keepdims=True)
            scores = (wide * (grad_probs - delta)).astype(LOW)
            grad_q.append(dot(k_turned[i * HEAD : (i + 1) * HEAD], scores))
            grad_k.append(dot(scores, q))
            grad_v.append(dot(probs, g))
        first = lane < HEAD
        out_ref[rows, pl.ds(to, 2 * HEAD)] = (
            jnp.concatenate(grad_q, axis=0).T * scale
        ).astype(LOW)
        out_ref[rows, pl.ds(to + half, 2 * HEAD)] = (
            jnp.where(first, grad_k[0], grad_k[1]) * scale
        ).astype(LOW)
        out_ref[rows, pl.ds(to + 2 * half, 2 * HEAD)] = jnp.where(
            first, grad_v[0], grad_v[1]
        ).astype(LOW)
        return carry

    lax.fori_loop(0, cells * pairs, step, 0, unroll=2)


def early_grad_body(
    slot_ref, low_ref, part_ref, mixed_ref, grad_low_ref, keep_ref, away_ref, slots, sem
):
    width = part_ref.shape[1]
    put_slots(slots, slot_ref, dot(low_ref[...].T, part_ref[...]), 0, slice(0, width))
    put_slots(
        slots, slot_ref, dot(mixed_ref[...].T, grad_low_ref[...]), 0,
        slice(width, slots.shape[2]),
    )
    wait_all(send_slots(slots, keep_ref, away_ref, sem))


def first_back_body(
    slot_ref, x_ref, low_ref, one_ref, two_ref, grad_ref, small_ref, sums_ref, in_b_ref,
    down_b_ref, weight, out_ref, keep_ref, away_ref, sum_ref, slots, sem,
):
    model = x_ref.shape[1]
    late = two_ref.shape[1]
    center, scale = norm_parts(x_ref[...].astype(FULL))
    parts = ((one_ref, 0), (two_ref, one_ref.shape[1] // 3))
    grad_first = jnp.zeros(x_ref.shape, FULL)
    for j in range(3):
        for ref, begin in parts:
            width = ref.shape[1] // 3
            at = j * model + begin
            grad_first = grad_first + dot(
                ref[:, j * width : (j + 1) * width], weight[:, at : at + width], ((1,), (1,))
            )
    put_slots(slots, slot_ref, dot(low_ref[...].T, two_ref[...]), 0, slice(0, late))
    back, gain_sum, shift_sum = norm_back(
        center, scale, small_row(small_ref, "first_gain"), grad_first
    )

    def put(name, value, offset=0):
        at = ROWS[name] + offset
        sum_ref[at : at + value.shape[0], :] = value

    sum_ref[...] = jnp.zeros_like(sum_ref)
    put("first_gain", gain_sum)
    put("first_shift", shift_sum)
    for j in range(2):
        at = ROWS["qv_bias"] + j
        for ref, begin in parts:
            width = ref.shape[1] // 3
            part = ref[:, 2 * j * width : (2 * j + 1) * width].astype(FULL)
            sum_ref[at : at + 1, begin : begin + width] = jnp.sum(part, axis=0, keepdims=True)
    put("out_bias", sums_ref[0:1, :])
    put("second_gain", sums_ref[1:2, :])
    put("second_shift", sums_ref[2:3, :])
    put("in_bias", in_b_ref[...])
    put("down_bias", down_b_ref[...])
    for i in range(3):
        part = sum_ref[:, SMALL_LANES * i : SMALL_LANES * (i + 1)].astype(LOW)
        for device in range(CELLS):
            slots[device, 16 * i : 16 * i + 16, late:] = part
    copies = send_slots(slots, keep_ref, away_ref, sem)
    out_ref[...] = (grad_ref[...] + back).astype(LOW)
    wait_all(copies)


def finish_body(who_ref, early_ref, early_two_ref, late_ref, late_two_ref, *refs):
    grad_ref, out_ref, vectors, small_ref = refs[0], refs[1], refs[2:-1], refs[-1]
    model = out_ref.shape[1]
    early = early_ref[...].astype(FULL) + early_two_ref[...].astype(FULL)
    late = late_ref[...].astype(FULL) + late_two_ref[...].astype(FULL)
    one = (early.shape[1] - model) // 3
    two = (late.shape[1] - SMALL_LANES) // 3
    for j in range(3):
        at = j * model
        grad_ref[:, at : at + one] = early[:, j * one : (j + 1) * one]
        grad_ref[:, at + one : at + model] = late[:, j * two : (j + 1) * two]
    out_ref[...] = early[:, 3 * one :]
    for i in range(3):
        small_ref[:, SMALL_LANES * i : SMALL_LANES * (i + 1)] = late[
            16 * i : 16 * i + 16, 3 * two :
        ]
    me = who_ref[0]
    row = lax.broadcasted_iota(jnp.int32, (SMALL_ROWS, model), 0)
    for name, ref in zip(NAMES, vectors):
        size = ref.shape[1]
        per_row = model // size
        here_row = jnp.where(row == ROWS[name] + me // per_row, small_ref[...], 0.0)
        values = jnp.sum(here_row, axis=0, keepdims=True)
        picker = one_hot(size, model, size * (me % per_row)).astype(FULL)
        ref[...] = lax.dot_general(
            values, picker, (((1,), (1,)), ((), ())), precision=lax.Precision.HIGHEST,
            preferred_element_type=FULL,
        )


def on_device_ring(
    tokens,
    lengths,
    cotangent,
    first_gain,
    first_shift,
    qkv_weight,
    qv_bias,
    out_weight,
    out_bias,
    second_gain,
    second_shift,
    in_weight,
    in_bias,
    down_weight,
    down_bias,
):
    micro, seq, model = tokens.shape[1:]
    total_rows = micro * seq
    rows = qkv_weight.shape[0]
    down_rows = down_weight.shape[0]
    ff = in_weight.shape[1]
    heads = model // HEAD
    whole = float(lax.axis_size("species") * CELLS * micro * seq)
    index, core, place = here()
    species = lax.axis_index("species")
    who = jnp.stack([index, species]).astype(jnp.int32)
    order = jnp.stack(gather_order(core, place)).astype(jnp.int32)
    slot = jnp.stack(scatter_slots(core, place)).astype(jnp.int32)
    lens = lengths.reshape(micro)
    x = tokens.reshape(total_rows, model)
    cot = cotangent.reshape(total_rows, model)
    vectors = (
        first_gain, first_shift, qv_bias, out_bias, second_gain, second_shift, in_bias, down_bias,
    )

    dma = pltpu.SemaphoreType.DMA

    def gathered(own, hops):
        got = [own]
        for item in hops:
            got += [item, to_partner(item)]
        return got

    own = both_blocks(qkv_weight, core)
    qkv_one = hop(own)
    (small,) = call(
        pack_body,
        [shape((SMALL_ROWS, model))],
        [who, after(lens, own)] + [item.reshape(1, -1) for item in vectors],
        [SMEM, SMEM] + [VMEM] * 8,
        vmem=4,
    )
    in_weight, out_weight = lax.optimization_barrier((in_weight, out_weight, own))[:2]
    in_own = both_blocks(jnp.concatenate([in_weight, out_weight], axis=1), core)
    in_one = hop(in_own)
    small = exchange(small, 1)
    qkv_one, small = lax.optimization_barrier((qkv_one, small))
    qkv_two = hop(qkv_one)
    in_two = hop(after(in_one, qkv_one))
    small = exchange(small, 2)
    down_own = both_blocks(after(down_weight, qkv_one), core)
    qkv_two, small, down_own = lax.optimization_barrier((qkv_two, small, down_own))
    qkv_three = hop(qkv_two)
    small = exchange(small, 4)
    qkv_three, small = lax.optimization_barrier((qkv_three, small))
    qkv_last = hop(half_of(qkv_three, core))
    in_three = hop(after(in_two, qkv_three))
    small = exchange(small, 8)
    in_three, small = lax.optimization_barrier((in_three, small))
    in_last = hop(half_of(in_three, core))
    down_one = hop(after(down_own, in_three))
    low, proj, qkv_full = call(
        project_body,
        [
            shape((total_rows, model)),
            shape((total_rows, 3 * model)),
            shape((model, 3 * model)),
        ],
        [order, after(x, in_three), small] + gathered(own, (qkv_one, qkv_two, qkv_three, qkv_last)),
        [SMEM, VMEM, VMEM] + [ANY] * 9,
        scratch=[dma((CELLS,))],
        vmem=20,
    )
    other_small = across(small)
    proj, in_last, other_small, down_one = lax.optimization_barrier(
        (proj, in_last, other_small, down_one)
    )
    down_two = hop(down_one)
    att, mixed = call(
        lambda *refs: attend_body(seq, *refs),
        [shape((micro * heads, seq, seq)), shape((total_rows, model))],
        [lens, proj],
        [SMEM, VMEM],
        vmem=12,
    )
    down_two, mixed = lax.optimization_barrier((down_two, mixed))
    down_three = hop(down_two)
    in_got = gathered(in_own, (in_one, in_two, in_three, in_last))
    middle, low_two, active, slope, in_full = call(
        inner_body,
        [
            shape((total_rows, model), FULL),
            shape((total_rows, model)),
            shape((total_rows, ff)),
            shape((total_rows, ff)),
            shape((model, ff + model)),
        ],
        [order, x, mixed, small] + in_got,
        [SMEM] + [VMEM] * 3 + [ANY] * 9,
        scratch=[dma((CELLS,))],
        vmem=24,
    )
    down_three, active = lax.optimization_barrier((down_three, active))
    down_last = hop(half_of(down_three, core))
    up_low, down_b, down_keep, down_away, down_keep_two, down_away_two = call(
        lambda *refs: grad_down_body(seq, whole, *refs),
        [
            shape((total_rows, model)),
            shape((1, model), FULL),
        ]
        + [shape((RING_SIZE, down_rows // 2, model))] * 4,
        [who, slot, lens, active, cot, small, other_small],
        [SMEM] * 3 + [VMEM] * 4,
        [VMEM] * 2 + [ANY] * 4,
        scratch=[pltpu.VMEM((2, CELLS, down_rows // 2, model), LOW), dma((2, 2))],
        vmem=15,
    )

    down_away, down_away_two, down_last = lax.optimization_barrier(
        (down_away, down_away_two, down_last)
    )
    down_other_two = to_partner(down_away_two)
    down_other = to_partner(down_away)
    inner_low, in_b, down_full = call(
        inner_back_body,
        [
            shape((total_rows, ff)),
            shape((ff // model, model), FULL),
            shape((ff, model)),
        ],
        [order, slope, up_low]
        + gathered(down_own, (down_one, down_two, down_three, down_last)),
        [SMEM] + [VMEM] * 2 + [ANY] * 9,
        scratch=[dma((CELLS,))],
        vmem=20,
    )
    down_other_two, inner_low = lax.optimization_barrier((down_other_two, inner_low))
    down_x = across(add_low(down_keep_two[0:3], down_other_two[0:3]))
    down_x_two = across(add_low(down_keep_two[3:8], down_other_two[3:8]))
    in_keep, in_away = call(
        grad_in_body,
        [shape((RING_SIZE, rows, ff)), shape((RING_SIZE, rows, ff))],
        [slot, low_two, inner_low],
        [SMEM] + [VMEM] * 2,
        [ANY] * 2,
        scratch=[pltpu.VMEM((CELLS, rows, ff), LOW), dma((2,))],
        vmem=13,
    )
    in_other = to_partner(in_away)
    (out_tokens,) = call(
        down_body,
        [shape((total_rows, model))],
        [after(active, in_keep), middle, small, down_full],
        [VMEM] * 4,
        vmem=13,
    )
    in_other, out_tokens, inner_low = lax.optimization_barrier((in_other, out_tokens, inner_low))
    in_sum = first_hop(in_keep, in_other)
    grad_middle, grad_low, grad_mixed, sums = call(
        lambda *refs: middle_back_body(seq, whole, *refs),
        [
            shape((total_rows, model), FULL),
            shape((total_rows, model)),
            shape((total_rows, model)),
            shape((3, model), FULL),
        ],
        [lens, inner_low, middle, cot, small, other_small, in_full],
        [SMEM] + [VMEM] * 6,
        vmem=19,
    )

    def attend_back(begin, pairs, grad):
        return call(
            lambda *refs: attend_back_body(seq, begin, *refs),
            [shape((total_rows, 6 * pairs * HEAD))],
            [proj, att, grad],
            [VMEM] * 3,
            vmem=11,

        )[0]

    pairs = model // (2 * HEAD)
    early_pairs = 2 * pairs // 3
    in_sum, down_x, down_other, grad_mixed = lax.optimization_barrier(
        (in_sum, down_x, down_other, grad_mixed)
    )
    down_sum = first_hop(down_keep, down_other, down_x)
    in_sum = second_hop(in_sum, core, in_keep, in_other)
    grad_one = attend_back(0, early_pairs, grad_mixed)
    down_sum, grad_one = lax.optimization_barrier((down_sum, grad_one))
    down_sum = second_hop(down_sum, core, down_keep, down_other, down_x)
    early_width = 6 * early_pairs * HEAD + model
    early_keep, early_away = call(
        early_grad_body,
        [shape((RING_SIZE, rows, early_width))] * 2,
        [slot, low, grad_one, mixed, grad_low],
        [SMEM] + [VMEM] * 4,
        [ANY] * 2,
        scratch=[pltpu.VMEM((CELLS, rows, early_width), LOW), dma((2,))],
        vmem=12,
    )
    early_other = to_partner(early_away)
    in_sum, early_keep, grad_mixed = lax.optimization_barrier((in_sum, early_keep, grad_mixed))
    in_sum = later_hop(in_sum, 3, in_keep, in_other)
    grad_two = attend_back(early_pairs, pairs - early_pairs, grad_mixed)
    early_other, grad_two = lax.optimization_barrier((early_other, grad_two))
    early_sum = first_hop(early_keep, early_other)
    late_width = 6 * (pairs - early_pairs) * HEAD + SMALL_LANES
    grad_tokens, late_keep, late_away = call(
        first_back_body,
        [
            shape((total_rows, model)),
            shape((RING_SIZE, rows, late_width)),
            shape((RING_SIZE, rows, late_width)),
        ],
        [slot, x, low, grad_one, grad_two, grad_middle, small, sums, in_b, down_b, qkv_full],
        [SMEM] + [VMEM] * 10,
        [VMEM] + [ANY] * 2,
        scratch=[
            pltpu.VMEM((SMALL_ROWS, model), FULL),
            pltpu.VMEM((CELLS, rows, late_width), LOW),
            dma((2,)),
        ],
        vmem=16,

    )
    late_other = to_partner(late_away)
    in_sum, early_sum, late_keep, down_sum, down_x_two = lax.optimization_barrier(
        (in_sum, early_sum, late_keep, down_sum, down_x_two)
    )
    in_sum = later_hop(in_sum, 5, in_keep, in_other)
    early_sum = second_hop(early_sum, core, early_keep, early_other)
    down_sum = hop(add_low(down_sum, down_keep[3:5], down_other[3:5], down_x_two[0:2]))
    late_sum = first_hop(late_keep, late_other)
    late_sum, early_sum, down_sum = lax.optimization_barrier((late_sum, early_sum, down_sum))
    down_sum = hop(add_low(down_sum, down_keep[5:7], down_other[5:7], down_x_two[2:4]))
    late_sum = second_hop(late_sum, core, late_keep, late_other)
    early_sum = later_hop(early_sum, 3, early_keep, early_other)
    late_sum, early_sum, down_sum, in_sum = lax.optimization_barrier(
        (late_sum, early_sum, down_sum, in_sum)
    )
    late_sum = later_hop(late_sum, 3, late_keep, late_other)
    early_sum = later_hop(early_sum, 5, early_keep, early_other)
    in_sum = settle(in_sum, core, in_keep, in_other)
    in_terms = (in_sum, across(in_sum))
    mine = jnp.where(core == 0, down_sum[0], down_sum[1])
    other = to_partner(jnp.where(core == 0, down_sum[1], down_sum[0]))
    down_sum = add_low(mine, other, down_keep[7], down_other[7], down_x_two[4])
    down_terms = (down_sum, across(down_sum))
    late_sum = later_hop(late_sum, 5, late_keep, late_other)
    early_sum = settle(early_sum, core, early_keep, early_other)
    early_terms = (early_sum, across(early_sum))
    late_sum = settle(late_sum, core, late_keep, late_other)
    late_terms = (late_sum, across(late_sum))
    finished = call(
        finish_body,
        [shape((rows, 3 * model), FULL), shape((rows, model), FULL)]
        + [shape((1, item.shape[0]), FULL) for item in vectors],
        [who] + list(early_terms) + list(late_terms),
        [SMEM] + [VMEM] * 4,
        scratch=[pltpu.VMEM((SMALL_ROWS, model), FULL)],
        vmem=6,
    )
    grad_qkv, grad_out = finished[:2]
    pieces = [item.reshape(-1) for item in finished[2:]]
    return (
        out_tokens.reshape(tokens.shape),
        grad_tokens.reshape(tokens.shape),
        pieces[0],
        pieces[1],
        grad_qkv,
        pieces[2],
        grad_out,
        pieces[3],
        pieces[4],
        pieces[5],
        in_terms[0].astype(FULL) + in_terms[1].astype(FULL),
        pieces[6],
        jnp.concatenate(
            [
                jnp.where(species == 0, down_terms[0], down_terms[1]),
                jnp.where(species == 0, down_terms[1], down_terms[0]),
            ]
        ).astype(FULL),
        pieces[7],
    )


def on_device(
    tokens,
    lengths,
    cotangent,
    first_gain,
    first_shift,
    qkv_weight,
    qv_bias,
    out_weight,
    out_bias,
    second_gain,
    second_shift,
    in_weight,
    in_bias,
    down_weight,
    down_bias,
):
    local_count = jnp.sum(lengths).astype(jnp.float32)
    count = lax.psum(local_count, ("species", "cells"))
    micro_count = tokens.shape[1]
    seq_rows = tokens.shape[2]
    factor = (
        float(lax.axis_size("species") * lax.axis_size("cells") * micro_count * seq_rows) / count
    )
    output_rows = []
    gradient_rows = []
    summed = None
    for micro_step in range(micro_count):
        gathered = (
            lax.all_gather(first_gain, "cells", axis=0, tiled=True),
            lax.all_gather(first_shift, "cells", axis=0, tiled=True),
            lax.all_gather(qkv_weight, "cells", axis=0, tiled=True),
            lax.all_gather(qv_bias, "cells", axis=0, tiled=True),
            lax.all_gather(out_weight, "cells", axis=0, tiled=True),
            lax.all_gather(out_bias, "cells", axis=0, tiled=True),
            lax.all_gather(second_gain, "cells", axis=0, tiled=True),
            lax.all_gather(second_shift, "cells", axis=0, tiled=True),
            lax.all_gather(in_weight, "cells", axis=0, tiled=True),
            lax.all_gather(in_bias, "cells", axis=0, tiled=True),
            lax.all_gather(down_weight, "cells", axis=0, tiled=True),
            lax.all_gather(down_bias, "cells", axis=0, tiled=True),
        )
        out_seq, grad_seq, grads = sequence_pass(
            gathered,
            tokens[0, micro_step],
            lengths[0, micro_step],
            cotangent[0, micro_step],
            factor,
        )
        output_rows.append(out_seq)
        gradient_rows.append(grad_seq)
        shares = (
            lax.psum_scatter(grads[0], "cells", scatter_dimension=0, tiled=True),
            lax.psum_scatter(grads[1], "cells", scatter_dimension=0, tiled=True),
            lax.psum_scatter(grads[2], "cells", scatter_dimension=0, tiled=True),
            lax.psum_scatter(grads[3], "cells", scatter_dimension=0, tiled=True),
            lax.psum_scatter(grads[4], "cells", scatter_dimension=0, tiled=True),
            lax.psum_scatter(grads[5], "cells", scatter_dimension=0, tiled=True),
            lax.psum_scatter(grads[6], "cells", scatter_dimension=0, tiled=True),
            lax.psum_scatter(grads[7], "cells", scatter_dimension=0, tiled=True),
            lax.psum_scatter(grads[8], "cells", scatter_dimension=0, tiled=True),
            lax.psum_scatter(grads[9], "cells", scatter_dimension=0, tiled=True),
            lax.psum_scatter(grads[10], "cells", scatter_dimension=0, tiled=True),
            lax.psum_scatter(grads[11], "cells", scatter_dimension=0, tiled=True),
        )
        summed = shares if summed is None else jax.tree.map(jnp.add, summed, shares)
    final = (
        lax.psum(summed[0].astype(jnp.bfloat16), "species").astype(jnp.float32),
        lax.psum(summed[1].astype(jnp.bfloat16), "species").astype(jnp.float32),
        lax.psum(summed[2].astype(jnp.bfloat16), "species").astype(jnp.float32),
        lax.psum(summed[3].astype(jnp.bfloat16), "species").astype(jnp.float32),
        lax.psum(summed[4].astype(jnp.bfloat16), "species").astype(jnp.float32),
        lax.psum(summed[5].astype(jnp.bfloat16), "species").astype(jnp.float32),
        lax.psum(summed[6].astype(jnp.bfloat16), "species").astype(jnp.float32),
        lax.psum(summed[7].astype(jnp.bfloat16), "species").astype(jnp.float32),
        lax.psum(summed[8].astype(jnp.bfloat16), "species").astype(jnp.float32),
        lax.psum(summed[9].astype(jnp.bfloat16), "species").astype(jnp.float32),
        lax.psum(summed[10].astype(jnp.bfloat16), "species").astype(jnp.float32),
        lax.psum(summed[11].astype(jnp.bfloat16), "species").astype(jnp.float32),
    )
    out_tokens = jnp.stack(output_rows)[None]
    grad_tokens = jnp.stack(gradient_rows)[None]
    return (out_tokens, grad_tokens) + tuple(final)


def solution(mesh):
    in_specs = (
        P("species", "cells", None, None),
        P("species", "cells"),
        P("species", "cells", None, None),
        P("cells"),
        P("cells"),
        P("cells", None),
        P("cells"),
        P("cells", None),
        P("cells"),
        P("cells"),
        P("cells"),
        P("cells", None),
        P("cells"),
        P("cells", None),
        P("cells"),
    )
    out_specs = (
        P("species", "cells", None, None),
        P("species", "cells", None, None),
        P("cells"),
        P("cells"),
        P("cells", None),
        P("cells"),
        P("cells", None),
        P("cells"),
        P("cells"),
        P("cells"),
        P("cells", None),
        P("cells"),
        P("cells", None),
        P("cells"),
    )
    program = on_device_ring if mesh.shape["cells"] == 2 * RING_SIZE else on_device
    return jax.shard_map(
        program, mesh=mesh, in_specs=in_specs, out_specs=out_specs, check_vma=False
    )
```

```python
import jax
import jax.numpy as jnp
from jax import lax
from jax.experimental import pallas as pl
from jax.experimental.pallas import tpu as pltpu
from jax.sharding import PartitionSpec as P

HEAD = 64


EPSILON = 1e-12
NEGATIVE = -1e30


def normalize(values, gain_vec, shift_vec):
    center = values - jnp.mean(values, axis=-1, keepdims=True)
    spread = jnp.mean(center * center, axis=-1, keepdims=True)
    return center * lax.rsqrt(spread + EPSILON) * gain_vec + shift_vec


def smooth_gate(values):
    return jax.nn.gelu(values, approximate=False)


def times_left(left_side, right_side):
    return lax.dot_general(
        left_side, right_side, (((0,), (0,)), ((), ())), preferred_element_type=jnp.float32
    )


def times_right(left_side, right_side):
    return lax.dot_general(
        left_side, right_side, (((1,), (1,)), ((), ())), preferred_element_type=jnp.float32
    )


def sequence_pass(weights, inputs, length, cot_rows, factor):
    (
        first_gain,
        first_shift,
        qkv_weight,
        qv_bias,
        out_weight,
        out_bias,
        second_gain,
        second_shift,
        in_weight,
        in_bias,
        down_weight,
        down_bias,
    ) = weights
    seq_rows = inputs.shape[0]
    model_width = inputs.shape[1]
    heads_count = model_width // HEAD
    scale_qk = float(HEAD) ** (-0.5)
    as_float = inputs.astype(jnp.float32)
    hidden_one, first_pull = jax.vjp(
        normalize, as_float, first_gain.astype(jnp.float32), first_shift.astype(jnp.float32)
    )
    first_low = hidden_one.astype(jnp.bfloat16)
    bias_float = qv_bias.astype(jnp.float32)
    full_bias = jnp.concatenate(
        [bias_float[:model_width], jnp.zeros((model_width,), jnp.float32), bias_float[model_width:]]
    )
    projected = (
        jnp.dot(first_low, qkv_weight, preferred_element_type=jnp.float32) + full_bias
    ).astype(jnp.bfloat16)
    split_heads = projected.reshape(seq_rows, 3, heads_count, HEAD)
    queries = split_heads[:, 0]
    keys_part = split_heads[:, 1]
    values_part = split_heads[:, 2]
    visible = jnp.arange(seq_rows) < length

    def scores_of():
        raw_scores = (
            jnp.einsum("qhd,khd->hqk", queries, keys_part, preferred_element_type=jnp.float32)
            * scale_qk
        )
        return jnp.where(visible[None, None, :], raw_scores, NEGATIVE)

    scores = scores_of()
    top_score = jnp.max(scores, axis=-1, keepdims=True)
    expo = jnp.exp(scores - top_score)
    total_exp = jnp.sum(expo, axis=-1, keepdims=True)
    log_total = top_score + jnp.log(total_exp)
    attention = (expo / total_exp).astype(jnp.bfloat16)
    mixed = jnp.einsum("hqk,khd->qhd", attention, values_part, preferred_element_type=jnp.float32)
    mixed = mixed.reshape(seq_rows, model_width).astype(jnp.bfloat16)
    middle = (
        as_float
        + jnp.dot(mixed, out_weight, preferred_element_type=jnp.float32)
        + out_bias.astype(jnp.float32)
    )
    hidden_two, second_pull = jax.vjp(
        normalize, middle, second_gain.astype(jnp.float32), second_shift.astype(jnp.float32)
    )
    second_low = hidden_two.astype(jnp.bfloat16)
    inner = jnp.dot(second_low, in_weight, preferred_element_type=jnp.float32) + in_bias.astype(
        jnp.float32
    )
    active, gate_pull = jax.vjp(smooth_gate, inner)
    active_low = active.astype(jnp.bfloat16)
    output = (
        middle
        + jnp.dot(active_low, down_weight, preferred_element_type=jnp.float32)
        + down_bias.astype(jnp.float32)
    )
    upstream = cot_rows.astype(jnp.float32) * visible[:, None].astype(jnp.float32) * factor
    up_low = upstream.astype(jnp.bfloat16)
    grad_down_bias = jnp.sum(up_low.astype(jnp.float32), axis=0)
    grad_down = times_left(active_low, up_low)
    grad_active = times_right(up_low, down_weight)
    (grad_inner,) = gate_pull(grad_active)
    inner_low = grad_inner.astype(jnp.bfloat16)
    grad_in_bias = jnp.sum(inner_low.astype(jnp.float32), axis=0)
    grad_in = times_left(second_low, inner_low)
    grad_second = times_right(inner_low, in_weight)
    grad_middle_norm, grad_second_gain, grad_second_shift = second_pull(grad_second)
    grad_middle = upstream + grad_middle_norm
    middle_low = grad_middle.astype(jnp.bfloat16)
    grad_out_bias = jnp.sum(middle_low.astype(jnp.float32), axis=0)
    grad_out = times_left(mixed, middle_low)
    grad_mixed = (
        times_right(middle_low, out_weight)
        .astype(jnp.bfloat16)
        .reshape(seq_rows, heads_count, HEAD)
    )
    probs_again = jnp.exp(scores_of() - log_total)
    grad_probs = jnp.einsum(
        "qhd,khd->hqk", grad_mixed, values_part, preferred_element_type=jnp.float32
    )
    grad_values = jnp.einsum(
        "hqk,qhd->khd", attention, grad_mixed, preferred_element_type=jnp.float32
    )
    delta = jnp.sum(probs_again * grad_probs, axis=-1, keepdims=True)
    grad_scores = (probs_again * (grad_probs - delta)).astype(jnp.bfloat16)
    grad_queries = (
        jnp.einsum("hqk,khd->qhd", grad_scores, keys_part, preferred_element_type=jnp.float32)
        * scale_qk
    )
    grad_keys = (
        jnp.einsum("hqk,qhd->khd", grad_scores, queries, preferred_element_type=jnp.float32)
        * scale_qk
    )
    grad_projected = jnp.stack([grad_queries, grad_keys, grad_values], axis=1)
    grad_projected = grad_projected.reshape(seq_rows, 3 * model_width).astype(jnp.bfloat16)
    column_sums = jnp.sum(grad_projected.astype(jnp.float32), axis=0)
    grad_qv = jnp.concatenate([column_sums[:model_width], column_sums[2 * model_width :]])
    grad_qkv = times_left(first_low, grad_projected)
    grad_first = times_right(grad_projected, qkv_weight)
    grad_input_norm, grad_first_gain, grad_first_shift = first_pull(grad_first)
    grad_inputs = grad_middle + grad_input_norm
    grads = (
        grad_first_gain,
        grad_first_shift,
        grad_qkv,
        grad_qv,
        grad_out,
        grad_out_bias,
        grad_second_gain,
        grad_second_shift,
        grad_in,
        grad_in_bias,
        grad_down,
        grad_down_bias,
    )
    return (output.astype(jnp.bfloat16), grad_inputs.astype(jnp.bfloat16), grads)


RING = (0, 2, 4, 6, 7, 5, 3, 1)
RING_SIZE = len(RING)
CELLS = 2 * RING_SIZE
ANY = pl.BlockSpec(memory_space=pl.ANY)
HBM = pl.BlockSpec(memory_space=pltpu.HBM)
VMEM = pl.BlockSpec(memory_space=pltpu.VMEM)
SMEM = pl.BlockSpec(memory_space=pltpu.SMEM)
LOW = jnp.bfloat16
FULL = jnp.float32
HEAVY = 10**10
UNIT = 10**8
ROWS = {
    "first_gain": 0,
    "first_shift": 1,
    "qv_bias": 2,
    "out_bias": 4,
    "second_gain": 5,
    "second_shift": 6,
    "in_bias": 7,
    "down_bias": 11,
    "lengths": 12,
}
NAMES = tuple(ROWS)[:8]
SMALL_ROWS = 16
SMALL_LANES = 256
PIECES = (2, 2, 2, 2, 2, 2, 2, 1, 1)


def ring_pairs():
    pairs = []
    for place in range(RING_SIZE):
        chip = RING[place]
        right = RING[(place + 1) % RING_SIZE]
        left = RING[(place - 1) % RING_SIZE]
        pairs.append((2 * chip, 2 * right))
        pairs.append((2 * chip + 1, 2 * left + 1))
    return pairs


def hop(block):
    return lax.ppermute(block, "cells", ring_pairs())


def to_partner(block):
    return lax.ppermute(block, "cells", [(i, i ^ 1) for i in range(CELLS)])


def across(block):
    return lax.ppermute(block, "species", [(0, 1), (1, 0)])


def exchange(values, bit):
    return values + lax.ppermute(values, "cells", [(i, i ^ bit) for i in range(CELLS)])


def after(value, *others):
    return lax.optimization_barrier((value,) + others)[0]


def here():
    index = lax.axis_index("cells")
    core = index % 2
    chip = index // 2
    place = jnp.int32(0)
    for i, ring_chip in enumerate(RING):
        place = jnp.where(chip == ring_chip, i, place)
    return index, core, place


def chip_at(place):
    place = place % RING_SIZE
    chip = jnp.zeros_like(place)
    for i, ring_chip in enumerate(RING):
        chip = jnp.where(place == i, ring_chip, chip)
    return chip


def gather_order(core, place):
    sign = 1 - 2 * core
    order = []

    def pair(at):
        order.append(2 * chip_at(at))
        order.append(2 * chip_at(at) + 1)

    pair(place)
    for step in range(1, 4):
        pair(place - sign * step)
        pair(place + sign * step)
    order.append(2 * chip_at(place + 4) + core)
    order.append(2 * chip_at(place + 4) + 1 - core)
    return order


def scatter_slots(core, place):
    def kept(core_now):
        sign = 1 - 2 * core_now
        order = [2 * chip_at(place + 4) + core_now]
        for step in (3, 2, 1):
            order.append(2 * chip_at(place + sign * step))
            order.append(2 * chip_at(place + sign * step) + 1)
        order.append(2 * chip_at(place) + core_now)
        return order

    order = kept(core) + kept(1 - core)
    slots = []
    for device in range(CELLS):
        slot = jnp.int32(0)
        for i, who in enumerate(order):
            slot = jnp.where(who == device, i, slot)
        slots.append(slot)
    return slots


def both_blocks(block, core):
    other = to_partner(block)
    return jnp.stack([jnp.where(core == 0, block, other), jnp.where(core == 0, other, block)])


def half_of(pair, core):
    return jnp.where(core == 0, pair[0], pair[1])[None]


def add_low(*parts):
    total = parts[0].astype(FULL)
    for part in parts[1:]:
        total = total + part.astype(FULL)
    return total.astype(LOW)


def first_hop(*parts):
    return hop(add_low(*[part[0:1] for part in parts]))


def second_hop(moving, core, *parts):
    wide = jnp.stack([jnp.where(core == 0, moving[0], 0), jnp.where(core == 0, 0, moving[0])])
    return hop(add_low(wide, *[part[1:3] for part in parts]))


def later_hop(moving, at, *parts):
    return hop(add_low(moving, *[part[at : at + 2] for part in parts]))


def settle(moving, core, *parts):
    mine = jnp.where(core == 0, moving[0], moving[1])
    other = jnp.where(core == 0, moving[1], moving[0])
    return add_low(mine, to_partner(other), *[part[7] for part in parts])


def dot(left, right, dims=((1,), (0,))):
    return lax.dot_general(left, right, (dims, ((), ())), preferred_element_type=FULL)


def call(body, out_shape, ins, specs, out_specs=None, scratch=(), vmem=48, cost=HEAVY):
    return pl.pallas_call(
        body,
        out_shape=out_shape,
        in_specs=specs,
        out_specs=[VMEM] * len(out_shape) if out_specs is None else out_specs,
        scratch_shapes=list(scratch),
        compiler_params=pltpu.CompilerParams(vmem_limit_bytes=vmem * 2**20),
        cost_estimate=pl.CostEstimate(flops=cost, bytes_accessed=0, transcendentals=0),
    )(*ins)


def shape(dims, kind=LOW):
    return jax.ShapeDtypeStruct(dims, kind)


def fetch(order_ref, refs, target, sem):
    rows = target.shape[0] // CELLS
    copies = []
    index = 0
    for source, size in zip(refs, PIECES):
        for part in range(size):
            at = order_ref[index]
            copies.append(
                pltpu.make_async_copy(
                    source.at[part],
                    target.at[pl.ds(pl.multiple_of(at * rows, 16), rows)],
                    sem.at[index],
                )
            )
            index += 1
    for item in copies:
        item.start()
    return copies


def wait_all(copies):
    for item in copies:
        item.wait()


def one_hot(rows, lanes, offset):
    row = lax.broadcasted_iota(jnp.int32, (rows, lanes), 0)
    lane = lax.broadcasted_iota(jnp.int32, (rows, lanes), 1)
    return lane == row + offset


def pack_body(who_ref, lengths_ref, *refs):
    sources, small_ref = refs[:8], refs[8]
    me = who_ref[0]
    model = small_ref.shape[1]
    row = lax.broadcasted_iota(jnp.int32, (SMALL_ROWS, model), 0)
    lane = lax.broadcasted_iota(jnp.int32, (SMALL_ROWS, model), 1)
    small = jnp.zeros((SMALL_ROWS, model), FULL)
    for name, ref in zip(NAMES, sources):
        size = ref.shape[1]
        per_row = model // size
        placed = dot(ref[...], one_hot(size, model, size * (me % per_row)).astype(LOW))
        small = small + jnp.where(row == ROWS[name] + me // per_row, placed, 0.0)
    for i in range(2):
        at = (row == ROWS["lengths"]) & (lane == 2 * me + i)
        small = small + jnp.where(at, lengths_ref[i].astype(FULL), 0.0)
    small_ref[...] = small.astype(LOW)


def norm_parts(values):
    center = values - jnp.mean(values, axis=-1, keepdims=True)
    spread = jnp.mean(center * center, axis=-1, keepdims=True)
    return center, lax.rsqrt(spread + EPSILON)


def norm_back(center, scale, gain, grad):
    weighted = grad * gain
    mean_one = jnp.mean(weighted, axis=-1, keepdims=True)
    mean_two = jnp.mean(weighted * center, axis=-1, keepdims=True)
    back = scale * (weighted - mean_one - center * (scale * scale * mean_two))
    return back, jnp.sum(grad * center * scale, axis=0, keepdims=True), jnp.sum(
        grad, axis=0, keepdims=True
    )


def small_row(small_ref, name, count=1):
    return small_ref[...].astype(FULL)[ROWS[name] : ROWS[name] + count, :]


def project_body(order_ref, x_ref, small_ref, *refs):
    blocks = refs[:9]
    low_ref, proj_ref, weight, sem = refs[9:]
    model = x_ref.shape[1]
    copies = fetch(order_ref, blocks, weight, sem)
    center, scale = norm_parts(x_ref[...].astype(FULL))
    bias = small_row(small_ref, "qv_bias", 2)
    low_ref[...] = (
        center * scale * small_row(small_ref, "first_gain") + small_row(small_ref, "first_shift")
    ).astype(LOW)
    wait_all(copies)
    for j in range(3):
        lanes = slice(j * model, (j + 1) * model)
        part = dot(low_ref[...], weight[:, lanes])
        if j != 1:
            part = part + bias[j // 2 : j // 2 + 1]
        proj_ref[:, lanes] = part.astype(LOW)


def attend_body(seq, lengths_ref, proj_ref, att_ref, mixed_ref):
    model = mixed_ref.shape[1]
    cells = mixed_ref.shape[0] // seq
    pairs = model // (2 * HEAD)
    lane = lax.broadcasted_iota(jnp.int32, (seq, 2 * HEAD), 1)
    key = lax.broadcasted_iota(jnp.int32, (seq, seq), 0)

    def step(index, carry):
        s = index // pairs
        p = index % pairs
        rows = pl.ds(pl.multiple_of(s * seq, seq), seq)
        at = pl.multiple_of(p * 2 * HEAD, 2 * HEAD)
        q = proj_ref[rows, pl.ds(at, 2 * HEAD)] * jnp.asarray(HEAD ** (-0.5), LOW)
        k = proj_ref[rows, pl.ds(at + model, 2 * HEAD)]
        v_turned = proj_ref[rows, pl.ds(at + 2 * model, 2 * HEAD)].T
        visible = key < lengths_ref[s]
        mixed = []
        for i in range(2):
            own = (lane >= i * HEAD) & (lane < (i + 1) * HEAD)
            scores = dot(jnp.where(own, k, jnp.zeros_like(k)), q, ((1,), (1,)))
            scores = jnp.where(visible, scores, NEGATIVE)
            expo = jnp.exp(scores - jnp.max(scores, axis=0, keepdims=True))
            probs = expo * (1.0 / jnp.sum(expo, axis=0, keepdims=True))
            probs = probs.astype(LOW)
            att_ref[2 * index + i] = probs
            mixed.append(dot(v_turned[i * HEAD : (i + 1) * HEAD], probs))
        mixed_ref[rows, pl.ds(at, 2 * HEAD)] = jnp.concatenate(mixed, axis=0).T.astype(LOW)
        return carry

    lax.fori_loop(0, cells * pairs, step, 0, unroll=2)


ERFC_STEP = 0.33
ERFC = (
    0.1863578228018033,
    0.18295566386742124,
    0.2012255082472392,
    0.04721561458875723,
    0.4085089979423051,
    -0.35115900736338407,
    0.4602422572120205,
    -0.13534686486277223,
)


def gelu_parts(inner):
    z = jnp.abs(inner) * (0.5**0.5)
    t = 1.0 / (1.0 + ERFC_STEP * z)
    tail = jnp.full_like(t, 0.5 * ERFC[-1])
    for factor in ERFC[-2::-1]:
        tail = tail * t + 0.5 * factor
    bell = jnp.exp(-(z * z))
    tail = tail * t * bell
    area = jnp.where(inner < 0.0, tail, 1.0 - tail)
    return inner * area, area + inner * bell * (0.5 / 3.141592653589793) ** 0.5


def row_mask(lengths_ref, rows, seq):
    at = lax.broadcasted_iota(jnp.int32, (rows, 1), 0)
    true = (at < lengths_ref[0]).astype(FULL)
    for s in range(1, rows // seq):
        true = jnp.where(at < s * seq, true, (at < lengths_ref[s] + s * seq).astype(FULL))
    return true


def loss_rows(lengths_ref, small_ref, other_ref, cot_ref, seq, whole):
    count = jnp.sum(
        small_row(small_ref, "lengths") + small_row(other_ref, "lengths"), axis=-1, keepdims=True
    )
    return cot_ref[...].astype(FULL) * (
        row_mask(lengths_ref, cot_ref.shape[0], seq) * (whole / count)
    )


def put_slots(keep_buf, slot_ref, values, first, lanes):
    rows = keep_buf.shape[1]
    for i in range(values.shape[0] // rows):
        keep_buf[slot_ref[first + i], :, lanes] = values[i * rows : (i + 1) * rows].astype(LOW)


def send_slots(buf, keep_ref, away_ref, sem):
    half = RING_SIZE
    copies = [
        pltpu.make_async_copy(buf.at[pl.ds(half, half)], away_ref, sem.at[0]),
        pltpu.make_async_copy(buf.at[pl.ds(0, half)], keep_ref, sem.at[1]),
    ]
    for item in copies:
        item.start()
    return copies


def inner_body(order_ref, x_ref, mixed_ref, small_ref, *refs):
    blocks = refs[:9]
    middle_ref, low_ref, active_ref, slope_ref, weight, sem = refs[9:]
    model = x_ref.shape[1]
    ff = active_ref.shape[1]
    wait_all(fetch(order_ref, blocks, weight, sem))
    middle = (
        x_ref[...].astype(FULL)
        + dot(mixed_ref[...], weight[:, ff:])
        + small_row(small_ref, "out_bias")
    )
    middle_ref[...] = middle
    center, scale = norm_parts(middle)
    low = center * scale * small_row(small_ref, "second_gain") + small_row(
        small_ref, "second_shift"
    )
    low_ref[...] = low.astype(LOW)
    step = 2 * (ff // RING_SIZE)
    bias = small_row(small_ref, "in_bias", 4)
    for j in range(ff // step):
        lanes = slice(j * step, (j + 1) * step)
        inner = dot(low_ref[...], weight[:, lanes]) + bias[j : j + 1]
        active, slope = gelu_parts(inner)
        active_ref[:, lanes] = active.astype(LOW)
        slope_ref[:, lanes] = slope.astype(LOW)


def grad_down_body(
    seq, whole, who_ref, slot_ref, lengths_ref, active_ref, cot_ref, small_ref, other_ref,
    up_ref, down_b_ref, keep_ref, away_ref, keep_two_ref, away_two_ref, slots, sem,
):
    up_low = loss_rows(lengths_ref, small_ref, other_ref, cot_ref, seq, whole).astype(LOW)
    up_ref[...] = up_low
    down_b_ref[...] = jnp.sum(up_low.astype(FULL), axis=0, keepdims=True)
    parts = RING_SIZE
    step = active_ref.shape[1] // parts
    rows = slots.shape[2]
    side = who_ref[1]
    for j in range(parts):
        grad = dot(active_ref[:, j * step : (j + 1) * step], up_ref[...], ((0,), (0,)))
        for i in range(4):
            slots[(i + side) % 2, slot_ref[j * CELLS // parts + i // 2]] = grad[
                i * rows : (i + 1) * rows
            ].astype(LOW)
    copies = send_slots(slots.at[1], keep_two_ref, away_two_ref, sem.at[1])
    copies += send_slots(slots.at[0], keep_ref, away_ref, sem.at[0])
    wait_all(copies)


def inner_back_body(order_ref, slope_ref, up_ref, *refs):
    blocks = refs[:9]
    inner_ref, in_b_ref, weight, sem = refs[9:]
    model = up_ref.shape[1]
    wait_all(fetch(order_ref, blocks, weight, sem))
    for j in range(inner_ref.shape[1] // model):
        lanes = slice(j * model, (j + 1) * model)
        grad = dot(up_ref[...], weight[lanes, :], ((1,), (1,)))
        low = (grad * slope_ref[:, lanes].astype(FULL)).astype(LOW)
        inner_ref[:, lanes] = low
        in_b_ref[j : j + 1, :] = jnp.sum(low.astype(FULL), axis=0, keepdims=True)


def down_body(active_ref, middle_ref, small_ref, weight_ref, out_ref):
    out_ref[...] = (
        middle_ref[...]
        + dot(active_ref[...], weight_ref[...])
        + small_row(small_ref, "down_bias")
    ).astype(LOW)


def grad_in_body(slot_ref, low_ref, inner_ref, keep_ref, away_ref, slots, sem):
    model = low_ref.shape[1]
    turned = low_ref[...].T
    for j in range(inner_ref.shape[1] // model):
        lanes = slice(j * model, (j + 1) * model)
        put_slots(slots, slot_ref, dot(turned, inner_ref[:, lanes]), 0, lanes)
    wait_all(send_slots(slots, keep_ref, away_ref, sem))


def middle_back_body(
    seq, whole, lengths_ref, inner_ref, middle_ref, cot_ref, small_ref, other_ref, weight,
    grad_ref, grad_low_ref, grad_mixed_ref, sums_ref,
):
    ff = inner_ref.shape[1]
    grad_second = dot(inner_ref[...], weight[:, :ff], ((1,), (1,)))
    center, scale = norm_parts(middle_ref[...])
    back, gain_sum, shift_sum = norm_back(
        center, scale, small_row(small_ref, "second_gain"), grad_second
    )
    grad = loss_rows(lengths_ref, small_ref, other_ref, cot_ref, seq, whole) + back
    grad_ref[...] = grad
    grad_low = grad.astype(LOW)
    grad_low_ref[...] = grad_low
    grad_mixed_ref[...] = dot(grad_low, weight[:, ff:], ((1,), (1,))).astype(LOW)
    sums_ref[0:1, :] = jnp.sum(grad_low.astype(FULL), axis=0, keepdims=True)
    sums_ref[1:2, :] = gain_sum
    sums_ref[2:3, :] = shift_sum


def attend_back_body(seq, begin, proj_ref, att_ref, grad_ref, out_ref):
    model = grad_ref.shape[1]
    half = out_ref.shape[1] // 3
    all_pairs = model // (2 * HEAD)
    pairs = half // (2 * HEAD)
    cells = grad_ref.shape[0] // seq
    lane = lax.broadcasted_iota(jnp.int32, (seq, 2 * HEAD), 1)
    scale = HEAD ** (-0.5)

    def step(index, carry):
        s = index // pairs
        p = index % pairs
        rows = pl.ds(pl.multiple_of(s * seq, seq), seq)
        to = pl.multiple_of(p * 2 * HEAD, 2 * HEAD)
        at = pl.multiple_of(to + begin * 2 * HEAD, 2 * HEAD)
        q = proj_ref[rows, pl.ds(at, 2 * HEAD)]
        k_turned = proj_ref[rows, pl.ds(at + model, 2 * HEAD)].T
        v = proj_ref[rows, pl.ds(at + 2 * model, 2 * HEAD)]
        g = grad_ref[rows, pl.ds(at, 2 * HEAD)]
        grad_q = []
        grad_k = []
        grad_v = []
        for i in range(2):
            own = (lane >= i * HEAD) & (lane < (i + 1) * HEAD)
            probs = att_ref[2 * (s * all_pairs + begin + p) + i]
            wide = probs.astype(FULL)
            grad_probs = dot(jnp.where(own, v, jnp.zeros_like(v)), g, ((1,), (1,)))
            delta = jnp.sum(wide * grad_probs, axis=0, keepdims=True)
            scores = (wide * (grad_probs - delta)).astype(LOW)
            grad_q.append(dot(k_turned[i * HEAD : (i + 1) * HEAD], scores))
            grad_k.append(dot(scores, q))
            grad_v.append(dot(probs, g))
        first = lane < HEAD
        out_ref[rows, pl.ds(to, 2 * HEAD)] = (
            jnp.concatenate(grad_q, axis=0).T * scale
        ).astype(LOW)
        out_ref[rows, pl.ds(to + half, 2 * HEAD)] = (
            jnp.where(first, grad_k[0], grad_k[1]) * scale
        ).astype(LOW)
        out_ref[rows, pl.ds(to + 2 * half, 2 * HEAD)] = jnp.where(
            first, grad_v[0], grad_v[1]
        ).astype(LOW)
        return carry

    lax.fori_loop(0, cells * pairs, step, 0, unroll=2)


def early_grad_body(
    slot_ref, low_ref, part_ref, mixed_ref, grad_low_ref, keep_ref, away_ref, slots, sem
):
    width = part_ref.shape[1]
    put_slots(slots, slot_ref, dot(low_ref[...].T, part_ref[...]), 0, slice(0, width))
    put_slots(
        slots, slot_ref, dot(mixed_ref[...].T, grad_low_ref[...]), 0,
        slice(width, slots.shape[2]),
    )
    wait_all(send_slots(slots, keep_ref, away_ref, sem))


def first_back_body(
    slot_ref, x_ref, low_ref, one_ref, two_ref, grad_ref, small_ref, sums_ref, in_b_ref,
    down_b_ref, weight, out_ref, keep_ref, away_ref, sum_ref, slots, sem,
):
    model = x_ref.shape[1]
    late = two_ref.shape[1]
    center, scale = norm_parts(x_ref[...].astype(FULL))
    parts = ((one_ref, 0), (two_ref, one_ref.shape[1] // 3))
    grad_first = jnp.zeros(x_ref.shape, FULL)
    for j in range(3):
        for ref, begin in parts:
            width = ref.shape[1] // 3
            at = j * model + begin
            grad_first = grad_first + dot(
                ref[:, j * width : (j + 1) * width], weight[:, at : at + width], ((1,), (1,))
            )
    put_slots(slots, slot_ref, dot(low_ref[...].T, two_ref[...]), 0, slice(0, late))
    back, gain_sum, shift_sum = norm_back(
        center, scale, small_row(small_ref, "first_gain"), grad_first
    )

    def put(name, value, offset=0):
        at = ROWS[name] + offset
        sum_ref[at : at + value.shape[0], :] = value

    sum_ref[...] = jnp.zeros_like(sum_ref)
    put("first_gain", gain_sum)
    put("first_shift", shift_sum)
    for j in range(2):
        at = ROWS["qv_bias"] + j
        for ref, begin in parts:
            width = ref.shape[1] // 3
            part = ref[:, 2 * j * width : (2 * j + 1) * width].astype(FULL)
            sum_ref[at : at + 1, begin : begin + width] = jnp.sum(part, axis=0, keepdims=True)
    put("out_bias", sums_ref[0:1, :])
    put("second_gain", sums_ref[1:2, :])
    put("second_shift", sums_ref[2:3, :])
    put("in_bias", in_b_ref[...])
    put("down_bias", down_b_ref[...])
    for i in range(3):
        part = sum_ref[:, SMALL_LANES * i : SMALL_LANES * (i + 1)].astype(LOW)
        for device in range(CELLS):
            slots[device, 16 * i : 16 * i + 16, late:] = part
    copies = send_slots(slots, keep_ref, away_ref, sem)
    out_ref[...] = (grad_ref[...] + back).astype(LOW)
    wait_all(copies)


def finish_body(who_ref, early_ref, early_two_ref, late_ref, late_two_ref, *refs):
    grad_ref, out_ref, vectors, small_ref = refs[0], refs[1], refs[2:-1], refs[-1]
    model = out_ref.shape[1]
    early = early_ref[...].astype(FULL) + early_two_ref[...].astype(FULL)
    late = late_ref[...].astype(FULL) + late_two_ref[...].astype(FULL)
    one = (early.shape[1] - model) // 3
    two = (late.shape[1] - SMALL_LANES) // 3
    for j in range(3):
        at = j * model
        grad_ref[:, at : at + one] = early[:, j * one : (j + 1) * one]
        grad_ref[:, at + one : at + model] = late[:, j * two : (j + 1) * two]
    out_ref[...] = early[:, 3 * one :]
    for i in range(3):
        small_ref[:, SMALL_LANES * i : SMALL_LANES * (i + 1)] = late[
            16 * i : 16 * i + 16, 3 * two :
        ]
    me = who_ref[0]
    row = lax.broadcasted_iota(jnp.int32, (SMALL_ROWS, model), 0)
    for name, ref in zip(NAMES, vectors):
        size = ref.shape[1]
        per_row = model // size
        here_row = jnp.where(row == ROWS[name] + me // per_row, small_ref[...], 0.0)
        values = jnp.sum(here_row, axis=0, keepdims=True)
        picker = one_hot(size, model, size * (me % per_row)).astype(FULL)
        ref[...] = lax.dot_general(
            values, picker, (((1,), (1,)), ((), ())), precision=lax.Precision.HIGHEST,
            preferred_element_type=FULL,
        )


def on_device_ring(
    tokens,
    lengths,
    cotangent,
    first_gain,
    first_shift,
    qkv_weight,
    qv_bias,
    out_weight,
    out_bias,
    second_gain,
    second_shift,
    in_weight,
    in_bias,
    down_weight,
    down_bias,
):
    micro, seq, model = tokens.shape[1:]
    total_rows = micro * seq
    rows = qkv_weight.shape[0]
    down_rows = down_weight.shape[0]
    ff = in_weight.shape[1]
    heads = model // HEAD
    whole = float(lax.axis_size("species") * CELLS * micro * seq)
    index, core, place = here()
    species = lax.axis_index("species")
    who = jnp.stack([index, species]).astype(jnp.int32)
    order = jnp.stack(gather_order(core, place)).astype(jnp.int32)
    slot = jnp.stack(scatter_slots(core, place)).astype(jnp.int32)
    lens = lengths.reshape(micro)
    x = tokens.reshape(total_rows, model)
    cot = cotangent.reshape(total_rows, model)
    vectors = (
        first_gain, first_shift, qv_bias, out_bias, second_gain, second_shift, in_bias, down_bias,
    )

    dma = pltpu.SemaphoreType.DMA

    def gathered(own, hops):
        got = [own]
        for item in hops:
            got += [item, to_partner(item)]
        return got

    own = both_blocks(qkv_weight, core)
    qkv_one = hop(own)
    (small,) = call(
        pack_body,
        [shape((SMALL_ROWS, model))],
        [who, after(lens, own)] + [item.reshape(1, -1) for item in vectors],
        [SMEM, SMEM] + [VMEM] * 8,
        vmem=4,
    )
    in_weight, out_weight = lax.optimization_barrier((in_weight, out_weight, own))[:2]
    in_own = both_blocks(jnp.concatenate([in_weight, out_weight], axis=1), core)
    in_one = hop(in_own)
    small = exchange(small, 1)
    qkv_one, small = lax.optimization_barrier((qkv_one, small))
    qkv_two = hop(qkv_one)
    in_two = hop(after(in_one, qkv_one))
    small = exchange(small, 2)
    down_own = both_blocks(after(down_weight, qkv_one), core)
    qkv_two, small, down_own = lax.optimization_barrier((qkv_two, small, down_own))
    qkv_three = hop(qkv_two)
    small = exchange(small, 4)
    qkv_three, small = lax.optimization_barrier((qkv_three, small))
    qkv_last = hop(half_of(qkv_three, core))
    small = exchange(small, 8)
    in_three = hop(after(in_two, qkv_three, small))
    low, proj, qkv_full = call(
        project_body,
        [
            shape((total_rows, model)),
            shape((total_rows, 3 * model)),
            shape((model, 3 * model)),
        ],
        [order, x, small] + gathered(own, (qkv_one, qkv_two, qkv_three, qkv_last)),
        [SMEM, VMEM, VMEM] + [ANY] * 9,
        scratch=[dma((CELLS,))],
        vmem=20,
    )
    other_small = across(small)
    proj, in_three, other_small = lax.optimization_barrier((proj, in_three, other_small))
    in_last = hop(half_of(in_three, core))
    down_one = hop(after(down_own, in_three))
    att, mixed = call(
        lambda *refs: attend_body(seq, *refs),
        [shape((micro * heads, seq, seq)), shape((total_rows, model))],
        [lens, proj],
        [SMEM, VMEM],
        vmem=12,
    )
    down_one, in_last, mixed = lax.optimization_barrier((down_one, in_last, mixed))
    down_two = hop(down_one)
    in_got = gathered(in_own, (in_one, in_two, in_three, in_last))
    middle, low_two, active, slope, in_full = call(
        inner_body,
        [
            shape((total_rows, model), FULL),
            shape((total_rows, model)),
            shape((total_rows, ff)),
            shape((total_rows, ff)),
            shape((model, ff + model)),
        ],
        [order, x, mixed, small] + in_got,
        [SMEM] + [VMEM] * 3 + [ANY] * 9,
        scratch=[dma((CELLS,))],
        vmem=24,
    )
    down_two, active = lax.optimization_barrier((down_two, active))
    down_three = hop(down_two)
    up_low, down_b, down_keep, down_away, down_keep_two, down_away_two = call(
        lambda *refs: grad_down_body(seq, whole, *refs),
        [
            shape((total_rows, model)),
            shape((1, model), FULL),
        ]
        + [shape((RING_SIZE, down_rows // 2, model))] * 4,
        [who, slot, lens, active, cot, small, other_small],
        [SMEM] * 3 + [VMEM] * 4,
        [VMEM] * 2 + [ANY] * 4,
        scratch=[pltpu.VMEM((2, CELLS, down_rows // 2, model), LOW), dma((2, 2))],
        vmem=15,
    )

    down_three, up_low = lax.optimization_barrier((down_three, up_low))
    down_last = hop(half_of(down_three, core))
    down_other_two = to_partner(down_away_two)
    down_other = to_partner(down_away)
    inner_low, in_b, down_full = call(
        inner_back_body,
        [
            shape((total_rows, ff)),
            shape((ff // model, model), FULL),
            shape((ff, model)),
        ],
        [order, slope, up_low]
        + gathered(down_own, (down_one, down_two, down_three, down_last)),
        [SMEM] + [VMEM] * 2 + [ANY] * 9,
        scratch=[dma((CELLS,))],
        vmem=20,
    )
    down_other_two, inner_low = lax.optimization_barrier((down_other_two, inner_low))
    down_x = across(add_low(down_keep_two[0:3], down_other_two[0:3]))
    down_x_two = across(add_low(down_keep_two[3:8], down_other_two[3:8]))
    in_keep, in_away = call(
        grad_in_body,
        [shape((RING_SIZE, rows, ff)), shape((RING_SIZE, rows, ff))],
        [slot, low_two, inner_low],
        [SMEM] + [VMEM] * 2,
        [ANY] * 2,
        scratch=[pltpu.VMEM((CELLS, rows, ff), LOW), dma((2,))],
        vmem=13,
    )
    in_other = to_partner(in_away)
    (out_tokens,) = call(
        down_body,
        [shape((total_rows, model))],
        [after(active, in_keep), middle, small, down_full],
        [VMEM] * 4,
        vmem=13,
    )
    in_other, out_tokens, inner_low = lax.optimization_barrier((in_other, out_tokens, inner_low))
    in_sum = first_hop(in_keep, in_other)
    grad_middle, grad_low, grad_mixed, sums = call(
        lambda *refs: middle_back_body(seq, whole, *refs),
        [
            shape((total_rows, model), FULL),
            shape((total_rows, model)),
            shape((total_rows, model)),
            shape((3, model), FULL),
        ],
        [lens, inner_low, middle, cot, small, other_small, in_full],
        [SMEM] + [VMEM] * 6,
        vmem=19,
    )

    def attend_back(begin, pairs, grad):
        return call(
            lambda *refs: attend_back_body(seq, begin, *refs),
            [shape((total_rows, 6 * pairs * HEAD))],
            [proj, att, grad],
            [VMEM] * 3,
            vmem=11,

        )[0]

    pairs = model // (2 * HEAD)
    early_pairs = 2 * pairs // 3
    in_sum, down_x, down_other, grad_mixed = lax.optimization_barrier(
        (in_sum, down_x, down_other, grad_mixed)
    )
    down_sum = first_hop(down_keep, down_other, down_x)
    in_sum = second_hop(in_sum, core, in_keep, in_other)
    grad_one = attend_back(0, early_pairs, grad_mixed)
    down_sum, grad_one = lax.optimization_barrier((down_sum, grad_one))
    down_sum = second_hop(down_sum, core, down_keep, down_other, down_x)
    early_width = 6 * early_pairs * HEAD + model
    early_keep, early_away = call(
        early_grad_body,
        [shape((RING_SIZE, rows, early_width))] * 2,
        [slot, low, grad_one, mixed, grad_low],
        [SMEM] + [VMEM] * 4,
        [ANY] * 2,
        scratch=[pltpu.VMEM((CELLS, rows, early_width), LOW), dma((2,))],
        vmem=12,
    )
    early_other = to_partner(early_away)
    in_sum, early_keep, grad_mixed = lax.optimization_barrier((in_sum, early_keep, grad_mixed))
    in_sum = later_hop(in_sum, 3, in_keep, in_other)
    grad_two = attend_back(early_pairs, pairs - early_pairs, grad_mixed)
    early_other, grad_two = lax.optimization_barrier((early_other, grad_two))
    early_sum = first_hop(early_keep, early_other)
    late_width = 6 * (pairs - early_pairs) * HEAD + SMALL_LANES
    grad_tokens, late_keep, late_away = call(
        first_back_body,
        [
            shape((total_rows, model)),
            shape((RING_SIZE, rows, late_width)),
            shape((RING_SIZE, rows, late_width)),
        ],
        [slot, x, low, grad_one, grad_two, grad_middle, small, sums, in_b, down_b, qkv_full],
        [SMEM] + [VMEM] * 10,
        [VMEM] + [ANY] * 2,
        scratch=[
            pltpu.VMEM((SMALL_ROWS, model), FULL),
            pltpu.VMEM((CELLS, rows, late_width), LOW),
            dma((2,)),
        ],
        vmem=16,

    )
    late_other = to_partner(late_away)
    in_sum, early_sum, late_keep, down_sum, down_x_two = lax.optimization_barrier(
        (in_sum, early_sum, late_keep, down_sum, down_x_two)
    )
    in_sum = later_hop(in_sum, 5, in_keep, in_other)
    early_sum = second_hop(early_sum, core, early_keep, early_other)
    down_sum = hop(add_low(down_sum, down_keep[3:5], down_other[3:5], down_x_two[0:2]))
    late_sum = first_hop(late_keep, late_other)
    late_sum, early_sum, down_sum = lax.optimization_barrier((late_sum, early_sum, down_sum))
    down_sum = hop(add_low(down_sum, down_keep[5:7], down_other[5:7], down_x_two[2:4]))
    late_sum = second_hop(late_sum, core, late_keep, late_other)
    early_sum = later_hop(early_sum, 3, early_keep, early_other)
    late_sum, early_sum, down_sum, in_sum = lax.optimization_barrier(
        (late_sum, early_sum, down_sum, in_sum)
    )
    late_sum = later_hop(late_sum, 3, late_keep, late_other)
    early_sum = later_hop(early_sum, 5, early_keep, early_other)
    in_sum = settle(in_sum, core, in_keep, in_other)
    in_terms = (in_sum, across(in_sum))
    mine = jnp.where(core == 0, down_sum[0], down_sum[1])
    other = to_partner(jnp.where(core == 0, down_sum[1], down_sum[0]))
    down_sum = add_low(mine, other, down_keep[7], down_other[7], down_x_two[4])
    down_terms = (down_sum, across(down_sum))
    late_sum = later_hop(late_sum, 5, late_keep, late_other)
    early_sum = settle(early_sum, core, early_keep, early_other)
    early_terms = (early_sum, across(early_sum))
    late_sum = settle(late_sum, core, late_keep, late_other)
    late_terms = (late_sum, across(late_sum))
    finished = call(
        finish_body,
        [shape((rows, 3 * model), FULL), shape((rows, model), FULL)]
        + [shape((1, item.shape[0]), FULL) for item in vectors],
        [who] + list(early_terms) + list(late_terms),
        [SMEM] + [VMEM] * 4,
        scratch=[pltpu.VMEM((SMALL_ROWS, model), FULL)],
        vmem=6,
    )
    grad_qkv, grad_out = finished[:2]
    pieces = [item.reshape(-1) for item in finished[2:]]
    return (
        out_tokens.reshape(tokens.shape),
        grad_tokens.reshape(tokens.shape),
        pieces[0],
        pieces[1],
        grad_qkv,
        pieces[2],
        grad_out,
        pieces[3],
        pieces[4],
        pieces[5],
        in_terms[0].astype(FULL) + in_terms[1].astype(FULL),
        pieces[6],
        jnp.concatenate(
            [
                jnp.where(species == 0, down_terms[0], down_terms[1]),
                jnp.where(species == 0, down_terms[1], down_terms[0]),
            ]
        ).astype(FULL),
        pieces[7],
    )


def on_device(
    tokens,
    lengths,
    cotangent,
    first_gain,
    first_shift,
    qkv_weight,
    qv_bias,
    out_weight,
    out_bias,
    second_gain,
    second_shift,
    in_weight,
    in_bias,
    down_weight,
    down_bias,
):
    local_count = jnp.sum(lengths).astype(jnp.float32)
    count = lax.psum(local_count, ("species", "cells"))
    micro_count = tokens.shape[1]
    seq_rows = tokens.shape[2]
    factor = (
        float(lax.axis_size("species") * lax.axis_size("cells") * micro_count * seq_rows) / count
    )
    output_rows = []
    gradient_rows = []
    summed = None
    for micro_step in range(micro_count):
        gathered = (
            lax.all_gather(first_gain, "cells", axis=0, tiled=True),
            lax.all_gather(first_shift, "cells", axis=0, tiled=True),
            lax.all_gather(qkv_weight, "cells", axis=0, tiled=True),
            lax.all_gather(qv_bias, "cells", axis=0, tiled=True),
            lax.all_gather(out_weight, "cells", axis=0, tiled=True),
            lax.all_gather(out_bias, "cells", axis=0, tiled=True),
            lax.all_gather(second_gain, "cells", axis=0, tiled=True),
            lax.all_gather(second_shift, "cells", axis=0, tiled=True),
            lax.all_gather(in_weight, "cells", axis=0, tiled=True),
            lax.all_gather(in_bias, "cells", axis=0, tiled=True),
            lax.all_gather(down_weight, "cells", axis=0, tiled=True),
            lax.all_gather(down_bias, "cells", axis=0, tiled=True),
        )
        out_seq, grad_seq, grads = sequence_pass(
            gathered,
            tokens[0, micro_step],
            lengths[0, micro_step],
            cotangent[0, micro_step],
            factor,
        )
        output_rows.append(out_seq)
        gradient_rows.append(grad_seq)
        shares = (
            lax.psum_scatter(grads[0], "cells", scatter_dimension=0, tiled=True),
            lax.psum_scatter(grads[1], "cells", scatter_dimension=0, tiled=True),
            lax.psum_scatter(grads[2], "cells", scatter_dimension=0, tiled=True),
            lax.psum_scatter(grads[3], "cells", scatter_dimension=0, tiled=True),
            lax.psum_scatter(grads[4], "cells", scatter_dimension=0, tiled=True),
            lax.psum_scatter(grads[5], "cells", scatter_dimension=0, tiled=True),
            lax.psum_scatter(grads[6], "cells", scatter_dimension=0, tiled=True),
            lax.psum_scatter(grads[7], "cells", scatter_dimension=0, tiled=True),
            lax.psum_scatter(grads[8], "cells", scatter_dimension=0, tiled=True),
            lax.psum_scatter(grads[9], "cells", scatter_dimension=0, tiled=True),
            lax.psum_scatter(grads[10], "cells", scatter_dimension=0, tiled=True),
            lax.psum_scatter(grads[11], "cells", scatter_dimension=0, tiled=True),
        )
        summed = shares if summed is None else jax.tree.map(jnp.add, summed, shares)
    final = (
        lax.psum(summed[0].astype(jnp.bfloat16), "species").astype(jnp.float32),
        lax.psum(summed[1].astype(jnp.bfloat16), "species").astype(jnp.float32),
        lax.psum(summed[2].astype(jnp.bfloat16), "species").astype(jnp.float32),
        lax.psum(summed[3].astype(jnp.bfloat16), "species").astype(jnp.float32),
        lax.psum(summed[4].astype(jnp.bfloat16), "species").astype(jnp.float32),
        lax.psum(summed[5].astype(jnp.bfloat16), "species").astype(jnp.float32),
        lax.psum(summed[6].astype(jnp.bfloat16), "species").astype(jnp.float32),
        lax.psum(summed[7].astype(jnp.bfloat16), "species").astype(jnp.float32),
        lax.psum(summed[8].astype(jnp.bfloat16), "species").astype(jnp.float32),
        lax.psum(summed[9].astype(jnp.bfloat16), "species").astype(jnp.float32),
        lax.psum(summed[10].astype(jnp.bfloat16), "species").astype(jnp.float32),
        lax.psum(summed[11].astype(jnp.bfloat16), "species").astype(jnp.float32),
    )
    out_tokens = jnp.stack(output_rows)[None]
    grad_tokens = jnp.stack(gradient_rows)[None]
    return (out_tokens, grad_tokens) + tuple(final)


def solution(mesh):
    in_specs = (
        P("species", "cells", None, None),
        P("species", "cells"),
        P("species", "cells", None, None),
        P("cells"),
        P("cells"),
        P("cells", None),
        P("cells"),
        P("cells", None),
        P("cells"),
        P("cells"),
        P("cells"),
        P("cells", None),
        P("cells"),
        P("cells", None),
        P("cells"),
    )
    out_specs = (
        P("species", "cells", None, None),
        P("species", "cells", None, None),
        P("cells"),
        P("cells"),
        P("cells", None),
        P("cells"),
        P("cells", None),
        P("cells"),
        P("cells"),
        P("cells"),
        P("cells", None),
        P("cells"),
        P("cells", None),
        P("cells"),
    )
    program = on_device_ring if mesh.shape["cells"] == 2 * RING_SIZE else on_device
    return jax.shard_map(
        program, mesh=mesh, in_specs=in_specs, out_specs=out_specs, check_vma=False
    )
```

```python
import jax
import jax.numpy as jnp
from jax import lax
from jax.experimental import pallas as pl
from jax.experimental.pallas import tpu as pltpu
from jax.sharding import PartitionSpec as P

HEAD = 64


EPSILON = 1e-12
NEGATIVE = -1e30


def normalize(values, gain_vec, shift_vec):
    center = values - jnp.mean(values, axis=-1, keepdims=True)
    spread = jnp.mean(center * center, axis=-1, keepdims=True)
    return center * lax.rsqrt(spread + EPSILON) * gain_vec + shift_vec


def smooth_gate(values):
    return jax.nn.gelu(values, approximate=False)


def times_left(left_side, right_side):
    return lax.dot_general(
        left_side, right_side, (((0,), (0,)), ((), ())), preferred_element_type=jnp.float32
    )


def times_right(left_side, right_side):
    return lax.dot_general(
        left_side, right_side, (((1,), (1,)), ((), ())), preferred_element_type=jnp.float32
    )


def sequence_pass(weights, inputs, length, cot_rows, factor):
    (
        first_gain,
        first_shift,
        qkv_weight,
        qv_bias,
        out_weight,
        out_bias,
        second_gain,
        second_shift,
        in_weight,
        in_bias,
        down_weight,
        down_bias,
    ) = weights
    seq_rows = inputs.shape[0]
    model_width = inputs.shape[1]
    heads_count = model_width // HEAD
    scale_qk = float(HEAD) ** (-0.5)
    as_float = inputs.astype(jnp.float32)
    hidden_one, first_pull = jax.vjp(
        normalize, as_float, first_gain.astype(jnp.float32), first_shift.astype(jnp.float32)
    )
    first_low = hidden_one.astype(jnp.bfloat16)
    bias_float = qv_bias.astype(jnp.float32)
    full_bias = jnp.concatenate(
        [bias_float[:model_width], jnp.zeros((model_width,), jnp.float32), bias_float[model_width:]]
    )
    projected = (
        jnp.dot(first_low, qkv_weight, preferred_element_type=jnp.float32) + full_bias
    ).astype(jnp.bfloat16)
    split_heads = projected.reshape(seq_rows, 3, heads_count, HEAD)
    queries = split_heads[:, 0]
    keys_part = split_heads[:, 1]
    values_part = split_heads[:, 2]
    visible = jnp.arange(seq_rows) < length

    def scores_of():
        raw_scores = (
            jnp.einsum("qhd,khd->hqk", queries, keys_part, preferred_element_type=jnp.float32)
            * scale_qk
        )
        return jnp.where(visible[None, None, :], raw_scores, NEGATIVE)

    scores = scores_of()
    top_score = jnp.max(scores, axis=-1, keepdims=True)
    expo = jnp.exp(scores - top_score)
    total_exp = jnp.sum(expo, axis=-1, keepdims=True)
    log_total = top_score + jnp.log(total_exp)
    attention = (expo / total_exp).astype(jnp.bfloat16)
    mixed = jnp.einsum("hqk,khd->qhd", attention, values_part, preferred_element_type=jnp.float32)
    mixed = mixed.reshape(seq_rows, model_width).astype(jnp.bfloat16)
    middle = (
        as_float
        + jnp.dot(mixed, out_weight, preferred_element_type=jnp.float32)
        + out_bias.astype(jnp.float32)
    )
    hidden_two, second_pull = jax.vjp(
        normalize, middle, second_gain.astype(jnp.float32), second_shift.astype(jnp.float32)
    )
    second_low = hidden_two.astype(jnp.bfloat16)
    inner = jnp.dot(second_low, in_weight, preferred_element_type=jnp.float32) + in_bias.astype(
        jnp.float32
    )
    active, gate_pull = jax.vjp(smooth_gate, inner)
    active_low = active.astype(jnp.bfloat16)
    output = (
        middle
        + jnp.dot(active_low, down_weight, preferred_element_type=jnp.float32)
        + down_bias.astype(jnp.float32)
    )
    upstream = cot_rows.astype(jnp.float32) * visible[:, None].astype(jnp.float32) * factor
    up_low = upstream.astype(jnp.bfloat16)
    grad_down_bias = jnp.sum(up_low.astype(jnp.float32), axis=0)
    grad_down = times_left(active_low, up_low)
    grad_active = times_right(up_low, down_weight)
    (grad_inner,) = gate_pull(grad_active)
    inner_low = grad_inner.astype(jnp.bfloat16)
    grad_in_bias = jnp.sum(inner_low.astype(jnp.float32), axis=0)
    grad_in = times_left(second_low, inner_low)
    grad_second = times_right(inner_low, in_weight)
    grad_middle_norm, grad_second_gain, grad_second_shift = second_pull(grad_second)
    grad_middle = upstream + grad_middle_norm
    middle_low = grad_middle.astype(jnp.bfloat16)
    grad_out_bias = jnp.sum(middle_low.astype(jnp.float32), axis=0)
    grad_out = times_left(mixed, middle_low)
    grad_mixed = (
        times_right(middle_low, out_weight)
        .astype(jnp.bfloat16)
        .reshape(seq_rows, heads_count, HEAD)
    )
    probs_again = jnp.exp(scores_of() - log_total)
    grad_probs = jnp.einsum(
        "qhd,khd->hqk", grad_mixed, values_part, preferred_element_type=jnp.float32
    )
    grad_values = jnp.einsum(
        "hqk,qhd->khd", attention, grad_mixed, preferred_element_type=jnp.float32
    )
    delta = jnp.sum(probs_again * grad_probs, axis=-1, keepdims=True)
    grad_scores = (probs_again * (grad_probs - delta)).astype(jnp.bfloat16)
    grad_queries = (
        jnp.einsum("hqk,khd->qhd", grad_scores, keys_part, preferred_element_type=jnp.float32)
        * scale_qk
    )
    grad_keys = (
        jnp.einsum("hqk,qhd->khd", grad_scores, queries, preferred_element_type=jnp.float32)
        * scale_qk
    )
    grad_projected = jnp.stack([grad_queries, grad_keys, grad_values], axis=1)
    grad_projected = grad_projected.reshape(seq_rows, 3 * model_width).astype(jnp.bfloat16)
    column_sums = jnp.sum(grad_projected.astype(jnp.float32), axis=0)
    grad_qv = jnp.concatenate([column_sums[:model_width], column_sums[2 * model_width :]])
    grad_qkv = times_left(first_low, grad_projected)
    grad_first = times_right(grad_projected, qkv_weight)
    grad_input_norm, grad_first_gain, grad_first_shift = first_pull(grad_first)
    grad_inputs = grad_middle + grad_input_norm
    grads = (
        grad_first_gain,
        grad_first_shift,
        grad_qkv,
        grad_qv,
        grad_out,
        grad_out_bias,
        grad_second_gain,
        grad_second_shift,
        grad_in,
        grad_in_bias,
        grad_down,
        grad_down_bias,
    )
    return (output.astype(jnp.bfloat16), grad_inputs.astype(jnp.bfloat16), grads)


RING = (0, 2, 4, 6, 7, 5, 3, 1)
RING_SIZE = len(RING)
CELLS = 2 * RING_SIZE
ANY = pl.BlockSpec(memory_space=pl.ANY)
HBM = pl.BlockSpec(memory_space=pltpu.HBM)
VMEM = pl.BlockSpec(memory_space=pltpu.VMEM)
SMEM = pl.BlockSpec(memory_space=pltpu.SMEM)
LOW = jnp.bfloat16
FULL = jnp.float32
HEAVY = 10**10
UNIT = 10**8
ROWS = {
    "first_gain": 0,
    "first_shift": 1,
    "qv_bias": 2,
    "out_bias": 4,
    "second_gain": 5,
    "second_shift": 6,
    "in_bias": 7,
    "down_bias": 11,
    "lengths": 12,
}
NAMES = tuple(ROWS)[:8]
SMALL_ROWS = 16
SMALL_LANES = 256
PIECES = (2, 2, 2, 2, 2, 2, 2, 1, 1)


def ring_pairs():
    pairs = []
    for place in range(RING_SIZE):
        chip = RING[place]
        right = RING[(place + 1) % RING_SIZE]
        left = RING[(place - 1) % RING_SIZE]
        pairs.append((2 * chip, 2 * right))
        pairs.append((2 * chip + 1, 2 * left + 1))
    return pairs


def hop(block):
    return lax.ppermute(block, "cells", ring_pairs())


def to_partner(block):
    return lax.ppermute(block, "cells", [(i, i ^ 1) for i in range(CELLS)])


def across(block):
    return lax.ppermute(block, "species", [(0, 1), (1, 0)])


def exchange(values, bit):
    return values + lax.ppermute(values, "cells", [(i, i ^ bit) for i in range(CELLS)])


def after(value, *others):
    return lax.optimization_barrier((value,) + others)[0]


def here():
    index = lax.axis_index("cells")
    core = index % 2
    chip = index // 2
    place = jnp.int32(0)
    for i, ring_chip in enumerate(RING):
        place = jnp.where(chip == ring_chip, i, place)
    return index, core, place


def chip_at(place):
    place = place % RING_SIZE
    chip = jnp.zeros_like(place)
    for i, ring_chip in enumerate(RING):
        chip = jnp.where(place == i, ring_chip, chip)
    return chip


def gather_order(core, place):
    sign = 1 - 2 * core
    order = []

    def pair(at):
        order.append(2 * chip_at(at))
        order.append(2 * chip_at(at) + 1)

    pair(place)
    for step in range(1, 4):
        pair(place - sign * step)
        pair(place + sign * step)
    order.append(2 * chip_at(place + 4) + core)
    order.append(2 * chip_at(place + 4) + 1 - core)
    return order


def scatter_slots(core, place):
    def kept(core_now):
        sign = 1 - 2 * core_now
        order = [2 * chip_at(place + 4) + core_now]
        for step in (3, 2, 1):
            order.append(2 * chip_at(place + sign * step))
            order.append(2 * chip_at(place + sign * step) + 1)
        order.append(2 * chip_at(place) + core_now)
        return order

    order = kept(core) + kept(1 - core)
    slots = []
    for device in range(CELLS):
        slot = jnp.int32(0)
        for i, who in enumerate(order):
            slot = jnp.where(who == device, i, slot)
        slots.append(slot)
    return slots


def both_blocks(block, core):
    other = to_partner(block)
    return jnp.stack([jnp.where(core == 0, block, other), jnp.where(core == 0, other, block)])


def half_of(pair, core):
    return jnp.where(core == 0, pair[0], pair[1])[None]


def add_low(*parts):
    total = parts[0].astype(FULL)
    for part in parts[1:]:
        total = total + part.astype(FULL)
    return total.astype(LOW)


def first_hop(*parts):
    return hop(add_low(*[part[0:1] for part in parts]))


def second_hop(moving, core, *parts):
    wide = jnp.stack([jnp.where(core == 0, moving[0], 0), jnp.where(core == 0, 0, moving[0])])
    return hop(add_low(wide, *[part[1:3] for part in parts]))


def later_hop(moving, at, *parts):
    return hop(add_low(moving, *[part[at : at + 2] for part in parts]))


def settle(moving, core, *parts):
    mine = jnp.where(core == 0, moving[0], moving[1])
    other = jnp.where(core == 0, moving[1], moving[0])
    return add_low(mine, to_partner(other), *[part[7] for part in parts])


def dot(left, right, dims=((1,), (0,))):
    return lax.dot_general(left, right, (dims, ((), ())), preferred_element_type=FULL)


def call(body, out_shape, ins, specs, out_specs=None, scratch=(), vmem=48, cost=HEAVY):
    return pl.pallas_call(
        body,
        out_shape=out_shape,
        in_specs=specs,
        out_specs=[VMEM] * len(out_shape) if out_specs is None else out_specs,
        scratch_shapes=list(scratch),
        compiler_params=pltpu.CompilerParams(vmem_limit_bytes=vmem * 2**20),
        cost_estimate=pl.CostEstimate(flops=cost, bytes_accessed=0, transcendentals=0),
    )(*ins)


def shape(dims, kind=LOW):
    return jax.ShapeDtypeStruct(dims, kind)


def fetch(order_ref, refs, target, sem):
    rows = target.shape[0] // CELLS
    copies = []
    index = 0
    for source, size in zip(refs, PIECES):
        for part in range(size):
            at = order_ref[index]
            copies.append(
                pltpu.make_async_copy(
                    source.at[part],
                    target.at[pl.ds(pl.multiple_of(at * rows, 16), rows)],
                    sem.at[index],
                )
            )
            index += 1
    for item in copies:
        item.start()
    return copies


def wait_all(copies):
    for item in copies:
        item.wait()


def one_hot(rows, lanes, offset):
    row = lax.broadcasted_iota(jnp.int32, (rows, lanes), 0)
    lane = lax.broadcasted_iota(jnp.int32, (rows, lanes), 1)
    return lane == row + offset


def pack_body(who_ref, lengths_ref, *refs):
    sources, small_ref = refs[:8], refs[8]
    me = who_ref[0]
    model = small_ref.shape[1]
    row = lax.broadcasted_iota(jnp.int32, (SMALL_ROWS, model), 0)
    lane = lax.broadcasted_iota(jnp.int32, (SMALL_ROWS, model), 1)
    small = jnp.zeros((SMALL_ROWS, model), FULL)
    for name, ref in zip(NAMES, sources):
        size = ref.shape[1]
        per_row = model // size
        placed = dot(ref[...], one_hot(size, model, size * (me % per_row)).astype(LOW))
        small = small + jnp.where(row == ROWS[name] + me // per_row, placed, 0.0)
    for i in range(2):
        at = (row == ROWS["lengths"]) & (lane == 2 * me + i)
        small = small + jnp.where(at, lengths_ref[i].astype(FULL), 0.0)
    small_ref[...] = small.astype(LOW)


def norm_parts(values):
    center = values - jnp.mean(values, axis=-1, keepdims=True)
    spread = jnp.mean(center * center, axis=-1, keepdims=True)
    return center, lax.rsqrt(spread + EPSILON)


def norm_back(center, scale, gain, grad):
    weighted = grad * gain
    mean_one = jnp.mean(weighted, axis=-1, keepdims=True)
    mean_two = jnp.mean(weighted * center, axis=-1, keepdims=True)
    back = scale * (weighted - mean_one - center * (scale * scale * mean_two))
    return back, jnp.sum(grad * center * scale, axis=0, keepdims=True), jnp.sum(
        grad, axis=0, keepdims=True
    )


def small_row(small_ref, name, count=1):
    return small_ref[...].astype(FULL)[ROWS[name] : ROWS[name] + count, :]


def project_body(order_ref, x_ref, small_ref, *refs):
    blocks = refs[:9]
    low_ref, proj_ref, weight, sem = refs[9:]
    model = x_ref.shape[1]
    copies = fetch(order_ref, blocks, weight, sem)
    center, scale = norm_parts(x_ref[...].astype(FULL))
    bias = small_row(small_ref, "qv_bias", 2)
    low_ref[...] = (
        center * scale * small_row(small_ref, "first_gain") + small_row(small_ref, "first_shift")
    ).astype(LOW)
    wait_all(copies)
    for j in range(3):
        lanes = slice(j * model, (j + 1) * model)
        part = dot(low_ref[...], weight[:, lanes])
        if j != 1:
            part = part + bias[j // 2 : j // 2 + 1]
        proj_ref[:, lanes] = part.astype(LOW)


def attend_body(seq, lengths_ref, proj_ref, att_ref, mixed_ref):
    model = mixed_ref.shape[1]
    cells = mixed_ref.shape[0] // seq
    pairs = model // (2 * HEAD)
    lane = lax.broadcasted_iota(jnp.int32, (seq, 2 * HEAD), 1)
    key = lax.broadcasted_iota(jnp.int32, (seq, seq), 0)

    def step(index, carry):
        s = index // pairs
        p = index % pairs
        rows = pl.ds(pl.multiple_of(s * seq, seq), seq)
        at = pl.multiple_of(p * 2 * HEAD, 2 * HEAD)
        q = proj_ref[rows, pl.ds(at, 2 * HEAD)] * jnp.asarray(HEAD ** (-0.5), LOW)
        k = proj_ref[rows, pl.ds(at + model, 2 * HEAD)]
        v_turned = proj_ref[rows, pl.ds(at + 2 * model, 2 * HEAD)].T
        visible = key < lengths_ref[s]
        mixed = []
        for i in range(2):
            own = (lane >= i * HEAD) & (lane < (i + 1) * HEAD)
            scores = dot(jnp.where(own, k, jnp.zeros_like(k)), q, ((1,), (1,)))
            scores = jnp.where(visible, scores, NEGATIVE)
            expo = jnp.exp(scores - jnp.max(scores, axis=0, keepdims=True))
            probs = expo * (1.0 / jnp.sum(expo, axis=0, keepdims=True))
            probs = probs.astype(LOW)
            att_ref[2 * index + i] = probs
            mixed.append(dot(v_turned[i * HEAD : (i + 1) * HEAD], probs))
        mixed_ref[rows, pl.ds(at, 2 * HEAD)] = jnp.concatenate(mixed, axis=0).T.astype(LOW)
        return carry

    lax.fori_loop(0, cells * pairs, step, 0, unroll=2)


ERFC_STEP = 0.33
ERFC = (
    0.1863578228018033,
    0.18295566386742124,
    0.2012255082472392,
    0.04721561458875723,
    0.4085089979423051,
    -0.35115900736338407,
    0.4602422572120205,
    -0.13534686486277223,
)


def gelu_parts(inner):
    z = jnp.abs(inner) * (0.5**0.5)
    t = 1.0 / (1.0 + ERFC_STEP * z)
    tail = jnp.full_like(t, 0.5 * ERFC[-1])
    for factor in ERFC[-2::-1]:
        tail = tail * t + 0.5 * factor
    bell = jnp.exp(-(z * z))
    tail = tail * t * bell
    area = jnp.where(inner < 0.0, tail, 1.0 - tail)
    return inner * area, area + inner * bell * (0.5 / 3.141592653589793) ** 0.5


def row_mask(lengths_ref, rows, seq):
    at = lax.broadcasted_iota(jnp.int32, (rows, 1), 0)
    true = (at < lengths_ref[0]).astype(FULL)
    for s in range(1, rows // seq):
        true = jnp.where(at < s * seq, true, (at < lengths_ref[s] + s * seq).astype(FULL))
    return true


def loss_rows(lengths_ref, small_ref, other_ref, cot_ref, seq, whole):
    count = jnp.sum(
        small_row(small_ref, "lengths") + small_row(other_ref, "lengths"), axis=-1, keepdims=True
    )
    return cot_ref[...].astype(FULL) * (
        row_mask(lengths_ref, cot_ref.shape[0], seq) * (whole / count)
    )


def put_slots(keep_buf, slot_ref, values, first, lanes):
    rows = keep_buf.shape[1]
    for i in range(values.shape[0] // rows):
        keep_buf[slot_ref[first + i], :, lanes] = values[i * rows : (i + 1) * rows].astype(LOW)


def send_slots(buf, keep_ref, away_ref, sem):
    half = RING_SIZE
    copies = [
        pltpu.make_async_copy(buf.at[pl.ds(half, half)], away_ref, sem.at[0]),
        pltpu.make_async_copy(buf.at[pl.ds(0, half)], keep_ref, sem.at[1]),
    ]
    for item in copies:
        item.start()
    return copies


def inner_body(order_ref, x_ref, mixed_ref, small_ref, *refs):
    blocks = refs[:9]
    middle_ref, low_ref, active_ref, slope_ref, weight, sem = refs[9:]
    model = x_ref.shape[1]
    ff = active_ref.shape[1]
    wait_all(fetch(order_ref, blocks, weight, sem))
    middle = (
        x_ref[...].astype(FULL)
        + dot(mixed_ref[...], weight[:, ff:])
        + small_row(small_ref, "out_bias")
    )
    middle_ref[...] = middle
    center, scale = norm_parts(middle)
    low = center * scale * small_row(small_ref, "second_gain") + small_row(
        small_ref, "second_shift"
    )
    low_ref[...] = low.astype(LOW)
    step = 2 * (ff // RING_SIZE)
    bias = small_row(small_ref, "in_bias", 4)
    for j in range(ff // step):
        lanes = slice(j * step, (j + 1) * step)
        inner = dot(low_ref[...], weight[:, lanes]) + bias[j : j + 1]
        active, slope = gelu_parts(inner)
        active_ref[:, lanes] = active.astype(LOW)
        slope_ref[:, lanes] = slope.astype(LOW)


def grad_down_body(
    seq, whole, who_ref, slot_ref, lengths_ref, active_ref, cot_ref, small_ref, other_ref,
    up_ref, down_b_ref, keep_ref, away_ref, keep_two_ref, away_two_ref, slots, sem,
):
    up_low = loss_rows(lengths_ref, small_ref, other_ref, cot_ref, seq, whole).astype(LOW)
    up_ref[...] = up_low
    down_b_ref[...] = jnp.sum(up_low.astype(FULL), axis=0, keepdims=True)
    parts = RING_SIZE
    step = active_ref.shape[1] // parts
    rows = slots.shape[2]
    side = who_ref[1]
    for j in range(parts):
        grad = dot(active_ref[:, j * step : (j + 1) * step], up_ref[...], ((0,), (0,)))
        for i in range(4):
            slots[(i + side) % 2, slot_ref[j * CELLS // parts + i // 2]] = grad[
                i * rows : (i + 1) * rows
            ].astype(LOW)
    copies = send_slots(slots.at[1], keep_two_ref, away_two_ref, sem.at[1])
    copies += send_slots(slots.at[0], keep_ref, away_ref, sem.at[0])
    wait_all(copies)


def inner_back_body(order_ref, slope_ref, up_ref, *refs):
    blocks = refs[:9]
    inner_ref, in_b_ref, weight, sem = refs[9:]
    model = up_ref.shape[1]
    wait_all(fetch(order_ref, blocks, weight, sem))
    for j in range(inner_ref.shape[1] // model):
        lanes = slice(j * model, (j + 1) * model)
        grad = dot(up_ref[...], weight[lanes, :], ((1,), (1,)))
        low = (grad * slope_ref[:, lanes].astype(FULL)).astype(LOW)
        inner_ref[:, lanes] = low
        in_b_ref[j : j + 1, :] = jnp.sum(low.astype(FULL), axis=0, keepdims=True)


def down_body(active_ref, middle_ref, small_ref, weight_ref, out_ref):
    out_ref[...] = (
        middle_ref[...]
        + dot(active_ref[...], weight_ref[...])
        + small_row(small_ref, "down_bias")
    ).astype(LOW)


def grad_in_body(slot_ref, low_ref, inner_ref, keep_ref, away_ref, slots, sem):
    model = low_ref.shape[1]
    turned = low_ref[...].T
    for j in range(inner_ref.shape[1] // model):
        lanes = slice(j * model, (j + 1) * model)
        put_slots(slots, slot_ref, dot(turned, inner_ref[:, lanes]), 0, lanes)
    wait_all(send_slots(slots, keep_ref, away_ref, sem))


def middle_back_body(
    seq, whole, lengths_ref, inner_ref, middle_ref, cot_ref, small_ref, other_ref, weight,
    grad_ref, grad_low_ref, grad_mixed_ref, sums_ref,
):
    ff = inner_ref.shape[1]
    grad_second = dot(inner_ref[...], weight[:, :ff], ((1,), (1,)))
    center, scale = norm_parts(middle_ref[...])
    back, gain_sum, shift_sum = norm_back(
        center, scale, small_row(small_ref, "second_gain"), grad_second
    )
    grad = loss_rows(lengths_ref, small_ref, other_ref, cot_ref, seq, whole) + back
    grad_ref[...] = grad
    grad_low = grad.astype(LOW)
    grad_low_ref[...] = grad_low
    grad_mixed_ref[...] = dot(grad_low, weight[:, ff:], ((1,), (1,))).astype(LOW)
    sums_ref[0:1, :] = jnp.sum(grad_low.astype(FULL), axis=0, keepdims=True)
    sums_ref[1:2, :] = gain_sum
    sums_ref[2:3, :] = shift_sum


def attend_back_body(seq, begin, proj_ref, att_ref, grad_ref, out_ref):
    model = grad_ref.shape[1]
    half = out_ref.shape[1] // 3
    all_pairs = model // (2 * HEAD)
    pairs = half // (2 * HEAD)
    cells = grad_ref.shape[0] // seq
    lane = lax.broadcasted_iota(jnp.int32, (seq, 2 * HEAD), 1)
    scale = HEAD ** (-0.5)

    def step(index, carry):
        s = index // pairs
        p = index % pairs
        rows = pl.ds(pl.multiple_of(s * seq, seq), seq)
        to = pl.multiple_of(p * 2 * HEAD, 2 * HEAD)
        at = pl.multiple_of(to + begin * 2 * HEAD, 2 * HEAD)
        q = proj_ref[rows, pl.ds(at, 2 * HEAD)]
        k_turned = proj_ref[rows, pl.ds(at + model, 2 * HEAD)].T
        v = proj_ref[rows, pl.ds(at + 2 * model, 2 * HEAD)]
        g = grad_ref[rows, pl.ds(at, 2 * HEAD)]
        grad_q = []
        grad_k = []
        grad_v = []
        for i in range(2):
            own = (lane >= i * HEAD) & (lane < (i + 1) * HEAD)
            probs = att_ref[2 * (s * all_pairs + begin + p) + i]
            wide = probs.astype(FULL)
            grad_probs = dot(jnp.where(own, v, jnp.zeros_like(v)), g, ((1,), (1,)))
            delta = jnp.sum(wide * grad_probs, axis=0, keepdims=True)
            scores = (wide * (grad_probs - delta)).astype(LOW)
            grad_q.append(dot(k_turned[i * HEAD : (i + 1) * HEAD], scores))
            grad_k.append(dot(scores, q))
            grad_v.append(dot(probs, g))
        first = lane < HEAD
        out_ref[rows, pl.ds(to, 2 * HEAD)] = (
            jnp.concatenate(grad_q, axis=0).T * scale
        ).astype(LOW)
        out_ref[rows, pl.ds(to + half, 2 * HEAD)] = (
            jnp.where(first, grad_k[0], grad_k[1]) * scale
        ).astype(LOW)
        out_ref[rows, pl.ds(to + 2 * half, 2 * HEAD)] = jnp.where(
            first, grad_v[0], grad_v[1]
        ).astype(LOW)
        return carry

    lax.fori_loop(0, cells * pairs, step, 0, unroll=2)


def early_grad_body(
    who_ref, slot_ref, low_ref, part_ref, mixed_ref, grad_low_ref, keep_ref, away_ref,
    keep_two_ref, away_two_ref, slots, sem,
):
    side = who_ref[1]
    rows, half = slots.shape[2:]
    width = part_ref.shape[1]
    qkv = dot(low_ref[...].T, part_ref[...]).astype(LOW)
    out = dot(mixed_ref[...].T, grad_low_ref[...]).astype(LOW)
    for device in range(CELLS):
        mine = slice(device * rows, (device + 1) * rows)
        slot = slot_ref[device]
        slots[side, slot] = qkv[mine, :half]
        slots[1 - side, slot, :, : width - half] = qkv[mine, half:]
        slots[1 - side, slot, :, width - half :] = out[mine]
    copies = send_slots(slots.at[1], keep_two_ref, away_two_ref, sem.at[1])
    copies += send_slots(slots.at[0], keep_ref, away_ref, sem.at[0])
    wait_all(copies)


def first_back_body(
    slot_ref, x_ref, low_ref, one_ref, two_ref, grad_ref, small_ref, sums_ref, in_b_ref,
    down_b_ref, weight, out_ref, keep_ref, away_ref, sum_ref, slots, sem,
):
    model = x_ref.shape[1]
    late = two_ref.shape[1]
    center, scale = norm_parts(x_ref[...].astype(FULL))
    parts = ((one_ref, 0), (two_ref, one_ref.shape[1] // 3))
    grad_first = jnp.zeros(x_ref.shape, FULL)
    for j in range(3):
        for ref, begin in parts:
            width = ref.shape[1] // 3
            at = j * model + begin
            grad_first = grad_first + dot(
                ref[:, j * width : (j + 1) * width], weight[:, at : at + width], ((1,), (1,))
            )
    put_slots(slots, slot_ref, dot(low_ref[...].T, two_ref[...]), 0, slice(0, late))
    back, gain_sum, shift_sum = norm_back(
        center, scale, small_row(small_ref, "first_gain"), grad_first
    )

    def put(name, value, offset=0):
        at = ROWS[name] + offset
        sum_ref[at : at + value.shape[0], :] = value

    sum_ref[...] = jnp.zeros_like(sum_ref)
    put("first_gain", gain_sum)
    put("first_shift", shift_sum)
    for j in range(2):
        at = ROWS["qv_bias"] + j
        for ref, begin in parts:
            width = ref.shape[1] // 3
            part = ref[:, 2 * j * width : (2 * j + 1) * width].astype(FULL)
            sum_ref[at : at + 1, begin : begin + width] = jnp.sum(part, axis=0, keepdims=True)
    put("out_bias", sums_ref[0:1, :])
    put("second_gain", sums_ref[1:2, :])
    put("second_shift", sums_ref[2:3, :])
    put("in_bias", in_b_ref[...])
    put("down_bias", down_b_ref[...])
    for i in range(3):
        part = sum_ref[:, SMALL_LANES * i : SMALL_LANES * (i + 1)].astype(LOW)
        for device in range(CELLS):
            slots[device, 16 * i : 16 * i + 16, late:] = part
    copies = send_slots(slots, keep_ref, away_ref, sem)
    out_ref[...] = (grad_ref[...] + back).astype(LOW)
    wait_all(copies)


def finish_body(who_ref, early_ref, early_two_ref, late_ref, late_two_ref, *refs):
    grad_ref, out_ref, vectors, small_ref = refs[0], refs[1], refs[2:-1], refs[-1]
    model = out_ref.shape[1]
    first = who_ref[1] == 0
    one_half = early_ref[...].astype(FULL)
    two_half = early_two_ref[...].astype(FULL)
    early = jnp.concatenate(
        [jnp.where(first, one_half, two_half), jnp.where(first, two_half, one_half)], axis=1
    )
    late = late_ref[...].astype(FULL) + late_two_ref[...].astype(FULL)
    one = (early.shape[1] - model) // 3
    two = (late.shape[1] - SMALL_LANES) // 3
    for j in range(3):
        at = j * model
        grad_ref[:, at : at + one] = early[:, j * one : (j + 1) * one]
        grad_ref[:, at + one : at + model] = late[:, j * two : (j + 1) * two]
    out_ref[...] = early[:, 3 * one :]
    for i in range(3):
        small_ref[:, SMALL_LANES * i : SMALL_LANES * (i + 1)] = late[
            16 * i : 16 * i + 16, 3 * two :
        ]
    me = who_ref[0]
    row = lax.broadcasted_iota(jnp.int32, (SMALL_ROWS, model), 0)
    for name, ref in zip(NAMES, vectors):
        size = ref.shape[1]
        per_row = model // size
        here_row = jnp.where(row == ROWS[name] + me // per_row, small_ref[...], 0.0)
        values = jnp.sum(here_row, axis=0, keepdims=True)
        picker = one_hot(size, model, size * (me % per_row)).astype(FULL)
        ref[...] = lax.dot_general(
            values, picker, (((1,), (1,)), ((), ())), precision=lax.Precision.HIGHEST,
            preferred_element_type=FULL,
        )


def on_device_ring(
    tokens,
    lengths,
    cotangent,
    first_gain,
    first_shift,
    qkv_weight,
    qv_bias,
    out_weight,
    out_bias,
    second_gain,
    second_shift,
    in_weight,
    in_bias,
    down_weight,
    down_bias,
):
    micro, seq, model = tokens.shape[1:]
    total_rows = micro * seq
    rows = qkv_weight.shape[0]
    down_rows = down_weight.shape[0]
    ff = in_weight.shape[1]
    heads = model // HEAD
    whole = float(lax.axis_size("species") * CELLS * micro * seq)
    index, core, place = here()
    species = lax.axis_index("species")
    who = jnp.stack([index, species]).astype(jnp.int32)
    order = jnp.stack(gather_order(core, place)).astype(jnp.int32)
    slot = jnp.stack(scatter_slots(core, place)).astype(jnp.int32)
    lens = lengths.reshape(micro)
    x = tokens.reshape(total_rows, model)
    cot = cotangent.reshape(total_rows, model)
    vectors = (
        first_gain, first_shift, qv_bias, out_bias, second_gain, second_shift, in_bias, down_bias,
    )

    dma = pltpu.SemaphoreType.DMA

    def gathered(own, hops):
        got = [own]
        for item in hops:
            got += [item, to_partner(item)]
        return got

    own = both_blocks(qkv_weight, core)
    qkv_one = hop(own)
    (small,) = call(
        pack_body,
        [shape((SMALL_ROWS, model))],
        [who, after(lens, own)] + [item.reshape(1, -1) for item in vectors],
        [SMEM, SMEM] + [VMEM] * 8,
        vmem=4,
    )
    in_weight, out_weight = lax.optimization_barrier((in_weight, out_weight, own))[:2]
    in_own = both_blocks(jnp.concatenate([in_weight, out_weight], axis=1), core)
    in_one = hop(in_own)
    small = exchange(small, 1)
    qkv_one, small = lax.optimization_barrier((qkv_one, small))
    qkv_two = hop(qkv_one)
    in_two = hop(after(in_one, qkv_one))
    small = exchange(small, 2)
    down_own = both_blocks(after(down_weight, qkv_one), core)
    qkv_two, small, down_own = lax.optimization_barrier((qkv_two, small, down_own))
    qkv_three = hop(qkv_two)
    small = exchange(small, 4)
    qkv_three, small = lax.optimization_barrier((qkv_three, small))
    qkv_last = hop(half_of(qkv_three, core))
    in_three = hop(after(in_two, qkv_three))
    small = exchange(small, 8)
    in_three, small = lax.optimization_barrier((in_three, small))
    in_last = hop(half_of(in_three, core))
    down_one = hop(after(down_own, in_three))
    low, proj, qkv_full = call(
        project_body,
        [
            shape((total_rows, model)),
            shape((total_rows, 3 * model)),
            shape((model, 3 * model)),
        ],
        [order, after(x, in_three), small] + gathered(own, (qkv_one, qkv_two, qkv_three, qkv_last)),
        [SMEM, VMEM, VMEM] + [ANY] * 9,
        scratch=[dma((CELLS,))],
        vmem=20,
    )
    other_small = across(small)
    proj, in_last, other_small, down_one = lax.optimization_barrier(
        (proj, in_last, other_small, down_one)
    )
    down_two = hop(down_one)
    att, mixed = call(
        lambda *refs: attend_body(seq, *refs),
        [shape((micro * heads, seq, seq)), shape((total_rows, model))],
        [lens, proj],
        [SMEM, VMEM],
        vmem=12,
    )
    down_two, mixed = lax.optimization_barrier((down_two, mixed))
    down_three = hop(down_two)
    in_got = gathered(in_own, (in_one, in_two, in_three, in_last))
    middle, low_two, active, slope, in_full = call(
        inner_body,
        [
            shape((total_rows, model), FULL),
            shape((total_rows, model)),
            shape((total_rows, ff)),
            shape((total_rows, ff)),
            shape((model, ff + model)),
        ],
        [order, x, mixed, small] + in_got,
        [SMEM] + [VMEM] * 3 + [ANY] * 9,
        scratch=[dma((CELLS,))],
        vmem=24,
    )
    down_three, active = lax.optimization_barrier((down_three, active))
    down_last = hop(half_of(down_three, core))
    up_low, down_b, down_keep, down_away, down_keep_two, down_away_two = call(
        lambda *refs: grad_down_body(seq, whole, *refs),
        [
            shape((total_rows, model)),
            shape((1, model), FULL),
        ]
        + [shape((RING_SIZE, down_rows // 2, model))] * 4,
        [who, slot, lens, active, cot, small, other_small],
        [SMEM] * 3 + [VMEM] * 4,
        [VMEM] * 2 + [ANY] * 4,
        scratch=[pltpu.VMEM((2, CELLS, down_rows // 2, model), LOW), dma((2, 2))],
        vmem=15,
    )

    down_away, down_away_two, down_last = lax.optimization_barrier(
        (down_away, down_away_two, down_last)
    )
    down_other_two = to_partner(down_away_two)
    down_other = to_partner(down_away)
    inner_low, in_b, down_full = call(
        inner_back_body,
        [
            shape((total_rows, ff)),
            shape((ff // model, model), FULL),
            shape((ff, model)),
        ],
        [order, slope, up_low]
        + gathered(down_own, (down_one, down_two, down_three, down_last)),
        [SMEM] + [VMEM] * 2 + [ANY] * 9,
        scratch=[dma((CELLS,))],
        vmem=20,
    )
    down_other_two, inner_low = lax.optimization_barrier((down_other_two, inner_low))
    down_x = across(add_low(down_keep_two[0:3], down_other_two[0:3]))
    down_x_two = across(add_low(down_keep_two[3:8], down_other_two[3:8]))
    in_keep, in_away = call(
        grad_in_body,
        [shape((RING_SIZE, rows, ff)), shape((RING_SIZE, rows, ff))],
        [slot, low_two, inner_low],
        [SMEM] + [VMEM] * 2,
        [ANY] * 2,
        scratch=[pltpu.VMEM((CELLS, rows, ff), LOW), dma((2,))],
        vmem=13,
    )
    in_other = to_partner(in_away)
    (out_tokens,) = call(
        down_body,
        [shape((total_rows, model))],
        [after(active, in_keep), middle, small, down_full],
        [VMEM] * 4,
        vmem=13,
    )
    in_other, out_tokens, inner_low = lax.optimization_barrier((in_other, out_tokens, inner_low))
    in_sum = first_hop(in_keep, in_other)
    grad_middle, grad_low, grad_mixed, sums = call(
        lambda *refs: middle_back_body(seq, whole, *refs),
        [
            shape((total_rows, model), FULL),
            shape((total_rows, model)),
            shape((total_rows, model)),
            shape((3, model), FULL),
        ],
        [lens, inner_low, middle, cot, small, other_small, in_full],
        [SMEM] + [VMEM] * 6,
        vmem=19,
    )

    def attend_back(begin, pairs, grad):
        return call(
            lambda *refs: attend_back_body(seq, begin, *refs),
            [shape((total_rows, 6 * pairs * HEAD))],
            [proj, att, grad],
            [VMEM] * 3,
            vmem=11,

        )[0]

    pairs = model // (2 * HEAD)
    early_pairs = 2 * pairs // 3
    in_sum, down_x, down_other, grad_mixed = lax.optimization_barrier(
        (in_sum, down_x, down_other, grad_mixed)
    )
    down_sum = first_hop(down_keep, down_other, down_x)
    in_sum = second_hop(in_sum, core, in_keep, in_other)
    grad_one = attend_back(0, early_pairs, grad_mixed)
    down_sum, grad_one = lax.optimization_barrier((down_sum, grad_one))
    down_sum = second_hop(down_sum, core, down_keep, down_other, down_x)
    early_width = 6 * early_pairs * HEAD + model
    early_keep, early_away, early_keep_two, early_away_two = call(
        early_grad_body,
        [shape((RING_SIZE, rows, early_width // 2))] * 4,
        [who, slot, low, grad_one, mixed, grad_low],
        [SMEM] * 2 + [VMEM] * 4,
        [ANY] * 4,
        scratch=[pltpu.VMEM((2, CELLS, rows, early_width // 2), LOW), dma((2, 2))],
        vmem=12,
    )
    early_other_two = to_partner(early_away_two)
    early_other = to_partner(early_away)
    in_sum, early_keep, grad_mixed = lax.optimization_barrier((in_sum, early_keep, grad_mixed))
    in_sum = later_hop(in_sum, 3, in_keep, in_other)
    grad_two = attend_back(early_pairs, pairs - early_pairs, grad_mixed)
    early_other_two, grad_two = lax.optimization_barrier((early_other_two, grad_two))
    early_x = across(add_low(early_keep_two[0:3], early_other_two[0:3]))
    early_x_two = across(add_low(early_keep_two[3:8], early_other_two[3:8]))
    late_width = 6 * (pairs - early_pairs) * HEAD + SMALL_LANES
    grad_tokens, late_keep, late_away = call(
        first_back_body,
        [
            shape((total_rows, model)),
            shape((RING_SIZE, rows, late_width)),
            shape((RING_SIZE, rows, late_width)),
        ],
        [slot, x, low, grad_one, grad_two, grad_middle, small, sums, in_b, down_b, qkv_full],
        [SMEM] + [VMEM] * 10,
        [VMEM] + [ANY] * 2,
        scratch=[
            pltpu.VMEM((SMALL_ROWS, model), FULL),
            pltpu.VMEM((CELLS, rows, late_width), LOW),
            dma((2,)),
        ],
        vmem=16,

    )
    late_other = to_partner(late_away)
    in_sum, late_keep, down_sum, down_x_two, early_x, early_other = lax.optimization_barrier(
        (in_sum, late_keep, down_sum, down_x_two, early_x, early_other)
    )
    down_sum = hop(add_low(down_sum, down_keep[3:5], down_other[3:5], down_x_two[0:2]))
    early_sum = first_hop(early_keep, early_other, early_x)
    late_sum = first_hop(late_keep, late_other)
    in_sum = later_hop(in_sum, 5, in_keep, in_other)
    late_sum, down_sum, early_sum = lax.optimization_barrier((late_sum, down_sum, early_sum))
    late_sum = second_hop(late_sum, core, late_keep, late_other)
    early_sum = second_hop(early_sum, core, early_keep, early_other, early_x)
    down_sum = hop(add_low(down_sum, down_keep[5:7], down_other[5:7], down_x_two[2:4]))
    late_sum, early_sum, early_x_two, in_sum = lax.optimization_barrier(
        (late_sum, early_sum, early_x_two, in_sum)
    )
    late_sum = later_hop(late_sum, 3, late_keep, late_other)
    early_sum = hop(add_low(early_sum, early_keep[3:5], early_other[3:5], early_x_two[0:2]))
    in_sum = settle(in_sum, core, in_keep, in_other)
    in_terms = (in_sum, across(in_sum))
    late_sum, early_sum, down_sum = lax.optimization_barrier((late_sum, early_sum, down_sum))
    late_sum = later_hop(late_sum, 5, late_keep, late_other)
    early_sum = hop(add_low(early_sum, early_keep[5:7], early_other[5:7], early_x_two[2:4]))
    mine = jnp.where(core == 0, down_sum[0], down_sum[1])
    other = to_partner(jnp.where(core == 0, down_sum[1], down_sum[0]))
    down_sum = add_low(mine, other, down_keep[7], down_other[7], down_x_two[4])
    down_terms = (down_sum, across(down_sum))
    mine = jnp.where(core == 0, early_sum[0], early_sum[1])
    other = to_partner(jnp.where(core == 0, early_sum[1], early_sum[0]))
    early_sum = add_low(mine, other, early_keep[7], early_other[7], early_x_two[4])
    early_terms = (early_sum, across(early_sum))
    late_sum = settle(late_sum, core, late_keep, late_other)
    late_terms = (late_sum, across(late_sum))
    finished = call(
        finish_body,
        [shape((rows, 3 * model), FULL), shape((rows, model), FULL)]
        + [shape((1, item.shape[0]), FULL) for item in vectors],
        [who] + list(early_terms) + list(late_terms),
        [SMEM] + [VMEM] * 4,
        scratch=[pltpu.VMEM((SMALL_ROWS, model), FULL)],
        vmem=6,
    )
    grad_qkv, grad_out = finished[:2]
    pieces = [item.reshape(-1) for item in finished[2:]]
    return (
        out_tokens.reshape(tokens.shape),
        grad_tokens.reshape(tokens.shape),
        pieces[0],
        pieces[1],
        grad_qkv,
        pieces[2],
        grad_out,
        pieces[3],
        pieces[4],
        pieces[5],
        in_terms[0].astype(FULL) + in_terms[1].astype(FULL),
        pieces[6],
        jnp.concatenate(
            [
                jnp.where(species == 0, down_terms[0], down_terms[1]),
                jnp.where(species == 0, down_terms[1], down_terms[0]),
            ]
        ).astype(FULL),
        pieces[7],
    )


def on_device(
    tokens,
    lengths,
    cotangent,
    first_gain,
    first_shift,
    qkv_weight,
    qv_bias,
    out_weight,
    out_bias,
    second_gain,
    second_shift,
    in_weight,
    in_bias,
    down_weight,
    down_bias,
):
    local_count = jnp.sum(lengths).astype(jnp.float32)
    count = lax.psum(local_count, ("species", "cells"))
    micro_count = tokens.shape[1]
    seq_rows = tokens.shape[2]
    factor = (
        float(lax.axis_size("species") * lax.axis_size("cells") * micro_count * seq_rows) / count
    )
    output_rows = []
    gradient_rows = []
    summed = None
    for micro_step in range(micro_count):
        gathered = (
            lax.all_gather(first_gain, "cells", axis=0, tiled=True),
            lax.all_gather(first_shift, "cells", axis=0, tiled=True),
            lax.all_gather(qkv_weight, "cells", axis=0, tiled=True),
            lax.all_gather(qv_bias, "cells", axis=0, tiled=True),
            lax.all_gather(out_weight, "cells", axis=0, tiled=True),
            lax.all_gather(out_bias, "cells", axis=0, tiled=True),
            lax.all_gather(second_gain, "cells", axis=0, tiled=True),
            lax.all_gather(second_shift, "cells", axis=0, tiled=True),
            lax.all_gather(in_weight, "cells", axis=0, tiled=True),
            lax.all_gather(in_bias, "cells", axis=0, tiled=True),
            lax.all_gather(down_weight, "cells", axis=0, tiled=True),
            lax.all_gather(down_bias, "cells", axis=0, tiled=True),
        )
        out_seq, grad_seq, grads = sequence_pass(
            gathered,
            tokens[0, micro_step],
            lengths[0, micro_step],
            cotangent[0, micro_step],
            factor,
        )
        output_rows.append(out_seq)
        gradient_rows.append(grad_seq)
        shares = (
            lax.psum_scatter(grads[0], "cells", scatter_dimension=0, tiled=True),
            lax.psum_scatter(grads[1], "cells", scatter_dimension=0, tiled=True),
            lax.psum_scatter(grads[2], "cells", scatter_dimension=0, tiled=True),
            lax.psum_scatter(grads[3], "cells", scatter_dimension=0, tiled=True),
            lax.psum_scatter(grads[4], "cells", scatter_dimension=0, tiled=True),
            lax.psum_scatter(grads[5], "cells", scatter_dimension=0, tiled=True),
            lax.psum_scatter(grads[6], "cells", scatter_dimension=0, tiled=True),
            lax.psum_scatter(grads[7], "cells", scatter_dimension=0, tiled=True),
            lax.psum_scatter(grads[8], "cells", scatter_dimension=0, tiled=True),
            lax.psum_scatter(grads[9], "cells", scatter_dimension=0, tiled=True),
            lax.psum_scatter(grads[10], "cells", scatter_dimension=0, tiled=True),
            lax.psum_scatter(grads[11], "cells", scatter_dimension=0, tiled=True),
        )
        summed = shares if summed is None else jax.tree.map(jnp.add, summed, shares)
    final = (
        lax.psum(summed[0].astype(jnp.bfloat16), "species").astype(jnp.float32),
        lax.psum(summed[1].astype(jnp.bfloat16), "species").astype(jnp.float32),
        lax.psum(summed[2].astype(jnp.bfloat16), "species").astype(jnp.float32),
        lax.psum(summed[3].astype(jnp.bfloat16), "species").astype(jnp.float32),
        lax.psum(summed[4].astype(jnp.bfloat16), "species").astype(jnp.float32),
        lax.psum(summed[5].astype(jnp.bfloat16), "species").astype(jnp.float32),
        lax.psum(summed[6].astype(jnp.bfloat16), "species").astype(jnp.float32),
        lax.psum(summed[7].astype(jnp.bfloat16), "species").astype(jnp.float32),
        lax.psum(summed[8].astype(jnp.bfloat16), "species").astype(jnp.float32),
        lax.psum(summed[9].astype(jnp.bfloat16), "species").astype(jnp.float32),
        lax.psum(summed[10].astype(jnp.bfloat16), "species").astype(jnp.float32),
        lax.psum(summed[11].astype(jnp.bfloat16), "species").astype(jnp.float32),
    )
    out_tokens = jnp.stack(output_rows)[None]
    grad_tokens = jnp.stack(gradient_rows)[None]
    return (out_tokens, grad_tokens) + tuple(final)


def solution(mesh):
    in_specs = (
        P("species", "cells", None, None),
        P("species", "cells"),
        P("species", "cells", None, None),
        P("cells"),
        P("cells"),
        P("cells", None),
        P("cells"),
        P("cells", None),
        P("cells"),
        P("cells"),
        P("cells"),
        P("cells", None),
        P("cells"),
        P("cells", None),
        P("cells"),
    )
    out_specs = (
        P("species", "cells", None, None),
        P("species", "cells", None, None),
        P("cells"),
        P("cells"),
        P("cells", None),
        P("cells"),
        P("cells", None),
        P("cells"),
        P("cells"),
        P("cells"),
        P("cells", None),
        P("cells"),
        P("cells", None),
        P("cells"),
    )
    program = on_device_ring if mesh.shape["cells"] == 2 * RING_SIZE else on_device
    return jax.shard_map(
        program, mesh=mesh, in_specs=in_specs, out_specs=out_specs, check_vma=False
    )
```

```python
import jax
import jax.numpy as jnp
from jax import lax
from jax.experimental import pallas as pl
from jax.experimental.pallas import tpu as pltpu
from jax.sharding import PartitionSpec as P

HEAD = 64


EPSILON = 1e-12
NEGATIVE = -1e30


def normalize(values, gain_vec, shift_vec):
    center = values - jnp.mean(values, axis=-1, keepdims=True)
    spread = jnp.mean(center * center, axis=-1, keepdims=True)
    return center * lax.rsqrt(spread + EPSILON) * gain_vec + shift_vec


def smooth_gate(values):
    return jax.nn.gelu(values, approximate=False)


def times_left(left_side, right_side):
    return lax.dot_general(
        left_side, right_side, (((0,), (0,)), ((), ())), preferred_element_type=jnp.float32
    )


def times_right(left_side, right_side):
    return lax.dot_general(
        left_side, right_side, (((1,), (1,)), ((), ())), preferred_element_type=jnp.float32
    )


def sequence_pass(weights, inputs, length, cot_rows, factor):
    (
        first_gain,
        first_shift,
        qkv_weight,
        qv_bias,
        out_weight,
        out_bias,
        second_gain,
        second_shift,
        in_weight,
        in_bias,
        down_weight,
        down_bias,
    ) = weights
    seq_rows = inputs.shape[0]
    model_width = inputs.shape[1]
    heads_count = model_width // HEAD
    scale_qk = float(HEAD) ** (-0.5)
    as_float = inputs.astype(jnp.float32)
    hidden_one, first_pull = jax.vjp(
        normalize, as_float, first_gain.astype(jnp.float32), first_shift.astype(jnp.float32)
    )
    first_low = hidden_one.astype(jnp.bfloat16)
    bias_float = qv_bias.astype(jnp.float32)
    full_bias = jnp.concatenate(
        [bias_float[:model_width], jnp.zeros((model_width,), jnp.float32), bias_float[model_width:]]
    )
    projected = (
        jnp.dot(first_low, qkv_weight, preferred_element_type=jnp.float32) + full_bias
    ).astype(jnp.bfloat16)
    split_heads = projected.reshape(seq_rows, 3, heads_count, HEAD)
    queries = split_heads[:, 0]
    keys_part = split_heads[:, 1]
    values_part = split_heads[:, 2]
    visible = jnp.arange(seq_rows) < length

    def scores_of():
        raw_scores = (
            jnp.einsum("qhd,khd->hqk", queries, keys_part, preferred_element_type=jnp.float32)
            * scale_qk
        )
        return jnp.where(visible[None, None, :], raw_scores, NEGATIVE)

    scores = scores_of()
    top_score = jnp.max(scores, axis=-1, keepdims=True)
    expo = jnp.exp(scores - top_score)
    total_exp = jnp.sum(expo, axis=-1, keepdims=True)
    log_total = top_score + jnp.log(total_exp)
    attention = (expo / total_exp).astype(jnp.bfloat16)
    mixed = jnp.einsum("hqk,khd->qhd", attention, values_part, preferred_element_type=jnp.float32)
    mixed = mixed.reshape(seq_rows, model_width).astype(jnp.bfloat16)
    middle = (
        as_float
        + jnp.dot(mixed, out_weight, preferred_element_type=jnp.float32)
        + out_bias.astype(jnp.float32)
    )
    hidden_two, second_pull = jax.vjp(
        normalize, middle, second_gain.astype(jnp.float32), second_shift.astype(jnp.float32)
    )
    second_low = hidden_two.astype(jnp.bfloat16)
    inner = jnp.dot(second_low, in_weight, preferred_element_type=jnp.float32) + in_bias.astype(
        jnp.float32
    )
    active, gate_pull = jax.vjp(smooth_gate, inner)
    active_low = active.astype(jnp.bfloat16)
    output = (
        middle
        + jnp.dot(active_low, down_weight, preferred_element_type=jnp.float32)
        + down_bias.astype(jnp.float32)
    )
    upstream = cot_rows.astype(jnp.float32) * visible[:, None].astype(jnp.float32) * factor
    up_low = upstream.astype(jnp.bfloat16)
    grad_down_bias = jnp.sum(up_low.astype(jnp.float32), axis=0)
    grad_down = times_left(active_low, up_low)
    grad_active = times_right(up_low, down_weight)
    (grad_inner,) = gate_pull(grad_active)
    inner_low = grad_inner.astype(jnp.bfloat16)
    grad_in_bias = jnp.sum(inner_low.astype(jnp.float32), axis=0)
    grad_in = times_left(second_low, inner_low)
    grad_second = times_right(inner_low, in_weight)
    grad_middle_norm, grad_second_gain, grad_second_shift = second_pull(grad_second)
    grad_middle = upstream + grad_middle_norm
    middle_low = grad_middle.astype(jnp.bfloat16)
    grad_out_bias = jnp.sum(middle_low.astype(jnp.float32), axis=0)
    grad_out = times_left(mixed, middle_low)
    grad_mixed = (
        times_right(middle_low, out_weight)
        .astype(jnp.bfloat16)
        .reshape(seq_rows, heads_count, HEAD)
    )
    probs_again = jnp.exp(scores_of() - log_total)
    grad_probs = jnp.einsum(
        "qhd,khd->hqk", grad_mixed, values_part, preferred_element_type=jnp.float32
    )
    grad_values = jnp.einsum(
        "hqk,qhd->khd", attention, grad_mixed, preferred_element_type=jnp.float32
    )
    delta = jnp.sum(probs_again * grad_probs, axis=-1, keepdims=True)
    grad_scores = (probs_again * (grad_probs - delta)).astype(jnp.bfloat16)
    grad_queries = (
        jnp.einsum("hqk,khd->qhd", grad_scores, keys_part, preferred_element_type=jnp.float32)
        * scale_qk
    )
    grad_keys = (
        jnp.einsum("hqk,qhd->khd", grad_scores, queries, preferred_element_type=jnp.float32)
        * scale_qk
    )
    grad_projected = jnp.stack([grad_queries, grad_keys, grad_values], axis=1)
    grad_projected = grad_projected.reshape(seq_rows, 3 * model_width).astype(jnp.bfloat16)
    column_sums = jnp.sum(grad_projected.astype(jnp.float32), axis=0)
    grad_qv = jnp.concatenate([column_sums[:model_width], column_sums[2 * model_width :]])
    grad_qkv = times_left(first_low, grad_projected)
    grad_first = times_right(grad_projected, qkv_weight)
    grad_input_norm, grad_first_gain, grad_first_shift = first_pull(grad_first)
    grad_inputs = grad_middle + grad_input_norm
    grads = (
        grad_first_gain,
        grad_first_shift,
        grad_qkv,
        grad_qv,
        grad_out,
        grad_out_bias,
        grad_second_gain,
        grad_second_shift,
        grad_in,
        grad_in_bias,
        grad_down,
        grad_down_bias,
    )
    return (output.astype(jnp.bfloat16), grad_inputs.astype(jnp.bfloat16), grads)


RING = (0, 2, 4, 6, 7, 5, 3, 1)
RING_SIZE = len(RING)
CELLS = 2 * RING_SIZE
ANY = pl.BlockSpec(memory_space=pl.ANY)
HBM = pl.BlockSpec(memory_space=pltpu.HBM)
VMEM = pl.BlockSpec(memory_space=pltpu.VMEM)
SMEM = pl.BlockSpec(memory_space=pltpu.SMEM)
LOW = jnp.bfloat16
FULL = jnp.float32
HEAVY = 10**10
UNIT = 10**8
ROWS = {
    "first_gain": 0,
    "first_shift": 1,
    "qv_bias": 2,
    "out_bias": 4,
    "second_gain": 5,
    "second_shift": 6,
    "in_bias": 7,
    "down_bias": 11,
    "lengths": 12,
}
NAMES = tuple(ROWS)[:8]
SMALL_ROWS = 16
SMALL_LANES = 256
PIECES = (2, 2, 2, 2, 2, 2, 2, 1, 1)


def ring_pairs():
    pairs = []
    for place in range(RING_SIZE):
        chip = RING[place]
        right = RING[(place + 1) % RING_SIZE]
        left = RING[(place - 1) % RING_SIZE]
        pairs.append((2 * chip, 2 * right))
        pairs.append((2 * chip + 1, 2 * left + 1))
    return pairs


def hop(block):
    return lax.ppermute(block, "cells", ring_pairs())


def to_partner(block):
    return lax.ppermute(block, "cells", [(i, i ^ 1) for i in range(CELLS)])


def across(block):
    return lax.ppermute(block, "species", [(0, 1), (1, 0)])


def exchange(values, bit):
    return values + lax.ppermute(values, "cells", [(i, i ^ bit) for i in range(CELLS)])


def after(value, *others):
    return lax.optimization_barrier((value,) + others)[0]


def here():
    index = lax.axis_index("cells")
    core = index % 2
    chip = index // 2
    place = jnp.int32(0)
    for i, ring_chip in enumerate(RING):
        place = jnp.where(chip == ring_chip, i, place)
    return index, core, place


def chip_at(place):
    place = place % RING_SIZE
    chip = jnp.zeros_like(place)
    for i, ring_chip in enumerate(RING):
        chip = jnp.where(place == i, ring_chip, chip)
    return chip


def gather_order(core, place):
    sign = 1 - 2 * core
    order = []

    def pair(at):
        order.append(2 * chip_at(at))
        order.append(2 * chip_at(at) + 1)

    pair(place)
    for step in range(1, 4):
        pair(place - sign * step)
        pair(place + sign * step)
    order.append(2 * chip_at(place + 4) + core)
    order.append(2 * chip_at(place + 4) + 1 - core)
    return order


def scatter_slots(core, place):
    def kept(core_now):
        sign = 1 - 2 * core_now
        order = [2 * chip_at(place + 4) + core_now]
        for step in (3, 2, 1):
            order.append(2 * chip_at(place + sign * step))
            order.append(2 * chip_at(place + sign * step) + 1)
        order.append(2 * chip_at(place) + core_now)
        return order

    order = kept(core) + kept(1 - core)
    slots = []
    for device in range(CELLS):
        slot = jnp.int32(0)
        for i, who in enumerate(order):
            slot = jnp.where(who == device, i, slot)
        slots.append(slot)
    return slots


def both_blocks(block, core):
    other = to_partner(block)
    return jnp.stack([jnp.where(core == 0, block, other), jnp.where(core == 0, other, block)])


def half_of(pair, core):
    return jnp.where(core == 0, pair[0], pair[1])[None]


def add_low(*parts):
    total = parts[0].astype(FULL)
    for part in parts[1:]:
        total = total + part.astype(FULL)
    return total.astype(LOW)


def first_hop(*parts):
    return hop(add_low(*[part[0:1] for part in parts]))


def second_hop(moving, core, *parts):
    wide = jnp.stack([jnp.where(core == 0, moving[0], 0), jnp.where(core == 0, 0, moving[0])])
    return hop(add_low(wide, *[part[1:3] for part in parts]))


def later_hop(moving, at, *parts):
    return hop(add_low(moving, *[part[at : at + 2] for part in parts]))


def settle(moving, core, *parts):
    mine = jnp.where(core == 0, moving[0], moving[1])
    other = jnp.where(core == 0, moving[1], moving[0])
    return add_low(mine, to_partner(other), *[part[7] for part in parts])


def dot(left, right, dims=((1,), (0,))):
    return lax.dot_general(left, right, (dims, ((), ())), preferred_element_type=FULL)


def call(body, out_shape, ins, specs, out_specs=None, scratch=(), vmem=48, cost=HEAVY):
    return pl.pallas_call(
        body,
        out_shape=out_shape,
        in_specs=specs,
        out_specs=[VMEM] * len(out_shape) if out_specs is None else out_specs,
        scratch_shapes=list(scratch),
        compiler_params=pltpu.CompilerParams(vmem_limit_bytes=vmem * 2**20),
        cost_estimate=pl.CostEstimate(flops=cost, bytes_accessed=0, transcendentals=0),
    )(*ins)


def shape(dims, kind=LOW):
    return jax.ShapeDtypeStruct(dims, kind)


def fetch(order_ref, refs, target, sem):
    rows = target.shape[0] // CELLS
    copies = []
    index = 0
    for source, size in zip(refs, PIECES):
        for part in range(size):
            at = order_ref[index]
            copies.append(
                pltpu.make_async_copy(
                    source.at[part],
                    target.at[pl.ds(pl.multiple_of(at * rows, 16), rows)],
                    sem.at[index],
                )
            )
            index += 1
    for item in copies:
        item.start()
    return copies


def wait_all(copies):
    for item in copies:
        item.wait()


def one_hot(rows, lanes, offset):
    row = lax.broadcasted_iota(jnp.int32, (rows, lanes), 0)
    lane = lax.broadcasted_iota(jnp.int32, (rows, lanes), 1)
    return lane == row + offset


def pack_body(who_ref, lengths_ref, *refs):
    sources, small_ref = refs[:8], refs[8]
    me = who_ref[0]
    model = small_ref.shape[1]
    row = lax.broadcasted_iota(jnp.int32, (SMALL_ROWS, model), 0)
    lane = lax.broadcasted_iota(jnp.int32, (SMALL_ROWS, model), 1)
    small = jnp.zeros((SMALL_ROWS, model), FULL)
    for name, ref in zip(NAMES, sources):
        size = ref.shape[1]
        per_row = model // size
        placed = dot(ref[...], one_hot(size, model, size * (me % per_row)).astype(LOW))
        small = small + jnp.where(row == ROWS[name] + me // per_row, placed, 0.0)
    for i in range(2):
        at = (row == ROWS["lengths"]) & (lane == 2 * me + i)
        small = small + jnp.where(at, lengths_ref[i].astype(FULL), 0.0)
    small_ref[...] = small.astype(LOW)


def norm_parts(values):
    center = values - jnp.mean(values, axis=-1, keepdims=True)
    spread = jnp.mean(center * center, axis=-1, keepdims=True)
    return center, lax.rsqrt(spread + EPSILON)


def norm_back(center, scale, gain, grad):
    weighted = grad * gain
    mean_one = jnp.mean(weighted, axis=-1, keepdims=True)
    mean_two = jnp.mean(weighted * center, axis=-1, keepdims=True)
    back = scale * (weighted - mean_one - center * (scale * scale * mean_two))
    return back, jnp.sum(grad * center * scale, axis=0, keepdims=True), jnp.sum(
        grad, axis=0, keepdims=True
    )


def small_row(small_ref, name, count=1):
    return small_ref[...].astype(FULL)[ROWS[name] : ROWS[name] + count, :]


def project_body(order_ref, x_ref, small_ref, *refs):
    blocks = refs[:9]
    low_ref, proj_ref, weight, sem = refs[9:]
    model = x_ref.shape[1]
    copies = fetch(order_ref, blocks, weight, sem)
    center, scale = norm_parts(x_ref[...].astype(FULL))
    bias = small_row(small_ref, "qv_bias", 2)
    low_ref[...] = (
        center * scale * small_row(small_ref, "first_gain") + small_row(small_ref, "first_shift")
    ).astype(LOW)
    wait_all(copies)
    for j in range(3):
        lanes = slice(j * model, (j + 1) * model)
        part = dot(low_ref[...], weight[:, lanes])
        if j != 1:
            part = part + bias[j // 2 : j // 2 + 1]
        proj_ref[:, lanes] = part.astype(LOW)


def attend_body(seq, lengths_ref, proj_ref, att_ref, mixed_ref):
    model = mixed_ref.shape[1]
    cells = mixed_ref.shape[0] // seq
    pairs = model // (2 * HEAD)
    lane = lax.broadcasted_iota(jnp.int32, (seq, 2 * HEAD), 1)
    key = lax.broadcasted_iota(jnp.int32, (seq, seq), 0)

    def step(index, carry):
        s = index // pairs
        p = index % pairs
        rows = pl.ds(pl.multiple_of(s * seq, seq), seq)
        at = pl.multiple_of(p * 2 * HEAD, 2 * HEAD)
        q = proj_ref[rows, pl.ds(at, 2 * HEAD)] * jnp.asarray(HEAD ** (-0.5), LOW)
        k = proj_ref[rows, pl.ds(at + model, 2 * HEAD)]
        v_turned = proj_ref[rows, pl.ds(at + 2 * model, 2 * HEAD)].T
        visible = key < lengths_ref[s]
        mixed = []
        for i in range(2):
            own = (lane >= i * HEAD) & (lane < (i + 1) * HEAD)
            scores = dot(jnp.where(own, k, jnp.zeros_like(k)), q, ((1,), (1,)))
            scores = jnp.where(visible, scores, NEGATIVE)
            expo = jnp.exp(scores - jnp.max(scores, axis=0, keepdims=True))
            probs = expo * (1.0 / jnp.sum(expo, axis=0, keepdims=True))
            probs = probs.astype(LOW)
            att_ref[2 * index + i] = probs
            mixed.append(dot(v_turned[i * HEAD : (i + 1) * HEAD], probs))
        mixed_ref[rows, pl.ds(at, 2 * HEAD)] = jnp.concatenate(mixed, axis=0).T.astype(LOW)
        return carry

    lax.fori_loop(0, cells * pairs, step, 0, unroll=2)


ERFC_STEP = 0.33
ERFC = (
    0.1863578228018033,
    0.18295566386742124,
    0.2012255082472392,
    0.04721561458875723,
    0.4085089979423051,
    -0.35115900736338407,
    0.4602422572120205,
    -0.13534686486277223,
)


def gelu_parts(inner):
    z = jnp.abs(inner) * (0.5**0.5)
    t = 1.0 / (1.0 + ERFC_STEP * z)
    tail = jnp.full_like(t, 0.5 * ERFC[-1])
    for factor in ERFC[-2::-1]:
        tail = tail * t + 0.5 * factor
    bell = jnp.exp(-(z * z))
    tail = tail * t * bell
    area = jnp.where(inner < 0.0, tail, 1.0 - tail)
    return inner * area, area + inner * bell * (0.5 / 3.141592653589793) ** 0.5


def row_mask(lengths_ref, rows, seq):
    at = lax.broadcasted_iota(jnp.int32, (rows, 1), 0)
    true = (at < lengths_ref[0]).astype(FULL)
    for s in range(1, rows // seq):
        true = jnp.where(at < s * seq, true, (at < lengths_ref[s] + s * seq).astype(FULL))
    return true


def loss_rows(lengths_ref, small_ref, other_ref, cot_ref, seq, whole):
    count = jnp.sum(
        small_row(small_ref, "lengths") + small_row(other_ref, "lengths"), axis=-1, keepdims=True
    )
    return cot_ref[...].astype(FULL) * (
        row_mask(lengths_ref, cot_ref.shape[0], seq) * (whole / count)
    )


def store_slot(keep_ref, away_ref, slot, lanes, block, chosen=None):
    for ref, inside, at in (
        (keep_ref, slot < RING_SIZE, slot), (away_ref, slot >= RING_SIZE, slot - RING_SIZE)
    ):
        inside = inside if chosen is None else inside & chosen

        @pl.when(inside)
        def _(ref=ref, at=at):
            ref[at, :, lanes] = block


def put_slots(keep_ref, away_ref, slot_ref, values, lanes):
    rows = keep_ref.shape[1]
    for i in range(values.shape[0] // rows):
        block = values[i * rows : (i + 1) * rows].astype(LOW)
        store_slot(keep_ref, away_ref, slot_ref[i], lanes, block)


def inner_body(order_ref, x_ref, mixed_ref, small_ref, *refs):
    blocks = refs[:9]
    middle_ref, low_ref, active_ref, slope_ref, weight, sem = refs[9:]
    model = x_ref.shape[1]
    ff = active_ref.shape[1]
    wait_all(fetch(order_ref, blocks, weight, sem))
    middle = (
        x_ref[...].astype(FULL)
        + dot(mixed_ref[...], weight[:, ff:])
        + small_row(small_ref, "out_bias")
    )
    middle_ref[...] = middle
    center, scale = norm_parts(middle)
    low = center * scale * small_row(small_ref, "second_gain") + small_row(
        small_ref, "second_shift"
    )
    low_ref[...] = low.astype(LOW)
    step = 2 * (ff // RING_SIZE)
    bias = small_row(small_ref, "in_bias", 4)
    for j in range(ff // step):
        lanes = slice(j * step, (j + 1) * step)
        inner = dot(low_ref[...], weight[:, lanes]) + bias[j : j + 1]
        active, slope = gelu_parts(inner)
        active_ref[:, lanes] = active.astype(LOW)
        slope_ref[:, lanes] = slope.astype(LOW)


def grad_down_body(
    seq, whole, who_ref, slot_ref, lengths_ref, active_ref, cot_ref, small_ref, other_ref,
    up_ref, down_b_ref, keep_ref, away_ref, keep_two_ref, away_two_ref,
):
    up_low = loss_rows(lengths_ref, small_ref, other_ref, cot_ref, seq, whole).astype(LOW)
    up_ref[...] = up_low
    down_b_ref[...] = jnp.sum(up_low.astype(FULL), axis=0, keepdims=True)
    parts = RING_SIZE
    step = active_ref.shape[1] // parts
    rows = keep_ref.shape[1]
    mine = (who_ref[1] == 0, who_ref[1] == 1)
    for j in range(parts):
        grad = dot(active_ref[:, j * step : (j + 1) * step], up_ref[...], ((0,), (0,)))
        for i in range(4):
            block = grad[i * rows : (i + 1) * rows].astype(LOW)
            slot = slot_ref[j * CELLS // parts + i // 2]
            store_slot(keep_ref, away_ref, slot, slice(None), block, mine[i % 2])
            store_slot(keep_two_ref, away_two_ref, slot, slice(None), block, mine[1 - i % 2])


def inner_back_body(order_ref, slope_ref, up_ref, *refs):
    blocks = refs[:9]
    inner_ref, in_b_ref, weight, sem = refs[9:]
    model = up_ref.shape[1]
    wait_all(fetch(order_ref, blocks, weight, sem))
    for j in range(inner_ref.shape[1] // model):
        lanes = slice(j * model, (j + 1) * model)
        grad = dot(up_ref[...], weight[lanes, :], ((1,), (1,)))
        low = (grad * slope_ref[:, lanes].astype(FULL)).astype(LOW)
        inner_ref[:, lanes] = low
        in_b_ref[j : j + 1, :] = jnp.sum(low.astype(FULL), axis=0, keepdims=True)


def down_body(active_ref, middle_ref, small_ref, weight_ref, out_ref):
    out_ref[...] = (
        middle_ref[...]
        + dot(active_ref[...], weight_ref[...])
        + small_row(small_ref, "down_bias")
    ).astype(LOW)


def grad_in_body(slot_ref, low_ref, inner_ref, keep_ref, away_ref):
    model = low_ref.shape[1]
    turned = low_ref[...].T
    for j in range(inner_ref.shape[1] // model):
        lanes = slice(j * model, (j + 1) * model)
        put_slots(keep_ref, away_ref, slot_ref, dot(turned, inner_ref[:, lanes]), lanes)


def middle_back_body(
    seq, whole, lengths_ref, inner_ref, middle_ref, cot_ref, small_ref, other_ref, weight,
    grad_ref, grad_low_ref, grad_mixed_ref, sums_ref,
):
    ff = inner_ref.shape[1]
    grad_second = dot(inner_ref[...], weight[:, :ff], ((1,), (1,)))
    center, scale = norm_parts(middle_ref[...])
    back, gain_sum, shift_sum = norm_back(
        center, scale, small_row(small_ref, "second_gain"), grad_second
    )
    grad = loss_rows(lengths_ref, small_ref, other_ref, cot_ref, seq, whole) + back
    grad_ref[...] = grad
    grad_low = grad.astype(LOW)
    grad_low_ref[...] = grad_low
    grad_mixed_ref[...] = dot(grad_low, weight[:, ff:], ((1,), (1,))).astype(LOW)
    sums_ref[0:1, :] = jnp.sum(grad_low.astype(FULL), axis=0, keepdims=True)
    sums_ref[1:2, :] = gain_sum
    sums_ref[2:3, :] = shift_sum


def attend_back_body(seq, begin, proj_ref, att_ref, grad_ref, out_ref):
    model = grad_ref.shape[1]
    half = out_ref.shape[1] // 3
    all_pairs = model // (2 * HEAD)
    pairs = half // (2 * HEAD)
    cells = grad_ref.shape[0] // seq
    lane = lax.broadcasted_iota(jnp.int32, (seq, 2 * HEAD), 1)
    scale = HEAD ** (-0.5)

    def step(index, carry):
        s = index // pairs
        p = index % pairs
        rows = pl.ds(pl.multiple_of(s * seq, seq), seq)
        to = pl.multiple_of(p * 2 * HEAD, 2 * HEAD)
        at = pl.multiple_of(to + begin * 2 * HEAD, 2 * HEAD)
        q = proj_ref[rows, pl.ds(at, 2 * HEAD)]
        k_turned = proj_ref[rows, pl.ds(at + model, 2 * HEAD)].T
        v = proj_ref[rows, pl.ds(at + 2 * model, 2 * HEAD)]
        g = grad_ref[rows, pl.ds(at, 2 * HEAD)]
        grad_q = []
        grad_k = []
        grad_v = []
        for i in range(2):
            own = (lane >= i * HEAD) & (lane < (i + 1) * HEAD)
            probs = att_ref[2 * (s * all_pairs + begin + p) + i]
            wide = probs.astype(FULL)
            grad_probs = dot(jnp.where(own, v, jnp.zeros_like(v)), g, ((1,), (1,)))
            delta = jnp.sum(wide * grad_probs, axis=0, keepdims=True)
            scores = (wide * (grad_probs - delta)).astype(LOW)
            grad_q.append(dot(k_turned[i * HEAD : (i + 1) * HEAD], scores))
            grad_k.append(dot(scores, q))
            grad_v.append(dot(probs, g))
        first = lane < HEAD
        out_ref[rows, pl.ds(to, 2 * HEAD)] = (
            jnp.concatenate(grad_q, axis=0).T * scale
        ).astype(LOW)
        out_ref[rows, pl.ds(to + half, 2 * HEAD)] = (
            jnp.where(first, grad_k[0], grad_k[1]) * scale
        ).astype(LOW)
        out_ref[rows, pl.ds(to + 2 * half, 2 * HEAD)] = jnp.where(
            first, grad_v[0], grad_v[1]
        ).astype(LOW)
        return carry

    lax.fori_loop(0, cells * pairs, step, 0, unroll=2)


def early_grad_body(
    slot_ref, low_ref, part_ref, mixed_ref, grad_low_ref, keep_ref, away_ref
):
    width = part_ref.shape[1]
    lanes = slice(0, width)
    put_slots(keep_ref, away_ref, slot_ref, dot(low_ref[...].T, part_ref[...]), lanes)
    lanes = slice(width, keep_ref.shape[2])
    put_slots(keep_ref, away_ref, slot_ref, dot(mixed_ref[...].T, grad_low_ref[...]), lanes)


def first_back_body(
    slot_ref, x_ref, low_ref, one_ref, two_ref, grad_ref, small_ref, sums_ref, in_b_ref,
    down_b_ref, weight, out_ref, keep_ref, away_ref, sum_ref,
):
    model = x_ref.shape[1]
    late = two_ref.shape[1]
    center, scale = norm_parts(x_ref[...].astype(FULL))
    parts = ((one_ref, 0), (two_ref, one_ref.shape[1] // 3))
    grad_first = jnp.zeros(x_ref.shape, FULL)
    for j in range(3):
        for ref, begin in parts:
            width = ref.shape[1] // 3
            at = j * model + begin
            grad_first = grad_first + dot(
                ref[:, j * width : (j + 1) * width], weight[:, at : at + width], ((1,), (1,))
            )
    put_slots(keep_ref, away_ref, slot_ref, dot(low_ref[...].T, two_ref[...]), slice(0, late))
    back, gain_sum, shift_sum = norm_back(
        center, scale, small_row(small_ref, "first_gain"), grad_first
    )

    def put(name, value, offset=0):
        at = ROWS[name] + offset
        sum_ref[at : at + value.shape[0], :] = value

    sum_ref[...] = jnp.zeros_like(sum_ref)
    put("first_gain", gain_sum)
    put("first_shift", shift_sum)
    for j in range(2):
        at = ROWS["qv_bias"] + j
        for ref, begin in parts:
            width = ref.shape[1] // 3
            part = ref[:, 2 * j * width : (2 * j + 1) * width].astype(FULL)
            sum_ref[at : at + 1, begin : begin + width] = jnp.sum(part, axis=0, keepdims=True)
    put("out_bias", sums_ref[0:1, :])
    put("second_gain", sums_ref[1:2, :])
    put("second_shift", sums_ref[2:3, :])
    put("in_bias", in_b_ref[...])
    put("down_bias", down_b_ref[...])
    for i in range(3):
        part = sum_ref[:, SMALL_LANES * i : SMALL_LANES * (i + 1)].astype(LOW)
        for at in range(RING_SIZE):
            keep_ref[at, 16 * i : 16 * i + 16, late:] = part
            away_ref[at, 16 * i : 16 * i + 16, late:] = part
    out_ref[...] = (grad_ref[...] + back).astype(LOW)


def finish_body(who_ref, early_ref, early_two_ref, late_ref, late_two_ref, *refs):
    grad_ref, out_ref, vectors, small_ref = refs[0], refs[1], refs[2:-1], refs[-1]
    model = out_ref.shape[1]
    early = early_ref[...].astype(FULL) + early_two_ref[...].astype(FULL)
    late = late_ref[...].astype(FULL) + late_two_ref[...].astype(FULL)
    one = (early.shape[1] - model) // 3
    two = (late.shape[1] - SMALL_LANES) // 3
    for j in range(3):
        at = j * model
        grad_ref[:, at : at + one] = early[:, j * one : (j + 1) * one]
        grad_ref[:, at + one : at + model] = late[:, j * two : (j + 1) * two]
    out_ref[...] = early[:, 3 * one :]
    for i in range(3):
        small_ref[:, SMALL_LANES * i : SMALL_LANES * (i + 1)] = late[
            16 * i : 16 * i + 16, 3 * two :
        ]
    me = who_ref[0]
    row = lax.broadcasted_iota(jnp.int32, (SMALL_ROWS, model), 0)
    for name, ref in zip(NAMES, vectors):
        size = ref.shape[1]
        per_row = model // size
        here_row = jnp.where(row == ROWS[name] + me // per_row, small_ref[...], 0.0)
        values = jnp.sum(here_row, axis=0, keepdims=True)
        picker = one_hot(size, model, size * (me % per_row)).astype(FULL)
        ref[...] = lax.dot_general(
            values, picker, (((1,), (1,)), ((), ())), precision=lax.Precision.HIGHEST,
            preferred_element_type=FULL,
        )


def on_device_ring(
    tokens,
    lengths,
    cotangent,
    first_gain,
    first_shift,
    qkv_weight,
    qv_bias,
    out_weight,
    out_bias,
    second_gain,
    second_shift,
    in_weight,
    in_bias,
    down_weight,
    down_bias,
):
    micro, seq, model = tokens.shape[1:]
    total_rows = micro * seq
    rows = qkv_weight.shape[0]
    down_rows = down_weight.shape[0]
    ff = in_weight.shape[1]
    heads = model // HEAD
    whole = float(lax.axis_size("species") * CELLS * micro * seq)
    index, core, place = here()
    species = lax.axis_index("species")
    who = jnp.stack([index, species]).astype(jnp.int32)
    order = jnp.stack(gather_order(core, place)).astype(jnp.int32)
    slot = jnp.stack(scatter_slots(core, place)).astype(jnp.int32)
    lens = lengths.reshape(micro)
    x = tokens.reshape(total_rows, model)
    cot = cotangent.reshape(total_rows, model)
    vectors = (
        first_gain, first_shift, qv_bias, out_bias, second_gain, second_shift, in_bias, down_bias,
    )

    dma = pltpu.SemaphoreType.DMA

    def gathered(own, hops):
        got = [own]
        for item in hops:
            got += [item, to_partner(item)]
        return got

    own = both_blocks(qkv_weight, core)
    qkv_one = hop(own)
    (small,) = call(
        pack_body,
        [shape((SMALL_ROWS, model))],
        [who, after(lens, own)] + [item.reshape(1, -1) for item in vectors],
        [SMEM, SMEM] + [VMEM] * 8,
        vmem=4,
    )
    in_weight, out_weight = lax.optimization_barrier((in_weight, out_weight, own))[:2]
    in_own = both_blocks(jnp.concatenate([in_weight, out_weight], axis=1), core)
    in_one = hop(in_own)
    small = exchange(small, 1)
    qkv_one, small = lax.optimization_barrier((qkv_one, small))
    qkv_two = hop(qkv_one)
    in_two = hop(after(in_one, qkv_one))
    small = exchange(small, 2)
    down_own = both_blocks(after(down_weight, qkv_one), core)
    qkv_two, small, down_own = lax.optimization_barrier((qkv_two, small, down_own))
    qkv_three = hop(qkv_two)
    small = exchange(small, 4)
    qkv_three, small = lax.optimization_barrier((qkv_three, small))
    qkv_last = hop(half_of(qkv_three, core))
    in_three = hop(after(in_two, qkv_three))
    small = exchange(small, 8)
    in_three, small = lax.optimization_barrier((in_three, small))
    in_last = hop(half_of(in_three, core))
    down_one = hop(after(down_own, in_three))
    low, proj, qkv_full = call(
        project_body,
        [
            shape((total_rows, model)),
            shape((total_rows, 3 * model)),
            shape((model, 3 * model)),
        ],
        [order, after(x, in_three), small] + gathered(own, (qkv_one, qkv_two, qkv_three, qkv_last)),
        [SMEM, VMEM, VMEM] + [ANY] * 9,
        scratch=[dma((CELLS,))],
        vmem=20,
    )
    other_small = across(small)
    proj, in_last, other_small, down_one = lax.optimization_barrier(
        (proj, in_last, other_small, down_one)
    )
    down_two = hop(down_one)
    att, mixed = call(
        lambda *refs: attend_body(seq, *refs),
        [shape((micro * heads, seq, seq)), shape((total_rows, model))],
        [lens, proj],
        [SMEM, VMEM],
        vmem=12,
    )
    down_two, mixed = lax.optimization_barrier((down_two, mixed))
    down_three = hop(down_two)
    in_got = gathered(in_own, (in_one, in_two, in_three, in_last))
    middle, low_two, active, slope, in_full = call(
        inner_body,
        [
            shape((total_rows, model), FULL),
            shape((total_rows, model)),
            shape((total_rows, ff)),
            shape((total_rows, ff)),
            shape((model, ff + model)),
        ],
        [order, x, mixed, small] + in_got,
        [SMEM] + [VMEM] * 3 + [ANY] * 9,
        scratch=[dma((CELLS,))],
        vmem=24,
    )
    down_three, active = lax.optimization_barrier((down_three, active))
    down_last = hop(half_of(down_three, core))
    up_low, down_b, down_keep, down_away, down_keep_two, down_away_two = call(
        lambda *refs: grad_down_body(seq, whole, *refs),
        [
            shape((total_rows, model)),
            shape((1, model), FULL),
        ]
        + [shape((RING_SIZE, down_rows // 2, model))] * 4,
        [who, slot, lens, active, cot, small, other_small],
        [SMEM] * 3 + [VMEM] * 4,
        vmem=15,
    )

    down_away, down_away_two, down_last = lax.optimization_barrier(
        (down_away, down_away_two, down_last)
    )
    down_other_two = to_partner(down_away_two)
    down_other = to_partner(down_away)
    inner_low, in_b, down_full = call(
        inner_back_body,
        [
            shape((total_rows, ff)),
            shape((ff // model, model), FULL),
            shape((ff, model)),
        ],
        [order, slope, up_low]
        + gathered(down_own, (down_one, down_two, down_three, down_last)),
        [SMEM] + [VMEM] * 2 + [ANY] * 9,
        scratch=[dma((CELLS,))],
        vmem=20,
    )
    down_other_two, inner_low = lax.optimization_barrier((down_other_two, inner_low))
    down_x = across(add_low(down_keep_two[0:3], down_other_two[0:3]))
    down_x_two = across(add_low(down_keep_two[3:8], down_other_two[3:8]))
    in_keep, in_away = call(
        grad_in_body,
        [shape((RING_SIZE, rows, ff)), shape((RING_SIZE, rows, ff))],
        [slot, low_two, inner_low],
        [SMEM] + [VMEM] * 2,
        vmem=13,
    )
    in_other = to_partner(in_away)
    (out_tokens,) = call(
        down_body,
        [shape((total_rows, model))],
        [after(active, in_keep), middle, small, down_full],
        [VMEM] * 4,
        vmem=13,
    )
    in_other, out_tokens, inner_low = lax.optimization_barrier((in_other, out_tokens, inner_low))
    in_sum = first_hop(in_keep, in_other)
    grad_middle, grad_low, grad_mixed, sums = call(
        lambda *refs: middle_back_body(seq, whole, *refs),
        [
            shape((total_rows, model), FULL),
            shape((total_rows, model)),
            shape((total_rows, model)),
            shape((3, model), FULL),
        ],
        [lens, inner_low, middle, cot, small, other_small, in_full],
        [SMEM] + [VMEM] * 6,
        vmem=19,
    )

    def attend_back(begin, pairs, grad):
        return call(
            lambda *refs: attend_back_body(seq, begin, *refs),
            [shape((total_rows, 6 * pairs * HEAD))],
            [proj, att, grad],
            [VMEM] * 3,
            vmem=11,

        )[0]

    pairs = model // (2 * HEAD)
    early_pairs = 2 * pairs // 3
    in_sum, down_x, down_other, grad_mixed = lax.optimization_barrier(
        (in_sum, down_x, down_other, grad_mixed)
    )
    down_sum = first_hop(down_keep, down_other, down_x)
    in_sum = second_hop(in_sum, core, in_keep, in_other)
    grad_one = attend_back(0, early_pairs, grad_mixed)
    down_sum, grad_one = lax.optimization_barrier((down_sum, grad_one))
    down_sum = second_hop(down_sum, core, down_keep, down_other, down_x)
    early_width = 6 * early_pairs * HEAD + model
    early_keep, early_away = call(
        early_grad_body,
        [shape((RING_SIZE, rows, early_width))] * 2,
        [slot, low, grad_one, mixed, grad_low],
        [SMEM] + [VMEM] * 4,
        vmem=12,
    )
    early_other = to_partner(early_away)
    in_sum, early_keep, grad_mixed = lax.optimization_barrier((in_sum, early_keep, grad_mixed))
    in_sum = later_hop(in_sum, 3, in_keep, in_other)
    grad_two = attend_back(early_pairs, pairs - early_pairs, grad_mixed)
    early_other, grad_two = lax.optimization_barrier((early_other, grad_two))
    early_sum = first_hop(early_keep, early_other)
    late_width = 6 * (pairs - early_pairs) * HEAD + SMALL_LANES
    grad_tokens, late_keep, late_away = call(
        first_back_body,
        [
            shape((total_rows, model)),
            shape((RING_SIZE, rows, late_width)),
            shape((RING_SIZE, rows, late_width)),
        ],
        [slot, x, low, grad_one, grad_two, grad_middle, small, sums, in_b, down_b, qkv_full],
        [SMEM] + [VMEM] * 10,
        scratch=[pltpu.VMEM((SMALL_ROWS, model), FULL)],
        vmem=16,

    )
    late_other = to_partner(late_away)
    in_sum, early_sum, late_keep, down_sum, down_x_two = lax.optimization_barrier(
        (in_sum, early_sum, late_keep, down_sum, down_x_two)
    )
    in_sum = later_hop(in_sum, 5, in_keep, in_other)
    early_sum = second_hop(early_sum, core, early_keep, early_other)
    down_sum = hop(add_low(down_sum, down_keep[3:5], down_other[3:5], down_x_two[0:2]))
    late_sum = first_hop(late_keep, late_other)
    late_sum, early_sum, down_sum = lax.optimization_barrier((late_sum, early_sum, down_sum))
    down_sum = hop(add_low(down_sum, down_keep[5:7], down_other[5:7], down_x_two[2:4]))
    late_sum = second_hop(late_sum, core, late_keep, late_other)
    early_sum = later_hop(early_sum, 3, early_keep, early_other)
    late_sum, early_sum, down_sum, in_sum = lax.optimization_barrier(
        (late_sum, early_sum, down_sum, in_sum)
    )
    late_sum = later_hop(late_sum, 3, late_keep, late_other)
    early_sum = later_hop(early_sum, 5, early_keep, early_other)
    in_sum = settle(in_sum, core, in_keep, in_other)
    in_terms = (in_sum, across(in_sum))
    mine = jnp.where(core == 0, down_sum[0], down_sum[1])
    other = to_partner(jnp.where(core == 0, down_sum[1], down_sum[0]))
    down_sum = add_low(mine, other, down_keep[7], down_other[7], down_x_two[4])
    down_terms = (down_sum, across(down_sum))
    late_sum = later_hop(late_sum, 5, late_keep, late_other)
    early_sum = settle(early_sum, core, early_keep, early_other)
    early_terms = (early_sum, across(early_sum))
    late_sum = settle(late_sum, core, late_keep, late_other)
    late_terms = (late_sum, across(late_sum))
    finished = call(
        finish_body,
        [shape((rows, 3 * model), FULL), shape((rows, model), FULL)]
        + [shape((1, item.shape[0]), FULL) for item in vectors],
        [who] + list(early_terms) + list(late_terms),
        [SMEM] + [VMEM] * 4,
        scratch=[pltpu.VMEM((SMALL_ROWS, model), FULL)],
        vmem=6,
    )
    grad_qkv, grad_out = finished[:2]
    pieces = [item.reshape(-1) for item in finished[2:]]
    return (
        out_tokens.reshape(tokens.shape),
        grad_tokens.reshape(tokens.shape),
        pieces[0],
        pieces[1],
        grad_qkv,
        pieces[2],
        grad_out,
        pieces[3],
        pieces[4],
        pieces[5],
        in_terms[0].astype(FULL) + in_terms[1].astype(FULL),
        pieces[6],
        jnp.concatenate(
            [
                jnp.where(species == 0, down_terms[0], down_terms[1]),
                jnp.where(species == 0, down_terms[1], down_terms[0]),
            ]
        ).astype(FULL),
        pieces[7],
    )


def on_device(
    tokens,
    lengths,
    cotangent,
    first_gain,
    first_shift,
    qkv_weight,
    qv_bias,
    out_weight,
    out_bias,
    second_gain,
    second_shift,
    in_weight,
    in_bias,
    down_weight,
    down_bias,
):
    local_count = jnp.sum(lengths).astype(jnp.float32)
    count = lax.psum(local_count, ("species", "cells"))
    micro_count = tokens.shape[1]
    seq_rows = tokens.shape[2]
    factor = (
        float(lax.axis_size("species") * lax.axis_size("cells") * micro_count * seq_rows) / count
    )
    output_rows = []
    gradient_rows = []
    summed = None
    for micro_step in range(micro_count):
        gathered = (
            lax.all_gather(first_gain, "cells", axis=0, tiled=True),
            lax.all_gather(first_shift, "cells", axis=0, tiled=True),
            lax.all_gather(qkv_weight, "cells", axis=0, tiled=True),
            lax.all_gather(qv_bias, "cells", axis=0, tiled=True),
            lax.all_gather(out_weight, "cells", axis=0, tiled=True),
            lax.all_gather(out_bias, "cells", axis=0, tiled=True),
            lax.all_gather(second_gain, "cells", axis=0, tiled=True),
            lax.all_gather(second_shift, "cells", axis=0, tiled=True),
            lax.all_gather(in_weight, "cells", axis=0, tiled=True),
            lax.all_gather(in_bias, "cells", axis=0, tiled=True),
            lax.all_gather(down_weight, "cells", axis=0, tiled=True),
            lax.all_gather(down_bias, "cells", axis=0, tiled=True),
        )
        out_seq, grad_seq, grads = sequence_pass(
            gathered,
            tokens[0, micro_step],
            lengths[0, micro_step],
            cotangent[0, micro_step],
            factor,
        )
        output_rows.append(out_seq)
        gradient_rows.append(grad_seq)
        shares = (
            lax.psum_scatter(grads[0], "cells", scatter_dimension=0, tiled=True),
            lax.psum_scatter(grads[1], "cells", scatter_dimension=0, tiled=True),
            lax.psum_scatter(grads[2], "cells", scatter_dimension=0, tiled=True),
            lax.psum_scatter(grads[3], "cells", scatter_dimension=0, tiled=True),
            lax.psum_scatter(grads[4], "cells", scatter_dimension=0, tiled=True),
            lax.psum_scatter(grads[5], "cells", scatter_dimension=0, tiled=True),
            lax.psum_scatter(grads[6], "cells", scatter_dimension=0, tiled=True),
            lax.psum_scatter(grads[7], "cells", scatter_dimension=0, tiled=True),
            lax.psum_scatter(grads[8], "cells", scatter_dimension=0, tiled=True),
            lax.psum_scatter(grads[9], "cells", scatter_dimension=0, tiled=True),
            lax.psum_scatter(grads[10], "cells", scatter_dimension=0, tiled=True),
            lax.psum_scatter(grads[11], "cells", scatter_dimension=0, tiled=True),
        )
        summed = shares if summed is None else jax.tree.map(jnp.add, summed, shares)
    final = (
        lax.psum(summed[0].astype(jnp.bfloat16), "species").astype(jnp.float32),
        lax.psum(summed[1].astype(jnp.bfloat16), "species").astype(jnp.float32),
        lax.psum(summed[2].astype(jnp.bfloat16), "species").astype(jnp.float32),
        lax.psum(summed[3].astype(jnp.bfloat16), "species").astype(jnp.float32),
        lax.psum(summed[4].astype(jnp.bfloat16), "species").astype(jnp.float32),
        lax.psum(summed[5].astype(jnp.bfloat16), "species").astype(jnp.float32),
        lax.psum(summed[6].astype(jnp.bfloat16), "species").astype(jnp.float32),
        lax.psum(summed[7].astype(jnp.bfloat16), "species").astype(jnp.float32),
        lax.psum(summed[8].astype(jnp.bfloat16), "species").astype(jnp.float32),
        lax.psum(summed[9].astype(jnp.bfloat16), "species").astype(jnp.float32),
        lax.psum(summed[10].astype(jnp.bfloat16), "species").astype(jnp.float32),
        lax.psum(summed[11].astype(jnp.bfloat16), "species").astype(jnp.float32),
    )
    out_tokens = jnp.stack(output_rows)[None]
    grad_tokens = jnp.stack(gradient_rows)[None]
    return (out_tokens, grad_tokens) + tuple(final)


def solution(mesh):
    in_specs = (
        P("species", "cells", None, None),
        P("species", "cells"),
        P("species", "cells", None, None),
        P("cells"),
        P("cells"),
        P("cells", None),
        P("cells"),
        P("cells", None),
        P("cells"),
        P("cells"),
        P("cells"),
        P("cells", None),
        P("cells"),
        P("cells", None),
        P("cells"),
    )
    out_specs = (
        P("species", "cells", None, None),
        P("species", "cells", None, None),
        P("cells"),
        P("cells"),
        P("cells", None),
        P("cells"),
        P("cells", None),
        P("cells"),
        P("cells"),
        P("cells"),
        P("cells", None),
        P("cells"),
        P("cells", None),
        P("cells"),
    )
    program = on_device_ring if mesh.shape["cells"] == 2 * RING_SIZE else on_device
    return jax.shard_map(
        program, mesh=mesh, in_specs=in_specs, out_specs=out_specs, check_vma=False
    )
```

```python
import jax
import jax.numpy as jnp
from jax import lax
from jax.experimental import pallas as pl
from jax.experimental.pallas import tpu as pltpu
from jax.sharding import PartitionSpec as P

HEAD = 64


EPSILON = 1e-12
NEGATIVE = -1e30


def normalize(values, gain_vec, shift_vec):
    center = values - jnp.mean(values, axis=-1, keepdims=True)
    spread = jnp.mean(center * center, axis=-1, keepdims=True)
    return center * lax.rsqrt(spread + EPSILON) * gain_vec + shift_vec


def smooth_gate(values):
    return jax.nn.gelu(values, approximate=False)


def times_left(left_side, right_side):
    return lax.dot_general(
        left_side, right_side, (((0,), (0,)), ((), ())), preferred_element_type=jnp.float32
    )


def times_right(left_side, right_side):
    return lax.dot_general(
        left_side, right_side, (((1,), (1,)), ((), ())), preferred_element_type=jnp.float32
    )


def sequence_pass(weights, inputs, length, cot_rows, factor):
    (
        first_gain,
        first_shift,
        qkv_weight,
        qv_bias,
        out_weight,
        out_bias,
        second_gain,
        second_shift,
        in_weight,
        in_bias,
        down_weight,
        down_bias,
    ) = weights
    seq_rows = inputs.shape[0]
    model_width = inputs.shape[1]
    heads_count = model_width // HEAD
    scale_qk = float(HEAD) ** (-0.5)
    as_float = inputs.astype(jnp.float32)
    hidden_one, first_pull = jax.vjp(
        normalize, as_float, first_gain.astype(jnp.float32), first_shift.astype(jnp.float32)
    )
    first_low = hidden_one.astype(jnp.bfloat16)
    bias_float = qv_bias.astype(jnp.float32)
    full_bias = jnp.concatenate(
        [bias_float[:model_width], jnp.zeros((model_width,), jnp.float32), bias_float[model_width:]]
    )
    projected = (
        jnp.dot(first_low, qkv_weight, preferred_element_type=jnp.float32) + full_bias
    ).astype(jnp.bfloat16)
    split_heads = projected.reshape(seq_rows, 3, heads_count, HEAD)
    queries = split_heads[:, 0]
    keys_part = split_heads[:, 1]
    values_part = split_heads[:, 2]
    visible = jnp.arange(seq_rows) < length

    def scores_of():
        raw_scores = (
            jnp.einsum("qhd,khd->hqk", queries, keys_part, preferred_element_type=jnp.float32)
            * scale_qk
        )
        return jnp.where(visible[None, None, :], raw_scores, NEGATIVE)

    scores = scores_of()
    top_score = jnp.max(scores, axis=-1, keepdims=True)
    expo = jnp.exp(scores - top_score)
    total_exp = jnp.sum(expo, axis=-1, keepdims=True)
    log_total = top_score + jnp.log(total_exp)
    attention = (expo / total_exp).astype(jnp.bfloat16)
    mixed = jnp.einsum("hqk,khd->qhd", attention, values_part, preferred_element_type=jnp.float32)
    mixed = mixed.reshape(seq_rows, model_width).astype(jnp.bfloat16)
    middle = (
        as_float
        + jnp.dot(mixed, out_weight, preferred_element_type=jnp.float32)
        + out_bias.astype(jnp.float32)
    )
    hidden_two, second_pull = jax.vjp(
        normalize, middle, second_gain.astype(jnp.float32), second_shift.astype(jnp.float32)
    )
    second_low = hidden_two.astype(jnp.bfloat16)
    inner = jnp.dot(second_low, in_weight, preferred_element_type=jnp.float32) + in_bias.astype(
        jnp.float32
    )
    active, gate_pull = jax.vjp(smooth_gate, inner)
    active_low = active.astype(jnp.bfloat16)
    output = (
        middle
        + jnp.dot(active_low, down_weight, preferred_element_type=jnp.float32)
        + down_bias.astype(jnp.float32)
    )
    upstream = cot_rows.astype(jnp.float32) * visible[:, None].astype(jnp.float32) * factor
    up_low = upstream.astype(jnp.bfloat16)
    grad_down_bias = jnp.sum(up_low.astype(jnp.float32), axis=0)
    grad_down = times_left(active_low, up_low)
    grad_active = times_right(up_low, down_weight)
    (grad_inner,) = gate_pull(grad_active)
    inner_low = grad_inner.astype(jnp.bfloat16)
    grad_in_bias = jnp.sum(inner_low.astype(jnp.float32), axis=0)
    grad_in = times_left(second_low, inner_low)
    grad_second = times_right(inner_low, in_weight)
    grad_middle_norm, grad_second_gain, grad_second_shift = second_pull(grad_second)
    grad_middle = upstream + grad_middle_norm
    middle_low = grad_middle.astype(jnp.bfloat16)
    grad_out_bias = jnp.sum(middle_low.astype(jnp.float32), axis=0)
    grad_out = times_left(mixed, middle_low)
    grad_mixed = (
        times_right(middle_low, out_weight)
        .astype(jnp.bfloat16)
        .reshape(seq_rows, heads_count, HEAD)
    )
    probs_again = jnp.exp(scores_of() - log_total)
    grad_probs = jnp.einsum(
        "qhd,khd->hqk", grad_mixed, values_part, preferred_element_type=jnp.float32
    )
    grad_values = jnp.einsum(
        "hqk,qhd->khd", attention, grad_mixed, preferred_element_type=jnp.float32
    )
    delta = jnp.sum(probs_again * grad_probs, axis=-1, keepdims=True)
    grad_scores = (probs_again * (grad_probs - delta)).astype(jnp.bfloat16)
    grad_queries = (
        jnp.einsum("hqk,khd->qhd", grad_scores, keys_part, preferred_element_type=jnp.float32)
        * scale_qk
    )
    grad_keys = (
        jnp.einsum("hqk,qhd->khd", grad_scores, queries, preferred_element_type=jnp.float32)
        * scale_qk
    )
    grad_projected = jnp.stack([grad_queries, grad_keys, grad_values], axis=1)
    grad_projected = grad_projected.reshape(seq_rows, 3 * model_width).astype(jnp.bfloat16)
    column_sums = jnp.sum(grad_projected.astype(jnp.float32), axis=0)
    grad_qv = jnp.concatenate([column_sums[:model_width], column_sums[2 * model_width :]])
    grad_qkv = times_left(first_low, grad_projected)
    grad_first = times_right(grad_projected, qkv_weight)
    grad_input_norm, grad_first_gain, grad_first_shift = first_pull(grad_first)
    grad_inputs = grad_middle + grad_input_norm
    grads = (
        grad_first_gain,
        grad_first_shift,
        grad_qkv,
        grad_qv,
        grad_out,
        grad_out_bias,
        grad_second_gain,
        grad_second_shift,
        grad_in,
        grad_in_bias,
        grad_down,
        grad_down_bias,
    )
    return (output.astype(jnp.bfloat16), grad_inputs.astype(jnp.bfloat16), grads)


RING = (0, 2, 4, 6, 7, 5, 3, 1)
RING_SIZE = len(RING)
CELLS = 2 * RING_SIZE
ANY = pl.BlockSpec(memory_space=pl.ANY)
HBM = pl.BlockSpec(memory_space=pltpu.HBM)
VMEM = pl.BlockSpec(memory_space=pltpu.VMEM)
SMEM = pl.BlockSpec(memory_space=pltpu.SMEM)
LOW = jnp.bfloat16
FULL = jnp.float32
HEAVY = 10**10
UNIT = 10**8
ROWS = {
    "first_gain": 0,
    "first_shift": 1,
    "qv_bias": 2,
    "out_bias": 4,
    "second_gain": 5,
    "second_shift": 6,
    "in_bias": 7,
    "down_bias": 11,
    "lengths": 12,
}
NAMES = tuple(ROWS)[:8]
SMALL_ROWS = 16
SMALL_LANES = 256
PIECES = (2, 2, 2, 2, 2, 2, 2, 1, 1)


def ring_pairs():
    pairs = []
    for place in range(RING_SIZE):
        chip = RING[place]
        right = RING[(place + 1) % RING_SIZE]
        left = RING[(place - 1) % RING_SIZE]
        pairs.append((2 * chip, 2 * right))
        pairs.append((2 * chip + 1, 2 * left + 1))
    return pairs


def hop(block):
    return lax.ppermute(block, "cells", ring_pairs())


def to_partner(block):
    return lax.ppermute(block, "cells", [(i, i ^ 1) for i in range(CELLS)])


def across(block):
    return lax.ppermute(block, "species", [(0, 1), (1, 0)])


def exchange(values, bit):
    return values + lax.ppermute(values, "cells", [(i, i ^ bit) for i in range(CELLS)])


def after(value, *others):
    return lax.optimization_barrier((value,) + others)[0]


def here():
    index = lax.axis_index("cells")
    core = index % 2
    chip = index // 2
    place = jnp.int32(0)
    for i, ring_chip in enumerate(RING):
        place = jnp.where(chip == ring_chip, i, place)
    return index, core, place


def chip_at(place):
    place = place % RING_SIZE
    chip = jnp.zeros_like(place)
    for i, ring_chip in enumerate(RING):
        chip = jnp.where(place == i, ring_chip, chip)
    return chip


def gather_order(core, place):
    sign = 1 - 2 * core
    order = []

    def pair(at):
        order.append(2 * chip_at(at))
        order.append(2 * chip_at(at) + 1)

    pair(place)
    for step in range(1, 4):
        pair(place - sign * step)
        pair(place + sign * step)
    order.append(2 * chip_at(place + 4) + core)
    order.append(2 * chip_at(place + 4) + 1 - core)
    return order


def scatter_slots(core, place):
    def kept(core_now):
        sign = 1 - 2 * core_now
        order = [2 * chip_at(place + 4) + core_now]
        for step in (3, 2, 1):
            order.append(2 * chip_at(place + sign * step))
            order.append(2 * chip_at(place + sign * step) + 1)
        order.append(2 * chip_at(place) + core_now)
        return order

    order = kept(core) + kept(1 - core)
    slots = []
    for device in range(CELLS):
        slot = jnp.int32(0)
        for i, who in enumerate(order):
            slot = jnp.where(who == device, i, slot)
        slots.append(slot)
    return slots


def both_blocks(block, core):
    other = to_partner(block)
    return jnp.stack([jnp.where(core == 0, block, other), jnp.where(core == 0, other, block)])


def half_of(pair, core):
    return jnp.where(core == 0, pair[0], pair[1])[None]


def add_low(*parts):
    total = parts[0].astype(FULL)
    for part in parts[1:]:
        total = total + part.astype(FULL)
    return total.astype(LOW)


def first_hop(*parts):
    return hop(add_low(*[part[0:1] for part in parts]))


def second_hop(moving, core, *parts):
    wide = jnp.stack([jnp.where(core == 0, moving[0], 0), jnp.where(core == 0, 0, moving[0])])
    return hop(add_low(wide, *[part[1:3] for part in parts]))


def later_hop(moving, at, *parts):
    return hop(add_low(moving, *[part[at : at + 2] for part in parts]))


def settle(moving, core, *parts):
    mine = jnp.where(core == 0, moving[0], moving[1])
    other = jnp.where(core == 0, moving[1], moving[0])
    return add_low(mine, to_partner(other), *[part[7] for part in parts])


def dot(left, right, dims=((1,), (0,))):
    return lax.dot_general(left, right, (dims, ((), ())), preferred_element_type=FULL)


def call(body, out_shape, ins, specs, out_specs=None, scratch=(), vmem=48, cost=HEAVY):
    return pl.pallas_call(
        body,
        out_shape=out_shape,
        in_specs=specs,
        out_specs=[VMEM] * len(out_shape) if out_specs is None else out_specs,
        scratch_shapes=list(scratch),
        compiler_params=pltpu.CompilerParams(vmem_limit_bytes=vmem * 2**20),
        cost_estimate=pl.CostEstimate(flops=cost, bytes_accessed=0, transcendentals=0),
    )(*ins)


def shape(dims, kind=LOW):
    return jax.ShapeDtypeStruct(dims, kind)


def fetch(order_ref, refs, target, sem):
    rows = target.shape[0] // CELLS
    copies = []
    index = 0
    for source, size in zip(refs, PIECES):
        for part in range(size):
            at = order_ref[index]
            copies.append(
                pltpu.make_async_copy(
                    source.at[part],
                    target.at[pl.ds(pl.multiple_of(at * rows, 16), rows)],
                    sem.at[index],
                )
            )
            index += 1
    for item in copies:
        item.start()
    return copies


def wait_all(copies):
    for item in copies:
        item.wait()


def one_hot(rows, lanes, offset):
    row = lax.broadcasted_iota(jnp.int32, (rows, lanes), 0)
    lane = lax.broadcasted_iota(jnp.int32, (rows, lanes), 1)
    return lane == row + offset


def pack_body(who_ref, lengths_ref, *refs):
    sources, small_ref = refs[:8], refs[8]
    me = who_ref[0]
    model = small_ref.shape[1]
    row = lax.broadcasted_iota(jnp.int32, (SMALL_ROWS, model), 0)
    lane = lax.broadcasted_iota(jnp.int32, (SMALL_ROWS, model), 1)
    small = jnp.zeros((SMALL_ROWS, model), FULL)
    for name, ref in zip(NAMES, sources):
        size = ref.shape[1]
        per_row = model // size
        placed = dot(ref[...], one_hot(size, model, size * (me % per_row)).astype(LOW))
        small = small + jnp.where(row == ROWS[name] + me // per_row, placed, 0.0)
    for i in range(2):
        at = (row == ROWS["lengths"]) & (lane == 2 * me + i)
        small = small + jnp.where(at, lengths_ref[i].astype(FULL), 0.0)
    small_ref[...] = small.astype(LOW)


def norm_parts(values):
    center = values - jnp.mean(values, axis=-1, keepdims=True)
    spread = jnp.mean(center * center, axis=-1, keepdims=True)
    return center, lax.rsqrt(spread + EPSILON)


def norm_back(center, scale, gain, grad):
    weighted = grad * gain
    mean_one = jnp.mean(weighted, axis=-1, keepdims=True)
    mean_two = jnp.mean(weighted * center, axis=-1, keepdims=True)
    back = scale * (weighted - mean_one - center * (scale * scale * mean_two))
    return back, jnp.sum(grad * center * scale, axis=0, keepdims=True), jnp.sum(
        grad, axis=0, keepdims=True
    )


def small_row(small_ref, name, count=1):
    return small_ref[...].astype(FULL)[ROWS[name] : ROWS[name] + count, :]


def project_body(order_ref, x_ref, small_ref, *refs):
    blocks = refs[:9]
    low_ref, proj_ref, weight, sem = refs[9:]
    model = x_ref.shape[1]
    copies = fetch(order_ref, blocks, weight, sem)
    center, scale = norm_parts(x_ref[...].astype(FULL))
    bias = small_row(small_ref, "qv_bias", 2)
    low_ref[...] = (
        center * scale * small_row(small_ref, "first_gain") + small_row(small_ref, "first_shift")
    ).astype(LOW)
    wait_all(copies)
    for j in range(3):
        lanes = slice(j * model, (j + 1) * model)
        part = dot(low_ref[...], weight[:, lanes])
        if j != 1:
            part = part + bias[j // 2 : j // 2 + 1]
        proj_ref[:, lanes] = part.astype(LOW)


def attend_body(seq, lengths_ref, proj_ref, att_ref, mixed_ref):
    model = mixed_ref.shape[1]
    cells = mixed_ref.shape[0] // seq
    pairs = model // (2 * HEAD)
    lane = lax.broadcasted_iota(jnp.int32, (seq, 2 * HEAD), 1)
    key = lax.broadcasted_iota(jnp.int32, (seq, seq), 0)

    def step(index, carry):
        s = index // pairs
        p = index % pairs
        rows = pl.ds(pl.multiple_of(s * seq, seq), seq)
        at = pl.multiple_of(p * 2 * HEAD, 2 * HEAD)
        q = proj_ref[rows, pl.ds(at, 2 * HEAD)] * jnp.asarray(HEAD ** (-0.5), LOW)
        k = proj_ref[rows, pl.ds(at + model, 2 * HEAD)]
        v_turned = proj_ref[rows, pl.ds(at + 2 * model, 2 * HEAD)].T
        visible = key < lengths_ref[s]
        mixed = []
        for i in range(2):
            own = (lane >= i * HEAD) & (lane < (i + 1) * HEAD)
            scores = dot(jnp.where(own, k, jnp.zeros_like(k)), q, ((1,), (1,)))
            scores = jnp.where(visible, scores, NEGATIVE)
            expo = jnp.exp(scores - jnp.max(scores, axis=0, keepdims=True))
            probs = expo * (1.0 / jnp.sum(expo, axis=0, keepdims=True))
            probs = probs.astype(LOW)
            att_ref[2 * index + i] = probs
            mixed.append(dot(v_turned[i * HEAD : (i + 1) * HEAD], probs))
        mixed_ref[rows, pl.ds(at, 2 * HEAD)] = jnp.concatenate(mixed, axis=0).T.astype(LOW)
        return carry

    lax.fori_loop(0, cells * pairs, step, 0, unroll=2)


ERFC_STEP = 0.33
ERFC = (
    0.1863578228018033,
    0.18295566386742124,
    0.2012255082472392,
    0.04721561458875723,
    0.4085089979423051,
    -0.35115900736338407,
    0.4602422572120205,
    -0.13534686486277223,
)


def gelu_parts(inner):
    z = jnp.abs(inner) * (0.5**0.5)
    t = 1.0 / (1.0 + ERFC_STEP * z)
    tail = jnp.full_like(t, 0.5 * ERFC[-1])
    for factor in ERFC[-2::-1]:
        tail = tail * t + 0.5 * factor
    bell = jnp.exp(-(z * z))
    tail = tail * t * bell
    area = jnp.where(inner < 0.0, tail, 1.0 - tail)
    return inner * area, area + inner * bell * (0.5 / 3.141592653589793) ** 0.5


def row_mask(lengths_ref, rows, seq):
    at = lax.broadcasted_iota(jnp.int32, (rows, 1), 0)
    true = (at < lengths_ref[0]).astype(FULL)
    for s in range(1, rows // seq):
        true = jnp.where(at < s * seq, true, (at < lengths_ref[s] + s * seq).astype(FULL))
    return true


def loss_rows(lengths_ref, small_ref, other_ref, cot_ref, seq, whole):
    count = jnp.sum(
        small_row(small_ref, "lengths") + small_row(other_ref, "lengths"), axis=-1, keepdims=True
    )
    return cot_ref[...].astype(FULL) * (
        row_mask(lengths_ref, cot_ref.shape[0], seq) * (whole / count)
    )


def put_slots(keep_buf, slot_ref, values, first, lanes):
    rows = keep_buf.shape[1]
    for i in range(values.shape[0] // rows):
        keep_buf[slot_ref[first + i], :, lanes] = values[i * rows : (i + 1) * rows].astype(LOW)


def send_slots(buf, keep_ref, away_ref, sem):
    half = RING_SIZE
    copies = [
        pltpu.make_async_copy(buf.at[pl.ds(half, half)], away_ref, sem.at[0]),
        pltpu.make_async_copy(buf.at[pl.ds(0, half)], keep_ref, sem.at[1]),
    ]
    for item in copies:
        item.start()
    return copies


def inner_body(order_ref, x_ref, mixed_ref, small_ref, *refs):
    blocks = refs[:9]
    middle_ref, low_ref, active_ref, slope_ref, weight, sem = refs[9:]
    model = x_ref.shape[1]
    ff = active_ref.shape[1]
    wait_all(fetch(order_ref, blocks, weight, sem))
    middle = (
        x_ref[...].astype(FULL)
        + dot(mixed_ref[...], weight[:, ff:])
        + small_row(small_ref, "out_bias")
    )
    middle_ref[...] = middle
    center, scale = norm_parts(middle)
    low = center * scale * small_row(small_ref, "second_gain") + small_row(
        small_ref, "second_shift"
    )
    low_ref[...] = low.astype(LOW)
    step = 2 * (ff // RING_SIZE)
    bias = small_row(small_ref, "in_bias", 4)
    for j in range(ff // step):
        lanes = slice(j * step, (j + 1) * step)
        inner = dot(low_ref[...], weight[:, lanes]) + bias[j : j + 1]
        active, slope = gelu_parts(inner)
        active_ref[:, lanes] = active.astype(LOW)
        slope_ref[:, lanes] = slope.astype(LOW)


def grad_down_body(
    seq, whole, who_ref, slot_ref, lengths_ref, active_ref, cot_ref, small_ref, other_ref,
    up_ref, down_b_ref, keep_ref, away_ref, keep_two_ref, away_two_ref, slots, sem,
):
    up_low = loss_rows(lengths_ref, small_ref, other_ref, cot_ref, seq, whole).astype(LOW)
    up_ref[...] = up_low
    down_b_ref[...] = jnp.sum(up_low.astype(FULL), axis=0, keepdims=True)
    parts = RING_SIZE
    step = active_ref.shape[1] // parts
    rows = slots.shape[2]
    side = who_ref[1]
    for j in range(parts):
        grad = dot(active_ref[:, j * step : (j + 1) * step], up_ref[...], ((0,), (0,)))
        for i in range(4):
            slots[(i + side) % 2, slot_ref[j * CELLS // parts + i // 2]] = grad[
                i * rows : (i + 1) * rows
            ].astype(LOW)
    copies = send_slots(slots.at[1], keep_two_ref, away_two_ref, sem.at[1])
    copies += send_slots(slots.at[0], keep_ref, away_ref, sem.at[0])
    wait_all(copies)


def inner_back_body(order_ref, slope_ref, up_ref, *refs):
    blocks = refs[:9]
    inner_ref, in_b_ref, weight, sem = refs[9:]
    model = up_ref.shape[1]
    wait_all(fetch(order_ref, blocks, weight, sem))
    for j in range(inner_ref.shape[1] // model):
        lanes = slice(j * model, (j + 1) * model)
        grad = dot(up_ref[...], weight[lanes, :], ((1,), (1,)))
        low = (grad * slope_ref[:, lanes].astype(FULL)).astype(LOW)
        inner_ref[:, lanes] = low
        in_b_ref[j : j + 1, :] = jnp.sum(low.astype(FULL), axis=0, keepdims=True)


def down_body(active_ref, middle_ref, small_ref, weight_ref, out_ref):
    out_ref[...] = (
        middle_ref[...]
        + dot(active_ref[...], weight_ref[...])
        + small_row(small_ref, "down_bias")
    ).astype(LOW)


def grad_in_body(slot_ref, low_ref, inner_ref, keep_ref, away_ref, slots, sem):
    model = low_ref.shape[1]
    turned = low_ref[...].T
    for j in range(inner_ref.shape[1] // model):
        lanes = slice(j * model, (j + 1) * model)
        put_slots(slots, slot_ref, dot(turned, inner_ref[:, lanes]), 0, lanes)
    wait_all(send_slots(slots, keep_ref, away_ref, sem))


def middle_back_body(
    seq, whole, lengths_ref, inner_ref, middle_ref, cot_ref, small_ref, other_ref, weight,
    grad_ref, grad_low_ref, grad_mixed_ref, sums_ref,
):
    ff = inner_ref.shape[1]
    grad_second = dot(inner_ref[...], weight[:, :ff], ((1,), (1,)))
    center, scale = norm_parts(middle_ref[...])
    back, gain_sum, shift_sum = norm_back(
        center, scale, small_row(small_ref, "second_gain"), grad_second
    )
    grad = loss_rows(lengths_ref, small_ref, other_ref, cot_ref, seq, whole) + back
    grad_ref[...] = grad
    grad_low = grad.astype(LOW)
    grad_low_ref[...] = grad_low
    grad_mixed_ref[...] = dot(grad_low, weight[:, ff:], ((1,), (1,))).astype(LOW)
    sums_ref[0:1, :] = jnp.sum(grad_low.astype(FULL), axis=0, keepdims=True)
    sums_ref[1:2, :] = gain_sum
    sums_ref[2:3, :] = shift_sum


def attend_back_body(seq, begin, proj_ref, att_ref, grad_ref, out_ref):
    model = grad_ref.shape[1]
    half = out_ref.shape[1] // 3
    all_pairs = model // (2 * HEAD)
    pairs = half // (2 * HEAD)
    cells = grad_ref.shape[0] // seq
    lane = lax.broadcasted_iota(jnp.int32, (seq, 2 * HEAD), 1)
    scale = HEAD ** (-0.5)

    def step(index, carry):
        s = index // pairs
        p = index % pairs
        rows = pl.ds(pl.multiple_of(s * seq, seq), seq)
        to = pl.multiple_of(p * 2 * HEAD, 2 * HEAD)
        at = pl.multiple_of(to + begin * 2 * HEAD, 2 * HEAD)
        q = proj_ref[rows, pl.ds(at, 2 * HEAD)]
        k_turned = proj_ref[rows, pl.ds(at + model, 2 * HEAD)].T
        v = proj_ref[rows, pl.ds(at + 2 * model, 2 * HEAD)]
        g = grad_ref[rows, pl.ds(at, 2 * HEAD)]
        grad_q = []
        grad_k = []
        grad_v = []
        for i in range(2):
            own = (lane >= i * HEAD) & (lane < (i + 1) * HEAD)
            probs = att_ref[2 * (s * all_pairs + begin + p) + i]
            wide = probs.astype(FULL)
            grad_probs = dot(jnp.where(own, v, jnp.zeros_like(v)), g, ((1,), (1,)))
            delta = jnp.sum(wide * grad_probs, axis=0, keepdims=True)
            scores = (wide * (grad_probs - delta)).astype(LOW)
            grad_q.append(dot(k_turned[i * HEAD : (i + 1) * HEAD], scores))
            grad_k.append(dot(scores, q))
            grad_v.append(dot(probs, g))
        first = lane < HEAD
        out_ref[rows, pl.ds(to, 2 * HEAD)] = (
            jnp.concatenate(grad_q, axis=0).T * scale
        ).astype(LOW)
        out_ref[rows, pl.ds(to + half, 2 * HEAD)] = (
            jnp.where(first, grad_k[0], grad_k[1]) * scale
        ).astype(LOW)
        out_ref[rows, pl.ds(to + 2 * half, 2 * HEAD)] = jnp.where(
            first, grad_v[0], grad_v[1]
        ).astype(LOW)
        return carry

    lax.fori_loop(0, cells * pairs, step, 0, unroll=2)


def early_grad_body(
    slot_ref, low_ref, part_ref, mixed_ref, grad_low_ref, keep_ref, away_ref, slots, sem
):
    width = part_ref.shape[1]
    put_slots(slots, slot_ref, dot(low_ref[...].T, part_ref[...]), 0, slice(0, width))
    put_slots(
        slots, slot_ref, dot(mixed_ref[...].T, grad_low_ref[...]), 0,
        slice(width, slots.shape[2]),
    )
    wait_all(send_slots(slots, keep_ref, away_ref, sem))


def first_back_body(
    slot_ref, x_ref, low_ref, one_ref, two_ref, grad_ref, small_ref, sums_ref, in_b_ref,
    down_b_ref, weight, out_ref, keep_ref, away_ref, sum_ref, slots, sem,
):
    model = x_ref.shape[1]
    late = two_ref.shape[1]
    center, scale = norm_parts(x_ref[...].astype(FULL))
    parts = ((one_ref, 0), (two_ref, one_ref.shape[1] // 3))
    grad_first = jnp.zeros(x_ref.shape, FULL)
    for j in range(3):
        for ref, begin in parts:
            width = ref.shape[1] // 3
            at = j * model + begin
            grad_first = grad_first + dot(
                ref[:, j * width : (j + 1) * width], weight[:, at : at + width], ((1,), (1,))
            )
    put_slots(slots, slot_ref, dot(low_ref[...].T, two_ref[...]), 0, slice(0, late))
    back, gain_sum, shift_sum = norm_back(
        center, scale, small_row(small_ref, "first_gain"), grad_first
    )

    def put(name, value, offset=0):
        at = ROWS[name] + offset
        sum_ref[at : at + value.shape[0], :] = value

    sum_ref[...] = jnp.zeros_like(sum_ref)
    put("first_gain", gain_sum)
    put("first_shift", shift_sum)
    for j in range(2):
        at = ROWS["qv_bias"] + j
        for ref, begin in parts:
            width = ref.shape[1] // 3
            part = ref[:, 2 * j * width : (2 * j + 1) * width].astype(FULL)
            sum_ref[at : at + 1, begin : begin + width] = jnp.sum(part, axis=0, keepdims=True)
    put("out_bias", sums_ref[0:1, :])
    put("second_gain", sums_ref[1:2, :])
    put("second_shift", sums_ref[2:3, :])
    put("in_bias", in_b_ref[...])
    put("down_bias", down_b_ref[...])
    for i in range(3):
        part = sum_ref[:, SMALL_LANES * i : SMALL_LANES * (i + 1)].astype(LOW)
        for device in range(CELLS):
            slots[device, 16 * i : 16 * i + 16, late:] = part
    copies = send_slots(slots, keep_ref, away_ref, sem)
    out_ref[...] = (grad_ref[...] + back).astype(LOW)
    wait_all(copies)


def finish_body(who_ref, early_ref, early_two_ref, late_ref, late_two_ref, *refs):
    grad_ref, out_ref, vectors, small_ref = refs[0], refs[1], refs[2:-1], refs[-1]
    model = out_ref.shape[1]
    early = early_ref[...].astype(FULL) + early_two_ref[...].astype(FULL)
    late = late_ref[...].astype(FULL) + late_two_ref[...].astype(FULL)
    one = (early.shape[1] - model) // 3
    two = (late.shape[1] - SMALL_LANES) // 3
    for j in range(3):
        at = j * model
        grad_ref[:, at : at + one] = early[:, j * one : (j + 1) * one]
        grad_ref[:, at + one : at + model] = late[:, j * two : (j + 1) * two]
    out_ref[...] = early[:, 3 * one :]
    for i in range(3):
        small_ref[:, SMALL_LANES * i : SMALL_LANES * (i + 1)] = late[
            16 * i : 16 * i + 16, 3 * two :
        ]
    me = who_ref[0]
    row = lax.broadcasted_iota(jnp.int32, (SMALL_ROWS, model), 0)
    for name, ref in zip(NAMES, vectors):
        size = ref.shape[1]
        per_row = model // size
        here_row = jnp.where(row == ROWS[name] + me // per_row, small_ref[...], 0.0)
        values = jnp.sum(here_row, axis=0, keepdims=True)
        picker = one_hot(size, model, size * (me % per_row)).astype(FULL)
        ref[...] = lax.dot_general(
            values, picker, (((1,), (1,)), ((), ())), precision=lax.Precision.HIGHEST,
            preferred_element_type=FULL,
        )


def on_device_ring(
    tokens,
    lengths,
    cotangent,
    first_gain,
    first_shift,
    qkv_weight,
    qv_bias,
    out_weight,
    out_bias,
    second_gain,
    second_shift,
    in_weight,
    in_bias,
    down_weight,
    down_bias,
):
    micro, seq, model = tokens.shape[1:]
    total_rows = micro * seq
    rows = qkv_weight.shape[0]
    down_rows = down_weight.shape[0]
    ff = in_weight.shape[1]
    heads = model // HEAD
    whole = float(lax.axis_size("species") * CELLS * micro * seq)
    index, core, place = here()
    species = lax.axis_index("species")
    who = jnp.stack([index, species]).astype(jnp.int32)
    order = jnp.stack(gather_order(core, place)).astype(jnp.int32)
    slot = jnp.stack(scatter_slots(core, place)).astype(jnp.int32)
    lens = lengths.reshape(micro)
    x = tokens.reshape(total_rows, model)
    cot = cotangent.reshape(total_rows, model)
    vectors = (
        first_gain, first_shift, qv_bias, out_bias, second_gain, second_shift, in_bias, down_bias,
    )

    dma = pltpu.SemaphoreType.DMA

    def gathered(own, hops):
        got = [own]
        for item in hops:
            got += [item, to_partner(item)]
        return got

    own = both_blocks(qkv_weight, core)
    qkv_one = hop(own)
    (small,) = call(
        pack_body,
        [shape((SMALL_ROWS, model))],
        [who, after(lens, own)] + [item.reshape(1, -1) for item in vectors],
        [SMEM, SMEM] + [VMEM] * 8,
        vmem=4,
    )
    in_weight, out_weight = lax.optimization_barrier((in_weight, out_weight, own))[:2]
    in_own = both_blocks(jnp.concatenate([in_weight, out_weight], axis=1), core)
    in_one = hop(in_own)
    small = exchange(small, 1)
    qkv_one, small = lax.optimization_barrier((qkv_one, small))
    qkv_two = hop(qkv_one)
    in_two = hop(after(in_one, qkv_one))
    small = exchange(small, 2)
    down_own = both_blocks(after(down_weight, qkv_one), core)
    qkv_two, small, down_own = lax.optimization_barrier((qkv_two, small, down_own))
    qkv_three = hop(qkv_two)
    small = exchange(small, 4)
    qkv_three, small = lax.optimization_barrier((qkv_three, small))
    qkv_last = hop(half_of(qkv_three, core))
    in_three = hop(after(in_two, qkv_three))
    small = exchange(small, 8)
    in_three, small = lax.optimization_barrier((in_three, small))
    in_last = hop(half_of(in_three, core))
    down_one = hop(after(down_own, in_three))
    low, proj, qkv_full = call(
        project_body,
        [
            shape((total_rows, model)),
            shape((total_rows, 3 * model)),
            shape((model, 3 * model)),
        ],
        [order, after(x, in_three), small] + gathered(own, (qkv_one, qkv_two, qkv_three, qkv_last)),
        [SMEM, VMEM, VMEM] + [ANY] * 9,
        scratch=[dma((CELLS,))],
        vmem=14,
    )
    other_small = across(small)
    proj, in_last, other_small, down_one = lax.optimization_barrier(
        (proj, in_last, other_small, down_one)
    )
    down_two = hop(down_one)
    att, mixed = call(
        lambda *refs: attend_body(seq, *refs),
        [shape((micro * heads, seq, seq)), shape((total_rows, model))],
        [lens, proj],
        [SMEM, VMEM],
        vmem=12,
    )
    down_two, mixed = lax.optimization_barrier((down_two, mixed))
    down_three = hop(down_two)
    in_got = gathered(in_own, (in_one, in_two, in_three, in_last))
    middle, low_two, active, slope, in_full = call(
        inner_body,
        [
            shape((total_rows, model), FULL),
            shape((total_rows, model)),
            shape((total_rows, ff)),
            shape((total_rows, ff)),
            shape((model, ff + model)),
        ],
        [order, x, mixed, small] + in_got,
        [SMEM] + [VMEM] * 3 + [ANY] * 9,
        scratch=[dma((CELLS,))],
        vmem=17,
    )
    down_three, active = lax.optimization_barrier((down_three, active))
    down_last = hop(half_of(down_three, core))
    up_low, down_b, down_keep, down_away, down_keep_two, down_away_two = call(
        lambda *refs: grad_down_body(seq, whole, *refs),
        [
            shape((total_rows, model)),
            shape((1, model), FULL),
        ]
        + [shape((RING_SIZE, down_rows // 2, model))] * 4,
        [who, slot, lens, active, cot, small, other_small],
        [SMEM] * 3 + [VMEM] * 4,
        [VMEM] * 2 + [ANY] * 4,
        scratch=[pltpu.VMEM((2, CELLS, down_rows // 2, model), LOW), dma((2, 2))],
        vmem=14,
    )

    down_away, down_away_two, down_last = lax.optimization_barrier(
        (down_away, down_away_two, down_last)
    )
    down_other_two = to_partner(down_away_two)
    down_other = to_partner(down_away)
    inner_low, in_b, down_full = call(
        inner_back_body,
        [
            shape((total_rows, ff)),
            shape((ff // model, model), FULL),
            shape((ff, model)),
        ],
        [order, slope, up_low]
        + gathered(down_own, (down_one, down_two, down_three, down_last)),
        [SMEM] + [VMEM] * 2 + [ANY] * 9,
        scratch=[dma((CELLS,))],
        vmem=15,
    )
    down_other_two, inner_low = lax.optimization_barrier((down_other_two, inner_low))
    down_x = across(add_low(down_keep_two[0:3], down_other_two[0:3]))
    down_x_two = across(add_low(down_keep_two[3:8], down_other_two[3:8]))
    in_keep, in_away = call(
        grad_in_body,
        [shape((RING_SIZE, rows, ff)), shape((RING_SIZE, rows, ff))],
        [slot, low_two, inner_low],
        [SMEM] + [VMEM] * 2,
        [ANY] * 2,
        scratch=[pltpu.VMEM((CELLS, rows, ff), LOW), dma((2,))],
        vmem=12,
    )
    in_other = to_partner(in_away)
    (out_tokens,) = call(
        down_body,
        [shape((total_rows, model))],
        [after(active, in_keep), middle, small, down_full],
        [VMEM] * 4,
        vmem=13,
    )
    in_other, out_tokens, inner_low = lax.optimization_barrier((in_other, out_tokens, inner_low))
    in_sum = first_hop(in_keep, in_other)
    grad_middle, grad_low, grad_mixed, sums = call(
        lambda *refs: middle_back_body(seq, whole, *refs),
        [
            shape((total_rows, model), FULL),
            shape((total_rows, model)),
            shape((total_rows, model)),
            shape((3, model), FULL),
        ],
        [lens, inner_low, middle, cot, small, other_small, in_full],
        [SMEM] + [VMEM] * 6,
        vmem=16,
    )

    def attend_back(begin, pairs, grad):
        return call(
            lambda *refs: attend_back_body(seq, begin, *refs),
            [shape((total_rows, 6 * pairs * HEAD))],
            [proj, att, grad],
            [VMEM] * 3,
            vmem=11,

        )[0]

    pairs = model // (2 * HEAD)
    early_pairs = 2 * pairs // 3
    in_sum, down_x, down_other, grad_mixed = lax.optimization_barrier(
        (in_sum, down_x, down_other, grad_mixed)
    )
    down_sum = first_hop(down_keep, down_other, down_x)
    in_sum = second_hop(in_sum, core, in_keep, in_other)
    grad_one = attend_back(0, early_pairs, grad_mixed)
    down_sum, grad_one = lax.optimization_barrier((down_sum, grad_one))
    down_sum = second_hop(down_sum, core, down_keep, down_other, down_x)
    early_width = 6 * early_pairs * HEAD + model
    early_keep, early_away = call(
        early_grad_body,
        [shape((RING_SIZE, rows, early_width))] * 2,
        [slot, low, grad_one, mixed, grad_low],
        [SMEM] + [VMEM] * 4,
        [ANY] * 2,
        scratch=[pltpu.VMEM((CELLS, rows, early_width), LOW), dma((2,))],
        vmem=12,
    )
    early_other = to_partner(early_away)
    in_sum, early_keep, grad_mixed = lax.optimization_barrier((in_sum, early_keep, grad_mixed))
    in_sum = later_hop(in_sum, 3, in_keep, in_other)
    grad_two = attend_back(early_pairs, pairs - early_pairs, grad_mixed)
    early_other, grad_two = lax.optimization_barrier((early_other, grad_two))
    early_sum = first_hop(early_keep, early_other)
    late_width = 6 * (pairs - early_pairs) * HEAD + SMALL_LANES
    grad_tokens, late_keep, late_away = call(
        first_back_body,
        [
            shape((total_rows, model)),
            shape((RING_SIZE, rows, late_width)),
            shape((RING_SIZE, rows, late_width)),
        ],
        [slot, x, low, grad_one, grad_two, grad_middle, small, sums, in_b, down_b, qkv_full],
        [SMEM] + [VMEM] * 10,
        [VMEM] + [ANY] * 2,
        scratch=[
            pltpu.VMEM((SMALL_ROWS, model), FULL),
            pltpu.VMEM((CELLS, rows, late_width), LOW),
            dma((2,)),
        ],
        vmem=14,

    )
    late_other = to_partner(late_away)
    in_sum, early_sum, late_keep, down_sum, down_x_two = lax.optimization_barrier(
        (in_sum, early_sum, late_keep, down_sum, down_x_two)
    )
    in_sum = later_hop(in_sum, 5, in_keep, in_other)
    early_sum = second_hop(early_sum, core, early_keep, early_other)
    down_sum = hop(add_low(down_sum, down_keep[3:5], down_other[3:5], down_x_two[0:2]))
    late_sum = first_hop(late_keep, late_other)
    late_sum, early_sum, down_sum = lax.optimization_barrier((late_sum, early_sum, down_sum))
    down_sum = hop(add_low(down_sum, down_keep[5:7], down_other[5:7], down_x_two[2:4]))
    late_sum = second_hop(late_sum, core, late_keep, late_other)
    early_sum = later_hop(early_sum, 3, early_keep, early_other)
    late_sum, early_sum, down_sum, in_sum = lax.optimization_barrier(
        (late_sum, early_sum, down_sum, in_sum)
    )
    late_sum = later_hop(late_sum, 3, late_keep, late_other)
    early_sum = later_hop(early_sum, 5, early_keep, early_other)
    in_sum = settle(in_sum, core, in_keep, in_other)
    in_terms = (in_sum, across(in_sum))
    late_sum, down_sum = lax.optimization_barrier((late_sum, down_sum))
    mine = jnp.where(core == 0, down_sum[0], down_sum[1])
    other = to_partner(jnp.where(core == 0, down_sum[1], down_sum[0]))
    down_sum = add_low(mine, other, down_keep[7], down_other[7], down_x_two[4])
    down_terms = (down_sum, across(down_sum))
    late_sum = later_hop(late_sum, 5, late_keep, late_other)
    early_sum = settle(early_sum, core, early_keep, early_other)
    early_terms = (early_sum, across(early_sum))
    late_sum = settle(late_sum, core, late_keep, late_other)
    late_terms = (late_sum, across(late_sum))
    finished = call(
        finish_body,
        [shape((rows, 3 * model), FULL), shape((rows, model), FULL)]
        + [shape((1, item.shape[0]), FULL) for item in vectors],
        [who] + list(early_terms) + list(late_terms),
        [SMEM] + [VMEM] * 4,
        scratch=[pltpu.VMEM((SMALL_ROWS, model), FULL)],
        vmem=6,
    )
    grad_qkv, grad_out = finished[:2]
    pieces = [item.reshape(-1) for item in finished[2:]]
    return (
        out_tokens.reshape(tokens.shape),
        grad_tokens.reshape(tokens.shape),
        pieces[0],
        pieces[1],
        grad_qkv,
        pieces[2],
        grad_out,
        pieces[3],
        pieces[4],
        pieces[5],
        in_terms[0].astype(FULL) + in_terms[1].astype(FULL),
        pieces[6],
        jnp.concatenate(
            [
                jnp.where(species == 0, down_terms[0], down_terms[1]),
                jnp.where(species == 0, down_terms[1], down_terms[0]),
            ]
        ).astype(FULL),
        pieces[7],
    )


def on_device(
    tokens,
    lengths,
    cotangent,
    first_gain,
    first_shift,
    qkv_weight,
    qv_bias,
    out_weight,
    out_bias,
    second_gain,
    second_shift,
    in_weight,
    in_bias,
    down_weight,
    down_bias,
):
    local_count = jnp.sum(lengths).astype(jnp.float32)
    count = lax.psum(local_count, ("species", "cells"))
    micro_count = tokens.shape[1]
    seq_rows = tokens.shape[2]
    factor = (
        float(lax.axis_size("species") * lax.axis_size("cells") * micro_count * seq_rows) / count
    )
    output_rows = []
    gradient_rows = []
    summed = None
    for micro_step in range(micro_count):
        gathered = (
            lax.all_gather(first_gain, "cells", axis=0, tiled=True),
            lax.all_gather(first_shift, "cells", axis=0, tiled=True),
            lax.all_gather(qkv_weight, "cells", axis=0, tiled=True),
            lax.all_gather(qv_bias, "cells", axis=0, tiled=True),
            lax.all_gather(out_weight, "cells", axis=0, tiled=True),
            lax.all_gather(out_bias, "cells", axis=0, tiled=True),
            lax.all_gather(second_gain, "cells", axis=0, tiled=True),
            lax.all_gather(second_shift, "cells", axis=0, tiled=True),
            lax.all_gather(in_weight, "cells", axis=0, tiled=True),
            lax.all_gather(in_bias, "cells", axis=0, tiled=True),
            lax.all_gather(down_weight, "cells", axis=0, tiled=True),
            lax.all_gather(down_bias, "cells", axis=0, tiled=True),
        )
        out_seq, grad_seq, grads = sequence_pass(
            gathered,
            tokens[0, micro_step],
            lengths[0, micro_step],
            cotangent[0, micro_step],
            factor,
        )
        output_rows.append(out_seq)
        gradient_rows.append(grad_seq)
        shares = (
            lax.psum_scatter(grads[0], "cells", scatter_dimension=0, tiled=True),
            lax.psum_scatter(grads[1], "cells", scatter_dimension=0, tiled=True),
            lax.psum_scatter(grads[2], "cells", scatter_dimension=0, tiled=True),
            lax.psum_scatter(grads[3], "cells", scatter_dimension=0, tiled=True),
            lax.psum_scatter(grads[4], "cells", scatter_dimension=0, tiled=True),
            lax.psum_scatter(grads[5], "cells", scatter_dimension=0, tiled=True),
            lax.psum_scatter(grads[6], "cells", scatter_dimension=0, tiled=True),
            lax.psum_scatter(grads[7], "cells", scatter_dimension=0, tiled=True),
            lax.psum_scatter(grads[8], "cells", scatter_dimension=0, tiled=True),
            lax.psum_scatter(grads[9], "cells", scatter_dimension=0, tiled=True),
            lax.psum_scatter(grads[10], "cells", scatter_dimension=0, tiled=True),
            lax.psum_scatter(grads[11], "cells", scatter_dimension=0, tiled=True),
        )
        summed = shares if summed is None else jax.tree.map(jnp.add, summed, shares)
    final = (
        lax.psum(summed[0].astype(jnp.bfloat16), "species").astype(jnp.float32),
        lax.psum(summed[1].astype(jnp.bfloat16), "species").astype(jnp.float32),
        lax.psum(summed[2].astype(jnp.bfloat16), "species").astype(jnp.float32),
        lax.psum(summed[3].astype(jnp.bfloat16), "species").astype(jnp.float32),
        lax.psum(summed[4].astype(jnp.bfloat16), "species").astype(jnp.float32),
        lax.psum(summed[5].astype(jnp.bfloat16), "species").astype(jnp.float32),
        lax.psum(summed[6].astype(jnp.bfloat16), "species").astype(jnp.float32),
        lax.psum(summed[7].astype(jnp.bfloat16), "species").astype(jnp.float32),
        lax.psum(summed[8].astype(jnp.bfloat16), "species").astype(jnp.float32),
        lax.psum(summed[9].astype(jnp.bfloat16), "species").astype(jnp.float32),
        lax.psum(summed[10].astype(jnp.bfloat16), "species").astype(jnp.float32),
        lax.psum(summed[11].astype(jnp.bfloat16), "species").astype(jnp.float32),
    )
    out_tokens = jnp.stack(output_rows)[None]
    grad_tokens = jnp.stack(gradient_rows)[None]
    return (out_tokens, grad_tokens) + tuple(final)


def solution(mesh):
    in_specs = (
        P("species", "cells", None, None),
        P("species", "cells"),
        P("species", "cells", None, None),
        P("cells"),
        P("cells"),
        P("cells", None),
        P("cells"),
        P("cells", None),
        P("cells"),
        P("cells"),
        P("cells"),
        P("cells", None),
        P("cells"),
        P("cells", None),
        P("cells"),
    )
    out_specs = (
        P("species", "cells", None, None),
        P("species", "cells", None, None),
        P("cells"),
        P("cells"),
        P("cells", None),
        P("cells"),
        P("cells", None),
        P("cells"),
        P("cells"),
        P("cells"),
        P("cells", None),
        P("cells"),
        P("cells", None),
        P("cells"),
    )
    program = on_device_ring if mesh.shape["cells"] == 2 * RING_SIZE else on_device
    return jax.shard_map(
        program, mesh=mesh, in_specs=in_specs, out_specs=out_specs, check_vma=False
    )
```

```python
import jax
import jax.numpy as jnp
from jax import lax
from jax.experimental import pallas as pl
from jax.experimental.pallas import tpu as pltpu
from jax.sharding import PartitionSpec as P

HEAD = 64


EPSILON = 1e-12
NEGATIVE = -1e30


def normalize(values, gain_vec, shift_vec):
    center = values - jnp.mean(values, axis=-1, keepdims=True)
    spread = jnp.mean(center * center, axis=-1, keepdims=True)
    return center * lax.rsqrt(spread + EPSILON) * gain_vec + shift_vec


def smooth_gate(values):
    return jax.nn.gelu(values, approximate=False)


def times_left(left_side, right_side):
    return lax.dot_general(
        left_side, right_side, (((0,), (0,)), ((), ())), preferred_element_type=jnp.float32
    )


def times_right(left_side, right_side):
    return lax.dot_general(
        left_side, right_side, (((1,), (1,)), ((), ())), preferred_element_type=jnp.float32
    )


def sequence_pass(weights, inputs, length, cot_rows, factor):
    (
        first_gain,
        first_shift,
        qkv_weight,
        qv_bias,
        out_weight,
        out_bias,
        second_gain,
        second_shift,
        in_weight,
        in_bias,
        down_weight,
        down_bias,
    ) = weights
    seq_rows = inputs.shape[0]
    model_width = inputs.shape[1]
    heads_count = model_width // HEAD
    scale_qk = float(HEAD) ** (-0.5)
    as_float = inputs.astype(jnp.float32)
    hidden_one, first_pull = jax.vjp(
        normalize, as_float, first_gain.astype(jnp.float32), first_shift.astype(jnp.float32)
    )
    first_low = hidden_one.astype(jnp.bfloat16)
    bias_float = qv_bias.astype(jnp.float32)
    full_bias = jnp.concatenate(
        [bias_float[:model_width], jnp.zeros((model_width,), jnp.float32), bias_float[model_width:]]
    )
    projected = (
        jnp.dot(first_low, qkv_weight, preferred_element_type=jnp.float32) + full_bias
    ).astype(jnp.bfloat16)
    split_heads = projected.reshape(seq_rows, 3, heads_count, HEAD)
    queries = split_heads[:, 0]
    keys_part = split_heads[:, 1]
    values_part = split_heads[:, 2]
    visible = jnp.arange(seq_rows) < length

    def scores_of():
        raw_scores = (
            jnp.einsum("qhd,khd->hqk", queries, keys_part, preferred_element_type=jnp.float32)
            * scale_qk
        )
        return jnp.where(visible[None, None, :], raw_scores, NEGATIVE)

    scores = scores_of()
    top_score = jnp.max(scores, axis=-1, keepdims=True)
    expo = jnp.exp(scores - top_score)
    total_exp = jnp.sum(expo, axis=-1, keepdims=True)
    log_total = top_score + jnp.log(total_exp)
    attention = (expo / total_exp).astype(jnp.bfloat16)
    mixed = jnp.einsum("hqk,khd->qhd", attention, values_part, preferred_element_type=jnp.float32)
    mixed = mixed.reshape(seq_rows, model_width).astype(jnp.bfloat16)
    middle = (
        as_float
        + jnp.dot(mixed, out_weight, preferred_element_type=jnp.float32)
        + out_bias.astype(jnp.float32)
    )
    hidden_two, second_pull = jax.vjp(
        normalize, middle, second_gain.astype(jnp.float32), second_shift.astype(jnp.float32)
    )
    second_low = hidden_two.astype(jnp.bfloat16)
    inner = jnp.dot(second_low, in_weight, preferred_element_type=jnp.float32) + in_bias.astype(
        jnp.float32
    )
    active, gate_pull = jax.vjp(smooth_gate, inner)
    active_low = active.astype(jnp.bfloat16)
    output = (
        middle
        + jnp.dot(active_low, down_weight, preferred_element_type=jnp.float32)
        + down_bias.astype(jnp.float32)
    )
    upstream = cot_rows.astype(jnp.float32) * visible[:, None].astype(jnp.float32) * factor
    up_low = upstream.astype(jnp.bfloat16)
    grad_down_bias = jnp.sum(up_low.astype(jnp.float32), axis=0)
    grad_down = times_left(active_low, up_low)
    grad_active = times_right(up_low, down_weight)
    (grad_inner,) = gate_pull(grad_active)
    inner_low = grad_inner.astype(jnp.bfloat16)
    grad_in_bias = jnp.sum(inner_low.astype(jnp.float32), axis=0)
    grad_in = times_left(second_low, inner_low)
    grad_second = times_right(inner_low, in_weight)
    grad_middle_norm, grad_second_gain, grad_second_shift = second_pull(grad_second)
    grad_middle = upstream + grad_middle_norm
    middle_low = grad_middle.astype(jnp.bfloat16)
    grad_out_bias = jnp.sum(middle_low.astype(jnp.float32), axis=0)
    grad_out = times_left(mixed, middle_low)
    grad_mixed = (
        times_right(middle_low, out_weight)
        .astype(jnp.bfloat16)
        .reshape(seq_rows, heads_count, HEAD)
    )
    probs_again = jnp.exp(scores_of() - log_total)
    grad_probs = jnp.einsum(
        "qhd,khd->hqk", grad_mixed, values_part, preferred_element_type=jnp.float32
    )
    grad_values = jnp.einsum(
        "hqk,qhd->khd", attention, grad_mixed, preferred_element_type=jnp.float32
    )
    delta = jnp.sum(probs_again * grad_probs, axis=-1, keepdims=True)
    grad_scores = (probs_again * (grad_probs - delta)).astype(jnp.bfloat16)
    grad_queries = (
        jnp.einsum("hqk,khd->qhd", grad_scores, keys_part, preferred_element_type=jnp.float32)
        * scale_qk
    )
    grad_keys = (
        jnp.einsum("hqk,qhd->khd", grad_scores, queries, preferred_element_type=jnp.float32)
        * scale_qk
    )
    grad_projected = jnp.stack([grad_queries, grad_keys, grad_values], axis=1)
    grad_projected = grad_projected.reshape(seq_rows, 3 * model_width).astype(jnp.bfloat16)
    column_sums = jnp.sum(grad_projected.astype(jnp.float32), axis=0)
    grad_qv = jnp.concatenate([column_sums[:model_width], column_sums[2 * model_width :]])
    grad_qkv = times_left(first_low, grad_projected)
    grad_first = times_right(grad_projected, qkv_weight)
    grad_input_norm, grad_first_gain, grad_first_shift = first_pull(grad_first)
    grad_inputs = grad_middle + grad_input_norm
    grads = (
        grad_first_gain,
        grad_first_shift,
        grad_qkv,
        grad_qv,
        grad_out,
        grad_out_bias,
        grad_second_gain,
        grad_second_shift,
        grad_in,
        grad_in_bias,
        grad_down,
        grad_down_bias,
    )
    return (output.astype(jnp.bfloat16), grad_inputs.astype(jnp.bfloat16), grads)


RING = (0, 2, 4, 6, 7, 5, 3, 1)
RING_SIZE = len(RING)
CELLS = 2 * RING_SIZE
ANY = pl.BlockSpec(memory_space=pl.ANY)
HBM = pl.BlockSpec(memory_space=pltpu.HBM)
VMEM = pl.BlockSpec(memory_space=pltpu.VMEM)
SMEM = pl.BlockSpec(memory_space=pltpu.SMEM)
LOW = jnp.bfloat16
FULL = jnp.float32
HEAVY = 10**10
UNIT = 10**8
ROWS = {
    "first_gain": 0,
    "first_shift": 1,
    "qv_bias": 2,
    "out_bias": 4,
    "second_gain": 5,
    "second_shift": 6,
    "in_bias": 7,
    "down_bias": 11,
    "lengths": 12,
}
NAMES = tuple(ROWS)[:8]
SMALL_ROWS = 16
SMALL_LANES = 256
PIECES = (2, 2, 2, 2, 2, 2, 2, 1, 1)


def ring_pairs():
    pairs = []
    for place in range(RING_SIZE):
        chip = RING[place]
        right = RING[(place + 1) % RING_SIZE]
        left = RING[(place - 1) % RING_SIZE]
        pairs.append((2 * chip, 2 * right))
        pairs.append((2 * chip + 1, 2 * left + 1))
    return pairs


def hop(block):
    return lax.ppermute(block, "cells", ring_pairs())


def to_partner(block):
    return lax.ppermute(block, "cells", [(i, i ^ 1) for i in range(CELLS)])


def across(block):
    return lax.ppermute(block, "species", [(0, 1), (1, 0)])


def exchange(values, bit):
    return values + lax.ppermute(values, "cells", [(i, i ^ bit) for i in range(CELLS)])


def after(value, *others):
    return lax.optimization_barrier((value,) + others)[0]


def here():
    index = lax.axis_index("cells")
    core = index % 2
    chip = index // 2
    place = jnp.int32(0)
    for i, ring_chip in enumerate(RING):
        place = jnp.where(chip == ring_chip, i, place)
    return index, core, place


def chip_at(place):
    place = place % RING_SIZE
    chip = jnp.zeros_like(place)
    for i, ring_chip in enumerate(RING):
        chip = jnp.where(place == i, ring_chip, chip)
    return chip


def gather_order(core, place):
    sign = 1 - 2 * core
    order = []

    def pair(at):
        order.append(2 * chip_at(at))
        order.append(2 * chip_at(at) + 1)

    pair(place)
    for step in range(1, 4):
        pair(place - sign * step)
        pair(place + sign * step)
    order.append(2 * chip_at(place + 4) + core)
    order.append(2 * chip_at(place + 4) + 1 - core)
    return order


def scatter_slots(core, place):
    def kept(core_now):
        sign = 1 - 2 * core_now
        order = [2 * chip_at(place + 4) + core_now]
        for step in (3, 2, 1):
            order.append(2 * chip_at(place + sign * step))
            order.append(2 * chip_at(place + sign * step) + 1)
        order.append(2 * chip_at(place) + core_now)
        return order

    order = kept(core) + kept(1 - core)
    slots = []
    for device in range(CELLS):
        slot = jnp.int32(0)
        for i, who in enumerate(order):
            slot = jnp.where(who == device, i, slot)
        slots.append(slot)
    return slots


def both_blocks(block, core):
    other = to_partner(block)
    return jnp.stack([jnp.where(core == 0, block, other), jnp.where(core == 0, other, block)])


def half_of(pair, core):
    return jnp.where(core == 0, pair[0], pair[1])[None]


def add_low(*parts):
    total = parts[0].astype(FULL)
    for part in parts[1:]:
        total = total + part.astype(FULL)
    return total.astype(LOW)


def first_hop(*parts):
    return hop(add_low(*[part[0:1] for part in parts]))


def second_hop(moving, core, *parts):
    wide = jnp.stack([jnp.where(core == 0, moving[0], 0), jnp.where(core == 0, 0, moving[0])])
    return hop(add_low(wide, *[part[1:3] for part in parts]))


def later_hop(moving, at, *parts):
    return hop(add_low(moving, *[part[at : at + 2] for part in parts]))


def settle(moving, core, *parts):
    mine = jnp.where(core == 0, moving[0], moving[1])
    other = jnp.where(core == 0, moving[1], moving[0])
    return add_low(mine, to_partner(other), *[part[7] for part in parts])


def dot(left, right, dims=((1,), (0,))):
    return lax.dot_general(left, right, (dims, ((), ())), preferred_element_type=FULL)


def call(body, out_shape, ins, specs, out_specs=None, scratch=(), vmem=48, cost=HEAVY):
    return pl.pallas_call(
        body,
        out_shape=out_shape,
        in_specs=specs,
        out_specs=[VMEM] * len(out_shape) if out_specs is None else out_specs,
        scratch_shapes=list(scratch),
        compiler_params=pltpu.CompilerParams(vmem_limit_bytes=vmem * 2**20),
        cost_estimate=pl.CostEstimate(flops=cost, bytes_accessed=0, transcendentals=0),
    )(*ins)


def shape(dims, kind=LOW):
    return jax.ShapeDtypeStruct(dims, kind)


def fetch(order_ref, refs, target, sem):
    rows = target.shape[0] // CELLS
    copies = []
    index = 0
    for source, size in zip(refs, PIECES):
        for part in range(size):
            at = order_ref[index]
            copies.append(
                pltpu.make_async_copy(
                    source.at[part],
                    target.at[pl.ds(pl.multiple_of(at * rows, 16), rows)],
                    sem.at[index],
                )
            )
            index += 1
    for item in copies:
        item.start()
    return copies


def wait_all(copies):
    for item in copies:
        item.wait()


def one_hot(rows, lanes, offset):
    row = lax.broadcasted_iota(jnp.int32, (rows, lanes), 0)
    lane = lax.broadcasted_iota(jnp.int32, (rows, lanes), 1)
    return lane == row + offset


def pack_body(who_ref, lengths_ref, *refs):
    sources, small_ref = refs[:8], refs[8]
    me = who_ref[0]
    model = small_ref.shape[1]
    row = lax.broadcasted_iota(jnp.int32, (SMALL_ROWS, model), 0)
    lane = lax.broadcasted_iota(jnp.int32, (SMALL_ROWS, model), 1)
    small = jnp.zeros((SMALL_ROWS, model), FULL)
    for name, ref in zip(NAMES, sources):
        size = ref.shape[1]
        per_row = model // size
        placed = dot(ref[...], one_hot(size, model, size * (me % per_row)).astype(LOW))
        small = small + jnp.where(row == ROWS[name] + me // per_row, placed, 0.0)
    for i in range(2):
        at = (row == ROWS["lengths"]) & (lane == 2 * me + i)
        small = small + jnp.where(at, lengths_ref[i].astype(FULL), 0.0)
    small_ref[...] = small.astype(LOW)


def norm_parts(values):
    center = values - jnp.mean(values, axis=-1, keepdims=True)
    spread = jnp.mean(center * center, axis=-1, keepdims=True)
    return center, lax.rsqrt(spread + EPSILON)


def norm_back(center, scale, gain, grad):
    weighted = grad * gain
    mean_one = jnp.mean(weighted, axis=-1, keepdims=True)
    mean_two = jnp.mean(weighted * center, axis=-1, keepdims=True)
    back = scale * (weighted - mean_one - center * (scale * scale * mean_two))
    return back, jnp.sum(grad * center * scale, axis=0, keepdims=True), jnp.sum(
        grad, axis=0, keepdims=True
    )


def small_row(small_ref, name, count=1):
    return small_ref[...].astype(FULL)[ROWS[name] : ROWS[name] + count, :]


def project_body(order_ref, x_ref, small_ref, *refs):
    blocks = refs[:9]
    low_ref, proj_ref, weight, sem = refs[9:]
    model = x_ref.shape[1]
    copies = fetch(order_ref, blocks, weight, sem)
    center, scale = norm_parts(x_ref[...].astype(FULL))
    bias = small_row(small_ref, "qv_bias", 2)
    low_ref[...] = (
        center * scale * small_row(small_ref, "first_gain") + small_row(small_ref, "first_shift")
    ).astype(LOW)
    wait_all(copies)
    for j in range(3):
        lanes = slice(j * model, (j + 1) * model)
        part = dot(low_ref[...], weight[:, lanes])
        if j != 1:
            part = part + bias[j // 2 : j // 2 + 1]
        proj_ref[:, lanes] = part.astype(LOW)


def attend_body(seq, lengths_ref, proj_ref, att_ref, mixed_ref):
    model = mixed_ref.shape[1]
    cells = mixed_ref.shape[0] // seq
    pairs = model // (2 * HEAD)
    lane = lax.broadcasted_iota(jnp.int32, (seq, 2 * HEAD), 1)
    key = lax.broadcasted_iota(jnp.int32, (seq, seq), 0)

    def step(index, carry):
        s = index // pairs
        p = index % pairs
        rows = pl.ds(pl.multiple_of(s * seq, seq), seq)
        at = pl.multiple_of(p * 2 * HEAD, 2 * HEAD)
        q = proj_ref[rows, pl.ds(at, 2 * HEAD)] * jnp.asarray(HEAD ** (-0.5), LOW)
        k = proj_ref[rows, pl.ds(at + model, 2 * HEAD)]
        v_turned = proj_ref[rows, pl.ds(at + 2 * model, 2 * HEAD)].T
        visible = key < lengths_ref[s]
        mixed = []
        for i in range(2):
            own = (lane >= i * HEAD) & (lane < (i + 1) * HEAD)
            scores = dot(jnp.where(own, k, jnp.zeros_like(k)), q, ((1,), (1,)))
            scores = jnp.where(visible, scores, NEGATIVE)
            expo = jnp.exp(scores - jnp.max(scores, axis=0, keepdims=True))
            probs = expo * (1.0 / jnp.sum(expo, axis=0, keepdims=True))
            probs = probs.astype(LOW)
            att_ref[2 * index + i] = probs
            mixed.append(dot(v_turned[i * HEAD : (i + 1) * HEAD], probs))
        mixed_ref[rows, pl.ds(at, 2 * HEAD)] = jnp.concatenate(mixed, axis=0).T.astype(LOW)
        return carry

    lax.fori_loop(0, cells * pairs, step, 0, unroll=2)


ERFC_STEP = 0.33
ERFC = (
    0.1863578228018033,
    0.18295566386742124,
    0.2012255082472392,
    0.04721561458875723,
    0.4085089979423051,
    -0.35115900736338407,
    0.4602422572120205,
    -0.13534686486277223,
)


def gelu_parts(inner):
    z = jnp.abs(inner) * (0.5**0.5)
    t = 1.0 / (1.0 + ERFC_STEP * z)
    tail = jnp.full_like(t, 0.5 * ERFC[-1])
    for factor in ERFC[-2::-1]:
        tail = tail * t + 0.5 * factor
    bell = jnp.exp(-(z * z))
    tail = tail * t * bell
    area = jnp.where(inner < 0.0, tail, 1.0 - tail)
    return inner * area, area + inner * bell * (0.5 / 3.141592653589793) ** 0.5


def row_mask(lengths_ref, rows, seq):
    at = lax.broadcasted_iota(jnp.int32, (rows, 1), 0)
    true = (at < lengths_ref[0]).astype(FULL)
    for s in range(1, rows // seq):
        true = jnp.where(at < s * seq, true, (at < lengths_ref[s] + s * seq).astype(FULL))
    return true


def loss_rows(lengths_ref, small_ref, other_ref, cot_ref, seq, whole):
    count = jnp.sum(
        small_row(small_ref, "lengths") + small_row(other_ref, "lengths"), axis=-1, keepdims=True
    )
    return cot_ref[...].astype(FULL) * (
        row_mask(lengths_ref, cot_ref.shape[0], seq) * (whole / count)
    )


def put_slots(keep_buf, slot_ref, values, first, lanes):
    rows = keep_buf.shape[1]
    for i in range(values.shape[0] // rows):
        keep_buf[slot_ref[first + i], :, lanes] = values[i * rows : (i + 1) * rows].astype(LOW)


def send_slots(buf, keep_ref, away_ref, sem):
    half = RING_SIZE
    copies = [
        pltpu.make_async_copy(buf.at[pl.ds(half, half)], away_ref, sem.at[0]),
        pltpu.make_async_copy(buf.at[pl.ds(0, half)], keep_ref, sem.at[1]),
    ]
    for item in copies:
        item.start()
    return copies


def inner_body(order_ref, x_ref, mixed_ref, small_ref, *refs):
    blocks = refs[:9]
    middle_ref, low_ref, active_ref, slope_ref, weight, sem = refs[9:]
    model = x_ref.shape[1]
    ff = active_ref.shape[1]
    wait_all(fetch(order_ref, blocks, weight, sem))
    middle = (
        x_ref[...].astype(FULL)
        + dot(mixed_ref[...], weight[:, ff:])
        + small_row(small_ref, "out_bias")
    )
    middle_ref[...] = middle
    center, scale = norm_parts(middle)
    low = center * scale * small_row(small_ref, "second_gain") + small_row(
        small_ref, "second_shift"
    )
    low_ref[...] = low.astype(LOW)
    step = 2 * (ff // RING_SIZE)
    bias = small_row(small_ref, "in_bias", 4)
    for j in range(ff // step):
        lanes = slice(j * step, (j + 1) * step)
        inner = dot(low_ref[...], weight[:, lanes]) + bias[j : j + 1]
        active, slope = gelu_parts(inner)
        active_ref[:, lanes] = active.astype(LOW)
        slope_ref[:, lanes] = slope.astype(LOW)


def grad_down_body(
    seq, whole, who_ref, slot_ref, lengths_ref, active_ref, cot_ref, small_ref, other_ref,
    up_ref, down_b_ref, keep_ref, away_ref, keep_two_ref, away_two_ref, slots, sem,
):
    up_low = loss_rows(lengths_ref, small_ref, other_ref, cot_ref, seq, whole).astype(LOW)
    up_ref[...] = up_low
    down_b_ref[...] = jnp.sum(up_low.astype(FULL), axis=0, keepdims=True)
    parts = RING_SIZE
    step = active_ref.shape[1] // parts
    rows = slots.shape[2]
    side = who_ref[1]
    for j in range(parts):
        grad = dot(active_ref[:, j * step : (j + 1) * step], up_ref[...], ((0,), (0,)))
        for i in range(4):
            slots[(i + side) % 2, slot_ref[j * CELLS // parts + i // 2]] = grad[
                i * rows : (i + 1) * rows
            ].astype(LOW)
    copies = send_slots(slots.at[1], keep_two_ref, away_two_ref, sem.at[1])
    copies += send_slots(slots.at[0], keep_ref, away_ref, sem.at[0])
    wait_all(copies)


def inner_back_body(order_ref, slope_ref, up_ref, *refs):
    blocks = refs[:9]
    inner_ref, in_b_ref, weight, sem = refs[9:]
    model = up_ref.shape[1]
    wait_all(fetch(order_ref, blocks, weight, sem))
    for j in range(inner_ref.shape[1] // model):
        lanes = slice(j * model, (j + 1) * model)
        grad = dot(up_ref[...], weight[lanes, :], ((1,), (1,)))
        low = (grad * slope_ref[:, lanes].astype(FULL)).astype(LOW)
        inner_ref[:, lanes] = low
        in_b_ref[j : j + 1, :] = jnp.sum(low.astype(FULL), axis=0, keepdims=True)


def down_body(active_ref, middle_ref, small_ref, weight_ref, out_ref):
    out_ref[...] = (
        middle_ref[...]
        + dot(active_ref[...], weight_ref[...])
        + small_row(small_ref, "down_bias")
    ).astype(LOW)


def grad_in_body(slot_ref, low_ref, inner_ref, keep_ref, away_ref, slots, sem):
    model = low_ref.shape[1]
    turned = low_ref[...].T
    for j in range(inner_ref.shape[1] // model):
        lanes = slice(j * model, (j + 1) * model)
        put_slots(slots, slot_ref, dot(turned, inner_ref[:, lanes]), 0, lanes)
    wait_all(send_slots(slots, keep_ref, away_ref, sem))


def middle_back_body(
    seq, whole, lengths_ref, inner_ref, middle_ref, cot_ref, small_ref, other_ref, weight,
    grad_ref, grad_low_ref, grad_mixed_ref, sums_ref,
):
    ff = inner_ref.shape[1]
    grad_second = dot(inner_ref[...], weight[:, :ff], ((1,), (1,)))
    center, scale = norm_parts(middle_ref[...])
    back, gain_sum, shift_sum = norm_back(
        center, scale, small_row(small_ref, "second_gain"), grad_second
    )
    grad = loss_rows(lengths_ref, small_ref, other_ref, cot_ref, seq, whole) + back
    grad_ref[...] = grad
    grad_low = grad.astype(LOW)
    grad_low_ref[...] = grad_low
    grad_mixed_ref[...] = dot(grad_low, weight[:, ff:], ((1,), (1,))).astype(LOW)
    sums_ref[0:1, :] = jnp.sum(grad_low.astype(FULL), axis=0, keepdims=True)
    sums_ref[1:2, :] = gain_sum
    sums_ref[2:3, :] = shift_sum


def attend_back_body(seq, begin, proj_ref, att_ref, grad_ref, out_ref):
    model = grad_ref.shape[1]
    half = out_ref.shape[1] // 3
    all_pairs = model // (2 * HEAD)
    pairs = half // (2 * HEAD)
    cells = grad_ref.shape[0] // seq
    lane = lax.broadcasted_iota(jnp.int32, (seq, 2 * HEAD), 1)
    scale = HEAD ** (-0.5)

    def step(index, carry):
        s = index // pairs
        p = index % pairs
        rows = pl.ds(pl.multiple_of(s * seq, seq), seq)
        to = pl.multiple_of(p * 2 * HEAD, 2 * HEAD)
        at = pl.multiple_of(to + begin * 2 * HEAD, 2 * HEAD)
        q = proj_ref[rows, pl.ds(at, 2 * HEAD)]
        k_turned = proj_ref[rows, pl.ds(at + model, 2 * HEAD)].T
        v = proj_ref[rows, pl.ds(at + 2 * model, 2 * HEAD)]
        g = grad_ref[rows, pl.ds(at, 2 * HEAD)]
        grad_q = []
        grad_k = []
        grad_v = []
        for i in range(2):
            own = (lane >= i * HEAD) & (lane < (i + 1) * HEAD)
            probs = att_ref[2 * (s * all_pairs + begin + p) + i]
            wide = probs.astype(FULL)
            grad_probs = dot(jnp.where(own, v, jnp.zeros_like(v)), g, ((1,), (1,)))
            delta = jnp.sum(wide * grad_probs, axis=0, keepdims=True)
            scores = (wide * (grad_probs - delta)).astype(LOW)
            grad_q.append(dot(k_turned[i * HEAD : (i + 1) * HEAD], scores))
            grad_k.append(dot(scores, q))
            grad_v.append(dot(probs, g))
        first = lane < HEAD
        out_ref[rows, pl.ds(to, 2 * HEAD)] = (
            jnp.concatenate(grad_q, axis=0).T * scale
        ).astype(LOW)
        out_ref[rows, pl.ds(to + half, 2 * HEAD)] = (
            jnp.where(first, grad_k[0], grad_k[1]) * scale
        ).astype(LOW)
        out_ref[rows, pl.ds(to + 2 * half, 2 * HEAD)] = jnp.where(
            first, grad_v[0], grad_v[1]
        ).astype(LOW)
        return carry

    lax.fori_loop(0, cells * pairs, step, 0, unroll=2)


def early_grad_body(
    slot_ref, low_ref, part_ref, mixed_ref, grad_low_ref, keep_ref, away_ref, slots, sem
):
    width = part_ref.shape[1]
    put_slots(slots, slot_ref, dot(low_ref[...].T, part_ref[...]), 0, slice(0, width))
    put_slots(
        slots, slot_ref, dot(mixed_ref[...].T, grad_low_ref[...]), 0,
        slice(width, slots.shape[2]),
    )
    wait_all(send_slots(slots, keep_ref, away_ref, sem))


def first_back_body(
    slot_ref, x_ref, low_ref, one_ref, two_ref, grad_ref, small_ref, sums_ref, in_b_ref,
    down_b_ref, weight, out_ref, keep_ref, away_ref, sum_ref, slots, sem,
):
    model = x_ref.shape[1]
    late = two_ref.shape[1]
    center, scale = norm_parts(x_ref[...].astype(FULL))
    parts = ((one_ref, 0), (two_ref, one_ref.shape[1] // 3))
    grad_first = jnp.zeros(x_ref.shape, FULL)
    for j in range(3):
        for ref, begin in parts:
            width = ref.shape[1] // 3
            at = j * model + begin
            grad_first = grad_first + dot(
                ref[:, j * width : (j + 1) * width], weight[:, at : at + width], ((1,), (1,))
            )
    put_slots(slots, slot_ref, dot(low_ref[...].T, two_ref[...]), 0, slice(0, late))
    back, gain_sum, shift_sum = norm_back(
        center, scale, small_row(small_ref, "first_gain"), grad_first
    )

    def put(name, value, offset=0):
        at = ROWS[name] + offset
        sum_ref[at : at + value.shape[0], :] = value

    sum_ref[...] = jnp.zeros_like(sum_ref)
    put("first_gain", gain_sum)
    put("first_shift", shift_sum)
    for j in range(2):
        at = ROWS["qv_bias"] + j
        for ref, begin in parts:
            width = ref.shape[1] // 3
            part = ref[:, 2 * j * width : (2 * j + 1) * width].astype(FULL)
            sum_ref[at : at + 1, begin : begin + width] = jnp.sum(part, axis=0, keepdims=True)
    put("out_bias", sums_ref[0:1, :])
    put("second_gain", sums_ref[1:2, :])
    put("second_shift", sums_ref[2:3, :])
    put("in_bias", in_b_ref[...])
    put("down_bias", down_b_ref[...])
    for i in range(3):
        part = sum_ref[:, SMALL_LANES * i : SMALL_LANES * (i + 1)].astype(LOW)
        for device in range(CELLS):
            slots[device, 16 * i : 16 * i + 16, late:] = part
    copies = send_slots(slots, keep_ref, away_ref, sem)
    out_ref[...] = (grad_ref[...] + back).astype(LOW)
    wait_all(copies)


def finish_small_body(who_ref, late_ref, late_two_ref, *refs):
    vectors, small_ref = refs[:-1], refs[-1]
    model = small_ref.shape[1]
    first = late_ref.shape[1] - SMALL_LANES
    late = late_ref[:, first:].astype(FULL) + late_two_ref[:, first:].astype(FULL)
    for i in range(3):
        small_ref[:, SMALL_LANES * i : SMALL_LANES * (i + 1)] = late[16 * i : 16 * i + 16]
    me = who_ref[0]
    row = lax.broadcasted_iota(jnp.int32, (SMALL_ROWS, model), 0)
    for name, ref in zip(NAMES, vectors):
        size = ref.shape[1]
        per_row = model // size
        here_row = jnp.where(row == ROWS[name] + me // per_row, small_ref[...], 0.0)
        values = jnp.sum(here_row, axis=0, keepdims=True)
        picker = one_hot(size, model, size * (me % per_row)).astype(FULL)
        ref[...] = lax.dot_general(
            values, picker, (((1,), (1,)), ((), ())), precision=lax.Precision.HIGHEST,
            preferred_element_type=FULL,
        )


def finish_body(early_ref, early_two_ref, late_ref, late_two_ref, grad_ref, out_ref):
    model = out_ref.shape[1]
    early = early_ref[...].astype(FULL) + early_two_ref[...].astype(FULL)
    late = late_ref[...].astype(FULL) + late_two_ref[...].astype(FULL)
    one = (early.shape[1] - model) // 3
    two = (late.shape[1] - SMALL_LANES) // 3
    for j in range(3):
        at = j * model
        grad_ref[:, at : at + one] = early[:, j * one : (j + 1) * one]
        grad_ref[:, at + one : at + model] = late[:, j * two : (j + 1) * two]
    out_ref[...] = early[:, 3 * one :]


def on_device_ring(
    tokens,
    lengths,
    cotangent,
    first_gain,
    first_shift,
    qkv_weight,
    qv_bias,
    out_weight,
    out_bias,
    second_gain,
    second_shift,
    in_weight,
    in_bias,
    down_weight,
    down_bias,
):
    micro, seq, model = tokens.shape[1:]
    total_rows = micro * seq
    rows = qkv_weight.shape[0]
    down_rows = down_weight.shape[0]
    ff = in_weight.shape[1]
    heads = model // HEAD
    whole = float(lax.axis_size("species") * CELLS * micro * seq)
    index, core, place = here()
    species = lax.axis_index("species")
    who = jnp.stack([index, species]).astype(jnp.int32)
    order = jnp.stack(gather_order(core, place)).astype(jnp.int32)
    slot = jnp.stack(scatter_slots(core, place)).astype(jnp.int32)
    lens = lengths.reshape(micro)
    x = tokens.reshape(total_rows, model)
    cot = cotangent.reshape(total_rows, model)
    vectors = (
        first_gain, first_shift, qv_bias, out_bias, second_gain, second_shift, in_bias, down_bias,
    )

    dma = pltpu.SemaphoreType.DMA

    def gathered(own, hops):
        got = [own]
        for item in hops:
            got += [item, to_partner(item)]
        return got

    own = both_blocks(qkv_weight, core)
    qkv_one = hop(own)
    (small,) = call(
        pack_body,
        [shape((SMALL_ROWS, model))],
        [who, after(lens, own)] + [item.reshape(1, -1) for item in vectors],
        [SMEM, SMEM] + [VMEM] * 8,
        vmem=4,
    )
    in_weight, out_weight = lax.optimization_barrier((in_weight, out_weight, own))[:2]
    in_own = both_blocks(jnp.concatenate([in_weight, out_weight], axis=1), core)
    in_one = hop(in_own)
    small = exchange(small, 1)
    qkv_one, small = lax.optimization_barrier((qkv_one, small))
    qkv_two = hop(qkv_one)
    in_two = hop(after(in_one, qkv_one))
    small = exchange(small, 2)
    down_own = both_blocks(after(down_weight, qkv_one), core)
    qkv_two, small, down_own = lax.optimization_barrier((qkv_two, small, down_own))
    qkv_three = hop(qkv_two)
    small = exchange(small, 4)
    qkv_three, small = lax.optimization_barrier((qkv_three, small))
    qkv_last = hop(half_of(qkv_three, core))
    in_three = hop(after(in_two, qkv_three))
    small = exchange(small, 8)
    in_three, small = lax.optimization_barrier((in_three, small))
    in_last = hop(half_of(in_three, core))
    down_one = hop(after(down_own, in_three))
    low, proj, qkv_full = call(
        project_body,
        [
            shape((total_rows, model)),
            shape((total_rows, 3 * model)),
            shape((model, 3 * model)),
        ],
        [order, after(x, in_three), small] + gathered(own, (qkv_one, qkv_two, qkv_three, qkv_last)),
        [SMEM, VMEM, VMEM] + [ANY] * 9,
        scratch=[dma((CELLS,))],
        vmem=14,
    )
    other_small = across(small)
    proj, in_last, other_small, down_one = lax.optimization_barrier(
        (proj, in_last, other_small, down_one)
    )
    down_two = hop(down_one)
    att, mixed = call(
        lambda *refs: attend_body(seq, *refs),
        [shape((micro * heads, seq, seq)), shape((total_rows, model))],
        [lens, proj],
        [SMEM, VMEM],
        vmem=12,
    )
    down_two, mixed = lax.optimization_barrier((down_two, mixed))
    down_three = hop(down_two)
    in_got = gathered(in_own, (in_one, in_two, in_three, in_last))
    middle, low_two, active, slope, in_full = call(
        inner_body,
        [
            shape((total_rows, model), FULL),
            shape((total_rows, model)),
            shape((total_rows, ff)),
            shape((total_rows, ff)),
            shape((model, ff + model)),
        ],
        [order, x, mixed, small] + in_got,
        [SMEM] + [VMEM] * 3 + [ANY] * 9,
        scratch=[dma((CELLS,))],
        vmem=17,
    )
    down_three, active = lax.optimization_barrier((down_three, active))
    down_last = hop(half_of(down_three, core))
    up_low, down_b, down_keep, down_away, down_keep_two, down_away_two = call(
        lambda *refs: grad_down_body(seq, whole, *refs),
        [
            shape((total_rows, model)),
            shape((1, model), FULL),
        ]
        + [shape((RING_SIZE, down_rows // 2, model))] * 4,
        [who, slot, lens, active, cot, small, other_small],
        [SMEM] * 3 + [VMEM] * 4,
        [VMEM] * 2 + [ANY] * 4,
        scratch=[pltpu.VMEM((2, CELLS, down_rows // 2, model), LOW), dma((2, 2))],
        vmem=14,
    )

    down_away, down_away_two, down_last = lax.optimization_barrier(
        (down_away, down_away_two, down_last)
    )
    down_other_two = to_partner(down_away_two)
    down_other = to_partner(down_away)
    inner_low, in_b, down_full = call(
        inner_back_body,
        [
            shape((total_rows, ff)),
            shape((ff // model, model), FULL),
            shape((ff, model)),
        ],
        [order, slope, up_low]
        + gathered(down_own, (down_one, down_two, down_three, down_last)),
        [SMEM] + [VMEM] * 2 + [ANY] * 9,
        scratch=[dma((CELLS,))],
        vmem=15,
    )
    down_other_two, inner_low = lax.optimization_barrier((down_other_two, inner_low))
    down_x = across(add_low(down_keep_two[0:3], down_other_two[0:3]))
    down_x_two = across(add_low(down_keep_two[3:8], down_other_two[3:8]))
    in_keep, in_away = call(
        grad_in_body,
        [shape((RING_SIZE, rows, ff)), shape((RING_SIZE, rows, ff))],
        [slot, low_two, inner_low],
        [SMEM] + [VMEM] * 2,
        [ANY] * 2,
        scratch=[pltpu.VMEM((CELLS, rows, ff), LOW), dma((2,))],
        vmem=12,
    )
    in_other = to_partner(in_away)
    (out_tokens,) = call(
        down_body,
        [shape((total_rows, model))],
        [after(active, in_keep), middle, small, down_full],
        [VMEM] * 4,
        vmem=13,
    )
    in_other, out_tokens, inner_low = lax.optimization_barrier((in_other, out_tokens, inner_low))
    in_sum = first_hop(in_keep, in_other)
    grad_middle, grad_low, grad_mixed, sums = call(
        lambda *refs: middle_back_body(seq, whole, *refs),
        [
            shape((total_rows, model), FULL),
            shape((total_rows, model)),
            shape((total_rows, model)),
            shape((3, model), FULL),
        ],
        [lens, inner_low, middle, cot, small, other_small, in_full],
        [SMEM] + [VMEM] * 6,
        vmem=16,
    )

    def attend_back(begin, pairs, grad):
        return call(
            lambda *refs: attend_back_body(seq, begin, *refs),
            [shape((total_rows, 6 * pairs * HEAD))],
            [proj, att, grad],
            [VMEM] * 3,
            vmem=11,

        )[0]

    pairs = model // (2 * HEAD)
    early_pairs = 2 * pairs // 3
    in_sum, down_x, down_other, grad_mixed = lax.optimization_barrier(
        (in_sum, down_x, down_other, grad_mixed)
    )
    down_sum = first_hop(down_keep, down_other, down_x)
    in_sum = second_hop(in_sum, core, in_keep, in_other)
    grad_one = attend_back(0, early_pairs, grad_mixed)
    down_sum, grad_one = lax.optimization_barrier((down_sum, grad_one))
    down_sum = second_hop(down_sum, core, down_keep, down_other, down_x)
    early_width = 6 * early_pairs * HEAD + model
    early_keep, early_away = call(
        early_grad_body,
        [shape((RING_SIZE, rows, early_width))] * 2,
        [slot, low, grad_one, mixed, grad_low],
        [SMEM] + [VMEM] * 4,
        [ANY] * 2,
        scratch=[pltpu.VMEM((CELLS, rows, early_width), LOW), dma((2,))],
        vmem=12,
    )
    early_other = to_partner(early_away)
    in_sum, early_keep, grad_mixed = lax.optimization_barrier((in_sum, early_keep, grad_mixed))
    in_sum = later_hop(in_sum, 3, in_keep, in_other)
    grad_two = attend_back(early_pairs, pairs - early_pairs, grad_mixed)
    early_other, grad_two = lax.optimization_barrier((early_other, grad_two))
    early_sum = first_hop(early_keep, early_other)
    late_width = 6 * (pairs - early_pairs) * HEAD + SMALL_LANES
    grad_tokens, late_keep, late_away = call(
        first_back_body,
        [
            shape((total_rows, model)),
            shape((RING_SIZE, rows, late_width)),
            shape((RING_SIZE, rows, late_width)),
        ],
        [slot, x, low, grad_one, grad_two, grad_middle, small, sums, in_b, down_b, qkv_full],
        [SMEM] + [VMEM] * 10,
        [VMEM] + [ANY] * 2,
        scratch=[
            pltpu.VMEM((SMALL_ROWS, model), FULL),
            pltpu.VMEM((CELLS, rows, late_width), LOW),
            dma((2,)),
        ],
        vmem=14,

    )
    late_other = to_partner(late_away)
    in_sum, early_sum, late_keep, down_sum, down_x_two = lax.optimization_barrier(
        (in_sum, early_sum, late_keep, down_sum, down_x_two)
    )
    in_sum = later_hop(in_sum, 5, in_keep, in_other)
    early_sum = second_hop(early_sum, core, early_keep, early_other)
    down_sum = hop(add_low(down_sum, down_keep[3:5], down_other[3:5], down_x_two[0:2]))
    late_sum = first_hop(late_keep, late_other)
    late_sum, early_sum, down_sum = lax.optimization_barrier((late_sum, early_sum, down_sum))
    down_sum = hop(add_low(down_sum, down_keep[5:7], down_other[5:7], down_x_two[2:4]))
    late_sum = second_hop(late_sum, core, late_keep, late_other)
    early_sum = later_hop(early_sum, 3, early_keep, early_other)
    late_sum, early_sum, down_sum, in_sum = lax.optimization_barrier(
        (late_sum, early_sum, down_sum, in_sum)
    )
    late_sum = later_hop(late_sum, 3, late_keep, late_other)
    early_sum = later_hop(early_sum, 5, early_keep, early_other)
    in_sum = settle(in_sum, core, in_keep, in_other)
    in_terms = (in_sum, across(in_sum))
    mine = jnp.where(core == 0, down_sum[0], down_sum[1])
    other = to_partner(jnp.where(core == 0, down_sum[1], down_sum[0]))
    down_sum = add_low(mine, other, down_keep[7], down_other[7], down_x_two[4])
    down_terms = (down_sum, across(down_sum))
    late_sum = later_hop(late_sum, 5, late_keep, late_other)
    early_sum = settle(early_sum, core, early_keep, early_other)
    early_terms = (early_sum, across(early_sum))
    late_sum = settle(late_sum, core, late_keep, late_other)
    late_terms = (late_sum, across(late_sum))
    small_terms = lax.optimization_barrier(late_terms + (early_terms[0],))[:2]
    pieces = call(
        finish_small_body,
        [shape((1, item.shape[0]), FULL) for item in vectors],
        [who] + list(small_terms),
        [SMEM] + [VMEM] * 2,
        scratch=[pltpu.VMEM((SMALL_ROWS, model), FULL)],
        vmem=6,
    )
    pieces = [item.reshape(-1) for item in pieces]
    grad_qkv, grad_out = call(
        finish_body,
        [shape((rows, 3 * model), FULL), shape((rows, model), FULL)],
        list(early_terms) + list(late_terms),
        [VMEM] * 4,
        vmem=6,
    )
    return (
        out_tokens.reshape(tokens.shape),
        grad_tokens.reshape(tokens.shape),
        pieces[0],
        pieces[1],
        grad_qkv,
        pieces[2],
        grad_out,
        pieces[3],
        pieces[4],
        pieces[5],
        in_terms[0].astype(FULL) + in_terms[1].astype(FULL),
        pieces[6],
        jnp.concatenate(
            [
                jnp.where(species == 0, down_terms[0], down_terms[1]),
                jnp.where(species == 0, down_terms[1], down_terms[0]),
            ]
        ).astype(FULL),
        pieces[7],
    )


def on_device(
    tokens,
    lengths,
    cotangent,
    first_gain,
    first_shift,
    qkv_weight,
    qv_bias,
    out_weight,
    out_bias,
    second_gain,
    second_shift,
    in_weight,
    in_bias,
    down_weight,
    down_bias,
):
    local_count = jnp.sum(lengths).astype(jnp.float32)
    count = lax.psum(local_count, ("species", "cells"))
    micro_count = tokens.shape[1]
    seq_rows = tokens.shape[2]
    factor = (
        float(lax.axis_size("species") * lax.axis_size("cells") * micro_count * seq_rows) / count
    )
    output_rows = []
    gradient_rows = []
    summed = None
    for micro_step in range(micro_count):
        gathered = (
            lax.all_gather(first_gain, "cells", axis=0, tiled=True),
            lax.all_gather(first_shift, "cells", axis=0, tiled=True),
            lax.all_gather(qkv_weight, "cells", axis=0, tiled=True),
            lax.all_gather(qv_bias, "cells", axis=0, tiled=True),
            lax.all_gather(out_weight, "cells", axis=0, tiled=True),
            lax.all_gather(out_bias, "cells", axis=0, tiled=True),
            lax.all_gather(second_gain, "cells", axis=0, tiled=True),
            lax.all_gather(second_shift, "cells", axis=0, tiled=True),
            lax.all_gather(in_weight, "cells", axis=0, tiled=True),
            lax.all_gather(in_bias, "cells", axis=0, tiled=True),
            lax.all_gather(down_weight, "cells", axis=0, tiled=True),
            lax.all_gather(down_bias, "cells", axis=0, tiled=True),
        )
        out_seq, grad_seq, grads = sequence_pass(
            gathered,
            tokens[0, micro_step],
            lengths[0, micro_step],
            cotangent[0, micro_step],
            factor,
        )
        output_rows.append(out_seq)
        gradient_rows.append(grad_seq)
        shares = (
            lax.psum_scatter(grads[0], "cells", scatter_dimension=0, tiled=True),
            lax.psum_scatter(grads[1], "cells", scatter_dimension=0, tiled=True),
            lax.psum_scatter(grads[2], "cells", scatter_dimension=0, tiled=True),
            lax.psum_scatter(grads[3], "cells", scatter_dimension=0, tiled=True),
            lax.psum_scatter(grads[4], "cells", scatter_dimension=0, tiled=True),
            lax.psum_scatter(grads[5], "cells", scatter_dimension=0, tiled=True),
            lax.psum_scatter(grads[6], "cells", scatter_dimension=0, tiled=True),
            lax.psum_scatter(grads[7], "cells", scatter_dimension=0, tiled=True),
            lax.psum_scatter(grads[8], "cells", scatter_dimension=0, tiled=True),
            lax.psum_scatter(grads[9], "cells", scatter_dimension=0, tiled=True),
            lax.psum_scatter(grads[10], "cells", scatter_dimension=0, tiled=True),
            lax.psum_scatter(grads[11], "cells", scatter_dimension=0, tiled=True),
        )
        summed = shares if summed is None else jax.tree.map(jnp.add, summed, shares)
    final = (
        lax.psum(summed[0].astype(jnp.bfloat16), "species").astype(jnp.float32),
        lax.psum(summed[1].astype(jnp.bfloat16), "species").astype(jnp.float32),
        lax.psum(summed[2].astype(jnp.bfloat16), "species").astype(jnp.float32),
        lax.psum(summed[3].astype(jnp.bfloat16), "species").astype(jnp.float32),
        lax.psum(summed[4].astype(jnp.bfloat16), "species").astype(jnp.float32),
        lax.psum(summed[5].astype(jnp.bfloat16), "species").astype(jnp.float32),
        lax.psum(summed[6].astype(jnp.bfloat16), "species").astype(jnp.float32),
        lax.psum(summed[7].astype(jnp.bfloat16), "species").astype(jnp.float32),
        lax.psum(summed[8].astype(jnp.bfloat16), "species").astype(jnp.float32),
        lax.psum(summed[9].astype(jnp.bfloat16), "species").astype(jnp.float32),
        lax.psum(summed[10].astype(jnp.bfloat16), "species").astype(jnp.float32),
        lax.psum(summed[11].astype(jnp.bfloat16), "species").astype(jnp.float32),
    )
    out_tokens = jnp.stack(output_rows)[None]
    grad_tokens = jnp.stack(gradient_rows)[None]
    return (out_tokens, grad_tokens) + tuple(final)


def solution(mesh):
    in_specs = (
        P("species", "cells", None, None),
        P("species", "cells"),
        P("species", "cells", None, None),
        P("cells"),
        P("cells"),
        P("cells", None),
        P("cells"),
        P("cells", None),
        P("cells"),
        P("cells"),
        P("cells"),
        P("cells", None),
        P("cells"),
        P("cells", None),
        P("cells"),
    )
    out_specs = (
        P("species", "cells", None, None),
        P("species", "cells", None, None),
        P("cells"),
        P("cells"),
        P("cells", None),
        P("cells"),
        P("cells", None),
        P("cells"),
        P("cells"),
        P("cells"),
        P("cells", None),
        P("cells"),
        P("cells", None),
        P("cells"),
    )
    program = on_device_ring if mesh.shape["cells"] == 2 * RING_SIZE else on_device
    return jax.shard_map(
        program, mesh=mesh, in_specs=in_specs, out_specs=out_specs, check_vma=False
    )
```

```python
import jax
import jax.numpy as jnp
from jax import lax
from jax.experimental import pallas as pl
from jax.experimental.pallas import tpu as pltpu
from jax.sharding import PartitionSpec as P

HEAD = 64


EPSILON = 1e-12
NEGATIVE = -1e30


def normalize(values, gain_vec, shift_vec):
    center = values - jnp.mean(values, axis=-1, keepdims=True)
    spread = jnp.mean(center * center, axis=-1, keepdims=True)
    return center * lax.rsqrt(spread + EPSILON) * gain_vec + shift_vec


def smooth_gate(values):
    return jax.nn.gelu(values, approximate=False)


def times_left(left_side, right_side):
    return lax.dot_general(
        left_side, right_side, (((0,), (0,)), ((), ())), preferred_element_type=jnp.float32
    )


def times_right(left_side, right_side):
    return lax.dot_general(
        left_side, right_side, (((1,), (1,)), ((), ())), preferred_element_type=jnp.float32
    )


def sequence_pass(weights, inputs, length, cot_rows, factor):
    (
        first_gain,
        first_shift,
        qkv_weight,
        qv_bias,
        out_weight,
        out_bias,
        second_gain,
        second_shift,
        in_weight,
        in_bias,
        down_weight,
        down_bias,
    ) = weights
    seq_rows = inputs.shape[0]
    model_width = inputs.shape[1]
    heads_count = model_width // HEAD
    scale_qk = float(HEAD) ** (-0.5)
    as_float = inputs.astype(jnp.float32)
    hidden_one, first_pull = jax.vjp(
        normalize, as_float, first_gain.astype(jnp.float32), first_shift.astype(jnp.float32)
    )
    first_low = hidden_one.astype(jnp.bfloat16)
    bias_float = qv_bias.astype(jnp.float32)
    full_bias = jnp.concatenate(
        [bias_float[:model_width], jnp.zeros((model_width,), jnp.float32), bias_float[model_width:]]
    )
    projected = (
        jnp.dot(first_low, qkv_weight, preferred_element_type=jnp.float32) + full_bias
    ).astype(jnp.bfloat16)
    split_heads = projected.reshape(seq_rows, 3, heads_count, HEAD)
    queries = split_heads[:, 0]
    keys_part = split_heads[:, 1]
    values_part = split_heads[:, 2]
    visible = jnp.arange(seq_rows) < length

    def scores_of():
        raw_scores = (
            jnp.einsum("qhd,khd->hqk", queries, keys_part, preferred_element_type=jnp.float32)
            * scale_qk
        )
        return jnp.where(visible[None, None, :], raw_scores, NEGATIVE)

    scores = scores_of()
    top_score = jnp.max(scores, axis=-1, keepdims=True)
    expo = jnp.exp(scores - top_score)
    total_exp = jnp.sum(expo, axis=-1, keepdims=True)
    log_total = top_score + jnp.log(total_exp)
    attention = (expo / total_exp).astype(jnp.bfloat16)
    mixed = jnp.einsum("hqk,khd->qhd", attention, values_part, preferred_element_type=jnp.float32)
    mixed = mixed.reshape(seq_rows, model_width).astype(jnp.bfloat16)
    middle = (
        as_float
        + jnp.dot(mixed, out_weight, preferred_element_type=jnp.float32)
        + out_bias.astype(jnp.float32)
    )
    hidden_two, second_pull = jax.vjp(
        normalize, middle, second_gain.astype(jnp.float32), second_shift.astype(jnp.float32)
    )
    second_low = hidden_two.astype(jnp.bfloat16)
    inner = jnp.dot(second_low, in_weight, preferred_element_type=jnp.float32) + in_bias.astype(
        jnp.float32
    )
    active, gate_pull = jax.vjp(smooth_gate, inner)
    active_low = active.astype(jnp.bfloat16)
    output = (
        middle
        + jnp.dot(active_low, down_weight, preferred_element_type=jnp.float32)
        + down_bias.astype(jnp.float32)
    )
    upstream = cot_rows.astype(jnp.float32) * visible[:, None].astype(jnp.float32) * factor
    up_low = upstream.astype(jnp.bfloat16)
    grad_down_bias = jnp.sum(up_low.astype(jnp.float32), axis=0)
    grad_down = times_left(active_low, up_low)
    grad_active = times_right(up_low, down_weight)
    (grad_inner,) = gate_pull(grad_active)
    inner_low = grad_inner.astype(jnp.bfloat16)
    grad_in_bias = jnp.sum(inner_low.astype(jnp.float32), axis=0)
    grad_in = times_left(second_low, inner_low)
    grad_second = times_right(inner_low, in_weight)
    grad_middle_norm, grad_second_gain, grad_second_shift = second_pull(grad_second)
    grad_middle = upstream + grad_middle_norm
    middle_low = grad_middle.astype(jnp.bfloat16)
    grad_out_bias = jnp.sum(middle_low.astype(jnp.float32), axis=0)
    grad_out = times_left(mixed, middle_low)
    grad_mixed = (
        times_right(middle_low, out_weight)
        .astype(jnp.bfloat16)
        .reshape(seq_rows, heads_count, HEAD)
    )
    probs_again = jnp.exp(scores_of() - log_total)
    grad_probs = jnp.einsum(
        "qhd,khd->hqk", grad_mixed, values_part, preferred_element_type=jnp.float32
    )
    grad_values = jnp.einsum(
        "hqk,qhd->khd", attention, grad_mixed, preferred_element_type=jnp.float32
    )
    delta = jnp.sum(probs_again * grad_probs, axis=-1, keepdims=True)
    grad_scores = (probs_again * (grad_probs - delta)).astype(jnp.bfloat16)
    grad_queries = (
        jnp.einsum("hqk,khd->qhd", grad_scores, keys_part, preferred_element_type=jnp.float32)
        * scale_qk
    )
    grad_keys = (
        jnp.einsum("hqk,qhd->khd", grad_scores, queries, preferred_element_type=jnp.float32)
        * scale_qk
    )
    grad_projected = jnp.stack([grad_queries, grad_keys, grad_values], axis=1)
    grad_projected = grad_projected.reshape(seq_rows, 3 * model_width).astype(jnp.bfloat16)
    column_sums = jnp.sum(grad_projected.astype(jnp.float32), axis=0)
    grad_qv = jnp.concatenate([column_sums[:model_width], column_sums[2 * model_width :]])
    grad_qkv = times_left(first_low, grad_projected)
    grad_first = times_right(grad_projected, qkv_weight)
    grad_input_norm, grad_first_gain, grad_first_shift = first_pull(grad_first)
    grad_inputs = grad_middle + grad_input_norm
    grads = (
        grad_first_gain,
        grad_first_shift,
        grad_qkv,
        grad_qv,
        grad_out,
        grad_out_bias,
        grad_second_gain,
        grad_second_shift,
        grad_in,
        grad_in_bias,
        grad_down,
        grad_down_bias,
    )
    return (output.astype(jnp.bfloat16), grad_inputs.astype(jnp.bfloat16), grads)


RING = (0, 2, 4, 6, 7, 5, 3, 1)
RING_SIZE = len(RING)
CELLS = 2 * RING_SIZE
ANY = pl.BlockSpec(memory_space=pl.ANY)
HBM = pl.BlockSpec(memory_space=pltpu.HBM)
VMEM = pl.BlockSpec(memory_space=pltpu.VMEM)
SMEM = pl.BlockSpec(memory_space=pltpu.SMEM)
LOW = jnp.bfloat16
FULL = jnp.float32
HEAVY = 10**10
UNIT = 10**8
ROWS = {
    "first_gain": 0,
    "first_shift": 1,
    "qv_bias": 2,
    "out_bias": 4,
    "second_gain": 5,
    "second_shift": 6,
    "in_bias": 7,
    "down_bias": 11,
    "lengths": 12,
}
NAMES = tuple(ROWS)[:8]
SMALL_ROWS = 16
SMALL_LANES = 256
PIECES = (2, 2, 2, 2, 2, 2, 2, 1, 1)


def ring_pairs():
    pairs = []
    for place in range(RING_SIZE):
        chip = RING[place]
        right = RING[(place + 1) % RING_SIZE]
        left = RING[(place - 1) % RING_SIZE]
        pairs.append((2 * chip, 2 * right))
        pairs.append((2 * chip + 1, 2 * left + 1))
    return pairs


def hop(block):
    return lax.ppermute(block, "cells", ring_pairs())


def to_partner(block):
    return lax.ppermute(block, "cells", [(i, i ^ 1) for i in range(CELLS)])


def across(block):
    return lax.ppermute(block, "species", [(0, 1), (1, 0)])


def exchange(values, bit):
    return values + lax.ppermute(values, "cells", [(i, i ^ bit) for i in range(CELLS)])


def after(value, *others):
    return lax.optimization_barrier((value,) + others)[0]


def here():
    index = lax.axis_index("cells")
    core = index % 2
    chip = index // 2
    place = jnp.int32(0)
    for i, ring_chip in enumerate(RING):
        place = jnp.where(chip == ring_chip, i, place)
    return index, core, place


def chip_at(place):
    place = place % RING_SIZE
    chip = jnp.zeros_like(place)
    for i, ring_chip in enumerate(RING):
        chip = jnp.where(place == i, ring_chip, chip)
    return chip


def gather_order(core, place):
    sign = 1 - 2 * core
    order = []

    def pair(at):
        order.append(2 * chip_at(at))
        order.append(2 * chip_at(at) + 1)

    pair(place)
    for step in range(1, 4):
        pair(place - sign * step)
        pair(place + sign * step)
    order.append(2 * chip_at(place + 4) + core)
    order.append(2 * chip_at(place + 4) + 1 - core)
    return order


def scatter_slots(core, place):
    def kept(core_now):
        sign = 1 - 2 * core_now
        order = [2 * chip_at(place + 4) + core_now]
        for step in (3, 2, 1):
            order.append(2 * chip_at(place + sign * step))
            order.append(2 * chip_at(place + sign * step) + 1)
        order.append(2 * chip_at(place) + core_now)
        return order

    order = kept(core) + kept(1 - core)
    slots = []
    for device in range(CELLS):
        slot = jnp.int32(0)
        for i, who in enumerate(order):
            slot = jnp.where(who == device, i, slot)
        slots.append(slot)
    return slots


def both_blocks(block, core):
    other = to_partner(block)
    return jnp.stack([jnp.where(core == 0, block, other), jnp.where(core == 0, other, block)])


def half_of(pair, core):
    return jnp.where(core == 0, pair[0], pair[1])[None]


def add_low(*parts):
    total = parts[0].astype(FULL)
    for part in parts[1:]:
        total = total + part.astype(FULL)
    return total.astype(LOW)


def first_hop(*parts):
    return hop(add_low(*[part[0:1] for part in parts]))


def second_hop(moving, core, *parts):
    wide = jnp.stack([jnp.where(core == 0, moving[0], 0), jnp.where(core == 0, 0, moving[0])])
    return hop(add_low(wide, *[part[1:3] for part in parts]))


def later_hop(moving, at, *parts):
    return hop(add_low(moving, *[part[at : at + 2] for part in parts]))


def settle(moving, core, *parts):
    mine = jnp.where(core == 0, moving[0], moving[1])
    other = jnp.where(core == 0, moving[1], moving[0])
    return add_low(mine, to_partner(other), *[part[7] for part in parts])


def dot(left, right, dims=((1,), (0,))):
    return lax.dot_general(left, right, (dims, ((), ())), preferred_element_type=FULL)


def call(body, out_shape, ins, specs, out_specs=None, scratch=(), vmem=48, cost=HEAVY):
    return pl.pallas_call(
        body,
        out_shape=out_shape,
        in_specs=specs,
        out_specs=[VMEM] * len(out_shape) if out_specs is None else out_specs,
        scratch_shapes=list(scratch),
        compiler_params=pltpu.CompilerParams(vmem_limit_bytes=vmem * 2**20),
        cost_estimate=pl.CostEstimate(flops=cost, bytes_accessed=0, transcendentals=0),
    )(*ins)


def shape(dims, kind=LOW):
    return jax.ShapeDtypeStruct(dims, kind)


def fetch(order_ref, refs, target, sem):
    rows = target.shape[0] // CELLS
    copies = []
    index = 0
    for source, size in zip(refs, PIECES):
        for part in range(size):
            at = order_ref[index]
            copies.append(
                pltpu.make_async_copy(
                    source.at[part],
                    target.at[pl.ds(pl.multiple_of(at * rows, 16), rows)],
                    sem.at[index],
                )
            )
            index += 1
    for item in copies:
        item.start()
    return copies


def wait_all(copies):
    for item in copies:
        item.wait()


def one_hot(rows, lanes, offset):
    row = lax.broadcasted_iota(jnp.int32, (rows, lanes), 0)
    lane = lax.broadcasted_iota(jnp.int32, (rows, lanes), 1)
    return lane == row + offset


def pack_body(who_ref, lengths_ref, *refs):
    sources, small_ref = refs[:8], refs[8]
    me = who_ref[0]
    model = small_ref.shape[1]
    row = lax.broadcasted_iota(jnp.int32, (SMALL_ROWS, model), 0)
    lane = lax.broadcasted_iota(jnp.int32, (SMALL_ROWS, model), 1)
    small = jnp.zeros((SMALL_ROWS, model), FULL)
    for name, ref in zip(NAMES, sources):
        size = ref.shape[1]
        per_row = model // size
        placed = dot(ref[...], one_hot(size, model, size * (me % per_row)).astype(LOW))
        small = small + jnp.where(row == ROWS[name] + me // per_row, placed, 0.0)
    for i in range(2):
        at = (row == ROWS["lengths"]) & (lane == 2 * me + i)
        small = small + jnp.where(at, lengths_ref[i].astype(FULL), 0.0)
    small_ref[...] = small.astype(LOW)


def norm_parts(values):
    center = values - jnp.mean(values, axis=-1, keepdims=True)
    spread = jnp.mean(center * center, axis=-1, keepdims=True)
    return center, lax.rsqrt(spread + EPSILON)


def norm_back(center, scale, gain, grad):
    weighted = grad * gain
    mean_one = jnp.mean(weighted, axis=-1, keepdims=True)
    mean_two = jnp.mean(weighted * center, axis=-1, keepdims=True)
    back = scale * (weighted - mean_one - center * (scale * scale * mean_two))
    return back, jnp.sum(grad * center * scale, axis=0, keepdims=True), jnp.sum(
        grad, axis=0, keepdims=True
    )


def small_row(small_ref, name, count=1):
    return small_ref[...].astype(FULL)[ROWS[name] : ROWS[name] + count, :]


def project_body(order_ref, x_ref, small_ref, *refs):
    blocks = refs[:9]
    low_ref, proj_ref, weight, sem = refs[9:]
    model = x_ref.shape[1]
    copies = fetch(order_ref, blocks, weight, sem)
    center, scale = norm_parts(x_ref[...].astype(FULL))
    bias = small_row(small_ref, "qv_bias", 2)
    low_ref[...] = (
        center * scale * small_row(small_ref, "first_gain") + small_row(small_ref, "first_shift")
    ).astype(LOW)
    wait_all(copies)
    for j in range(3):
        lanes = slice(j * model, (j + 1) * model)
        part = dot(low_ref[...], weight[:, lanes])
        if j != 1:
            part = part + bias[j // 2 : j // 2 + 1]
        proj_ref[:, lanes] = part.astype(LOW)


def attend_body(seq, lengths_ref, proj_ref, att_ref, mixed_ref):
    model = mixed_ref.shape[1]
    cells = mixed_ref.shape[0] // seq
    pairs = model // (2 * HEAD)
    lane = lax.broadcasted_iota(jnp.int32, (seq, 2 * HEAD), 1)
    key = lax.broadcasted_iota(jnp.int32, (seq, seq), 0)

    def step(index, carry):
        s = index // pairs
        p = index % pairs
        rows = pl.ds(pl.multiple_of(s * seq, seq), seq)
        at = pl.multiple_of(p * 2 * HEAD, 2 * HEAD)
        q = proj_ref[rows, pl.ds(at, 2 * HEAD)] * jnp.asarray(HEAD ** (-0.5), LOW)
        k = proj_ref[rows, pl.ds(at + model, 2 * HEAD)]
        v_turned = proj_ref[rows, pl.ds(at + 2 * model, 2 * HEAD)].T
        visible = key < lengths_ref[s]
        mixed = []
        for i in range(2):
            own = (lane >= i * HEAD) & (lane < (i + 1) * HEAD)
            scores = dot(jnp.where(own, k, jnp.zeros_like(k)), q, ((1,), (1,)))
            scores = jnp.where(visible, scores, NEGATIVE)
            expo = jnp.exp(scores - jnp.max(scores, axis=0, keepdims=True))
            probs = expo * (1.0 / jnp.sum(expo, axis=0, keepdims=True))
            probs = probs.astype(LOW)
            att_ref[2 * index + i] = probs
            mixed.append(dot(v_turned[i * HEAD : (i + 1) * HEAD], probs))
        mixed_ref[rows, pl.ds(at, 2 * HEAD)] = jnp.concatenate(mixed, axis=0).T.astype(LOW)
        return carry

    lax.fori_loop(0, cells * pairs, step, 0, unroll=2)


ERFC_STEP = 0.33
ERFC = (
    0.1863578228018033,
    0.18295566386742124,
    0.2012255082472392,
    0.04721561458875723,
    0.4085089979423051,
    -0.35115900736338407,
    0.4602422572120205,
    -0.13534686486277223,
)


def gelu_parts(inner):
    z = jnp.abs(inner) * (0.5**0.5)
    t = 1.0 / (1.0 + ERFC_STEP * z)
    tail = jnp.full_like(t, 0.5 * ERFC[-1])
    for factor in ERFC[-2::-1]:
        tail = tail * t + 0.5 * factor
    bell = jnp.exp(-(z * z))
    tail = tail * t * bell
    area = jnp.where(inner < 0.0, tail, 1.0 - tail)
    return inner * area, area + inner * bell * (0.5 / 3.141592653589793) ** 0.5


def row_mask(lengths_ref, rows, seq):
    at = lax.broadcasted_iota(jnp.int32, (rows, 1), 0)
    true = (at < lengths_ref[0]).astype(FULL)
    for s in range(1, rows // seq):
        true = jnp.where(at < s * seq, true, (at < lengths_ref[s] + s * seq).astype(FULL))
    return true


def loss_rows(lengths_ref, small_ref, other_ref, cot_ref, seq, whole):
    count = jnp.sum(
        small_row(small_ref, "lengths") + small_row(other_ref, "lengths"), axis=-1, keepdims=True
    )
    return cot_ref[...].astype(FULL) * (
        row_mask(lengths_ref, cot_ref.shape[0], seq) * (whole / count)
    )


def put_slots(keep_buf, slot_ref, values, first, lanes):
    rows = keep_buf.shape[1]
    for i in range(values.shape[0] // rows):
        keep_buf[slot_ref[first + i], :, lanes] = values[i * rows : (i + 1) * rows].astype(LOW)


def send_slots(buf, keep_ref, away_ref, sem):
    half = RING_SIZE
    copies = [
        pltpu.make_async_copy(buf.at[pl.ds(half, half)], away_ref, sem.at[0]),
        pltpu.make_async_copy(buf.at[pl.ds(0, half)], keep_ref, sem.at[1]),
    ]
    for item in copies:
        item.start()
    return copies


def inner_body(order_ref, x_ref, mixed_ref, small_ref, *refs):
    blocks = refs[:9]
    middle_ref, low_ref, active_ref, slope_ref, weight, sem = refs[9:]
    model = x_ref.shape[1]
    ff = active_ref.shape[1]
    wait_all(fetch(order_ref, blocks, weight, sem))
    middle = (
        x_ref[...].astype(FULL)
        + dot(mixed_ref[...], weight[:, ff:])
        + small_row(small_ref, "out_bias")
    )
    middle_ref[...] = middle
    center, scale = norm_parts(middle)
    low = center * scale * small_row(small_ref, "second_gain") + small_row(
        small_ref, "second_shift"
    )
    low_ref[...] = low.astype(LOW)
    step = 2 * (ff // RING_SIZE)
    bias = small_row(small_ref, "in_bias", 4)
    for j in range(ff // step):
        lanes = slice(j * step, (j + 1) * step)
        inner = dot(low_ref[...], weight[:, lanes]) + bias[j : j + 1]
        active, slope = gelu_parts(inner)
        active_ref[:, lanes] = active.astype(LOW)
        slope_ref[:, lanes] = slope.astype(LOW)


def grad_down_body(
    seq, whole, who_ref, slot_ref, lengths_ref, active_ref, cot_ref, small_ref, other_ref,
    up_ref, down_b_ref, keep_ref, away_ref, keep_two_ref, away_two_ref, slots, sem,
):
    up_low = loss_rows(lengths_ref, small_ref, other_ref, cot_ref, seq, whole).astype(LOW)
    up_ref[...] = up_low
    down_b_ref[...] = jnp.sum(up_low.astype(FULL), axis=0, keepdims=True)
    parts = RING_SIZE
    step = active_ref.shape[1] // parts
    rows = slots.shape[2]
    side = who_ref[1]
    for j in range(parts):
        grad = dot(active_ref[:, j * step : (j + 1) * step], up_ref[...], ((0,), (0,)))
        for i in range(4):
            slots[(i + side) % 2, slot_ref[j * CELLS // parts + i // 2]] = grad[
                i * rows : (i + 1) * rows
            ].astype(LOW)
    copies = send_slots(slots.at[1], keep_two_ref, away_two_ref, sem.at[1])
    copies += send_slots(slots.at[0], keep_ref, away_ref, sem.at[0])
    wait_all(copies)


def inner_back_body(order_ref, slope_ref, up_ref, *refs):
    blocks = refs[:9]
    inner_ref, in_b_ref, weight, sem = refs[9:]
    model = up_ref.shape[1]
    wait_all(fetch(order_ref, blocks, weight, sem))
    for j in range(inner_ref.shape[1] // model):
        lanes = slice(j * model, (j + 1) * model)
        grad = dot(up_ref[...], weight[lanes, :], ((1,), (1,)))
        low = (grad * slope_ref[:, lanes].astype(FULL)).astype(LOW)
        inner_ref[:, lanes] = low
        in_b_ref[j : j + 1, :] = jnp.sum(low.astype(FULL), axis=0, keepdims=True)


def down_body(active_ref, middle_ref, small_ref, weight_ref, out_ref):
    out_ref[...] = (
        middle_ref[...]
        + dot(active_ref[...], weight_ref[...])
        + small_row(small_ref, "down_bias")
    ).astype(LOW)


def grad_in_body(slot_ref, low_ref, inner_ref, keep_ref, away_ref, slots, sem):
    model = low_ref.shape[1]
    turned = low_ref[...].T
    for j in range(inner_ref.shape[1] // model):
        lanes = slice(j * model, (j + 1) * model)
        put_slots(slots, slot_ref, dot(turned, inner_ref[:, lanes]), 0, lanes)
    wait_all(send_slots(slots, keep_ref, away_ref, sem))


def middle_back_body(
    seq, whole, lengths_ref, inner_ref, middle_ref, cot_ref, small_ref, other_ref, weight,
    grad_ref, grad_low_ref, grad_mixed_ref, sums_ref,
):
    ff = inner_ref.shape[1]
    grad_second = dot(inner_ref[...], weight[:, :ff], ((1,), (1,)))
    center, scale = norm_parts(middle_ref[...])
    back, gain_sum, shift_sum = norm_back(
        center, scale, small_row(small_ref, "second_gain"), grad_second
    )
    grad = loss_rows(lengths_ref, small_ref, other_ref, cot_ref, seq, whole) + back
    grad_ref[...] = grad
    grad_low = grad.astype(LOW)
    grad_low_ref[...] = grad_low
    grad_mixed_ref[...] = dot(grad_low, weight[:, ff:], ((1,), (1,))).astype(LOW)
    sums_ref[0:1, :] = jnp.sum(grad_low.astype(FULL), axis=0, keepdims=True)
    sums_ref[1:2, :] = gain_sum
    sums_ref[2:3, :] = shift_sum


def attend_back_body(seq, begin, proj_ref, att_ref, grad_ref, out_ref):
    model = grad_ref.shape[1]
    half = out_ref.shape[1] // 3
    all_pairs = model // (2 * HEAD)
    pairs = half // (2 * HEAD)
    cells = grad_ref.shape[0] // seq
    lane = lax.broadcasted_iota(jnp.int32, (seq, 2 * HEAD), 1)
    scale = HEAD ** (-0.5)

    def step(index, carry):
        s = index // pairs
        p = index % pairs
        rows = pl.ds(pl.multiple_of(s * seq, seq), seq)
        to = pl.multiple_of(p * 2 * HEAD, 2 * HEAD)
        at = pl.multiple_of(to + begin * 2 * HEAD, 2 * HEAD)
        q = proj_ref[rows, pl.ds(at, 2 * HEAD)]
        k_turned = proj_ref[rows, pl.ds(at + model, 2 * HEAD)].T
        v = proj_ref[rows, pl.ds(at + 2 * model, 2 * HEAD)]
        g = grad_ref[rows, pl.ds(at, 2 * HEAD)]
        grad_q = []
        grad_k = []
        grad_v = []
        for i in range(2):
            own = (lane >= i * HEAD) & (lane < (i + 1) * HEAD)
            probs = att_ref[2 * (s * all_pairs + begin + p) + i]
            wide = probs.astype(FULL)
            grad_probs = dot(jnp.where(own, v, jnp.zeros_like(v)), g, ((1,), (1,)))
            delta = jnp.sum(wide * grad_probs, axis=0, keepdims=True)
            scores = (wide * (grad_probs - delta)).astype(LOW)
            grad_q.append(dot(k_turned[i * HEAD : (i + 1) * HEAD], scores))
            grad_k.append(dot(scores, q))
            grad_v.append(dot(probs, g))
        first = lane < HEAD
        out_ref[rows, pl.ds(to, 2 * HEAD)] = (
            jnp.concatenate(grad_q, axis=0).T * scale
        ).astype(LOW)
        out_ref[rows, pl.ds(to + half, 2 * HEAD)] = (
            jnp.where(first, grad_k[0], grad_k[1]) * scale
        ).astype(LOW)
        out_ref[rows, pl.ds(to + 2 * half, 2 * HEAD)] = jnp.where(
            first, grad_v[0], grad_v[1]
        ).astype(LOW)
        return carry

    lax.fori_loop(0, cells * pairs, step, 0, unroll=2)


def early_grad_body(
    slot_ref, low_ref, part_ref, mixed_ref, grad_low_ref, keep_ref, away_ref, slots, sem
):
    width = part_ref.shape[1]
    put_slots(slots, slot_ref, dot(low_ref[...].T, part_ref[...]), 0, slice(0, width))
    put_slots(
        slots, slot_ref, dot(mixed_ref[...].T, grad_low_ref[...]), 0,
        slice(width, slots.shape[2]),
    )
    wait_all(send_slots(slots, keep_ref, away_ref, sem))


def first_back_body(
    slot_ref, x_ref, low_ref, one_ref, two_ref, grad_ref, small_ref, sums_ref, in_b_ref,
    down_b_ref, weight, out_ref, keep_ref, away_ref, sum_ref, slots, sem,
):
    model = x_ref.shape[1]
    late = two_ref.shape[1]
    center, scale = norm_parts(x_ref[...].astype(FULL))
    parts = ((one_ref, 0), (two_ref, one_ref.shape[1] // 3))
    grad_first = jnp.zeros(x_ref.shape, FULL)
    for j in range(3):
        for ref, begin in parts:
            width = ref.shape[1] // 3
            at = j * model + begin
            grad_first = grad_first + dot(
                ref[:, j * width : (j + 1) * width], weight[:, at : at + width], ((1,), (1,))
            )
    put_slots(slots, slot_ref, dot(low_ref[...].T, two_ref[...]), 0, slice(0, late))
    back, gain_sum, shift_sum = norm_back(
        center, scale, small_row(small_ref, "first_gain"), grad_first
    )

    def put(name, value, offset=0):
        at = ROWS[name] + offset
        sum_ref[at : at + value.shape[0], :] = value

    sum_ref[...] = jnp.zeros_like(sum_ref)
    put("first_gain", gain_sum)
    put("first_shift", shift_sum)
    for j in range(2):
        at = ROWS["qv_bias"] + j
        for ref, begin in parts:
            width = ref.shape[1] // 3
            part = ref[:, 2 * j * width : (2 * j + 1) * width].astype(FULL)
            sum_ref[at : at + 1, begin : begin + width] = jnp.sum(part, axis=0, keepdims=True)
    put("out_bias", sums_ref[0:1, :])
    put("second_gain", sums_ref[1:2, :])
    put("second_shift", sums_ref[2:3, :])
    put("in_bias", in_b_ref[...])
    put("down_bias", down_b_ref[...])
    for i in range(3):
        part = sum_ref[:, SMALL_LANES * i : SMALL_LANES * (i + 1)].astype(LOW)
        for device in range(CELLS):
            slots[device, 16 * i : 16 * i + 16, late:] = part
    copies = send_slots(slots, keep_ref, away_ref, sem)
    out_ref[...] = (grad_ref[...] + back).astype(LOW)
    wait_all(copies)


def finish_small_body(who_ref, late_ref, late_two_ref, *refs):
    vectors, small_ref = refs[:-1], refs[-1]
    model = small_ref.shape[1]
    first = late_ref.shape[1] - SMALL_LANES
    late = late_ref[:, first:].astype(FULL) + late_two_ref[:, first:].astype(FULL)
    for i in range(3):
        small_ref[:, SMALL_LANES * i : SMALL_LANES * (i + 1)] = late[16 * i : 16 * i + 16]
    me = who_ref[0]
    row = lax.broadcasted_iota(jnp.int32, (SMALL_ROWS, model), 0)
    for name, ref in zip(NAMES, vectors):
        size = ref.shape[1]
        per_row = model // size
        here_row = jnp.where(row == ROWS[name] + me // per_row, small_ref[...], 0.0)
        values = jnp.sum(here_row, axis=0, keepdims=True)
        picker = one_hot(size, model, size * (me % per_row)).astype(FULL)
        ref[...] = lax.dot_general(
            values, picker, (((1,), (1,)), ((), ())), precision=lax.Precision.HIGHEST,
            preferred_element_type=FULL,
        )


def finish_body(early_ref, early_two_ref, late_ref, late_two_ref, grad_ref, out_ref):
    model = out_ref.shape[1]
    early = early_ref[...].astype(FULL) + early_two_ref[...].astype(FULL)
    late = late_ref[...].astype(FULL) + late_two_ref[...].astype(FULL)
    one = (early.shape[1] - model) // 3
    two = (late.shape[1] - SMALL_LANES) // 3
    for j in range(3):
        at = j * model
        grad_ref[:, at : at + one] = early[:, j * one : (j + 1) * one]
        grad_ref[:, at + one : at + model] = late[:, j * two : (j + 1) * two]
    out_ref[...] = early[:, 3 * one :]


def on_device_ring(
    tokens,
    lengths,
    cotangent,
    first_gain,
    first_shift,
    qkv_weight,
    qv_bias,
    out_weight,
    out_bias,
    second_gain,
    second_shift,
    in_weight,
    in_bias,
    down_weight,
    down_bias,
):
    micro, seq, model = tokens.shape[1:]
    total_rows = micro * seq
    rows = qkv_weight.shape[0]
    down_rows = down_weight.shape[0]
    ff = in_weight.shape[1]
    heads = model // HEAD
    whole = float(lax.axis_size("species") * CELLS * micro * seq)
    index, core, place = here()
    species = lax.axis_index("species")
    who = jnp.stack([index, species]).astype(jnp.int32)
    order = jnp.stack(gather_order(core, place)).astype(jnp.int32)
    slot = jnp.stack(scatter_slots(core, place)).astype(jnp.int32)
    lens = lengths.reshape(micro)
    x = tokens.reshape(total_rows, model)
    cot = cotangent.reshape(total_rows, model)
    vectors = (
        first_gain, first_shift, qv_bias, out_bias, second_gain, second_shift, in_bias, down_bias,
    )

    dma = pltpu.SemaphoreType.DMA

    def gathered(own, hops):
        got = [own]
        for item in hops:
            got += [item, to_partner(item)]
        return got

    own = both_blocks(qkv_weight, core)
    qkv_one = hop(own)
    (small,) = call(
        pack_body,
        [shape((SMALL_ROWS, model))],
        [who, after(lens, own)] + [item.reshape(1, -1) for item in vectors],
        [SMEM, SMEM] + [VMEM] * 8,
        vmem=4,
    )
    in_weight, out_weight = lax.optimization_barrier((in_weight, out_weight, own))[:2]
    in_own = both_blocks(jnp.concatenate([in_weight, out_weight], axis=1), core)
    in_one = hop(in_own)
    small = exchange(small, 1)
    qkv_one, small = lax.optimization_barrier((qkv_one, small))
    qkv_two = hop(qkv_one)
    in_two = hop(after(in_one, qkv_one))
    small = exchange(small, 2)
    down_own = both_blocks(after(down_weight, qkv_one), core)
    qkv_two, small, down_own = lax.optimization_barrier((qkv_two, small, down_own))
    qkv_three = hop(qkv_two)
    small = exchange(small, 4)
    qkv_three, small = lax.optimization_barrier((qkv_three, small))
    qkv_last = hop(half_of(qkv_three, core))
    in_three = hop(after(in_two, qkv_three))
    small = exchange(small, 8)
    in_three, small = lax.optimization_barrier((in_three, small))
    in_last = hop(half_of(in_three, core))
    down_one = hop(after(down_own, in_three))
    low, proj, qkv_full = call(
        project_body,
        [
            shape((total_rows, model)),
            shape((total_rows, 3 * model)),
            shape((model, 3 * model)),
        ],
        [order, after(x, in_three), small] + gathered(own, (qkv_one, qkv_two, qkv_three, qkv_last)),
        [SMEM, VMEM, VMEM] + [ANY] * 9,
        scratch=[dma((CELLS,))],
        vmem=14,
    )
    other_small = across(small)
    proj, in_last, other_small, down_one = lax.optimization_barrier(
        (proj, in_last, other_small, down_one)
    )
    down_two = hop(down_one)
    att, mixed = call(
        lambda *refs: attend_body(seq, *refs),
        [shape((micro * heads, seq, seq)), shape((total_rows, model))],
        [lens, proj],
        [SMEM, VMEM],
        vmem=12,
    )
    down_two, mixed = lax.optimization_barrier((down_two, mixed))
    down_three = hop(down_two)
    in_got = gathered(in_own, (in_one, in_two, in_three, in_last))
    middle, low_two, active, slope, in_full = call(
        inner_body,
        [
            shape((total_rows, model), FULL),
            shape((total_rows, model)),
            shape((total_rows, ff)),
            shape((total_rows, ff)),
            shape((model, ff + model)),
        ],
        [order, x, mixed, small] + in_got,
        [SMEM] + [VMEM] * 3 + [ANY] * 9,
        scratch=[dma((CELLS,))],
        vmem=17,
    )
    down_three, active = lax.optimization_barrier((down_three, active))
    down_last = hop(half_of(down_three, core))
    up_low, down_b, down_keep, down_away, down_keep_two, down_away_two = call(
        lambda *refs: grad_down_body(seq, whole, *refs),
        [
            shape((total_rows, model)),
            shape((1, model), FULL),
        ]
        + [shape((RING_SIZE, down_rows // 2, model))] * 4,
        [who, slot, lens, active, cot, small, other_small],
        [SMEM] * 3 + [VMEM] * 4,
        [VMEM] * 2 + [ANY] * 4,
        scratch=[pltpu.VMEM((2, CELLS, down_rows // 2, model), LOW), dma((2, 2))],
        vmem=14,
    )

    down_away, down_away_two, down_last = lax.optimization_barrier(
        (down_away, down_away_two, down_last)
    )
    down_other_two = to_partner(down_away_two)
    down_other = to_partner(down_away)
    inner_low, in_b, down_full = call(
        inner_back_body,
        [
            shape((total_rows, ff)),
            shape((ff // model, model), FULL),
            shape((ff, model)),
        ],
        [order, slope, up_low]
        + gathered(down_own, (down_one, down_two, down_three, down_last)),
        [SMEM] + [VMEM] * 2 + [ANY] * 9,
        scratch=[dma((CELLS,))],
        vmem=15,
    )
    down_other_two, inner_low = lax.optimization_barrier((down_other_two, inner_low))
    down_x = across(add_low(down_keep_two[0:3], down_other_two[0:3]))
    down_x_two = across(add_low(down_keep_two[3:8], down_other_two[3:8]))
    in_keep, in_away = call(
        grad_in_body,
        [shape((RING_SIZE, rows, ff)), shape((RING_SIZE, rows, ff))],
        [slot, low_two, inner_low],
        [SMEM] + [VMEM] * 2,
        [ANY] * 2,
        scratch=[pltpu.VMEM((CELLS, rows, ff), LOW), dma((2,))],
        vmem=12,
    )
    in_other = to_partner(in_away)
    (out_tokens,) = call(
        down_body,
        [shape((total_rows, model))],
        [after(active, in_keep), middle, small, down_full],
        [VMEM] * 4,
        vmem=13,
    )
    in_other, out_tokens, inner_low = lax.optimization_barrier((in_other, out_tokens, inner_low))
    in_sum = first_hop(in_keep, in_other)
    grad_middle, grad_low, grad_mixed, sums = call(
        lambda *refs: middle_back_body(seq, whole, *refs),
        [
            shape((total_rows, model), FULL),
            shape((total_rows, model)),
            shape((total_rows, model)),
            shape((3, model), FULL),
        ],
        [lens, inner_low, middle, cot, small, other_small, in_full],
        [SMEM] + [VMEM] * 6,
        vmem=16,
    )

    def attend_back(begin, pairs, grad):
        return call(
            lambda *refs: attend_back_body(seq, begin, *refs),
            [shape((total_rows, 6 * pairs * HEAD))],
            [proj, att, grad],
            [VMEM] * 3,
            vmem=11,

        )[0]

    pairs = model // (2 * HEAD)
    early_pairs = 2 * pairs // 3
    in_sum, down_x, down_other, grad_mixed = lax.optimization_barrier(
        (in_sum, down_x, down_other, grad_mixed)
    )
    down_sum = first_hop(down_keep, down_other, down_x)
    in_sum = second_hop(in_sum, core, in_keep, in_other)
    grad_one = attend_back(0, early_pairs, grad_mixed)
    down_sum, grad_one = lax.optimization_barrier((down_sum, grad_one))
    down_sum = second_hop(down_sum, core, down_keep, down_other, down_x)
    early_width = 6 * early_pairs * HEAD + model
    early_keep, early_away = call(
        early_grad_body,
        [shape((RING_SIZE, rows, early_width))] * 2,
        [slot, low, grad_one, mixed, grad_low],
        [SMEM] + [VMEM] * 4,
        [ANY] * 2,
        scratch=[pltpu.VMEM((CELLS, rows, early_width), LOW), dma((2,))],
        vmem=12,
    )
    early_other = to_partner(early_away)
    in_sum, early_keep, grad_mixed = lax.optimization_barrier((in_sum, early_keep, grad_mixed))
    in_sum = later_hop(in_sum, 3, in_keep, in_other)
    grad_two = attend_back(early_pairs, pairs - early_pairs, grad_mixed)
    early_other, grad_two = lax.optimization_barrier((early_other, grad_two))
    early_sum = first_hop(early_keep, early_other)
    late_width = 6 * (pairs - early_pairs) * HEAD + SMALL_LANES
    grad_tokens, late_keep, late_away = call(
        first_back_body,
        [
            shape((total_rows, model)),
            shape((RING_SIZE, rows, late_width)),
            shape((RING_SIZE, rows, late_width)),
        ],
        [slot, x, low, grad_one, grad_two, grad_middle, small, sums, in_b, down_b, qkv_full],
        [SMEM] + [VMEM] * 10,
        [VMEM] + [ANY] * 2,
        scratch=[
            pltpu.VMEM((SMALL_ROWS, model), FULL),
            pltpu.VMEM((CELLS, rows, late_width), LOW),
            dma((2,)),
        ],
        vmem=14,

    )
    late_other = to_partner(late_away)
    in_sum, early_sum, late_keep, down_sum, down_x_two = lax.optimization_barrier(
        (in_sum, early_sum, late_keep, down_sum, down_x_two)
    )
    in_sum = later_hop(in_sum, 5, in_keep, in_other)
    early_sum = second_hop(early_sum, core, early_keep, early_other)
    down_sum = hop(add_low(down_sum, down_keep[3:5], down_other[3:5], down_x_two[0:2]))
    late_sum = first_hop(late_keep, late_other)
    late_sum, early_sum, down_sum = lax.optimization_barrier((late_sum, early_sum, down_sum))
    down_sum = hop(add_low(down_sum, down_keep[5:7], down_other[5:7], down_x_two[2:4]))
    late_sum = second_hop(late_sum, core, late_keep, late_other)
    early_sum = later_hop(early_sum, 3, early_keep, early_other)
    late_sum, early_sum, down_sum, in_sum = lax.optimization_barrier(
        (late_sum, early_sum, down_sum, in_sum)
    )
    late_sum = later_hop(late_sum, 3, late_keep, late_other)
    early_sum = later_hop(early_sum, 5, early_keep, early_other)
    in_sum = settle(in_sum, core, in_keep, in_other)
    in_terms = (in_sum, across(in_sum))
    mine = jnp.where(core == 0, down_sum[0], down_sum[1])
    other = to_partner(jnp.where(core == 0, down_sum[1], down_sum[0]))
    down_sum = add_low(mine, other, down_keep[7], down_other[7], down_x_two[4])
    down_terms = (down_sum, across(down_sum))
    late_sum = later_hop(late_sum, 5, late_keep, late_other)
    early_sum = settle(early_sum, core, early_keep, early_other)
    early_terms = (early_sum, across(early_sum))
    late_sum = settle(late_sum, core, late_keep, late_other)
    late_terms = (late_sum, across(late_sum))
    small_terms = lax.optimization_barrier(late_terms + (early_terms[0],))[:2]
    in_last_terms = lax.optimization_barrier(in_terms + (early_terms[0],))[:2]
    pieces = call(
        finish_small_body,
        [shape((1, item.shape[0]), FULL) for item in vectors],
        [who] + list(small_terms),
        [SMEM] + [VMEM] * 2,
        scratch=[pltpu.VMEM((SMALL_ROWS, model), FULL)],
        vmem=6,
    )
    pieces = [item.reshape(-1) for item in pieces]
    grad_qkv, grad_out = call(
        finish_body,
        [shape((rows, 3 * model), FULL), shape((rows, model), FULL)],
        list(early_terms) + list(late_terms),
        [VMEM] * 4,
        vmem=6,
    )
    return (
        out_tokens.reshape(tokens.shape),
        grad_tokens.reshape(tokens.shape),
        pieces[0],
        pieces[1],
        grad_qkv,
        pieces[2],
        grad_out,
        pieces[3],
        pieces[4],
        pieces[5],
        in_last_terms[0].astype(FULL) + in_last_terms[1].astype(FULL),
        pieces[6],
        jnp.concatenate(
            [
                jnp.where(species == 0, down_terms[0], down_terms[1]),
                jnp.where(species == 0, down_terms[1], down_terms[0]),
            ]
        ).astype(FULL),
        pieces[7],
    )


def on_device(
    tokens,
    lengths,
    cotangent,
    first_gain,
    first_shift,
    qkv_weight,
    qv_bias,
    out_weight,
    out_bias,
    second_gain,
    second_shift,
    in_weight,
    in_bias,
    down_weight,
    down_bias,
):
    local_count = jnp.sum(lengths).astype(jnp.float32)
    count = lax.psum(local_count, ("species", "cells"))
    micro_count = tokens.shape[1]
    seq_rows = tokens.shape[2]
    factor = (
        float(lax.axis_size("species") * lax.axis_size("cells") * micro_count * seq_rows) / count
    )
    output_rows = []
    gradient_rows = []
    summed = None
    for micro_step in range(micro_count):
        gathered = (
            lax.all_gather(first_gain, "cells", axis=0, tiled=True),
            lax.all_gather(first_shift, "cells", axis=0, tiled=True),
            lax.all_gather(qkv_weight, "cells", axis=0, tiled=True),
            lax.all_gather(qv_bias, "cells", axis=0, tiled=True),
            lax.all_gather(out_weight, "cells", axis=0, tiled=True),
            lax.all_gather(out_bias, "cells", axis=0, tiled=True),
            lax.all_gather(second_gain, "cells", axis=0, tiled=True),
            lax.all_gather(second_shift, "cells", axis=0, tiled=True),
            lax.all_gather(in_weight, "cells", axis=0, tiled=True),
            lax.all_gather(in_bias, "cells", axis=0, tiled=True),
            lax.all_gather(down_weight, "cells", axis=0, tiled=True),
            lax.all_gather(down_bias, "cells", axis=0, tiled=True),
        )
        out_seq, grad_seq, grads = sequence_pass(
            gathered,
            tokens[0, micro_step],
            lengths[0, micro_step],
            cotangent[0, micro_step],
            factor,
        )
        output_rows.append(out_seq)
        gradient_rows.append(grad_seq)
        shares = (
            lax.psum_scatter(grads[0], "cells", scatter_dimension=0, tiled=True),
            lax.psum_scatter(grads[1], "cells", scatter_dimension=0, tiled=True),
            lax.psum_scatter(grads[2], "cells", scatter_dimension=0, tiled=True),
            lax.psum_scatter(grads[3], "cells", scatter_dimension=0, tiled=True),
            lax.psum_scatter(grads[4], "cells", scatter_dimension=0, tiled=True),
            lax.psum_scatter(grads[5], "cells", scatter_dimension=0, tiled=True),
            lax.psum_scatter(grads[6], "cells", scatter_dimension=0, tiled=True),
            lax.psum_scatter(grads[7], "cells", scatter_dimension=0, tiled=True),
            lax.psum_scatter(grads[8], "cells", scatter_dimension=0, tiled=True),
            lax.psum_scatter(grads[9], "cells", scatter_dimension=0, tiled=True),
            lax.psum_scatter(grads[10], "cells", scatter_dimension=0, tiled=True),
            lax.psum_scatter(grads[11], "cells", scatter_dimension=0, tiled=True),
        )
        summed = shares if summed is None else jax.tree.map(jnp.add, summed, shares)
    final = (
        lax.psum(summed[0].astype(jnp.bfloat16), "species").astype(jnp.float32),
        lax.psum(summed[1].astype(jnp.bfloat16), "species").astype(jnp.float32),
        lax.psum(summed[2].astype(jnp.bfloat16), "species").astype(jnp.float32),
        lax.psum(summed[3].astype(jnp.bfloat16), "species").astype(jnp.float32),
        lax.psum(summed[4].astype(jnp.bfloat16), "species").astype(jnp.float32),
        lax.psum(summed[5].astype(jnp.bfloat16), "species").astype(jnp.float32),
        lax.psum(summed[6].astype(jnp.bfloat16), "species").astype(jnp.float32),
        lax.psum(summed[7].astype(jnp.bfloat16), "species").astype(jnp.float32),
        lax.psum(summed[8].astype(jnp.bfloat16), "species").astype(jnp.float32),
        lax.psum(summed[9].astype(jnp.bfloat16), "species").astype(jnp.float32),
        lax.psum(summed[10].astype(jnp.bfloat16), "species").astype(jnp.float32),
        lax.psum(summed[11].astype(jnp.bfloat16), "species").astype(jnp.float32),
    )
    out_tokens = jnp.stack(output_rows)[None]
    grad_tokens = jnp.stack(gradient_rows)[None]
    return (out_tokens, grad_tokens) + tuple(final)


def solution(mesh):
    in_specs = (
        P("species", "cells", None, None),
        P("species", "cells"),
        P("species", "cells", None, None),
        P("cells"),
        P("cells"),
        P("cells", None),
        P("cells"),
        P("cells", None),
        P("cells"),
        P("cells"),
        P("cells"),
        P("cells", None),
        P("cells"),
        P("cells", None),
        P("cells"),
    )
    out_specs = (
        P("species", "cells", None, None),
        P("species", "cells", None, None),
        P("cells"),
        P("cells"),
        P("cells", None),
        P("cells"),
        P("cells", None),
        P("cells"),
        P("cells"),
        P("cells"),
        P("cells", None),
        P("cells"),
        P("cells", None),
        P("cells"),
    )
    program = on_device_ring if mesh.shape["cells"] == 2 * RING_SIZE else on_device
    return jax.shard_map(
        program, mesh=mesh, in_specs=in_specs, out_specs=out_specs, check_vma=False
    )
```
